32 devices in a mesh: dp: 16 (over z, x, core), seq: 2 (over y).
Axes of the slice: x: 2, y: 2, z: 4, core: 2. Of those that a mesh axis runs over, the one named last changes fastest.
Arguments:
- activations: bfloat16 [32, 2048, 512], P('dp', 'seq'), may hold values from -1.5 to 1.5
- segments: int32 [32, 2048], P('dp', 'seq'), may hold values from 0 to 7, as said below
- first_gain: float32 [512], replicated, may hold values from 0.5 to 1.5
- first_shift: float32 [512], replicated, may hold values from -1.5 to 1.5
- input_weight: bfloat16 [512, 1536], replicated, may hold values from -0.25 to 0.25
- query_bias: float32 [512], replicated, may hold values from -1.5 to 1.5
- value_bias: float32 [512], replicated, may hold values from -1.5 to 1.5
- output_weight: bfloat16 [512, 512], replicated, may hold values from -4 to 4
- output_bias: float32 [512], replicated, may hold values from -2.5 to 2.5
- second_gain: float32 [512], replicated, may hold values from 0.5 to 1.5
- second_shift: float32 [512], replicated, may hold values from -1.5 to 1.5
- expand_weight: bfloat16 [512, 2048], replicated, may hold values from -0.25 to 0.25
- expand_bias: float32 [2048], replicated, may hold values from -1.5 to 1.5
- reduce_weight: bfloat16 [2048, 512], replicated, may hold values from -0.5 to 0.5
- reduce_bias: float32 [512], replicated, may hold values from -2.5 to 2.5
- cotangent: bfloat16 [32, 2048, 512], P('dp', 'seq'), may hold values from -6 to 6
Outputs:
- result: bfloat16 [32, 2048, 512], P('dp', 'seq')
- input_gradient: float32 [32, 2048, 512], P('dp', 'seq')
- first_gain_gradient: float32 [512], replicated
- first_shift_gradient: float32 [512], replicated
- input_weight_gradient: float32 [512, 1536], replicated
- query_bias_gradient: float32 [512], replicated
- value_bias_gradient: float32 [512], replicated
- output_weight_gradient: float32 [512, 512], replicated
- output_bias_gradient: float32 [512], replicated
- second_gain_gradient: float32 [512], replicated
- second_shift_gradient: float32 [512], replicated
- expand_weight_gradient: float32 [512, 2048], replicated
- expand_bias_gradient: float32 [2048], replicated
- reduce_weight_gradient: float32 [2048, 512], replicated
- reduce_bias_gradient: float32 [512], replicated
The draws below stay inside these ranges and needn't reach their ends.
Inputs may be any that keep to these rules, and one draw needn't show every extreme that they name: `segments`: within each row, segment numbers start at 0 and rise by 0 or 1 from one position to the next; they never exceed 7.
All inputs are finite; a program needn't handle non-finite values.
Results may differ from the reference program's by a relative error of at most 0.018.
Values may be sent and summed in bfloat16 or wider, within the bound.
No kernel may reach another device: no remote copies, remote signals or barrier semaphores. Data moves between devices by JAX's collectives and lax.ppermute only.
A program may use at most 384 MiB of HBM per device.

```python
import jax
import jax.numpy as jnp
from jax import lax

D = 512
H = 8
HD = 64
FF = 2048
DEPTH = 48
ROWS_DEV = 2
LEN = 2048
ROWS = 32


def draw_segments(key, part):
    key = jax.random.fold_in(key, 11)
    first_key, second_key = jax.random.split(key)
    spacing = max(LEN // 4, 2)
    breaks = jax.random.randint(first_key, (ROWS, LEN), 0, spacing) == 0
    column = jnp.arange(LEN, dtype=jnp.int32)[None, :]
    breaks = breaks & (column > 0)
    chosen = jax.random.randint(second_key, (ROWS // ROWS_DEV,), 0, ROWS_DEV)
    row_index = jnp.arange(ROWS, dtype=jnp.int32)
    inner = row_index % ROWS_DEV
    group_pick = chosen[row_index // ROWS_DEV]
    single = inner == group_pick
    forced_row = inner == (group_pick + 1) % ROWS_DEV
    forced_col = (column % (LEN // 8) == 0) & (column > 0)
    breaks = breaks | forced_row[:, None] & forced_col
    breaks = breaks & jnp.logical_not(single[:, None])
    counted = jnp.cumsum(breaks.astype(jnp.int32), axis=1)
    return jnp.minimum(counted, 7).astype(jnp.int32)


def steps_of(rng, shape, cuts, smallest, high):
    loudness = 1.0
    for axis_at, blocks in cuts:
        draws = jax.random.uniform(jax.random.fold_in(jax.random.fold_in(rng, 6), axis_at), (blocks,), jnp.float32, smallest / len(cuts), high / len(cuts))
        loudness = loudness * jnp.repeat(jnp.exp(draws), shape[axis_at] // blocks).reshape((-1,) + (1,) * (len(shape) - 1 - axis_at))
    return loudness


def normal_values(rng, dims, deviation, most, cuts=(), kind=jnp.bfloat16):
    drawn = deviation * jax.random.normal(rng, dims, jnp.float32)
    if cuts:
        drawn = drawn * steps_of(rng, dims, cuts, -0.22, 0.18)
    return jnp.clip(drawn, -most, most).astype(kind)


def setup_inputs(seed: int = 0) -> dict:
    keys = jax.random.split(jax.random.key(seed), 17)
    activations = normal_values(keys[0], (ROWS, LEN, D), 0.25, 1.5, ((0, 16), (1, 2)))
    segments = draw_segments(jax.random.fold_in(keys[16], 71), 0)
    first_gain = jnp.clip(1.0 + 0.1 * jax.random.normal(keys[2], (D,), jnp.float32), 0.5, 1.5)
    first_shift = normal_values(keys[3], (D,), 0.3, 1.5, (), jnp.float32)
    input_weight = normal_values(keys[4], (D, 3 * D), D ** -0.5, 0.25)
    query_bias = normal_values(keys[5], (D,), 0.3, 1.5, (), jnp.float32)
    value_bias = normal_values(keys[6], (D,), 0.3, 1.5, (), jnp.float32)
    output_weight = normal_values(keys[7], (D, D), 2 ** -0.5, 4.0)
    output_bias = normal_values(keys[8], (D,), 0.5, 2.5, (), jnp.float32)
    second_gain = jnp.clip(1.0 + 0.1 * jax.random.normal(keys[9], (D,), jnp.float32), 0.5, 1.5)
    second_shift = normal_values(keys[10], (D,), 0.3, 1.5, (), jnp.float32)
    expand_weight = normal_values(keys[11], (D, FF), D ** -0.5, 0.25)
    expand_bias = normal_values(keys[12], (FF,), 0.3, 1.5, (), jnp.float32)
    reduce_weight = normal_values(keys[13], (FF, D), (FF // 16) ** -0.5, 0.5)
    reduce_bias = normal_values(keys[14], (D,), 0.5, 2.5, (), jnp.float32)
    cotangent = normal_values(keys[15], (ROWS, LEN, D), 1.0, 6.0, ((0, 16), (1, 2)))
    return {"activations": activations, "segments": segments, "first_gain": first_gain, "first_shift": first_shift, "input_weight": input_weight, "query_bias": query_bias, "value_bias": value_bias, "output_weight": output_weight, "output_bias": output_bias, "second_gain": second_gain, "second_shift": second_shift, "expand_weight": expand_weight, "expand_bias": expand_bias, "reduce_weight": reduce_weight, "reduce_bias": reduce_bias, "cotangent": cotangent}


@jax.custom_vjp
def low(v):
    return lax.optimization_barrier(v.astype(jnp.bfloat16)).astype(jnp.float32)

@jax.custom_vjp
def low_back(v):
    return v

def low_keep(v):
    return (low(v), None)

def low_pass(kept, grad):
    return (grad,)

def back_keep(v):
    return (v, None)

def back_low(kept, grad):
    return (low(grad),)
low.defvjp(low_keep, low_pass)
low_back.defvjp(back_keep, back_low)
EPSILON = 1e-05
NEGATIVE = -1e+30
HIGHEST = lax.Precision.HIGHEST

def layer_norm(values, gain_vec, shift_vec):
    center = lax.optimization_barrier(jnp.mean(values, -1, keepdims=True))
    centered = values - center
    variance = lax.optimization_barrier(jnp.mean(centered * centered, -1, keepdims=True))
    return centered * lax.rsqrt(variance + EPSILON) * gain_vec + shift_vec

def matmul(left, right):
    return jnp.dot(left, right, precision=HIGHEST)

def attend_head(element):
    queries, keys_head, values_head, segment_row = element
    raw_scores = low_back(matmul(queries, keys_head.T))
    scores = raw_scores * HD ** (-0.5)
    places = jnp.arange(queries.shape[0], dtype=jnp.int32)
    allowed = (segment_row[:, None] == segment_row[None, :]) & (places[None, :] <= places[:, None])
    scores = jnp.where(allowed, scores, NEGATIVE)
    row_max = lax.optimization_barrier(jnp.max(scores, -1, keepdims=True))
    exponent = jnp.where(allowed, jnp.exp(scores - row_max), 0.0)
    weights = exponent / lax.optimization_barrier(jnp.sum(exponent, -1, keepdims=True))
    return matmul(low(weights), values_head)

def split_heads(block):
    row_count, length, width = block.shape
    return block.reshape(row_count, length, H, HD).transpose(0, 2, 1, 3).reshape(row_count * H, length, HD)

def merge_heads(block, row_count):
    length = block.shape[1]
    return block.reshape(row_count, H, length, HD).transpose(0, 2, 1, 3).reshape(row_count, length, H * HD)

def forward(values_in, segment_rows, params):
    first_gain, first_shift, input_weight, query_bias, value_bias, output_weight, output_bias, second_gain, second_shift, expand_weight, expand_bias, reduce_weight, reduce_bias = params
    row_count = values_in.shape[0]
    branch = DEPTH ** (-0.5)
    normed = low(layer_norm(values_in, first_gain, first_shift))
    bias_all = jnp.concatenate([query_bias, jnp.zeros_like(query_bias), value_bias])
    projected = low(low_back(matmul(normed.reshape(-1, D), input_weight) + bias_all))
    projected = projected.reshape(row_count, -1, 3 * D)
    heads_out = lax.map(jax.checkpoint(attend_head), (split_heads(projected[..., :D]), split_heads(projected[..., D:2 * D]), split_heads(projected[..., 2 * D:]), jnp.repeat(segment_rows, H, axis=0)))
    attended = low(low_back(merge_heads(heads_out, row_count)))
    mixed_out = low_back(matmul(attended.reshape(-1, D), output_weight) + output_bias)
    middle = values_in + branch * mixed_out.reshape(values_in.shape)
    second_low = low(layer_norm(middle, second_gain, second_shift))
    expanded = low_back(matmul(second_low.reshape(-1, D), expand_weight) + expand_bias)
    hidden = low(jax.nn.gelu(expanded, approximate=True))
    reduced = low_back(matmul(hidden, reduce_weight) + reduce_bias)
    return middle + branch * reduced.reshape(values_in.shape)

def reference(activations, segments, first_gain, first_shift, input_weight, query_bias, value_bias, output_weight, output_bias, second_gain, second_shift, expand_weight, expand_bias, reduce_weight, reduce_bias, cotangent):
    params = tuple((argument.astype(jnp.float32) for argument in (first_gain, first_shift, input_weight, query_bias, value_bias, output_weight, output_bias, second_gain, second_shift, expand_weight, expand_bias, reduce_weight, reduce_bias)))
    pair_count = activations.shape[0] // 2
    length = activations.shape[1]
    grouped_in = activations.reshape(pair_count, 2, length, D)
    grouped_seg = segments.reshape(pair_count, 2, length)
    grouped_cot = cotangent.reshape(pair_count, 2, length, D)

    def step_pair(totals, element):
        block_in, block_seg, block_cot = element

        def apply_layer(values_in, weights_all):
            return forward(values_in, block_seg, weights_all)
        output, pullback = jax.vjp(apply_layer, block_in.astype(jnp.float32), params)
        input_grad, weight_grads = pullback(block_cot.astype(jnp.float32))
        totals = tuple((running + increment for running, increment in zip(totals, weight_grads)))
        return (totals, (output.astype(jnp.bfloat16), input_grad))
    start = tuple((jnp.zeros_like(argument) for argument in params))
    totals, (outputs, input_grads) = lax.scan(step_pair, start, (grouped_in, grouped_seg, grouped_cot))
    return (outputs.reshape(activations.shape), input_grads.reshape(activations.shape), totals[0], totals[1], totals[2], totals[3], totals[4], totals[5], totals[6], totals[7], totals[8], totals[9], totals[10], totals[11], totals[12])
```

```python
import functools

import jax
import jax.numpy as jnp
from jax import lax
from jax.experimental import pallas as pl
from jax.experimental.pallas import tpu as pltpu
from jax.sharding import PartitionSpec as P

H = 8
HD = 64
DEPTH = 48
MICRO = 2
EPSILON = 1e-05
NEGATIVE = -1e30
BRANCH = DEPTH ** (-0.5)
SCALE = HD ** (-0.5)
SCALE2 = SCALE * 1.4426950408889634
GELU_A = 0.7978845608028654
GELU_B = GELU_A * 0.044715

BF = jnp.bfloat16
F32 = jnp.float32
NN = (((1,), (0,)), ((), ()))
NT = (((1,), (1,)), ((), ()))
VMEM_LIMIT = 58 << 20


def mm(left, right, dims=NN):
    return lax.dot_general(left, right, dims, preferred_element_type=F32)


def shape_of(dims, dtype):
    return jax.ShapeDtypeStruct(dims, dtype)


def params(limit=VMEM_LIMIT):
    return pltpu.CompilerParams(vmem_limit_bytes=limit)


def norm_parts(values):
    center = jnp.mean(values, -1, keepdims=True)
    centered = values - center
    variance = jnp.mean(centered * centered, -1, keepdims=True)
    scale = lax.rsqrt(variance + EPSILON)
    return centered * scale, scale


def norm_back(grad, unit, scale, gain):
    inner = grad * gain
    first = jnp.mean(inner, -1, keepdims=True)
    second = jnp.mean(inner * unit, -1, keepdims=True)
    return scale * (inner - first - unit * second)


def project_kernel(place, x_ref, gain_ref, shift_ref, weight_ref, bias_ref, *refs):
    full_ref, q_ref, k_ref, v_ref, kt_ref, vt_ref = refs[-6:]
    x = x_ref[...]
    unit, _ = norm_parts(x.astype(F32))
    normed = (unit * gain_ref[...] + shift_ref[...]).astype(BF)
    width = x.shape[1]
    out = (mm(normed, weight_ref[...]) + bias_ref[...]).astype(BF)
    full_ref[...] = x
    q_ref[...] = out[:, :width]
    k_ref[...] = out[:, width : 2 * width]
    v_ref[...] = out[:, 2 * width :]
    kt_ref[...] = out[:, width : 2 * width].T
    vt_ref[...] = out[:, 2 * width :].T


def project(half, x, gain, shift, weight, bias, before, tile):
    span, width = x.shape
    count = span // tile
    length = 2 * span
    fixed = lambda dims: pl.BlockSpec(dims, lambda t, h: (0, 0))
    rows = pl.BlockSpec((tile, width), lambda t, h: (h[0] * count + t, 0))
    cols = pl.BlockSpec((width, tile), lambda t, h: (0, h[0] * count + t))
    in_specs = [
        pl.BlockSpec((tile, width), lambda t, h: (t, 0)),
        fixed((1, width)),
        fixed((1, width)),
        fixed(weight.shape),
        fixed((1, 3 * width)),
    ]
    aliases = {}
    if before is not None:
        in_specs += [pl.BlockSpec(memory_space=pl.ANY)] * 6
        aliases = {6 + i: i for i in range(6)}
    nat, trn = shape_of((length, width), BF), shape_of((width, length), BF)
    return pl.pallas_call(
        project_kernel,
        grid_spec=pltpu.PrefetchScalarGridSpec(
            num_scalar_prefetch=1,
            grid=(count,),
            in_specs=in_specs,
            out_specs=[rows, rows, rows, rows, cols, cols],
        ),
        out_shape=[nat, nat, nat, nat, trn, trn],
        input_output_aliases=aliases,
        compiler_params=params(),
        name="project",
    )(half, x, gain, shift, weight, bias, *(before or ()))


def following(i, j, low_ref, count):
    ends = j == i
    after = jnp.where(ends, jnp.minimum(i + 1, count - 1), i)
    return after, jnp.where(ends, low_ref[after], j + 1)


def head_half(block, head):
    lane = lax.broadcasted_iota(jnp.int32, block.shape, 1)
    keep = (lane < HD) if head % 2 == 0 else (lane >= HD)
    return jnp.where(keep, block, jnp.zeros_like(block))


def pair_lanes(head):
    low = 2 * HD * (head // 2)
    return slice(low, low + 2 * HD)


class Blocks:
    def __init__(self, size, low_ref, mid_ref, start_ref, bias_ref):
        self.size, self.low, self.mid = size, low_ref, mid_ref
        self.start, self.bias = start_ref, bias_ref
        self.count = low_ref.shape[0]

    def at(self, index):
        return pl.ds(pl.multiple_of(index * self.size, self.size), self.size)

    def fill(self, slot, i, j):
        dims = (self.size, self.size)
        key = j * self.size + lax.broadcasted_iota(jnp.int32, dims, 0)
        query = i * self.size + lax.broadcasted_iota(jnp.int32, dims, 1)
        allowed = (key >= self.start[0:1, self.at(i)]) & (key <= query)
        self.bias[slot] = jnp.where(allowed, 0.0, NEGATIVE)

    def walk(self, steps, groups, early, late, row_end=None):
        self.bias[0] = jnp.zeros(self.bias.shape[1:], F32)
        self.fill(1, 0, 0)
        early(0, 0, 0, 1)

        def body(step, carry):
            i, j, slot = carry
            ni, nj = following(i, j, self.low, self.count)
            masked = (nj == ni) | (nj < self.mid[ni])
            other = 1 + lax.rem(step + 1, 2)
            nslot = jnp.where(masked, other, 0)

            @pl.when(masked)
            def _():
                self.fill(other, ni, nj)

            for head in range(groups):
                if head + 1 < groups:
                    early(head + 1, i, j, slot)
                else:
                    early(0, ni, nj, nslot)
                late(head, i, j)
            if row_end is not None:
                pl.when(j == i)(lambda: row_end(i))
            return ni, nj, nslot

        zero = jnp.int32(0)
        lax.fori_loop(0, steps, body, (zero, zero, jnp.int32(1)))


def forward_kernel(
    size, groups, low_ref, mid_ref, steps_ref, q_ref, k_ref, vt_ref, start_ref,
    out_ref, lse_ref, max_ref, new_ref, acc_ref, bias_ref, *scores,
):
    walk = Blocks(size, low_ref, mid_ref, start_ref, bias_ref)
    ones = jnp.ones((16, size), BF)

    def early(head, i, j, slot):
        lanes = pair_lanes(head)
        s = mm(head_half(k_ref[walk.at(j), lanes], head), q_ref[walk.at(i), lanes], NT)
        s = s + bias_ref[slot]
        scores[head][...] = s
        new_ref[head : head + 1, :] = jnp.max(s, 0, keepdims=True)

    def late(head, i, j):
        old = max_ref[head : head + 1, :]
        new = jnp.maximum(old, new_ref[head : head + 1, :])
        max_ref[head : head + 1, :] = new
        probs = jnp.exp2(scores[head][...] * SCALE2 - new * SCALE2)
        factor = jnp.exp2((old - new) * SCALE2)
        values = jnp.concatenate([vt_ref[HD * head : HD * head + HD, walk.at(j)], ones], 0)
        acc_ref[head] = acc_ref[head] * factor + mm(values, probs.astype(BF))

    def reset():
        max_ref[...] = jnp.full(max_ref.shape, NEGATIVE, F32)
        acc_ref[...] = jnp.zeros(acc_ref.shape, F32)

    def row_end(i):
        for head in range(groups):
            total = acc_ref[head, HD : HD + 1, :]
            out_ref[HD * head : HD * head + HD, walk.at(i)] = acc_ref[head, :HD, :] * (1.0 / total)
            lse_ref[0, head : head + 1, walk.at(i)] = max_ref[
                head : head + 1, :
            ] * SCALE2 + jnp.log2(total)
        reset()

    reset()
    walk.walk(steps_ref[0], groups, early, late, row_end)


def attend(tables, q, k, vt, start, size, groups):
    length, width = q.shape
    part = HD * groups
    calls = H // groups
    nat = pl.BlockSpec((length, part), lambda p, *_: (0, p))
    trn = pl.BlockSpec((part, length), lambda p, *_: (p, 0))
    return pl.pallas_call(
        functools.partial(forward_kernel, size, groups),
        grid_spec=pltpu.PrefetchScalarGridSpec(
            num_scalar_prefetch=3,
            grid=(calls,),
            in_specs=[nat, nat, trn, pl.BlockSpec((1, length), lambda p, *_: (0, 0))],
            out_specs=[trn, pl.BlockSpec((1, groups, length), lambda p, *_: (p, 0, 0))],
            scratch_shapes=[
                pltpu.VMEM((8, size), F32),
                pltpu.VMEM((8, size), F32),
                pltpu.VMEM((groups, HD + 16, size), F32),
                pltpu.VMEM((3, size, size), F32),
            ]
            + [pltpu.VMEM((size, size), F32)] * groups,
        ),
        out_shape=[shape_of((width, length), F32), shape_of((calls, groups, length), F32)],
        compiler_params=params(),
        name="attend",
    )(*tables, q, k, vt, start)


def backward_kernel(
    size, groups, low_ref, mid_ref, steps_ref, q_ref, k_ref, kt_ref, v_ref, do_ref, start_ref,
    lse_ref, delta_ref, dq_ref, dk_ref, dv_ref, dqt_acc, dk_acc, dv_acc, bias_ref, *slots,
):
    walk = Blocks(size, low_ref, mid_ref, start_ref, bias_ref)
    probs_of, grads_of = slots[:groups], slots[groups:]

    def early(head, i, j, slot):
        lanes = pair_lanes(head)
        s = mm(head_half(k_ref[walk.at(j), lanes], head), q_ref[walk.at(i), lanes], NT)
        dots = mm(head_half(v_ref[walk.at(j), lanes], head), do_ref[walk.at(i), lanes], NT)
        probs = jnp.exp2((s + bias_ref[slot]) * SCALE2 - lse_ref[0, head : head + 1, walk.at(i)])
        probs_of[head][...] = probs.astype(BF)
        grads_of[head][...] = (probs * (dots - delta_ref[0, head : head + 1, walk.at(i)])).astype(
            BF
        )

    def late(head, i, j):
        lanes = pair_lanes(head)
        rows = slice(HD * head, HD * head + HD)
        grads = grads_of[head][...]
        dv_acc[walk.at(j), lanes] += mm(
            probs_of[head][...], head_half(do_ref[walk.at(i), lanes], head)
        )
        dk_acc[walk.at(j), lanes] += mm(grads, head_half(q_ref[walk.at(i), lanes], head))
        dqt_acc[rows, walk.at(i)] += mm(kt_ref[rows, walk.at(j)], grads)

    for acc in (dqt_acc, dk_acc, dv_acc):
        acc[...] = jnp.zeros(acc.shape, F32)
    walk.walk(steps_ref[0], groups, early, late)
    dq_ref[...] = (dqt_acc[...] * SCALE).T.astype(BF)
    dk_ref[...] = (dk_acc[...] * SCALE).astype(BF)
    dv_ref[...] = dv_acc[...].astype(BF)


def attend_back(tables, q, k, kt, v, do, start, lse, delta, size, groups):
    length, width = q.shape
    part = HD * groups
    calls = H // groups
    nat = pl.BlockSpec((length, part), lambda p, *_: (0, p))
    trn = pl.BlockSpec((part, length), lambda p, *_: (p, 0))
    stat = pl.BlockSpec((1, groups, length), lambda p, *_: (p, 0, 0))
    return pl.pallas_call(
        functools.partial(backward_kernel, size, groups),
        grid_spec=pltpu.PrefetchScalarGridSpec(
            num_scalar_prefetch=3,
            grid=(calls,),
            in_specs=[
                nat, nat, trn, nat, nat, pl.BlockSpec((1, length), lambda p, *_: (0, 0)), stat, stat,
            ],
            out_specs=[nat] * 3,
            scratch_shapes=[
                pltpu.VMEM((part, length), F32),
                pltpu.VMEM((length, part), F32),
                pltpu.VMEM((length, part), F32),
                pltpu.VMEM((3, size, size), F32),
            ]
            + [pltpu.VMEM((size, size), BF)] * (2 * groups),
        ),
        out_shape=[shape_of((length, width), BF)] * 3,
        compiler_params=params(),
        name="attend_back",
    )(
        *tables, q, k, kt, v, do, start,
        lse.reshape(calls, groups, length), delta.reshape(calls, groups, length),
    )


def middle_kernel(
    chunk, tiles, half_ref, att_ref, x_ref, cot_ref, wo_ref, ob_ref, g2_ref, s2_ref, we_ref, wet_ref,
    eb_ref, wr_ref, wrt_ref, rb_ref, res_own, res_send, mid_ref, ag_ref, delta_ref, dwr_ref, dwe_ref,
    dwo_ref, vec_ref, deb_acc, hid_a, hid_b, exg_a, exg_b,
):
    step = pl.program_id(0)
    hidden_of, grad_of = (hid_a, hid_b), (exg_a, exg_b)

    @pl.when(step == 0)
    def _():
        for ref in (dwr_ref, dwe_ref, dwo_ref, vec_ref, deb_acc):
            ref[...] = jnp.zeros(ref.shape, F32)

    x = x_ref[...].astype(F32)
    cot = cot_ref[...].astype(F32)
    att_t = att_ref[...].astype(BF)
    mixed = mm(att_t.T, wo_ref[...]) + ob_ref[...]
    middle = x + BRANCH * mixed
    unit, scale = norm_parts(middle)
    second = (unit * g2_ref[...] + s2_ref[...]).astype(BF)
    reduced_grad = (BRANCH * cot).astype(BF)
    total = we_ref.shape[1]
    tile = x.shape[0]
    red_t = None
    back_t = None

    def stage_one(c):
        rows = slice(c * chunk, (c + 1) * chunk)
        v = mm(wet_ref[rows, :], second, NT) + eb_ref[rows, :]
        v2 = v * v
        t = jnp.tanh(v * (GELU_A + GELU_B * v2))
        h1 = 0.5 * t + 0.5
        gelu = v * h1
        slope = h1 + gelu * (1.0 - h1) * (2.0 * GELU_A + 6.0 * GELU_B * v2)
        hidden_of[c % 2][...] = gelu.astype(BF)
        grads = (mm(wr_ref[rows, :], reduced_grad, NT) * slope).astype(BF)
        grad_of[c % 2][...] = grads
        wide = grads.astype(F32)
        part = wide[:, 0:128]
        for n in range(1, tile // 128):
            part = part + wide[:, n * 128 : (n + 1) * 128]
        deb_acc[rows, :] += part

    stage_one(0)
    for c in range(total // chunk):
        if (c + 1) * chunk < total:
            stage_one(c + 1)
        rows = slice(c * chunk, (c + 1) * chunk)
        hidden, grads = hidden_of[c % 2][...], grad_of[c % 2][...]
        dwr_ref[rows, :] += mm(hidden, reduced_grad)
        dwe_ref[rows, :] += mm(grads, second)
        one, two = mm(wrt_ref[:, rows], hidden), mm(we_ref[:, rows], grads)
        red_t = one if red_t is None else red_t + one
        back_t = two if back_t is None else back_t + two
    result = (middle + BRANCH * (red_t.T + rb_ref[...])).astype(BF)

    @pl.when(step < tiles // 2)
    def _():
        res_send[...] = result

    @pl.when(step >= tiles // 2)
    def _():
        res_own[0] = result

    norm_grad = back_t.T
    middle_grad = cot + norm_back(norm_grad, unit, scale, g2_ref[...])
    mid_ref[...] = middle_grad
    mixed_grad = (BRANCH * middle_grad).astype(BF)
    dwo_ref[...] += mm(att_t, mixed_grad)
    att_grad = mm(mixed_grad, wo_ref[...], NT).astype(BF)
    ag_ref[...] = att_grad
    dots = att_grad.T.astype(F32) * att_ref[...]
    for head in range(H):
        delta_ref[head : head + 1, :] = jnp.sum(
            dots[HD * head : HD * head + HD, :], 0, keepdims=True
        )
    sums = (norm_grad * unit, norm_grad, mixed_grad.astype(F32), reduced_grad.astype(F32))
    for n, value in enumerate(sums):
        vec_ref[n : n + 1, :] += jnp.sum(value, 0, keepdims=True)

    @pl.when(step == tiles - 1)
    def _():
        width = vec_ref.shape[1]
        flat = jnp.sum(deb_acc[...].T, 0, keepdims=True)
        for n in range(total // width):
            vec_ref[4 + n : 5 + n, :] = flat[:, n * width : (n + 1) * width]


def middle_part(half, att_t, x, cot, wo, ob, g2, s2, we, wet, eb, wr, wrt, rb, tile, chunk):
    length, width = x.shape
    total = we.shape[1]
    tiles = length // tile
    part = tiles // 2
    where = lambda t, h: (t + (1 - h[0]) * part) % tiles
    fixed = lambda a: pl.BlockSpec(a.shape, lambda t, h: (0, 0), pipeline_mode=pl.Buffered(1))
    whole = lambda dims: pl.BlockSpec(dims, lambda t, h: (0, 0))
    rows = pl.BlockSpec((tile, width), lambda t, h: (where(t, h), 0))
    cols = pl.BlockSpec((width, tile), lambda t, h: (0, where(t, h)))
    vec_rows = 4 + total // width
    return pl.pallas_call(
        functools.partial(middle_kernel, chunk, tiles),
        grid_spec=pltpu.PrefetchScalarGridSpec(
            num_scalar_prefetch=1,
            grid=(tiles,),
            in_specs=[cols, rows, rows]
            + [fixed(a) for a in (wo, ob, g2, s2, we, wet, eb, wr, wrt, rb)],
            out_specs=[
                pl.BlockSpec((1, tile, width), lambda t, h: (h[0], jnp.maximum(t - part, 0), 0)),
                pl.BlockSpec((tile, width), lambda t, h: (jnp.minimum(t, part - 1), 0)),
                rows,
                rows,
                pl.BlockSpec((H, tile), lambda t, h: (0, where(t, h))),
                whole((total, width)),
                whole((total, width)),
                whole((width, width)),
                whole((vec_rows, width)),
            ],
            scratch_shapes=[pltpu.VMEM((total, 128), F32)]
            + [pltpu.VMEM((chunk, tile), BF)] * 4,
        ),
        out_shape=[
            shape_of((2, length // 2, width), BF),
            shape_of((length // 2, width), BF),
            shape_of((length, width), F32),
            shape_of((length, width), BF),
            shape_of((H, length), F32),
            shape_of((total, width), F32),
            shape_of((total, width), F32),
            shape_of((width, width), F32),
            shape_of((vec_rows, width), F32),
        ],
        compiler_params=params(),
        name="middle",
    )(half, att_t, x, cot, wo, ob, g2, s2, we, wet, eb, wr, wrt, rb)


def last_kernel(
    tiles, half_ref, dq_ref, dk_ref, dv_ref, x_ref, mid_ref, gain_ref, shift_ref, weight_ref,
    own_ref, send_ref, dw_ref, vec_ref,
):
    step = pl.program_id(0)

    @pl.when(step == 0)
    def _():
        for ref in (dw_ref, vec_ref):
            ref[...] = jnp.zeros(ref.shape, F32)

    width = x_ref.shape[1]
    unit, scale = norm_parts(x_ref[...].astype(F32))
    normed_t = (unit * gain_ref[...] + shift_ref[...]).astype(BF).T
    grads = (dq_ref[...], dk_ref[...], dv_ref[...])
    back = None
    for n, grad in enumerate(grads):
        cols = slice(n * width, (n + 1) * width)
        dw_ref[:, cols] += mm(normed_t, grad)
        one = mm(grad, weight_ref[:, cols], NT)
        back = one if back is None else back + one
    total = mid_ref[...] + norm_back(back, unit, scale, gain_ref[...])

    @pl.when(step < tiles // 2)
    def _():
        send_ref[...] = total.astype(BF)

    @pl.when(step >= tiles // 2)
    def _():
        own_ref[0] = total

    sums = (back * unit, back, grads[0].astype(F32), grads[2].astype(F32))
    for n, value in enumerate(sums):
        vec_ref[n : n + 1, :] += jnp.sum(value, 0, keepdims=True)


def last_part(half, dq, dk, dv, x, mid, gain, shift, weight, tile):
    length, width = x.shape
    tiles = length // tile
    part = tiles // 2
    where = lambda t, h: (t + (1 - h[0]) * part) % tiles
    rows = pl.BlockSpec((tile, width), lambda t, h: (where(t, h), 0))
    fixed = lambda a: pl.BlockSpec(a.shape, lambda t, h: (0, 0))
    whole = lambda dims: pl.BlockSpec(dims, lambda t, h: (0, 0))
    return pl.pallas_call(
        functools.partial(last_kernel, tiles),
        grid_spec=pltpu.PrefetchScalarGridSpec(
            num_scalar_prefetch=1,
            grid=(tiles,),
            in_specs=[rows] * 5 + [fixed(a) for a in (gain, shift, weight)],
            out_specs=[
                pl.BlockSpec((1, tile, width), lambda t, h: (h[0], jnp.maximum(t - part, 0), 0)),
                pl.BlockSpec((tile, width), lambda t, h: (jnp.minimum(t, part - 1), 0)),
                whole((width, 3 * width)),
                whole((8, width)),
            ],
        ),
        out_shape=[
            shape_of((2, length // 2, width), F32),
            shape_of((length // 2, width), BF),
            shape_of((width, 3 * width), F32),
            shape_of((8, width), F32),
        ],
        compiler_params=params(),
        name="last",
    )(half, dq, dk, dv, x, mid, gain, shift, weight)


def swapped(value):
    return lax.ppermute(value, "seq", [(0, 1), (1, 0)])


def tables_of(start, size):
    count = start.shape[0] // size
    low = (start[::size] // size).astype(jnp.int32)
    mid = ((start[size - 1 :: size] + size - 1) // size).astype(jnp.int32)
    steps = jnp.sum(jnp.arange(1, count + 1, dtype=jnp.int32) - low)[None]
    return low, mid, steps


def passed_along(block, axis, distance):
    devices = range(lax.axis_size(axis))
    route = [(i - distance, i) for i in devices if i - distance in devices]
    return lax.ppermute(block, axis, route)


def from_behind(value, axis, steps):
    count = lax.axis_size(axis)
    pairs = [(source, (source + steps) % count) for source in range(count)]
    return lax.ppermute(value, axis, pairs)


def layer_norm(values, gain_vec, shift_vec):
    center = jnp.mean(values, -1, keepdims=True)
    centered = values - center
    variance = jnp.mean(centered * centered, -1, keepdims=True)
    return centered * lax.rsqrt(variance + EPSILON) * gain_vec + shift_vec


def gelu_tanh(values):
    return jax.nn.gelu(values, approximate=True)


def plain_dot(left, right):
    return jnp.dot(left, right, preferred_element_type=jnp.float32)


def left_dot(left, right):
    return lax.dot_general(
        left, right, (((0,), (0,)), ((), ())), preferred_element_type=jnp.float32
    )


def right_dot(left, right):
    return lax.dot_general(
        left, right, (((1,), (1,)), ((), ())), preferred_element_type=jnp.float32
    )


def block_scores(queries, keys_block, query_seg, key_seg, query_places, key_start):
    row_count, key_len, width = keys_block.shape
    keys_heads = keys_block.reshape(row_count, key_len, H, HD)
    scores = jnp.einsum(
        "rqhd,rkhd->rhqk", queries, keys_heads, preferred_element_type=jnp.float32
    ) * HD ** (-0.5)
    key_places = key_start + jnp.arange(key_len, dtype=jnp.int32)
    allowed = (query_seg[:, None, :, None] == key_seg[:, None, None, :]) & (
        key_places[None, None, None, :] <= query_places[None, None, :, None]
    )
    return (scores, allowed)


def attend_block(state, queries, block, query_seg, query_places, key_start):
    run_max, run_sum, running = state
    keys_block, values_block, key_seg = block
    row_count, key_len, width = values_block.shape
    query_len = queries.shape[1]
    scores, allowed = block_scores(queries, keys_block, query_seg, key_seg, query_places, key_start)
    block_max = jnp.max(jnp.where(allowed, scores, NEGATIVE), -1)
    new_max = jnp.maximum(run_max, block_max)
    exponent = jnp.where(allowed, jnp.exp(scores - new_max[..., None]), 0.0)
    factor = jnp.exp(run_max - new_max)
    new_sum = run_sum * factor + jnp.sum(exponent, -1)
    values_heads = values_block.reshape(row_count, key_len, H, HD)
    addition = jnp.einsum(
        "rhqk,rkhd->rqhd",
        exponent.astype(jnp.bfloat16),
        values_heads,
        preferred_element_type=jnp.float32,
    )
    scaled = (
        running.reshape(row_count, query_len, H, HD) * jnp.transpose(factor, (0, 2, 1))[..., None]
    )
    return (new_max, new_sum, (scaled + addition).reshape(row_count, query_len, width))


def grad_block(queries, out_grad, log_sum, delta, block, query_seg, query_places, key_start):
    keys_block, values_block, key_seg = block
    row_count, key_len, width = keys_block.shape
    scores, allowed = block_scores(queries, keys_block, query_seg, key_seg, query_places, key_start)
    weights_block = jnp.where(allowed, jnp.exp(scores - log_sum[..., None]), 0.0)
    keys_heads = keys_block.reshape(row_count, key_len, H, HD)
    values_heads = values_block.reshape(row_count, key_len, H, HD)
    value_dots = jnp.einsum(
        "rqhd,rkhd->rhqk", out_grad, values_heads, preferred_element_type=jnp.float32
    )
    score_grad = (weights_block * (value_dots - delta[..., None]) * HD ** (-0.5)).astype(
        jnp.bfloat16
    )
    query_part = jnp.einsum(
        "rhqk,rkhd->rqhd", score_grad, keys_heads, preferred_element_type=jnp.float32
    ).reshape(row_count, -1, width)
    key_part = jnp.einsum(
        "rhqk,rqhd->rkhd", score_grad, queries, preferred_element_type=jnp.float32
    ).reshape(row_count, key_len, width)
    value_part = jnp.einsum(
        "rhqk,rqhd->rkhd",
        weights_block.astype(jnp.bfloat16),
        out_grad,
        preferred_element_type=jnp.float32,
    ).reshape(row_count, key_len, width)
    return (query_part, key_part, value_part)


def local(
    activations,
    segments,
    first_gain,
    first_shift,
    input_weight,
    query_bias,
    value_bias,
    output_weight,
    output_bias,
    second_gain,
    second_shift,
    expand_weight,
    expand_bias,
    reduce_weight,
    reduce_bias,
    cotangent,
):
    row_total, span_len, width = activations.shape
    cycle_size = lax.axis_size("seq")
    position = lax.axis_index("seq")
    micro_rows = row_total // MICRO
    branch = DEPTH ** (-0.5)
    bias_all = jnp.concatenate([query_bias, jnp.zeros_like(query_bias), value_bias])
    query_places = position * span_len + jnp.arange(span_len, dtype=jnp.int32)
    totals = [
        jnp.zeros(argument.shape, jnp.float32)
        for argument in (
            first_gain,
            first_shift,
            input_weight,
            query_bias,
            value_bias,
            output_weight,
            output_bias,
            second_gain,
            second_shift,
            expand_weight,
            expand_bias,
            reduce_weight,
            reduce_bias,
        )
    ]
    outputs_list = []
    grads_list = []
    for micro in range(MICRO):
        lower = micro * micro_rows
        values_in = activations[lower : lower + micro_rows].astype(jnp.float32)
        query_seg = segments[lower : lower + micro_rows]
        out_cot = cotangent[lower : lower + micro_rows].astype(jnp.float32)
        normed, first_pull = jax.vjp(layer_norm, values_in, first_gain, first_shift)
        normed_low = normed.astype(jnp.bfloat16).reshape(-1, width)
        projected = (plain_dot(normed_low, input_weight) + bias_all).astype(jnp.bfloat16)
        queries = projected[:, :width].reshape(micro_rows, span_len, H, HD)
        keys_own = projected[:, width : 2 * width].reshape(micro_rows, span_len, width)
        values_own = projected[:, 2 * width :].reshape(micro_rows, span_len, width)
        own_block = (keys_own, values_own, query_seg)
        start_state = (
            jnp.full((micro_rows, H, span_len), NEGATIVE, jnp.float32),
            jnp.zeros((micro_rows, H, span_len), jnp.float32),
            jnp.zeros((micro_rows, span_len, width), jnp.float32),
        )
        state = attend_block(
            start_state, queries, own_block, query_seg, query_places, position * span_len
        )

        def cycle_forward(step_index, carry):
            block, inner_state = carry
            block = passed_along((block[0], block[1], block[2]), "seq", 1)
            source = (position - step_index) % cycle_size
            inner_state = lax.cond(
                source < position,
                lambda current: attend_block(
                    current, queries, block, query_seg, query_places, source * span_len
                ),
                lambda current: current,
                inner_state,
            )
            return (block, inner_state)

        unused_block, state = lax.fori_loop(1, cycle_size, cycle_forward, (own_block, state))
        run_max, run_sum, running = state
        attended = (
            running.reshape(micro_rows, span_len, H, HD)
            / jnp.transpose(run_sum, (0, 2, 1))[..., None]
        ).reshape(micro_rows, span_len, width)
        log_sum = run_max + jnp.log(run_sum)
        attended_low = attended.astype(jnp.bfloat16).reshape(-1, width)
        mixed_out = plain_dot(attended_low, output_weight) + output_bias
        middle = values_in + branch * mixed_out.reshape(values_in.shape)
        second_norm, second_pull = jax.vjp(layer_norm, middle, second_gain, second_shift)
        second_low = second_norm.astype(jnp.bfloat16).reshape(-1, width)
        expanded = plain_dot(second_low, expand_weight) + expand_bias
        hidden, gelu_pull = jax.vjp(gelu_tanh, expanded)
        hidden_low = hidden.astype(jnp.bfloat16)
        reduced = plain_dot(hidden_low, reduce_weight) + reduce_bias
        outputs_list.append(
            (middle + branch * reduced.reshape(values_in.shape)).astype(jnp.bfloat16)
        )
        reduced_grad = (branch * out_cot).reshape(-1, width).astype(jnp.bfloat16)
        totals[12] = totals[12] + jnp.sum(reduced_grad.astype(jnp.float32), 0)
        totals[11] = totals[11] + left_dot(hidden_low, reduced_grad)
        (expanded_grad,) = gelu_pull(right_dot(reduced_grad, reduce_weight))
        expanded_low = expanded_grad.astype(jnp.bfloat16)
        totals[10] = totals[10] + jnp.sum(expanded_low.astype(jnp.float32), 0)
        totals[9] = totals[9] + left_dot(second_low, expanded_low)
        norm_in_grad = right_dot(expanded_low, expand_weight).reshape(values_in.shape)
        middle_part, gain_part, shift_part = second_pull(norm_in_grad)
        totals[7] = totals[7] + gain_part
        totals[8] = totals[8] + shift_part
        middle_grad = out_cot + middle_part
        mixed_grad = (branch * middle_grad).reshape(-1, width).astype(jnp.bfloat16)
        totals[6] = totals[6] + jnp.sum(mixed_grad.astype(jnp.float32), 0)
        totals[5] = totals[5] + left_dot(attended_low, mixed_grad)
        attended_grad = (
            right_dot(mixed_grad, output_weight)
            .astype(jnp.bfloat16)
            .reshape(micro_rows, span_len, H, HD)
        )
        delta = jnp.transpose(
            jnp.sum(
                attended_grad.astype(jnp.float32) * attended.reshape(micro_rows, span_len, H, HD),
                -1,
            ),
            (0, 2, 1),
        )
        query_grad, key_grad, value_grad = grad_block(
            queries,
            attended_grad,
            log_sum,
            delta,
            own_block,
            query_seg,
            query_places,
            position * span_len,
        )

        def cycle_backward(step_index, carry):
            block, partial_value, query_acc = carry
            block = passed_along((block[0], block[1], block[2]), "seq", 1)
            partial_value = (
                from_behind(partial_value[0].astype(jnp.bfloat16), "seq", 1).astype(jnp.float32),
                from_behind(partial_value[1].astype(jnp.bfloat16), "seq", 1).astype(jnp.float32),
            )
            source = (position - step_index) % cycle_size

            def work(current):
                partial_in, query_in = current
                query_part, key_part, value_part = grad_block(
                    queries,
                    attended_grad,
                    log_sum,
                    delta,
                    block,
                    query_seg,
                    query_places,
                    source * span_len,
                )
                return (
                    (partial_in[0] + key_part, partial_in[1] + value_part),
                    query_in + query_part,
                )

            partial_value, query_acc = lax.cond(
                source < position, work, lambda current: current, (partial_value, query_acc)
            )
            return (block, partial_value, query_acc)

        unused_block, partial_value, query_grad = lax.fori_loop(
            1, cycle_size, cycle_backward, (own_block, (key_grad, value_grad), query_grad)
        )
        key_grad, value_grad = (
            from_behind(partial_value[0].astype(jnp.bfloat16), "seq", 1).astype(jnp.float32),
            from_behind(partial_value[1].astype(jnp.bfloat16), "seq", 1).astype(jnp.float32),
        )
        qkv_grad = (
            jnp.concatenate([query_grad, key_grad, value_grad], -1)
            .reshape(-1, 3 * width)
            .astype(jnp.bfloat16)
        )
        totals[3] = totals[3] + jnp.sum(qkv_grad[:, :width].astype(jnp.float32), 0)
        totals[4] = totals[4] + jnp.sum(qkv_grad[:, 2 * width :].astype(jnp.float32), 0)
        totals[2] = totals[2] + left_dot(normed_low, qkv_grad)
        norm_grad = right_dot(qkv_grad, input_weight).reshape(values_in.shape)
        input_part, gain_one, shift_one = first_pull(norm_grad)
        totals[0] = totals[0] + gain_one
        totals[1] = totals[1] + shift_one
        grads_list.append(middle_grad + input_part)
    summed = lax.psum(
        (
            totals[0],
            totals[1],
            totals[2],
            totals[3],
            totals[4],
            totals[5],
            totals[6],
            totals[7],
            totals[8],
            totals[9],
            totals[10],
            totals[11],
            totals[12],
        ),
        ("dp", "seq"),
    )
    return (
        jnp.concatenate(outputs_list, 0),
        jnp.concatenate(grads_list, 0),
        summed[0],
        summed[1],
        summed[2],
        summed[3],
        summed[4],
        summed[5],
        summed[6],
        summed[7],
        summed[8],
        summed[9],
        summed[10],
        summed[11],
        summed[12],
    )


def local_rows(
    activations,
    segments,
    first_gain,
    first_shift,
    input_weight,
    query_bias,
    value_bias,
    output_weight,
    output_bias,
    second_gain,
    second_shift,
    expand_weight,
    expand_bias,
    reduce_weight,
    reduce_bias,
    cotangent,
):
    rows, span, width = activations.shape
    mine = lax.axis_index("seq")
    half = mine.astype(jnp.int32)[None]
    take = lambda array, index: lax.dynamic_index_in_dim(array, index, 0, keepdims=False)
    x_own = take(activations, mine)
    x_got = swapped(take(activations, 1 - mine))
    seg_got = swapped(take(segments, 1 - mine))
    cot_got = swapped(take(cotangent, 1 - mine))

    def in_order(own, got):
        return jnp.where(
            mine == 0, jnp.concatenate([own, got], 0), jnp.concatenate([got, own], 0)
        )

    row = lambda vector: vector.reshape(1, -1)
    bias = jnp.concatenate([query_bias, jnp.zeros_like(query_bias), value_bias])
    weights = (row(first_gain), row(first_shift), input_weight, row(bias))
    before = project(half, x_own, *weights, None, TILE)
    x, q, k, v, kt, vt = project(1 - half, x_got, *weights, before, TILE)
    seg = in_order(take(segments, mine), seg_got)
    numbers = jnp.arange(8, dtype=jnp.int32)[:, None]
    below = jnp.sum((seg[None] < numbers).astype(jnp.int32), 1, keepdims=True)
    start = jnp.sum(jnp.where(seg[None] == numbers, below, 0), 0)
    tables = tables_of(start, BLOCK)
    start = row(start)
    att_t, lse = attend(tables, q, k, vt, start, BLOCK, FORWARD_HEADS)
    cot = in_order(take(cotangent, mine), cot_got)
    result, result_send, mid, att_grad, delta, d_reduce, d_expand, d_output, vec = middle_part(
        half, att_t, x, cot, output_weight, row(output_bias), row(second_gain), row(second_shift),
        expand_weight, expand_weight.T, expand_bias.reshape(-1, 1), reduce_weight, reduce_weight.T,
        row(reduce_bias), TILE, CHUNK,
    )
    result_got = swapped(result_send)
    everyone = ("dp", "seq")
    sums = lax.psum(
        tuple(a.astype(BF) for a in (d_reduce, d_expand, d_output, vec)), everyone
    )
    dq, dk, dv = attend_back(
        tables, q, k, kt, v, att_grad, start, lse, delta, BLOCK, BACKWARD_HEADS
    )
    grad, grad_send, d_input, vec_last = last_part(
        half, dq, dk, dv, x, mid, row(first_gain), row(first_shift), input_weight, TILE
    )
    grad_got = swapped(grad_send)
    last_sums = lax.psum(tuple(a.astype(BF) for a in (d_input, vec_last)), everyone)
    place = lambda whole, got: lax.dynamic_update_index_in_dim(
        whole, got.astype(whole.dtype), 1 - mine, 0
    )
    d_reduce, d_expand, d_output, vec = (a.astype(F32) for a in sums)
    d_input, vec_last = (a.astype(F32) for a in last_sums)
    return (
        place(result, result_got),
        place(grad, grad_got),
        vec_last[0],
        vec_last[1],
        d_input,
        vec_last[2],
        vec_last[3],
        d_output,
        vec[2],
        vec[0],
        vec[1],
        d_expand.T,
        vec[4:].reshape(-1),
        d_reduce,
        vec[3],
    )


TILE = 512
CHUNK = 512
BLOCK = 512
FORWARD_HEADS = 8
BACKWARD_HEADS = 4


def solution(mesh):
    sizes = dict(zip(mesh.axis_names, mesh.devices.shape))
    tokens, places, whole = P("dp", "seq", None), P("dp", "seq"), P()
    in_specs = (tokens, places) + (whole,) * 13 + (tokens,)
    out_specs = (tokens, tokens) + (whole,) * 13

    def program(activations, *rest):
        rows = activations.shape[0] // sizes["dp"]
        span = activations.shape[1] // sizes["seq"]
        by_rows = sizes["seq"] == 2 and rows == 2 and span % BLOCK == 0
        return jax.shard_map(
            local_rows if by_rows else local,
            mesh=mesh,
            in_specs=in_specs,
            out_specs=out_specs,
            check_vma=False,
        )(activations, *rest)

    return program
```

```python
import functools

import jax
import jax.numpy as jnp
from jax import lax
from jax.experimental import pallas as pl
from jax.experimental.pallas import tpu as pltpu
from jax.sharding import PartitionSpec as P

H = 8
HD = 64
DEPTH = 48
MICRO = 2
EPSILON = 1e-05
NEGATIVE = -1e30
BRANCH = DEPTH ** (-0.5)
SCALE = HD ** (-0.5)
SCALE2 = SCALE * 1.4426950408889634
GELU_A = 0.7978845608028654
GELU_B = GELU_A * 0.044715

BF = jnp.bfloat16
F32 = jnp.float32
NN = (((1,), (0,)), ((), ()))
NT = (((1,), (1,)), ((), ()))
VMEM_LIMIT = 58 << 20


def mm(left, right, dims=NN):
    return lax.dot_general(left, right, dims, preferred_element_type=F32)


def shape_of(dims, dtype):
    return jax.ShapeDtypeStruct(dims, dtype)


def params(limit=VMEM_LIMIT):
    return pltpu.CompilerParams(vmem_limit_bytes=limit)


def norm_parts(values):
    center = jnp.mean(values, -1, keepdims=True)
    centered = values - center
    variance = jnp.mean(centered * centered, -1, keepdims=True)
    scale = lax.rsqrt(variance + EPSILON)
    return centered * scale, scale


def norm_back(grad, unit, scale, gain):
    inner = grad * gain
    first = jnp.mean(inner, -1, keepdims=True)
    second = jnp.mean(inner * unit, -1, keepdims=True)
    return scale * (inner - first - unit * second)


def largest_norms(block):
    lane = lax.broadcasted_iota(jnp.int32, (block.shape[1], 128), 1)
    column = lax.broadcasted_iota(jnp.int32, (block.shape[1], 128), 0)
    member = jnp.where(column // HD == lane, 1.0, 0.0).astype(BF)
    wide = block.astype(F32)
    return jnp.max(mm((wide * wide).astype(BF), member), 0, keepdims=True)


def project_kernel(place, x_ref, gain_ref, shift_ref, weight_ref, bias_ref, *refs):
    full_ref, q_ref, k_ref, v_ref, kt_ref, vt_ref, norm_ref = refs[-7:]
    x = x_ref[...]
    unit, _ = norm_parts(x.astype(F32))
    normed = (unit * gain_ref[...] + shift_ref[...]).astype(BF)
    width = x.shape[1]
    out = (mm(normed, weight_ref[...]) + bias_ref[...]).astype(BF)
    full_ref[...] = x
    q_ref[...] = out[:, :width]
    k_ref[...] = out[:, width : 2 * width]
    v_ref[...] = out[:, 2 * width :]
    kt_ref[...] = out[:, width : 2 * width].T
    vt_ref[...] = out[:, 2 * width :].T

    @pl.when(pl.program_id(0) == 0)
    def _():
        norm_ref[...] = jnp.zeros(norm_ref.shape, F32)

    for n in range(2):
        norm_ref[n : n + 1, :] = jnp.maximum(
            norm_ref[n : n + 1, :], largest_norms(out[:, n * width : (n + 1) * width])
        )


def project(half, x, gain, shift, weight, bias, before, tile):
    span, width = x.shape
    count = span // tile
    length = 2 * span
    fixed = lambda dims: pl.BlockSpec(dims, lambda t, h: (0, 0))
    rows = pl.BlockSpec((tile, width), lambda t, h: (h[0] * count + t, 0))
    cols = pl.BlockSpec((width, tile), lambda t, h: (0, h[0] * count + t))
    in_specs = [
        pl.BlockSpec((tile, width), lambda t, h: (t, 0)),
        fixed((1, width)),
        fixed((1, width)),
        fixed(weight.shape),
        fixed((1, 3 * width)),
    ]
    aliases = {}
    if before is not None:
        in_specs += [pl.BlockSpec(memory_space=pl.ANY)] * 6
        aliases = {6 + i: i for i in range(6)}
    nat, trn = shape_of((length, width), BF), shape_of((width, length), BF)
    return pl.pallas_call(
        project_kernel,
        grid_spec=pltpu.PrefetchScalarGridSpec(
            num_scalar_prefetch=1,
            grid=(count,),
            in_specs=in_specs,
            out_specs=[rows, rows, rows, rows, cols, cols, fixed((8, 128))],
        ),
        out_shape=[nat, nat, nat, nat, trn, trn, shape_of((8, 128), F32)],
        input_output_aliases=aliases,
        compiler_params=params(),
        name="project",
    )(half, x, gain, shift, weight, bias, *(before or ()))


def document_kernel(size, half_ref, own_ref, got_ref, start_ref, table_ref):
    span = own_ref.shape[1]
    place = lambda half: pl.ds(pl.multiple_of(half * span, span), span)
    start_ref[0:1, place(half_ref[0])] = own_ref[...]
    start_ref[0:1, place(1 - half_ref[0])] = got_ref[...]
    numbers = start_ref[...]
    start = jnp.zeros_like(numbers)
    for number in range(1, 8):
        before = jnp.sum((numbers < number).astype(jnp.int32), 1, keepdims=True)
        start = jnp.where(numbers == number, before, start)
    start_ref[...] = start
    count = start.shape[1] // size
    slots = table_ref.shape[0] - 1
    for slot in range(slots):
        table_ref[slot] = 0
    filled = jnp.int32(0)
    for i in range(count):
        block = start[:, i * size : (i + 1) * size]
        low, high = jnp.min(block), jnp.max(block)
        for j in range(i + 1):
            kind = jnp.where(high > j * size, 2, 1 if i == j else 0)
            active = low < (j + 1) * size

            table_ref[filled] = jnp.where(active, i + 256 * j + 65536 * kind, 0)
            filled = filled + active.astype(jnp.int32)
    table_ref[slots] = filled


def documents(half, own, got, size):
    length = 2 * own.shape[1]
    count = length // size
    row = lambda wide: pl.BlockSpec((1, wide), lambda t, h: (0, 0))
    return pl.pallas_call(
        functools.partial(document_kernel, size),
        grid_spec=pltpu.PrefetchScalarGridSpec(
            num_scalar_prefetch=1,
            grid=(1,),
            in_specs=[row(length // 2), row(length // 2)],
            out_specs=[row(length), pl.BlockSpec(memory_space=pltpu.SMEM)],
        ),
        out_shape=[
            shape_of((1, length), jnp.int32),
            shape_of((count * (count + 1) // 2 + 2,), jnp.int32),
        ],
        compiler_params=params(),
        name="documents",
    )(half, own, got)


def head_half(block, head):
    lane = lax.broadcasted_iota(jnp.int32, block.shape, 1)
    keep = (lane < HD) if head % 2 == 0 else (lane >= HD)
    return jnp.where(keep, block, jnp.zeros_like(block))


def pair_lanes(head):
    low = 2 * HD * (head // 2)
    return slice(low, low + 2 * HD)


class Blocks:
    def __init__(self, size, list_ref, start_ref, mask_ref, values):
        self.size, self.list = size, list_ref
        self.start, self.mask, self.values = start_ref, mask_ref, values

    def at(self, index):
        return pl.ds(pl.multiple_of(index * self.size, self.size), self.size)

    def places(self):
        dims = (self.size, self.size)
        return lax.broadcasted_iota(jnp.int32, dims, 0), lax.broadcasted_iota(jnp.int32, dims, 1)

    def fill(self, slot, i, j):
        key, query = self.places()
        key, query = key + j * self.size, query + i * self.size
        allowed = (key >= self.start[0:1, self.at(i)]) & (key <= query)
        self.mask[slot] = jnp.where(allowed, *self.values).astype(self.mask.dtype)

    def entry(self, step):
        packed = self.list[step]
        kind = packed // 65536
        return packed % 256, (packed // 256) % 256, jnp.where(kind == 2, 2 + lax.rem(step, 2), kind)

    def prepare(self, slot, i, j):
        pl.when(slot >= 2)(lambda: self.fill(slot, i, j))

    def walk(self, groups, early, late, row_end=None):
        steps = self.list[self.list.shape[0] - 1]
        self.mask[0] = jnp.full(self.mask.shape[1:], self.values[0], self.mask.dtype)
        key, query = self.places()
        self.mask[1] = jnp.where(key <= query, *self.values).astype(self.mask.dtype)
        i, j, slot = self.entry(0)
        self.prepare(slot, i, j)
        early(0, i, j, slot, False)

        def body(step, carry):
            i, j, slot = carry
            ni, nj, nslot = self.entry(step + 1)
            self.prepare(nslot, ni, nj)

            def work(corner, slot):
                for head in range(groups):
                    if head + 1 < groups:
                        early(head + 1, i, j, slot, corner)
                    else:
                        early(0, ni, nj, nslot, False)
                    late(head, i, j, corner)

            pl.when(slot == 0)(lambda: work(False, None))
            pl.when((slot > 0) & (i == j))(lambda: work(True, slot))
            pl.when((slot > 0) & (i != j))(lambda: work(False, slot))
            if row_end is not None:
                pl.when(j == i)(lambda: row_end(i))
            return ni, nj, nslot

        lax.fori_loop(0, steps, body, (i, j, slot))


def pieces(corner, size):
    if not corner:
        return [(slice(0, size), slice(0, size))]
    mid = size // 2
    return [(slice(0, mid), slice(0, size)), (slice(mid, size), slice(mid, size))]


def forward_kernel(
    size, groups, list_ref, small_ref, q_ref, k_ref, vt_ref, start_ref, out_ref, lse_ref, max_ref,
    new_ref, acc_ref, bias_ref, mask_ref, *slots,
):
    scores, probs_of = slots[:groups], slots[groups:]
    plain = Blocks(size, list_ref, start_ref, mask_ref, (1.0, 0.0))
    general = Blocks(size, list_ref, start_ref, bias_ref, (0.0, NEGATIVE))
    at = plain.at

    def part_at(index, part):
        low = index * size + part.start
        return pl.ds(pl.multiple_of(low, size // 2), part.stop - part.start)

    def products(head, i, j, keys, queries):
        lanes = pair_lanes(head)
        return mm(head_half(k_ref[part_at(j, keys), lanes], head), q_ref[part_at(i, queries), lanes], NT)

    def values(head, j, keys):
        block = vt_ref[HD * head : HD * head + HD, part_at(j, keys)]
        return jnp.concatenate([block, jnp.ones((16, keys.stop - keys.start), BF)], 0)

    def early_plain(head, i, j, slot, corner):
        for keys, queries in pieces(corner, size):
            probs = jnp.exp2(products(head, i, j, keys, queries) * SCALE2).astype(BF)
            if slot is not None:
                probs = probs * mask_ref[slot, keys, queries]
            probs_of[head][keys, queries] = probs

    def late_plain(head, i, j, corner):
        for keys, queries in pieces(corner, size):
            acc_ref[head, :, queries] += mm(values(head, j, keys), probs_of[head][keys, queries])

    whole = slice(0, size)

    def early(head, i, j, slot, corner):
        s = products(head, i, j, whole, whole)
        if slot is not None:
            s = s + bias_ref[slot]
        scores[head][...] = s
        new_ref[head : head + 1, :] = jnp.max(s, 0, keepdims=True)

    def late(head, i, j, corner):
        old = max_ref[head : head + 1, :]
        new = jnp.maximum(old, new_ref[head : head + 1, :])
        max_ref[head : head + 1, :] = new
        probs = jnp.exp2(scores[head][...] * SCALE2 - new * SCALE2)
        factor = jnp.exp2((old - new) * SCALE2)
        acc_ref[head] = acc_ref[head] * factor + mm(values(head, j, whole), probs.astype(BF))

    def reset(largest):
        max_ref[...] = jnp.full(max_ref.shape, largest, F32)
        acc_ref[...] = jnp.zeros(acc_ref.shape, F32)

    def row_end(largest, i):
        for head in range(groups):
            total = acc_ref[head, HD : HD + 1, :]
            out_ref[HD * head : HD * head + HD, at(i)] = acc_ref[head, :HD, :] * (1.0 / total)
            lse_ref[0, head : head + 1, at(i)] = max_ref[
                head : head + 1, :
            ] * SCALE2 + jnp.log2(total)
        reset(largest)

    @pl.when(small_ref[0] == 1)
    def _():
        reset(0.0)
        plain.walk(groups, early_plain, late_plain, functools.partial(row_end, 0.0))

    @pl.when(small_ref[0] != 1)
    def _():
        reset(NEGATIVE)
        general.walk(groups, early, late, functools.partial(row_end, NEGATIVE))


def attend(table, small, q, k, vt, start, size, groups):
    length, width = q.shape
    part = HD * groups
    calls = H // groups
    nat = pl.BlockSpec((length, part), lambda p, *_: (0, p))
    trn = pl.BlockSpec((part, length), lambda p, *_: (p, 0))
    return pl.pallas_call(
        functools.partial(forward_kernel, size, groups),
        grid_spec=pltpu.PrefetchScalarGridSpec(
            num_scalar_prefetch=2,
            grid=(calls,),
            in_specs=[nat, nat, trn, pl.BlockSpec((1, length), lambda p, *_: (0, 0))],
            out_specs=[trn, pl.BlockSpec((1, groups, length), lambda p, *_: (p, 0, 0))],
            scratch_shapes=[
                pltpu.VMEM((8, size), F32),
                pltpu.VMEM((8, size), F32),
                pltpu.VMEM((groups, HD + 16, size), F32),
                pltpu.VMEM((4, size, size), F32),
                pltpu.VMEM((4, size, size), BF),
            ]
            + [pltpu.VMEM((size, size), F32)] * groups
            + [pltpu.VMEM((size, size), BF)] * groups,
        ),
        out_shape=[shape_of((width, length), F32), shape_of((calls, groups, length), F32)],
        compiler_params=params(),
        name="attend",
    )(table, small, q, k, vt, start)


def backward_kernel(
    size, groups, first, list_ref, q_ref, k_ref, kt_ref, v_ref, do_ref, start_ref, lse_ref, delta_ref,
    dq_ref, dk_ref, dv_ref, dqt_acc, dk_acc, dv_acc, bias_ref, *slots,
):
    probs_of, grads_of = slots[:groups], slots[groups:]
    walk = Blocks(size, list_ref, start_ref, bias_ref, (0.0, NEGATIVE))

    def part_at(index, part):
        low = index * size + part.start
        return pl.ds(pl.multiple_of(low, size // 2), part.stop - part.start)

    def early(head, i, j, slot, corner):
        lanes = pair_lanes(head)
        for keys, queries in pieces(corner, size):
            at_j, at_i = part_at(j, keys), part_at(i, queries)
            stat = (slice(first + head, first + head + 1), at_i)
            s = mm(head_half(k_ref[at_j, lanes], head), q_ref[at_i, lanes], NT)
            dots = mm(head_half(v_ref[at_j, lanes], head), do_ref[at_i, lanes], NT)
            if slot is not None:
                s = s + bias_ref[slot, keys, queries]
            probs = jnp.exp2(s * SCALE2 - lse_ref[stat])
            probs_of[head][keys, queries] = probs.astype(BF)
            grads_of[head][keys, queries] = (probs * (dots - delta_ref[stat])).astype(BF)

    def late(head, i, j, corner):
        lanes = pair_lanes(head)
        rows = slice(HD * head, HD * head + HD)
        for keys, queries in pieces(corner, size):
            at_j, at_i = part_at(j, keys), part_at(i, queries)
            grads = grads_of[head][keys, queries]
            dv_acc[at_j, lanes] += mm(
                probs_of[head][keys, queries], head_half(do_ref[at_i, lanes], head)
            )
            dk_acc[at_j, lanes] += mm(grads, head_half(q_ref[at_i, lanes], head))
            dqt_acc[rows, at_i] += mm(kt_ref[rows, at_j], grads)

    for acc in (dqt_acc, dk_acc, dv_acc):
        acc[...] = jnp.zeros(acc.shape, F32)
    walk.walk(groups, early, late)
    dq_ref[...] = (dqt_acc[...] * SCALE).T.astype(BF)
    dk_ref[...] = (dk_acc[...] * SCALE).astype(BF)
    dv_ref[...] = dv_acc[...].astype(BF)


def attend_back(first, groups, table, q, k, kt, v, do, start, lse, delta, size):
    length = q.shape[0]
    part = HD * groups
    nat = pl.BlockSpec((pl.Element(length), pl.Element(part)), lambda g, *_: (0, first * HD))
    trn = pl.BlockSpec((pl.Element(part), pl.Element(length)), lambda g, *_: (first * HD, 0))
    only = lambda dims: pl.BlockSpec(dims, lambda g, *_: (0, 0))
    return pl.pallas_call(
        functools.partial(backward_kernel, size, groups, first),
        grid_spec=pltpu.PrefetchScalarGridSpec(
            num_scalar_prefetch=1,
            grid=(1,),
            in_specs=[nat, nat, trn, nat, nat, only((1, length)), only((H, length)), only((H, length))],
            out_specs=[only((length, part))] * 3,
            scratch_shapes=[
                pltpu.VMEM((part, length), F32),
                pltpu.VMEM((length, part), F32),
                pltpu.VMEM((length, part), F32),
                pltpu.VMEM((4, size, size), F32),
            ]
            + [pltpu.VMEM((size, size), BF)] * (2 * groups),
        ),
        out_shape=[shape_of((length, part), BF)] * 3,
        compiler_params=params(),
        name="attend_back",
    )(table, q, k, kt, v, do, start, lse, delta)


def feed_kernel(
    chunk, tiles, half_ref, att_ref, x_ref, cot_ref, wo_ref, ob_ref, g2_ref, s2_ref, wet_ref, eb_ref,
    wr_ref, mid_ref, hid_ref, exg_ref, sums_ref, deb_ref, acc_ref, deb_acc,
):
    step = pl.program_id(0)

    @pl.when(step == 0)
    def _():
        for ref in (acc_ref, deb_acc):
            ref[...] = jnp.zeros(ref.shape, F32)

    mixed = mm(att_ref[...].astype(BF).T, wo_ref[...]) + ob_ref[...]
    middle = x_ref[...].astype(F32) + BRANCH * mixed
    mid_ref[...] = middle
    unit, _ = norm_parts(middle)
    second = (unit * g2_ref[...] + s2_ref[...]).astype(BF)
    second_t = second.T
    reduced_grad = (BRANCH * cot_ref[...].astype(F32)).astype(BF)
    total = wr_ref.shape[0]
    tile, width = x_ref.shape

    def stage_one(c):
        rows = slice(c * chunk, (c + 1) * chunk)
        v = mm(wet_ref[rows, :], second, NT) + eb_ref[rows, :]
        v2 = v * v
        t = jnp.tanh(v * (GELU_A + GELU_B * v2))
        h1 = 0.5 * t + 0.5
        gelu = v * h1
        slope = h1 + gelu * (1.0 - h1) * (2.0 * GELU_A + 6.0 * GELU_B * v2)
        hid_ref[rows, :] = gelu.astype(BF)
        grads = (mm(wr_ref[rows, :], reduced_grad, NT) * slope).astype(BF)
        exg_ref[rows, :] = grads
        wide = grads.astype(F32)
        part = wide[:, 0:128]
        for n in range(1, tile // 128):
            part = part + wide[:, n * 128 : (n + 1) * 128]
        deb_acc[rows, :] += part

    stage_one(0)
    for c in range(total // chunk):
        if (c + 1) * chunk < total:
            stage_one(c + 1)
        rows = slice(c * chunk, (c + 1) * chunk)
        acc_ref[rows, :] += mm(hid_ref[rows, :], reduced_grad)
        for n in range(chunk // width):
            cut = slice(c * chunk + n * width, c * chunk + (n + 1) * width)
            there = slice(total + cut.start, total + cut.stop)
            acc_ref[there, :] += mm(second_t, exg_ref[cut, :], NT)

    @pl.when(step == tiles - 1)
    def _():
        sums_ref[...] = acc_ref[...].astype(BF)
        flat = jnp.sum(deb_acc[...].T, 0, keepdims=True)
        deb_ref[...] = jnp.zeros(deb_ref.shape, F32)
        for n in range(total // width):
            deb_ref[n : n + 1, :] = flat[:, n * width : (n + 1) * width]


def halves(tiles):
    return lambda t, h: (t + (1 - h[0]) * (tiles // 2)) % tiles


def feed_part(half, att_t, x, cot, wo, ob, g2, s2, wet, eb, wr, tile, chunk):
    length, width = x.shape
    total = wr.shape[0]
    tiles = length // tile
    where = halves(tiles)
    fixed = lambda a: pl.BlockSpec(a.shape, lambda t, h: (0, 0), pipeline_mode=pl.Buffered(1))
    whole = lambda dims: pl.BlockSpec(dims, lambda t, h: (0, 0))
    rows = pl.BlockSpec((tile, width), lambda t, h: (where(t, h), 0))
    cols = lambda high: pl.BlockSpec((high, tile), lambda t, h: (0, where(t, h)))
    return pl.pallas_call(
        functools.partial(feed_kernel, chunk, tiles),
        grid_spec=pltpu.PrefetchScalarGridSpec(
            num_scalar_prefetch=1,
            grid=(tiles,),
            in_specs=[cols(width), rows, rows] + [fixed(a) for a in (wo, ob, g2, s2, wet, eb, wr)],
            out_specs=[rows, cols(total), cols(total), whole((2 * total, width)), whole((8, width))],
            scratch_shapes=[pltpu.VMEM((2 * total, width), F32), pltpu.VMEM((total, 128), F32)],
        ),
        out_shape=[
            shape_of((length, width), F32),
            shape_of((total, length), BF),
            shape_of((total, length), BF),
            shape_of((2 * total, width), BF),
            shape_of((8, width), F32),
        ],
        compiler_params=params(),
        name="feed",
    )(half, att_t, x, cot, wo, ob, g2, s2, wet, eb, wr)


def middle_kernel(
    tiles, half_ref, att_ref, mid_ref, cot_ref, hid_ref, exg_ref, wo_ref, g2_ref, we_ref, wrt_ref,
    rb_ref, res_own, res_send, grad_ref, ag_ref, delta_ref, dwo_ref, vec_ref, acc_ref,
):
    step = pl.program_id(0)

    @pl.when(step == 0)
    def _():
        for ref in (acc_ref, vec_ref):
            ref[...] = jnp.zeros(ref.shape, F32)

    middle = mid_ref[...]
    cot = cot_ref[...].astype(F32)
    unit, scale = norm_parts(middle)
    norm_grad = mm(we_ref[...], exg_ref[...]).T
    result = (middle + BRANCH * (mm(wrt_ref[...], hid_ref[...]).T + rb_ref[...])).astype(BF)

    @pl.when(step < tiles // 2)
    def _():
        res_send[...] = result

    @pl.when(step >= tiles // 2)
    def _():
        res_own[0] = result

    middle_grad = cot + norm_back(norm_grad, unit, scale, g2_ref[...])
    grad_ref[...] = middle_grad
    mixed_grad = (BRANCH * middle_grad).astype(BF)
    acc_ref[...] += mm(att_ref[...].astype(BF), mixed_grad)
    att_grad = mm(mixed_grad, wo_ref[...], NT).astype(BF)
    ag_ref[...] = att_grad
    dots = att_grad.T.astype(F32) * att_ref[...]
    for head in range(H):
        delta_ref[head : head + 1, :] = jnp.sum(
            dots[HD * head : HD * head + HD, :], 0, keepdims=True
        )
    reduced_grad = (BRANCH * cot).astype(BF)
    sums = (norm_grad * unit, norm_grad, mixed_grad.astype(F32), reduced_grad.astype(F32))
    for n, value in enumerate(sums):
        vec_ref[n : n + 1, :] += jnp.sum(value, 0, keepdims=True)

    @pl.when(step == tiles - 1)
    def _():
        dwo_ref[...] = acc_ref[...].astype(BF)


def middle_part(half, att_t, mid, cot, hid, exg, wo, g2, we, wrt, rb, tile):
    length, width = mid.shape
    total = we.shape[1]
    tiles = length // tile
    part = tiles // 2
    where = halves(tiles)
    fixed = lambda a: pl.BlockSpec(a.shape, lambda t, h: (0, 0), pipeline_mode=pl.Buffered(1))
    whole = lambda dims: pl.BlockSpec(dims, lambda t, h: (0, 0))
    rows = pl.BlockSpec((tile, width), lambda t, h: (where(t, h), 0))
    cols = lambda high: pl.BlockSpec((high, tile), lambda t, h: (0, where(t, h)))
    return pl.pallas_call(
        functools.partial(middle_kernel, tiles),
        grid_spec=pltpu.PrefetchScalarGridSpec(
            num_scalar_prefetch=1,
            grid=(tiles,),
            in_specs=[cols(width), rows, rows, cols(total), cols(total)]
            + [fixed(a) for a in (wo, g2, we, wrt, rb)],
            out_specs=[
                pl.BlockSpec((1, tile, width), lambda t, h: (h[0], jnp.maximum(t - part, 0), 0)),
                pl.BlockSpec((tile, width), lambda t, h: (jnp.minimum(t, part - 1), 0)),
                rows,
                rows,
                cols(H),
                whole((width, width)),
                whole((8, width)),
            ],
            scratch_shapes=[pltpu.VMEM((width, width), F32)],
        ),
        out_shape=[
            shape_of((2, length // 2, width), BF),
            shape_of((length // 2, width), BF),
            shape_of((length, width), F32),
            shape_of((length, width), BF),
            shape_of((H, length), F32),
            shape_of((width, width), BF),
            shape_of((8, width), F32),
        ],
        compiler_params=params(),
        name="middle",
    )(half, att_t, mid, cot, hid, exg, wo, g2, we, wrt, rb)


def weight_kernel(parts, *refs):
    ins = refs[: 3 * parts]
    x_ref, gain_ref, shift_ref, extra_ref, dw_ref, acc_ref = refs[3 * parts :]
    step = pl.program_id(0)

    @pl.when(step == 0)
    def _():
        acc_ref[...] = jnp.zeros(acc_ref.shape, F32)

    width = x_ref.shape[1]
    unit, _ = norm_parts(x_ref[...].astype(F32))
    normed_t = (unit * gain_ref[...] + shift_ref[...]).astype(BF).T
    for n in range(3):
        grad = jnp.concatenate([ref[...] for ref in ins[n * parts : (n + 1) * parts]], 1)
        acc_ref[n * width : (n + 1) * width, :] += mm(normed_t, grad)

    @pl.when(step == pl.num_programs(0) - 1)
    def _():
        dw_ref[: 3 * width, :] = acc_ref[...].astype(BF)
        dw_ref[3 * width :, :] = extra_ref[...]


def weight_part(grads, x, gain, shift, extra, tile):
    length, width = x.shape
    rows = pl.BlockSpec((tile, width), lambda t: (t, 0))
    fixed = lambda a: pl.BlockSpec(a.shape, lambda t: (0, 0))
    flat = [part for group in grads for part in group]
    out = shape_of((4 * width, width), BF)
    return pl.pallas_call(
        functools.partial(weight_kernel, len(grads[0])),
        grid=(length // tile,),
        in_specs=[pl.BlockSpec((tile, part.shape[1]), lambda t: (t, 0)) for part in flat]
        + [rows, fixed(gain), fixed(shift), fixed(extra)],
        out_specs=fixed(out),
        scratch_shapes=[pltpu.VMEM((3 * width, width), F32)],
        out_shape=out,
        compiler_params=params(),
        name="weight",
    )(*flat, x, gain, shift, extra)


def last_kernel(parts, half_ref, *refs):
    ins, rest = refs[: 3 * parts], refs[3 * parts :]
    x_ref, mid_ref, gain_ref, weight_ref, own_ref, send_ref, vec_ref = rest
    step = pl.program_id(0)
    tiles = pl.num_programs(0)

    @pl.when(step == 0)
    def _():
        vec_ref[...] = jnp.zeros(vec_ref.shape, F32)

    width = x_ref.shape[1]
    unit, scale = norm_parts(x_ref[...].astype(F32))
    back = None
    grads = []
    for n in range(3):
        grad = jnp.concatenate([ref[...] for ref in ins[n * parts : (n + 1) * parts]], 1)
        one = mm(grad, weight_ref[:, n * width : (n + 1) * width], NT)
        back = one if back is None else back + one
        grads.append(grad)
    total = mid_ref[...] + norm_back(back, unit, scale, gain_ref[...])

    @pl.when(step < tiles // 2)
    def _():
        send_ref[...] = total.astype(BF)

    @pl.when(step >= tiles // 2)
    def _():
        own_ref[0] = total

    sums = (back * unit, back, grads[0].astype(F32), grads[2].astype(F32))
    for n, value in enumerate(sums):
        vec_ref[n : n + 1, :] += jnp.sum(value, 0, keepdims=True)


def last_part(half, grads, x, mid, gain, weight, tile):
    length, width = x.shape
    tiles = length // tile
    part = tiles // 2
    where = lambda t, h: (t + (1 - h[0]) * part) % tiles
    rows = pl.BlockSpec((tile, width), lambda t, h: (where(t, h), 0))
    fixed = lambda a: pl.BlockSpec(a.shape, lambda t, h: (0, 0))
    flat = [part for group in grads for part in group]
    vec = shape_of((8, width), F32)
    return pl.pallas_call(
        functools.partial(last_kernel, len(grads[0])),
        grid_spec=pltpu.PrefetchScalarGridSpec(
            num_scalar_prefetch=1,
            grid=(tiles,),
            in_specs=[
                pl.BlockSpec((tile, a.shape[1]), lambda t, h: (where(t, h), 0)) for a in flat
            ]
            + [rows] * 2
            + [fixed(gain), fixed(weight)],
            out_specs=[
                pl.BlockSpec((1, tile, width), lambda t, h: (h[0], jnp.maximum(t - part, 0), 0)),
                pl.BlockSpec((tile, width), lambda t, h: (jnp.minimum(t, part - 1), 0)),
                fixed(vec),
            ],
        ),
        out_shape=[shape_of((2, length // 2, width), F32), shape_of((length // 2, width), BF), vec],
        compiler_params=params(),
        name="last",
    )(half, *flat, x, mid, gain, weight)


def swapped(value):
    return lax.ppermute(value, "seq", [(0, 1), (1, 0)])


def side(hop):
    axis, bit = hop
    return (lax.axis_index(axis) // bit) % 2


def exchanged(value, hop):
    axis, bit = hop
    return lax.ppermute(value, axis, [(i, i ^ bit) for i in range(lax.axis_size(axis))])


def added(one, two):
    return (one.astype(F32) + two.astype(F32)).astype(BF)


def scatter(part, hop, whole=None):
    blocks, rows, width = part.shape
    mine = side(hop)
    piece = lambda place: lax.dynamic_slice_in_dim(part, place * (rows // 2), rows // 2, 1)
    send = piece(1 - mine)
    if whole is None:
        return added(piece(mine), exchanged(send, hop))
    send = jnp.concatenate([send.reshape(-1, width), whole], 0)
    got = exchanged(send, hop)
    cut = blocks * rows // 2
    return added(piece(mine), got[:cut].reshape(blocks, -1, width)), added(whole, got[cut:])


def gather(part, hop):
    got = exchanged(part, hop)
    return jnp.where(
        side(hop) == 0, jnp.concatenate([part, got], 1), jnp.concatenate([got, part], 1)
    )


def both(step, parts, hops, whole=None):
    first = step(parts[0], hops[0]) if whole is None else step(parts[0], hops[0], whole)
    second = step(parts[1], hops[1])
    return (first, second) if whole is None else ((first[0], second), first[1])


class AllSum:
    def __init__(self, rows):
        axes = {}
        for axis in ("dp", "seq"):
            size = lax.axis_size(axis)
            axes[axis] = [(axis, 1 << n) for n in range(size.bit_length() - 1)]
        self.core, one, two, *far = axes["dp"]
        self.pairs = [(one, two), (two, one)]
        self.rest = axes["seq"] + far
        self.state, self.whole = rows[None], None
        self.todo = [self.split] + [functools.partial(self.cross, p) for p in self.pairs]
        self.todo += [functools.partial(self.narrow, hop) for hop in self.rest]
        self.todo += [functools.partial(self.widen, hop) for hop in self.rest[::-1]]
        self.todo += [functools.partial(self.uncross, p) for p in self.pairs[::-1]] + [self.join]

    def scattered(self, parts, hops):
        if self.whole is None:
            return both(scatter, parts, hops)
        parts, self.whole = both(scatter, parts, hops, self.whole)
        return parts

    def split(self):
        part = scatter(self.state, self.core)
        mid = part.shape[1] // 2
        self.state = (part[:, :mid], part[:, mid:])

    def ride(self, whole):
        self.whole = added(whole, exchanged(whole, self.core))

    def cross(self, hops):
        self.state = self.scattered(self.state, hops)

    def narrow(self, hop):
        if isinstance(self.state, tuple):
            self.state = jnp.concatenate(self.state, 0)
        if self.whole is None:
            self.state = scatter(self.state, hop)
        else:
            self.state, self.whole = scatter(self.state, hop, self.whole)

    def widen(self, hop):
        self.state = gather(self.state, hop)

    def uncross(self, hops):
        if not isinstance(self.state, tuple):
            self.state = (self.state[:1], self.state[1:])
        self.state = both(gather, self.state, hops)

    def join(self):
        self.state = gather(jnp.concatenate(self.state, 1), self.core)[0]

    def step(self):
        self.todo.pop(0)()

    def beside(self, call, argument):
        argument = after(argument, self.state)
        self.step()
        out = call(argument)
        self.state = after(self.state, out)
        return out

    def result(self):
        while self.todo:
            self.step()
        return self.state


def after(value, earlier):
    return lax.optimization_barrier((value, earlier))[0]


def passed_along(block, axis, distance):
    devices = range(lax.axis_size(axis))
    route = [(i - distance, i) for i in devices if i - distance in devices]
    return lax.ppermute(block, axis, route)


def from_behind(value, axis, steps):
    count = lax.axis_size(axis)
    pairs = [(source, (source + steps) % count) for source in range(count)]
    return lax.ppermute(value, axis, pairs)


def layer_norm(values, gain_vec, shift_vec):
    center = jnp.mean(values, -1, keepdims=True)
    centered = values - center
    variance = jnp.mean(centered * centered, -1, keepdims=True)
    return centered * lax.rsqrt(variance + EPSILON) * gain_vec + shift_vec


def gelu_tanh(values):
    return jax.nn.gelu(values, approximate=True)


def plain_dot(left, right):
    return jnp.dot(left, right, preferred_element_type=jnp.float32)


def left_dot(left, right):
    return lax.dot_general(
        left, right, (((0,), (0,)), ((), ())), preferred_element_type=jnp.float32
    )


def right_dot(left, right):
    return lax.dot_general(
        left, right, (((1,), (1,)), ((), ())), preferred_element_type=jnp.float32
    )


def block_scores(queries, keys_block, query_seg, key_seg, query_places, key_start):
    row_count, key_len, width = keys_block.shape
    keys_heads = keys_block.reshape(row_count, key_len, H, HD)
    scores = jnp.einsum(
        "rqhd,rkhd->rhqk", queries, keys_heads, preferred_element_type=jnp.float32
    ) * HD ** (-0.5)
    key_places = key_start + jnp.arange(key_len, dtype=jnp.int32)
    allowed = (query_seg[:, None, :, None] == key_seg[:, None, None, :]) & (
        key_places[None, None, None, :] <= query_places[None, None, :, None]
    )
    return (scores, allowed)


def attend_block(state, queries, block, query_seg, query_places, key_start):
    run_max, run_sum, running = state
    keys_block, values_block, key_seg = block
    row_count, key_len, width = values_block.shape
    query_len = queries.shape[1]
    scores, allowed = block_scores(queries, keys_block, query_seg, key_seg, query_places, key_start)
    block_max = jnp.max(jnp.where(allowed, scores, NEGATIVE), -1)
    new_max = jnp.maximum(run_max, block_max)
    exponent = jnp.where(allowed, jnp.exp(scores - new_max[..., None]), 0.0)
    factor = jnp.exp(run_max - new_max)
    new_sum = run_sum * factor + jnp.sum(exponent, -1)
    values_heads = values_block.reshape(row_count, key_len, H, HD)
    addition = jnp.einsum(
        "rhqk,rkhd->rqhd",
        exponent.astype(jnp.bfloat16),
        values_heads,
        preferred_element_type=jnp.float32,
    )
    scaled = (
        running.reshape(row_count, query_len, H, HD) * jnp.transpose(factor, (0, 2, 1))[..., None]
    )
    return (new_max, new_sum, (scaled + addition).reshape(row_count, query_len, width))


def grad_block(queries, out_grad, log_sum, delta, block, query_seg, query_places, key_start):
    keys_block, values_block, key_seg = block
    row_count, key_len, width = keys_block.shape
    scores, allowed = block_scores(queries, keys_block, query_seg, key_seg, query_places, key_start)
    weights_block = jnp.where(allowed, jnp.exp(scores - log_sum[..., None]), 0.0)
    keys_heads = keys_block.reshape(row_count, key_len, H, HD)
    values_heads = values_block.reshape(row_count, key_len, H, HD)
    value_dots = jnp.einsum(
        "rqhd,rkhd->rhqk", out_grad, values_heads, preferred_element_type=jnp.float32
    )
    score_grad = (weights_block * (value_dots - delta[..., None]) * HD ** (-0.5)).astype(
        jnp.bfloat16
    )
    query_part = jnp.einsum(
        "rhqk,rkhd->rqhd", score_grad, keys_heads, preferred_element_type=jnp.float32
    ).reshape(row_count, -1, width)
    key_part = jnp.einsum(
        "rhqk,rqhd->rkhd", score_grad, queries, preferred_element_type=jnp.float32
    ).reshape(row_count, key_len, width)
    value_part = jnp.einsum(
        "rhqk,rqhd->rkhd",
        weights_block.astype(jnp.bfloat16),
        out_grad,
        preferred_element_type=jnp.float32,
    ).reshape(row_count, key_len, width)
    return (query_part, key_part, value_part)


def local(
    activations,
    segments,
    first_gain,
    first_shift,
    input_weight,
    query_bias,
    value_bias,
    output_weight,
    output_bias,
    second_gain,
    second_shift,
    expand_weight,
    expand_bias,
    reduce_weight,
    reduce_bias,
    cotangent,
):
    row_total, span_len, width = activations.shape
    cycle_size = lax.axis_size("seq")
    position = lax.axis_index("seq")
    micro_rows = row_total // MICRO
    branch = DEPTH ** (-0.5)
    bias_all = jnp.concatenate([query_bias, jnp.zeros_like(query_bias), value_bias])
    query_places = position * span_len + jnp.arange(span_len, dtype=jnp.int32)
    totals = [
        jnp.zeros(argument.shape, jnp.float32)
        for argument in (
            first_gain,
            first_shift,
            input_weight,
            query_bias,
            value_bias,
            output_weight,
            output_bias,
            second_gain,
            second_shift,
            expand_weight,
            expand_bias,
            reduce_weight,
            reduce_bias,
        )
    ]
    outputs_list = []
    grads_list = []
    for micro in range(MICRO):
        lower = micro * micro_rows
        values_in = activations[lower : lower + micro_rows].astype(jnp.float32)
        query_seg = segments[lower : lower + micro_rows]
        out_cot = cotangent[lower : lower + micro_rows].astype(jnp.float32)
        normed, first_pull = jax.vjp(layer_norm, values_in, first_gain, first_shift)
        normed_low = normed.astype(jnp.bfloat16).reshape(-1, width)
        projected = (plain_dot(normed_low, input_weight) + bias_all).astype(jnp.bfloat16)
        queries = projected[:, :width].reshape(micro_rows, span_len, H, HD)
        keys_own = projected[:, width : 2 * width].reshape(micro_rows, span_len, width)
        values_own = projected[:, 2 * width :].reshape(micro_rows, span_len, width)
        own_block = (keys_own, values_own, query_seg)
        start_state = (
            jnp.full((micro_rows, H, span_len), NEGATIVE, jnp.float32),
            jnp.zeros((micro_rows, H, span_len), jnp.float32),
            jnp.zeros((micro_rows, span_len, width), jnp.float32),
        )
        state = attend_block(
            start_state, queries, own_block, query_seg, query_places, position * span_len
        )

        def cycle_forward(step_index, carry):
            block, inner_state = carry
            block = passed_along((block[0], block[1], block[2]), "seq", 1)
            source = (position - step_index) % cycle_size
            inner_state = lax.cond(
                source < position,
                lambda current: attend_block(
                    current, queries, block, query_seg, query_places, source * span_len
                ),
                lambda current: current,
                inner_state,
            )
            return (block, inner_state)

        unused_block, state = lax.fori_loop(1, cycle_size, cycle_forward, (own_block, state))
        run_max, run_sum, running = state
        attended = (
            running.reshape(micro_rows, span_len, H, HD)
            / jnp.transpose(run_sum, (0, 2, 1))[..., None]
        ).reshape(micro_rows, span_len, width)
        log_sum = run_max + jnp.log(run_sum)
        attended_low = attended.astype(jnp.bfloat16).reshape(-1, width)
        mixed_out = plain_dot(attended_low, output_weight) + output_bias
        middle = values_in + branch * mixed_out.reshape(values_in.shape)
        second_norm, second_pull = jax.vjp(layer_norm, middle, second_gain, second_shift)
        second_low = second_norm.astype(jnp.bfloat16).reshape(-1, width)
        expanded = plain_dot(second_low, expand_weight) + expand_bias
        hidden, gelu_pull = jax.vjp(gelu_tanh, expanded)
        hidden_low = hidden.astype(jnp.bfloat16)
        reduced = plain_dot(hidden_low, reduce_weight) + reduce_bias
        outputs_list.append(
            (middle + branch * reduced.reshape(values_in.shape)).astype(jnp.bfloat16)
        )
        reduced_grad = (branch * out_cot).reshape(-1, width).astype(jnp.bfloat16)
        totals[12] = totals[12] + jnp.sum(reduced_grad.astype(jnp.float32), 0)
        totals[11] = totals[11] + left_dot(hidden_low, reduced_grad)
        (expanded_grad,) = gelu_pull(right_dot(reduced_grad, reduce_weight))
        expanded_low = expanded_grad.astype(jnp.bfloat16)
        totals[10] = totals[10] + jnp.sum(expanded_low.astype(jnp.float32), 0)
        totals[9] = totals[9] + left_dot(second_low, expanded_low)
        norm_in_grad = right_dot(expanded_low, expand_weight).reshape(values_in.shape)
        middle_part, gain_part, shift_part = second_pull(norm_in_grad)
        totals[7] = totals[7] + gain_part
        totals[8] = totals[8] + shift_part
        middle_grad = out_cot + middle_part
        mixed_grad = (branch * middle_grad).reshape(-1, width).astype(jnp.bfloat16)
        totals[6] = totals[6] + jnp.sum(mixed_grad.astype(jnp.float32), 0)
        totals[5] = totals[5] + left_dot(attended_low, mixed_grad)
        attended_grad = (
            right_dot(mixed_grad, output_weight)
            .astype(jnp.bfloat16)
            .reshape(micro_rows, span_len, H, HD)
        )
        delta = jnp.transpose(
            jnp.sum(
                attended_grad.astype(jnp.float32) * attended.reshape(micro_rows, span_len, H, HD),
                -1,
            ),
            (0, 2, 1),
        )
        query_grad, key_grad, value_grad = grad_block(
            queries,
            attended_grad,
            log_sum,
            delta,
            own_block,
            query_seg,
            query_places,
            position * span_len,
        )

        def cycle_backward(step_index, carry):
            block, partial_value, query_acc = carry
            block = passed_along((block[0], block[1], block[2]), "seq", 1)
            partial_value = (
                from_behind(partial_value[0].astype(jnp.bfloat16), "seq", 1).astype(jnp.float32),
                from_behind(partial_value[1].astype(jnp.bfloat16), "seq", 1).astype(jnp.float32),
            )
            source = (position - step_index) % cycle_size

            def work(current):
                partial_in, query_in = current
                query_part, key_part, value_part = grad_block(
                    queries,
                    attended_grad,
                    log_sum,
                    delta,
                    block,
                    query_seg,
                    query_places,
                    source * span_len,
                )
                return (
                    (partial_in[0] + key_part, partial_in[1] + value_part),
                    query_in + query_part,
                )

            partial_value, query_acc = lax.cond(
                source < position, work, lambda current: current, (partial_value, query_acc)
            )
            return (block, partial_value, query_acc)

        unused_block, partial_value, query_grad = lax.fori_loop(
            1, cycle_size, cycle_backward, (own_block, (key_grad, value_grad), query_grad)
        )
        key_grad, value_grad = (
            from_behind(partial_value[0].astype(jnp.bfloat16), "seq", 1).astype(jnp.float32),
            from_behind(partial_value[1].astype(jnp.bfloat16), "seq", 1).astype(jnp.float32),
        )
        qkv_grad = (
            jnp.concatenate([query_grad, key_grad, value_grad], -1)
            .reshape(-1, 3 * width)
            .astype(jnp.bfloat16)
        )
        totals[3] = totals[3] + jnp.sum(qkv_grad[:, :width].astype(jnp.float32), 0)
        totals[4] = totals[4] + jnp.sum(qkv_grad[:, 2 * width :].astype(jnp.float32), 0)
        totals[2] = totals[2] + left_dot(normed_low, qkv_grad)
        norm_grad = right_dot(qkv_grad, input_weight).reshape(values_in.shape)
        input_part, gain_one, shift_one = first_pull(norm_grad)
        totals[0] = totals[0] + gain_one
        totals[1] = totals[1] + shift_one
        grads_list.append(middle_grad + input_part)
    summed = lax.psum(
        (
            totals[0],
            totals[1],
            totals[2],
            totals[3],
            totals[4],
            totals[5],
            totals[6],
            totals[7],
            totals[8],
            totals[9],
            totals[10],
            totals[11],
            totals[12],
        ),
        ("dp", "seq"),
    )
    return (
        jnp.concatenate(outputs_list, 0),
        jnp.concatenate(grads_list, 0),
        summed[0],
        summed[1],
        summed[2],
        summed[3],
        summed[4],
        summed[5],
        summed[6],
        summed[7],
        summed[8],
        summed[9],
        summed[10],
        summed[11],
        summed[12],
    )


def local_rows(
    activations,
    segments,
    first_gain,
    first_shift,
    input_weight,
    query_bias,
    value_bias,
    output_weight,
    output_bias,
    second_gain,
    second_shift,
    expand_weight,
    expand_bias,
    reduce_weight,
    reduce_bias,
    cotangent,
):
    rows, span, width = activations.shape
    mine = lax.axis_index("seq")
    half = mine.astype(jnp.int32)[None]
    take = lambda array, index: lax.dynamic_index_in_dim(array, index, 0, keepdims=False)
    row = lambda vector: vector.reshape(1, -1)
    seg_got = swapped(take(segments, 1 - mine))
    x_got = swapped(after(take(activations, 1 - mine), seg_got))

    def in_order(own, got):
        return jnp.where(
            mine == 0, jnp.concatenate([own, got], 0), jnp.concatenate([got, own], 0)
        )

    bias = jnp.concatenate([query_bias, jnp.zeros_like(query_bias), value_bias])
    gain = row(first_gain)
    weights = (gain, row(first_shift), input_weight, row(bias))
    start, table = documents(half, row(take(segments, mine)), row(seg_got), BLOCK)
    *before, norms = project(half, take(activations, mine), *weights, None, TILE)
    cot_got = swapped(after(take(cotangent, 1 - mine), (x_got, norms)))
    x, q, k, v, kt, vt, more = project(1 - half, x_got, *weights, before, TILE)
    norms = jnp.maximum(norms, more)
    limit = jnp.max(norms[0] * norms[1]) * (SCALE2 * SCALE2)
    small = (limit < SMALL * SMALL).astype(jnp.int32)[None]
    att_t, lse = attend(table, small, q, k, vt, start, BLOCK, FORWARD_HEADS)
    lse = lse.reshape(H, -1)
    cot = in_order(take(cotangent, mine), cot_got)
    mid, hid, exg, sums, vec_expand = feed_part(
        half, att_t, x, cot, output_weight, row(output_bias), row(second_gain), row(second_shift),
        expand_weight.T, expand_bias.reshape(-1, 1), reduce_weight, TILE, CHUNK,
    )

    sums = AllSum(sums)
    result, result_send, mid_grad, att_grad, delta, d_output, vec = sums.beside(
        lambda half: middle_part(
            half, att_t, mid, cot, hid, exg, output_weight, row(second_gain), expand_weight,
            reduce_weight.T, row(reduce_bias), TILE,
        ),
        half,
    )
    result_got = swapped(result_send)
    grads = []
    first = 0
    for count in BACKWARD_HEADS:
        grads.append(
            sums.beside(
                lambda table: attend_back(
                    first, count, table, q, k, kt, v, att_grad, start, lse, delta, BLOCK
                ),
                table,
            )
        )
        first += count
    grads = [[g[n] for g in grads] for n in range(3)]
    dw = sums.beside(
        lambda gain: weight_part(grads, x, gain, row(first_shift), d_output, TILE), gain
    )
    tail = AllSum(dw)
    tail.step()
    grad, grad_send, vec_last = sums.beside(
        lambda half: last_part(half, grads, x, mid_grad, gain, input_weight, TILE), half
    )
    grad_got = swapped(grad_send)
    tail.ride(jnp.concatenate([vec[:4], vec_expand[:4], vec_last], 0).astype(BF))
    dw = tail.result()
    part = sums.result()
    place = lambda whole, got: lax.dynamic_update_index_in_dim(
        whole, got.astype(whole.dtype), 1 - mine, 0
    )
    total = expand_weight.shape[1]

    def beside(stack):
        blocks = stack.shape[0] // width
        return jnp.concatenate([stack[n * width : (n + 1) * width] for n in range(blocks)], 1).astype(F32)

    vectors = tail.whole.astype(F32)
    return (
        place(result, result_got),
        place(grad, grad_got),
        vectors[8],
        vectors[9],
        beside(dw[: 3 * width]),
        vectors[10],
        vectors[11],
        dw[3 * width :].astype(F32),
        vectors[2],
        vectors[0],
        vectors[1],
        beside(part[total:]),
        vectors[4:8].reshape(-1),
        part[:total].astype(F32),
        vectors[3],
    )


TILE = 512
CHUNK = 512
BLOCK = 512
SMALL = 60.0
FORWARD_HEADS = 8
BACKWARD_HEADS = (2, 2, 2, 2)


def solution(mesh):
    sizes = dict(zip(mesh.axis_names, mesh.devices.shape))
    tokens, places, whole = P("dp", "seq", None), P("dp", "seq"), P()
    in_specs = (tokens, places) + (whole,) * 13 + (tokens,)
    out_specs = (tokens, tokens) + (whole,) * 13

    def program(activations, *rest):
        rows = activations.shape[0] // sizes["dp"]
        span = activations.shape[1] // sizes["seq"]
        by_rows = sizes["seq"] == 2 and rows == 2 and span % BLOCK == 0 and sizes["dp"] == 16
        return jax.shard_map(
            local_rows if by_rows else local,
            mesh=mesh,
            in_specs=in_specs,
            out_specs=out_specs,
            check_vma=False,
        )(activations, *rest)

    return program
```

```python
import functools

import jax
import jax.numpy as jnp
from jax import lax
from jax.experimental import pallas as pl
from jax.experimental.pallas import tpu as pltpu
from jax.sharding import PartitionSpec as P

H = 8
HD = 64
DEPTH = 48
MICRO = 2
EPSILON = 1e-05
NEGATIVE = -1e30
BRANCH = DEPTH ** (-0.5)
SCALE = HD ** (-0.5)
SCALE2 = SCALE * 1.4426950408889634
GELU_A = 0.7978845608028654
GELU_B = GELU_A * 0.044715

BF = jnp.bfloat16
F32 = jnp.float32
NN = (((1,), (0,)), ((), ()))
NT = (((1,), (1,)), ((), ()))
VMEM_LIMIT = 58 << 20


def mm(left, right, dims=NN):
    return lax.dot_general(left, right, dims, preferred_element_type=F32)


def shape_of(dims, dtype):
    return jax.ShapeDtypeStruct(dims, dtype)


def params(limit=VMEM_LIMIT):
    return pltpu.CompilerParams(vmem_limit_bytes=limit)


def norm_parts(values):
    center = jnp.mean(values, -1, keepdims=True)
    centered = values - center
    variance = jnp.mean(centered * centered, -1, keepdims=True)
    scale = lax.rsqrt(variance + EPSILON)
    return centered * scale, scale


def norm_back(grad, unit, scale, gain):
    inner = grad * gain
    first = jnp.mean(inner, -1, keepdims=True)
    second = jnp.mean(inner * unit, -1, keepdims=True)
    return scale * (inner - first - unit * second)


def own_and_got(tiles):
    part = tiles // 2
    return (
        lambda t, h: (t + (1 - h[0]) * part) % tiles,
        lambda t, h: jnp.minimum(t, part - 1),
        lambda t, h: jnp.maximum(t - part, 0),
    )


def row_specs(tile, width, tiles):
    where, got, own = own_and_got(tiles)
    return (
        pl.BlockSpec((tile, width), lambda t, h: (got(t, h), 0)),
        pl.BlockSpec((1, tile, width), lambda t, h: (h[0], own(t, h), 0)),
    )


def either(got_ref, own_ref):
    early = pl.program_id(0) < pl.num_programs(0) // 2
    return jnp.where(early, got_ref[...], own_ref[0])


def once(array):
    return pl.BlockSpec(array.shape, lambda t, *_: (0,) * array.ndim, pipeline_mode=pl.Buffered(1))


def kept(dims):
    return pl.BlockSpec(dims, lambda t, *_: (0,) * len(dims))


def largest_norms(block):
    lane = lax.broadcasted_iota(jnp.int32, (block.shape[1], 128), 1)
    column = lax.broadcasted_iota(jnp.int32, (block.shape[1], 128), 0)
    member = jnp.where(column // HD == lane, 1.0, 0.0).astype(BF)
    wide = block.astype(F32)
    return jnp.max(mm((wide * wide).astype(BF), member), 0, keepdims=True)


def project_kernel(place, x_ref, gain_ref, shift_ref, weight_ref, bias_ref, *refs):
    q_ref, k_ref, v_ref, norm_ref = refs[-4:]
    width = weight_ref.shape[0]
    unit, _ = norm_parts(x_ref[...].reshape(-1, width).astype(F32))
    normed = (unit * gain_ref[...] + shift_ref[...]).astype(BF)

    @pl.when(pl.program_id(0) == 0)
    def _():
        norm_ref[...] = jnp.zeros(norm_ref.shape, F32)

    for n, ref in enumerate((q_ref, k_ref, v_ref)):
        cols = slice(n * width, (n + 1) * width)
        out = (mm(normed, weight_ref[:, cols]) + bias_ref[:, cols]).astype(BF)
        ref[...] = out
        if n < 2:
            norm_ref[n : n + 1, :] = jnp.maximum(norm_ref[n : n + 1, :], largest_norms(out))


def project(own, half, x, gain, shift, weight, bias, before, tile):
    span, width = x.shape[-2:]
    count = span // tile
    length = 2 * span
    if own:
        x_spec = pl.BlockSpec((1, tile, width), lambda t, h: (h[0], t, 0))
        here = lambda h: h[0]
    else:
        x_spec = pl.BlockSpec((tile, width), lambda t, h: (t, 0))
        here = lambda h: 1 - h[0]
    rows = pl.BlockSpec((tile, width), lambda t, h: (here(h) * count + t, 0))
    nat = shape_of((length, width), BF)
    return pl.pallas_call(
        project_kernel,
        grid_spec=pltpu.PrefetchScalarGridSpec(
            num_scalar_prefetch=1,
            grid=(count,),
            in_specs=[x_spec, once(gain), once(shift), once(weight), once(bias)]
            + [pl.BlockSpec(memory_space=pl.ANY)] * len(before),
            out_specs=[rows, rows, rows, kept((8, 128))],
        ),
        out_shape=[nat, nat, nat, shape_of((8, 128), F32)],
        input_output_aliases={6 + i: i for i in range(len(before))},
        compiler_params=params(),
        name="project",
    )(half, x, gain, shift, weight, bias, *before)


def document_kernel(size, half_ref, own_ref, got_ref, start_ref, table_ref):
    span = own_ref.shape[1]
    place = lambda half: pl.ds(pl.multiple_of(half * span, span), span)
    start_ref[0:1, place(half_ref[0])] = own_ref[...]
    start_ref[0:1, place(1 - half_ref[0])] = got_ref[...]
    numbers = start_ref[...]
    start = jnp.zeros_like(numbers)
    for number in range(1, 8):
        before = jnp.sum((numbers < number).astype(jnp.int32), 1, keepdims=True)
        start = jnp.where(numbers == number, before, start)
    start_ref[...] = start
    count = start.shape[1] // size
    slots = table_ref.shape[0] - 1
    for slot in range(slots):
        table_ref[slot] = 0
    filled = jnp.int32(0)
    for i in range(count):
        block = start[:, i * size : (i + 1) * size]
        low, high = jnp.min(block), jnp.max(block)
        for j in range(i + 1):
            kind = jnp.where(high > j * size, 2, 1 if i == j else 0)
            active = low < (j + 1) * size

            table_ref[filled] = jnp.where(active, i + 256 * j + 65536 * kind, 0)
            filled = filled + active.astype(jnp.int32)
    table_ref[slots] = filled


def documents(half, own, got, size):
    length = 2 * own.shape[1]
    count = length // size
    row = lambda wide: pl.BlockSpec((1, wide), lambda t, h: (0, 0))
    return pl.pallas_call(
        functools.partial(document_kernel, size),
        grid_spec=pltpu.PrefetchScalarGridSpec(
            num_scalar_prefetch=1,
            grid=(1,),
            in_specs=[row(length // 2), row(length // 2)],
            out_specs=[row(length), pl.BlockSpec(memory_space=pltpu.SMEM)],
        ),
        out_shape=[
            shape_of((1, length), jnp.int32),
            shape_of((count * (count + 1) // 2 + 2,), jnp.int32),
        ],
        compiler_params=params(),
        name="documents",
    )(half, own, got)


def head_half(block, head):
    lane = lax.broadcasted_iota(jnp.int32, block.shape, 1)
    keep = (lane < HD) if head % 2 == 0 else (lane >= HD)
    return jnp.where(keep, block, jnp.zeros_like(block))


def lanes_of(heads, group, head):
    low = HD * heads * group + 2 * HD * (head // 2)
    return pl.ds(pl.multiple_of(low, 2 * HD), 2 * HD)


def rows_of(heads, group, head):
    return pl.ds(pl.multiple_of(HD * heads * group + HD * head, HD), HD)


class Blocks:
    def __init__(self, size, list_ref, start_ref, mask_ref, values):
        self.size, self.list = size, list_ref
        self.start, self.mask, self.values = start_ref, mask_ref, values

    def at(self, index):
        return pl.ds(pl.multiple_of(index * self.size, self.size), self.size)

    def places(self):
        dims = (self.size, self.size)
        return lax.broadcasted_iota(jnp.int32, dims, 0), lax.broadcasted_iota(jnp.int32, dims, 1)

    def fill(self, slot, i, j):
        key, query = self.places()
        key, query = key + j * self.size, query + i * self.size
        allowed = (key >= self.start[0:1, self.at(i)]) & (key <= query)
        self.mask[slot] = jnp.where(allowed, *self.values).astype(self.mask.dtype)

    def entry(self, step):
        packed = self.list[step]
        kind = packed // 65536
        return packed % 256, (packed // 256) % 256, jnp.where(kind == 2, 2 + lax.rem(step, 2), kind)

    def prepare(self, slot, i, j):
        pl.when(slot >= 2)(lambda: self.fill(slot, i, j))

    def walk(self, variants, heads, loops, early, late, row_begin, step_end, row_end):
        steps = self.list[self.list.shape[0] - 1]
        self.mask[0] = jnp.full(self.mask.shape[1:], self.values[0], self.mask.dtype)
        key, query = self.places()
        self.mask[1] = jnp.where(key <= query, *self.values).astype(self.mask.dtype)
        i, j, slot = self.entry(0)
        self.prepare(slot, i, j)
        row_begin(i)
        zero = jnp.int32(0)
        early(zero, 0, i, j, slot, False)

        def body(turn, carry):
            i, j, slot = carry
            group = lax.rem(turn, loops)
            last = group == loops - 1
            after = self.entry(turn // loops + 1)
            ni, nj, nslot = (jnp.where(last, new, old) for new, old in zip(after, carry))
            ngroup = jnp.where(last, 0, group + 1)
            pl.when(last)(lambda: self.prepare(nslot, ni, nj))
            pl.when(ni > i)(lambda: row_begin(ni))

            def work(corner, slot):
                for head in range(heads):
                    if head + 1 < heads:
                        early(group, head + 1, i, j, slot, corner)
                    else:
                        early(ngroup, 0, ni, nj, nslot, False)
                    late(group, head, i, j, corner)

            if variants == 1:
                work(False, slot)
            elif variants == 2:
                pl.when(i != j)(lambda: work(False, slot))
                pl.when(i == j)(lambda: work(True, slot))
            else:
                pl.when(slot == 0)(lambda: work(False, None))
                pl.when((slot > 0) & (i == j))(lambda: work(True, slot))
                pl.when((slot > 0) & (i != j))(lambda: work(False, slot))

            @pl.when(last)
            def _():
                step_end(i, j)
                pl.when(j == i)(lambda: row_end(i))

            return ni, nj, nslot

        lax.fori_loop(0, steps * loops, body, (i, j, slot))


def pieces(corner, size):
    if not corner:
        return [(slice(0, size), slice(0, size))]
    mid = size // 2
    return [(slice(0, mid), slice(0, size)), (slice(mid, size), slice(mid, size))]


def part_at(size, index, part):
    low = index * size + part.start
    return pl.ds(pl.multiple_of(low, size // 2), part.stop - part.start)


class Blockwise:
    def __init__(self, size, first, source, target, sems):
        self.size, self.first = size, first
        self.source, self.target, self.sems = source, target, sems

    def copy(self, block):
        rows = pl.ds(pl.multiple_of(block * self.size, self.size), self.size)
        lanes = pl.ds(self.first, self.target.shape[1])
        return pltpu.make_async_copy(
            self.source.at[rows, lanes], self.target.at[rows, :], self.sems.at[block]
        )


def forward_kernel(
    size, list_ref, small_ref, q_hbm, k_hbm, v_hbm, start_ref, out_hbm, lse_ref, q_ref, k_ref, v_ref,
    vt_ref, stage_ref, in_sems, out_sems, max_ref, new_ref, acc_ref, bias_ref, mask_ref, *slots,
):
    heads = FORWARD_HEADS
    loops = H // heads
    scores, probs_of = slots[:heads], slots[heads:]
    plain = Blocks(size, list_ref, start_ref, mask_ref, (1.0, 0.0))
    general = Blocks(size, list_ref, start_ref, bias_ref, (0.0, NEGATIVE))
    at = plain.at
    count = q_ref.shape[0] // size
    loads = [
        Blockwise(size, 0, source, target, in_sems.at[n])
        for n, (source, target) in enumerate(((k_hbm, k_ref), (q_hbm, q_ref), (v_hbm, v_ref)))
    ]
    for block in range(count):
        for load in loads:
            load.copy(block).start()

    def store(i):
        cols = pl.ds(pl.multiple_of(i * size, size), size)
        return pltpu.make_async_copy(stage_ref.at[:, cols], out_hbm.at[:, cols], out_sems.at[i])

    def row_begin(i):
        for load in loads:
            load.copy(i).wait()
        vt_ref[:, at(i)] = v_ref[at(i), :].T

    def products(group, head, i, j, keys, queries):
        lanes = lanes_of(heads, group, head)
        block = head_half(k_ref[part_at(size, j, keys), lanes], head)
        return mm(block, q_ref[part_at(size, i, queries), lanes], NT)

    def values(group, head, j, keys):
        block = vt_ref[rows_of(heads, group, head), part_at(size, j, keys)]
        return jnp.concatenate([block, jnp.ones((16, keys.stop - keys.start), BF)], 0)

    def early_plain(group, head, i, j, slot, corner):
        for keys, queries in pieces(corner, size):
            probs = jnp.exp2(products(group, head, i, j, keys, queries) * SCALE2).astype(BF)
            if slot is not None:
                probs = probs * mask_ref[slot, keys, queries]
            probs_of[head][keys, queries] = probs

    def late_plain(group, head, i, j, corner):
        for keys, queries in pieces(corner, size):
            acc_ref[heads * group + head, :, queries] += mm(values(group, head, j, keys), probs_of[head][keys, queries])

    whole = slice(0, size)

    def early(group, head, i, j, slot, corner):
        s = products(group, head, i, j, whole, whole)
        if slot is not None:
            s = s + bias_ref[slot]
        scores[head][...] = s
        new_ref[heads * group + head] = jnp.max(s, 0, keepdims=True)

    def late(group, head, i, j, corner):
        place = heads * group + head
        old = max_ref[place]
        new = jnp.maximum(old, new_ref[place])
        max_ref[place] = new
        probs = jnp.exp2(scores[head][...] * SCALE2 - new * SCALE2)
        factor = jnp.exp2((old - new) * SCALE2)
        acc_ref[place] = acc_ref[place] * factor + mm(
            values(group, head, j, whole), probs.astype(BF)
        )

    def reset(largest):
        max_ref[...] = jnp.full(max_ref.shape, largest, F32)
        acc_ref[...] = jnp.zeros(acc_ref.shape, F32)

    def row_end(largest, i):
        def one(head, carry):
            total = acc_ref[head, HD : HD + 1, :]
            rows = pl.ds(pl.multiple_of(HD * head, HD), HD)
            stage_ref[rows, at(i)] = (acc_ref[head, :HD, :] * (1.0 / total)).astype(BF)
            lse_ref[head, :, at(i)] = max_ref[head] * SCALE2 + jnp.log2(total)
            return carry

        lax.fori_loop(0, H, one, 0)
        store(i).start()
        reset(largest)

    def run(variants, blocks, largest, early, late):
        reset(largest)
        blocks.walk(
            variants, heads, loops, early, late, row_begin, lambda i, j: None, functools.partial(row_end, largest)
        )

    pl.when(small_ref[0] == 1)(lambda: run(2, plain, 0.0, early_plain, late_plain))
    pl.when(small_ref[0] != 1)(lambda: run(1, general, NEGATIVE, early, late))
    for i in range(count):
        store(i).wait()


def attend(table, small, q, k, v, start, size):
    length, width = q.shape
    count = length // size
    far = pl.BlockSpec(memory_space=pl.ANY)
    near = pltpu.VMEM((length, width), BF)
    return pl.pallas_call(
        functools.partial(forward_kernel, size),
        grid_spec=pltpu.PrefetchScalarGridSpec(
            num_scalar_prefetch=2,
            grid=(1,),
            in_specs=[far, far, far, once(start)],
            out_specs=[far, kept((H, 1, length))],
            scratch_shapes=[
                near,
                near,
                near,
                pltpu.VMEM((width, length), BF),
                pltpu.VMEM((width, length), BF),
                pltpu.SemaphoreType.DMA((3, count)),
                pltpu.SemaphoreType.DMA((count,)),
                pltpu.VMEM((H, 1, size), F32),
                pltpu.VMEM((H, 1, size), F32),
                pltpu.VMEM((H, HD + 16, size), F32),
                pltpu.VMEM((4, size, size), F32),
                pltpu.VMEM((4, size, size), BF),
            ]
            + [pltpu.VMEM((size, size), F32)] * FORWARD_HEADS
            + [pltpu.VMEM((size, size), BF)] * FORWARD_HEADS,
        ),
        out_shape=[shape_of((width, length), BF), shape_of((H, 1, length), F32)],
        compiler_params=params(),
        name="attend",
    )(table, small, q, k, v, start)


def backward_kernel(
    size, heads, first, list_ref, q_hbm, k_hbm, v_hbm, do_hbm, start_ref, lse_ref, delta_ref,
    dq_hbm, dk_hbm, dv_hbm, q_ref, k_ref, v_ref, do_ref, kt_ref, dq_ref, dk_ref, dv_ref, in_sems,
    out_sems, dqt_acc, dk_acc, dv_acc, bias_ref, *slots,
):
    probs_of, grads_of = slots[:heads], slots[heads:]
    walk = Blocks(size, list_ref, start_ref, bias_ref, (0.0, NEGATIVE))
    at = walk.at
    count = q_ref.shape[0] // size
    pairs = ((k_hbm, k_ref), (q_hbm, q_ref), (v_hbm, v_ref), (do_hbm, do_ref))
    loads = [
        Blockwise(size, first * HD, source, target, in_sems.at[n])
        for n, (source, target) in enumerate(pairs)
    ]
    for block in range(count):
        for load in loads:
            load.copy(block).start()

    def store(n, block):
        source, target = ((dq_ref, dq_hbm), (dk_ref, dk_hbm), (dv_ref, dv_hbm))[n]
        rows = at(block)
        return pltpu.make_async_copy(
            source.at[rows, :], target.at[rows, :], out_sems.at[n, block]
        )

    def row_begin(i):
        for load in loads:
            load.copy(i).wait()
        kt_ref[:, at(i)] = k_ref[at(i), :].T
        dk_acc[at(i), :] = jnp.zeros((size, dk_acc.shape[1]), F32)
        dv_acc[at(i), :] = jnp.zeros((size, dv_acc.shape[1]), F32)

    def early(group, head, i, j, slot, corner):
        lanes = slice(2 * HD * (head // 2), 2 * HD * (head // 2) + 2 * HD)
        for keys, queries in pieces(corner, size):
            at_j, at_i = part_at(size, j, keys), part_at(size, i, queries)
            stat = (first + head, slice(None), at_i)
            s = mm(head_half(k_ref[at_j, lanes], head), q_ref[at_i, lanes], NT)
            dots = mm(head_half(v_ref[at_j, lanes], head), do_ref[at_i, lanes], NT)
            if slot is not None:
                s = s + bias_ref[slot, keys, queries]
            probs = jnp.exp2(s * SCALE2 - lse_ref[stat])
            probs_of[head][keys, queries] = probs.astype(BF)
            grads_of[head][keys, queries] = (probs * (dots - delta_ref[stat])).astype(BF)

    def late(group, head, i, j, corner):
        lanes = slice(2 * HD * (head // 2), 2 * HD * (head // 2) + 2 * HD)
        rows = slice(HD * head, HD * head + HD)
        for keys, queries in pieces(corner, size):
            at_j, at_i = part_at(size, j, keys), part_at(size, i, queries)
            grads = grads_of[head][keys, queries]
            dv_acc[at_j, lanes] += mm(
                probs_of[head][keys, queries], head_half(do_ref[at_i, lanes], head)
            )
            dk_acc[at_j, lanes] += mm(grads, head_half(q_ref[at_i, lanes], head))
            dqt_acc[rows, queries] += mm(kt_ref[rows, at_j], grads)

    def finish(j):
        dk_ref[at(j), :] = (dk_acc[at(j), :] * SCALE).astype(BF)
        dv_ref[at(j), :] = dv_acc[at(j), :].astype(BF)
        store(1, j).start()
        store(2, j).start()

    def step_end(i, j):
        pl.when(i == count - 1)(lambda: finish(j))

    def row_end(i):
        dq_ref[at(i), :] = (dqt_acc[...] * SCALE).T.astype(BF)
        store(0, i).start()
        dqt_acc[...] = jnp.zeros(dqt_acc.shape, F32)

    dqt_acc[...] = jnp.zeros(dqt_acc.shape, F32)
    walk.walk(3, heads, 1, early, late, row_begin, step_end, row_end)
    lowest = jnp.int32(count)
    for slot in range(list_ref.shape[0] - 1):
        lowest = lowest - jnp.where(list_ref[slot] % 256 == count - 1, 1, 0)
    for j in range(count):
        pl.when(j < lowest)(functools.partial(finish, j))
    for j in range(count):
        for n in range(3):
            store(n, j).wait()


def attend_back(first, groups, table, q, k, v, do, start, lse, delta, size):
    length = q.shape[0]
    part = HD * groups
    count = length // size
    far = pl.BlockSpec(memory_space=pl.ANY)
    near = pltpu.VMEM((length, part), BF)
    pairs = count * (count + 1) // 2 * size * size * groups
    return pl.pallas_call(
        functools.partial(backward_kernel, size, groups, first),
        cost_estimate=pl.CostEstimate(
            flops=10 * HD * pairs, bytes_accessed=16 * length * part, transcendentals=pairs
        ),
        grid_spec=pltpu.PrefetchScalarGridSpec(
            num_scalar_prefetch=1,
            grid=(1,),
            in_specs=[far] * 4 + [once(start), once(lse), once(delta)],
            out_specs=[far] * 3,
            scratch_shapes=[near] * 4
            + [pltpu.VMEM((part, length), BF)]
            + [near] * 3
            + [
                pltpu.SemaphoreType.DMA((4, count)),
                pltpu.SemaphoreType.DMA((3, count)),
                pltpu.VMEM((part, size), F32),
                pltpu.VMEM((length, part), F32),
                pltpu.VMEM((length, part), F32),
                pltpu.VMEM((4, size, size), F32),
            ]
            + [pltpu.VMEM((size, size), BF)] * (2 * groups),
        ),
        out_shape=[shape_of((length, part), BF)] * 3,
        compiler_params=params(),
        name="attend_back",
    )(table, q, k, v, do, start, lse, delta)


def feed_kernel(
    chunk, place_ref, att_ref, x_got, x_own, cot_got, cot_own, wo_ref, ob_ref, g2_ref, s2_ref, we_ref,
    eb_ref, wr_ref, hid_ref, exg_ref, keep_ref, send_ref, deb_ref, acc_ref, deb_acc, wet_ref, ebt_ref,
):
    step = pl.program_id(0)
    tile, width = x_got.shape
    total = wr_ref.shape[0]

    @pl.when(step == 0)
    def _():
        for ref in (acc_ref, deb_acc):
            ref[...] = jnp.zeros(ref.shape, F32)
        wet_ref[...] = we_ref[...].T
        ebt_ref[...] = jnp.broadcast_to(eb_ref[...], (128, total)).T

    mixed = mm(att_ref[...].T, wo_ref[...]) + ob_ref[...]
    middle = either(x_got, x_own).astype(F32) + BRANCH * mixed
    unit, _ = norm_parts(middle)
    second = (unit * g2_ref[...] + s2_ref[...]).astype(BF)
    second_t = second.T
    reduced_grad = (BRANCH * either(cot_got, cot_own).astype(F32)).astype(BF)

    def stage_one(c):
        rows = slice(c * chunk, (c + 1) * chunk)
        bias = jnp.concatenate([ebt_ref[rows, :]] * (tile // 128), 1)
        v = mm(wet_ref[rows, :], second, NT) + bias
        v2 = v * v
        t = jnp.tanh(v * (GELU_A + GELU_B * v2))
        h1 = 0.5 * t + 0.5
        gelu = v * h1
        slope = h1 + gelu * (1.0 - h1) * (2.0 * GELU_A + 6.0 * GELU_B * v2)
        hid_ref[rows, :] = gelu.astype(BF)
        grads = (mm(wr_ref[rows, :], reduced_grad, NT) * slope).astype(BF)
        exg_ref[rows, :] = grads
        wide = grads.astype(F32)
        part = wide[:, 0:128]
        for n in range(1, tile // 128):
            part = part + wide[:, n * 128 : (n + 1) * 128]
        deb_acc[rows, :] += part

    stage_one(0)
    for c in range(total // chunk):
        if (c + 1) * chunk < total:
            stage_one(c + 1)
        rows = slice(c * chunk, (c + 1) * chunk)
        acc_ref[rows, :] += mm(hid_ref[rows, :], reduced_grad)
        for n in range(chunk // width):
            cut = slice(c * chunk + n * width, c * chunk + (n + 1) * width)
            there = slice(total + cut.start, total + cut.stop)
            acc_ref[there, :] += mm(second_t, exg_ref[cut, :], NT)

    last = step == pl.num_programs(0) - 1
    halves = slice(0, total), slice(total, 2 * total)
    for core in range(2):

        @pl.when(last & (place_ref[1] == core))
        def _():
            keep_ref[...] = acc_ref[halves[core], :].astype(BF)
            send_ref[...] = acc_ref[halves[1 - core], :].astype(BF)

    @pl.when(last)
    def _():
        flat = jnp.sum(deb_acc[...].T, 0, keepdims=True)
        deb_ref[...] = jnp.zeros(deb_ref.shape, F32)
        for n in range(total // width):
            deb_ref[n : n + 1, :] = flat[:, n * width : (n + 1) * width]


def feed_part(place, att_t, x_got, x_own, cot_got, cot_own, wo, ob, g2, s2, we, eb, wr, tile, chunk):
    width, length = att_t.shape
    total = wr.shape[0]
    tiles = length // tile
    where, _, _ = own_and_got(tiles)
    pair = list(row_specs(tile, width, tiles))
    cols = lambda high: pl.BlockSpec((high, tile), lambda t, h: (0, where(t, h)))
    return pl.pallas_call(
        functools.partial(feed_kernel, chunk),
        grid_spec=pltpu.PrefetchScalarGridSpec(
            num_scalar_prefetch=1,
            grid=(tiles,),
            in_specs=[cols(width)] + pair * 2 + [once(a) for a in (wo, ob, g2, s2, we, eb, wr)],
            out_specs=[cols(total), cols(total), kept((total, width)), kept((total, width)), kept((8, width))],
            scratch_shapes=[
                pltpu.VMEM((2 * total, width), F32),
                pltpu.VMEM((total, 128), F32),
                pltpu.VMEM((total, width), BF),
                pltpu.VMEM((total, 128), F32),
            ],
        ),
        out_shape=[
            shape_of((total, length), BF),
            shape_of((total, length), BF),
            shape_of((total, width), BF),
            shape_of((total, width), BF),
            shape_of((8, width), F32),
        ],
        compiler_params=params(),
        name="feed",
    )(place, att_t, x_got, x_own, cot_got, cot_own, wo, ob, g2, s2, we, eb, wr)


def middle_kernel(
    place_ref, att_ref, x_got, x_own, cot_got, cot_own, hid_ref, exg_ref, wo_ref, ob_ref, g2_ref,
    we_ref, wr_ref, rb_ref, res_own, res_send, grad_ref, ag_ref, delta_ref, dwo_ref, vec_ref, acc_ref,
    wrt_ref,
):
    step = pl.program_id(0)
    tiles = pl.num_programs(0)

    @pl.when(step == 0)
    def _():
        for ref in (acc_ref, vec_ref):
            ref[...] = jnp.zeros(ref.shape, F32)
        wrt_ref[...] = wr_ref[...].T

    att_t = att_ref[...]
    mixed = mm(att_t.T, wo_ref[...]) + ob_ref[...]
    middle = either(x_got, x_own).astype(F32) + BRANCH * mixed
    cot = either(cot_got, cot_own).astype(F32)
    unit, scale = norm_parts(middle)
    norm_grad = mm(we_ref[...], exg_ref[...]).T
    result = (middle + BRANCH * (mm(wrt_ref[...], hid_ref[...]).T + rb_ref[...])).astype(BF)

    @pl.when(step < tiles // 2)
    def _():
        res_send[...] = result

    @pl.when(step >= tiles // 2)
    def _():
        res_own[0] = result

    middle_grad = cot + norm_back(norm_grad, unit, scale, g2_ref[...])
    grad_ref[...] = middle_grad
    mixed_grad = (BRANCH * middle_grad).astype(BF)
    acc_ref[...] += mm(att_t, mixed_grad)
    att_grad = mm(mixed_grad, wo_ref[...], NT).astype(BF)
    ag_ref[...] = att_grad
    dots = att_grad.T.astype(F32) * att_t.astype(F32)
    for head in range(H):
        delta_ref[head] = jnp.sum(dots[HD * head : HD * head + HD, :], 0, keepdims=True)
    reduced_grad = (BRANCH * cot).astype(BF)
    sums = (norm_grad * unit, norm_grad, mixed_grad.astype(F32), reduced_grad.astype(F32))
    for n, value in enumerate(sums):
        vec_ref[n : n + 1, :] += jnp.sum(value, 0, keepdims=True)

    @pl.when(step == tiles - 1)
    def _():
        dwo_ref[...] = acc_ref[...].astype(BF)


def middle_part(place, att_t, x_got, x_own, cot_got, cot_own, hid, exg, wo, ob, g2, we, wr, rb, tile):
    width, length = att_t.shape
    total = wr.shape[0]
    tiles = length // tile
    where, got, own = own_and_got(tiles)
    pair = list(row_specs(tile, width, tiles))
    rows = pl.BlockSpec((tile, width), lambda t, h: (where(t, h), 0))
    cols = lambda high: pl.BlockSpec((high, tile), lambda t, h: (0, where(t, h)))
    return pl.pallas_call(
        middle_kernel,
        cost_estimate=pl.CostEstimate(
            flops=2 * length * width * (2 * total + 3 * width),
            bytes_accessed=8 * length * total,
            transcendentals=0,
        ),
        grid_spec=pltpu.PrefetchScalarGridSpec(
            num_scalar_prefetch=1,
            grid=(tiles,),
            in_specs=[cols(width)]
            + pair * 2
            + [cols(total), cols(total)]
            + [once(a) for a in (wo, ob, g2, we, wr, rb)],
            out_specs=[
                pair[1],
                pair[0],
                rows,
                rows,
                pl.BlockSpec((H, 1, tile), lambda t, h: (0, 0, where(t, h))),
                kept((width, width)),
                kept((8, width)),
            ],
            scratch_shapes=[pltpu.VMEM((width, width), F32), pltpu.VMEM((width, total), BF)],
        ),
        out_shape=[
            shape_of((2, length // 2, width), BF),
            shape_of((length // 2, width), BF),
            shape_of((length, width), F32),
            shape_of((length, width), BF),
            shape_of((H, 1, length), F32),
            shape_of((width, width), BF),
            shape_of((8, width), F32),
        ],
        compiler_params=params(),
        name="middle",
    )(place, att_t, x_got, x_own, cot_got, cot_own, hid, exg, wo, ob, g2, we, wr, rb)


def weight_kernel(parts, place_ref, *refs):
    ins = refs[: 3 * parts]
    x_got, x_own, gain_ref, shift_ref, extra_ref, keep_ref, send_ref, acc_ref = refs[3 * parts :]
    step = pl.program_id(0)

    @pl.when(step == 0)
    def _():
        acc_ref[...] = jnp.zeros(acc_ref.shape, F32)

    width = x_got.shape[1]
    unit, _ = norm_parts(either(x_got, x_own).astype(F32))
    normed_t = (unit * gain_ref[...] + shift_ref[...]).astype(BF).T
    for n in range(3):
        grad = jnp.concatenate([ref[...] for ref in ins[n * parts : (n + 1) * parts]], 1)
        acc_ref[n * width : (n + 1) * width, :] += mm(normed_t, grad)

    last = step == pl.num_programs(0) - 1
    for core in range(2):

        @pl.when(last & (place_ref[1] == core))
        def _():
            lower, upper = (keep_ref, send_ref) if core == 0 else (send_ref, keep_ref)
            lower[...] = acc_ref[: 2 * width, :].astype(BF)
            upper[:width, :] = acc_ref[2 * width :, :].astype(BF)
            upper[width:, :] = extra_ref[...]


def weight_part(place, grads, x_got, x_own, gain, shift, extra, tile):
    span, width = x_got.shape
    tiles = 2 * span // tile
    where, _, _ = own_and_got(tiles)
    flat = [part for group in grads for part in group]
    out = shape_of((2 * width, width), BF)
    return pl.pallas_call(
        functools.partial(weight_kernel, len(grads[0])),
        cost_estimate=pl.CostEstimate(
            flops=6 * width * width * width * tiles, bytes_accessed=20 * width * width * tiles, transcendentals=0
        ),
        grid_spec=pltpu.PrefetchScalarGridSpec(
            num_scalar_prefetch=1,
            grid=(tiles,),
            in_specs=[
                pl.BlockSpec((tile, a.shape[1]), lambda t, h: (where(t, h), 0)) for a in flat
            ]
            + list(row_specs(tile, width, tiles))
            + [once(a) for a in (gain, shift, extra)],
            out_specs=[kept(out.shape)] * 2,
            scratch_shapes=[pltpu.VMEM((3 * width, width), F32)],
        ),
        out_shape=[out, out],
        compiler_params=params(),
        name="weight",
    )(place, *flat, x_got, x_own, gain, shift, extra)


def last_kernel(parts, place_ref, *refs):
    ins, rest = refs[: 3 * parts], refs[3 * parts :]
    x_got, x_own, mid_ref, gain_ref, weight_ref, own_ref, send_ref, vec_ref = rest
    step = pl.program_id(0)
    tiles = pl.num_programs(0)

    @pl.when(step == 0)
    def _():
        vec_ref[...] = jnp.zeros(vec_ref.shape, F32)

    width = x_got.shape[1]
    unit, scale = norm_parts(either(x_got, x_own).astype(F32))
    back = None
    grads = []
    for n in range(3):
        grad = jnp.concatenate([ref[...] for ref in ins[n * parts : (n + 1) * parts]], 1)
        one = mm(grad, weight_ref[:, n * width : (n + 1) * width], NT)
        back = one if back is None else back + one
        grads.append(grad)
    total = mid_ref[...] + norm_back(back, unit, scale, gain_ref[...])

    @pl.when(step < tiles // 2)
    def _():
        send_ref[...] = total.astype(BF)

    @pl.when(step >= tiles // 2)
    def _():
        own_ref[0] = total

    sums = (back * unit, back, grads[0].astype(F32), grads[2].astype(F32))
    for n, value in enumerate(sums):
        vec_ref[n : n + 1, :] += jnp.sum(value, 0, keepdims=True)


def last_part(place, grads, x_got, x_own, mid, gain, weight, tile):
    length, width = mid.shape
    tiles = length // tile
    where, _, _ = own_and_got(tiles)
    rows = pl.BlockSpec((tile, width), lambda t, h: (where(t, h), 0))
    flat = [part for group in grads for part in group]
    pair = list(row_specs(tile, width, tiles))
    return pl.pallas_call(
        functools.partial(last_kernel, len(grads[0])),
        cost_estimate=pl.CostEstimate(
            flops=6 * width * width * width * tiles, bytes_accessed=20 * width * width * tiles, transcendentals=0
        ),
        grid_spec=pltpu.PrefetchScalarGridSpec(
            num_scalar_prefetch=1,
            grid=(tiles,),
            in_specs=[
                pl.BlockSpec((tile, a.shape[1]), lambda t, h: (where(t, h), 0)) for a in flat
            ]
            + pair
            + [rows, once(gain), once(weight)],
            out_specs=[pair[1], pair[0], kept((8, width))],
        ),
        out_shape=[
            shape_of((2, length // 2, width), F32),
            shape_of((length // 2, width), BF),
            shape_of((8, width), F32),
        ],
        compiler_params=params(),
        name="last",
    )(place, *flat, x_got, x_own, mid, gain, weight)


def swapped(value):
    return lax.ppermute(value, "seq", [(0, 1), (1, 0)])


def side(hop):
    axis, bit = hop
    return (lax.axis_index(axis) // bit) % 2


def place_of(hops):
    place = 0
    for hop in hops:
        place = 2 * place + side(hop)
    return place


def exchanged(value, hops):
    axes = tuple(dict.fromkeys(axis for axis, _ in hops))
    flips = [sum(bit for axis, bit in hops if axis == name) for name in axes]
    sizes = [lax.axis_size(name) for name in axes]
    if len(axes) == 1:
        return lax.ppermute(value, axes[0], [(i, i ^ flips[0]) for i in range(sizes[0])])
    pairs = [
        (i * sizes[1] + j, (i ^ flips[0]) * sizes[1] + (j ^ flips[1]))
        for i in range(sizes[0])
        for j in range(sizes[1])
    ]
    return lax.ppermute(value, axes, pairs)


def partners(hops):
    count = len(hops)
    return [
        ([hop for n, hop in enumerate(hops) if (flip >> (count - 1 - n)) & 1], flip)
        for flip in range(1, 1 << count)
    ]


def added(*values):
    total = values[0].astype(F32)
    for value in values[1:]:
        total = total + value.astype(F32)
    return total.astype(BF)


def scatter(part, hops):
    rows = part.shape[1] >> len(hops)
    mine = place_of(hops)
    piece = lambda place: lax.dynamic_slice_in_dim(part, place * rows, rows, 1)
    got = [exchanged(piece(mine ^ flip), chosen) for chosen, flip in partners(hops)]
    return added(piece(mine), *got)


def gather(part, hops, whole=None):
    mine = place_of(hops)
    blocks, rows, width = part.shape
    got, others = [(part, mine)], []
    for chosen, flip in partners(hops):
        if whole is None:
            got.append((exchanged(part, chosen), mine ^ flip))
            continue
        both = exchanged(jnp.concatenate([part.reshape(-1, width), whole], 0), chosen)
        got.append((both[: blocks * rows].reshape(part.shape), mine ^ flip))
        others.append(both[blocks * rows :])
    if len(hops) == 1:
        one, two = got[0][0], got[1][0]
        out = jnp.where(mine == 0, jnp.concatenate([one, two], 1), jnp.concatenate([two, one], 1))
    else:
        out = jnp.zeros((blocks, rows << len(hops), width), part.dtype)
        for piece, place in got:
            out = lax.dynamic_update_slice_in_dim(out, piece, place * rows, 1)
    return out if whole is None else (out, added(whole, *others))


def hops():
    found = []
    for axis in ("dp", "seq"):
        size = lax.axis_size(axis)
        found.append([(axis, 1 << n) for n in range(size.bit_length() - 1)])
    core, one, two, far = found[0]
    return [core], [one, two], [far], found[1]


class AllSum:
    def __init__(self, keep, send, core):
        self.core, self.whole = core, None
        self.state = (keep[None], send[None])

    def split(self):
        keep, send = self.state
        self.state = added(keep, exchanged(send, self.core))

    def cross(self, one, two):
        if not isinstance(self.state, tuple):
            mid = self.state.shape[1] // 2
            self.state = (self.state[:, :mid], self.state[:, mid:])
        self.state = tuple(scatter(part, hops) for part, hops in zip(self.state, (one, two)))

    def uncross(self, one, two):
        if not isinstance(self.state, tuple):
            self.state = (self.state[:1], self.state[1:])
        self.state = tuple(gather(part, hops) for part, hops in zip(self.state, (one, two)))

    def join(self):
        self.state = gather(jnp.concatenate(self.state, 1), self.core)

    def ride(self, whole, hops):
        self.whole = added(whole, exchanged(whole, hops))

    def narrow(self, hops):
        if isinstance(self.state, tuple):
            self.state = jnp.concatenate(self.state, 0)
        self.state = scatter(self.state, hops)

    def meet(self, hops):
        self.state = added(self.state, exchanged(self.state, hops))

    def widen(self, hops):
        if self.whole is None:
            self.state = gather(self.state, hops)
        else:
            self.state, self.whole = gather(self.state, hops, self.whole)

    def beside(self, call, argument, step, *hops):
        argument = after(argument, self.state)
        step(*hops)
        out = call(argument)
        self.state = after(self.state, out)
        return out


def after(value, earlier):
    return lax.optimization_barrier((value, earlier))[0]


def passed_along(block, axis, distance):
    devices = range(lax.axis_size(axis))
    route = [(i - distance, i) for i in devices if i - distance in devices]
    return lax.ppermute(block, axis, route)


def from_behind(value, axis, steps):
    count = lax.axis_size(axis)
    pairs = [(source, (source + steps) % count) for source in range(count)]
    return lax.ppermute(value, axis, pairs)


def layer_norm(values, gain_vec, shift_vec):
    center = jnp.mean(values, -1, keepdims=True)
    centered = values - center
    variance = jnp.mean(centered * centered, -1, keepdims=True)
    return centered * lax.rsqrt(variance + EPSILON) * gain_vec + shift_vec


def gelu_tanh(values):
    return jax.nn.gelu(values, approximate=True)


def plain_dot(left, right):
    return jnp.dot(left, right, preferred_element_type=jnp.float32)


def left_dot(left, right):
    return lax.dot_general(
        left, right, (((0,), (0,)), ((), ())), preferred_element_type=jnp.float32
    )


def right_dot(left, right):
    return lax.dot_general(
        left, right, (((1,), (1,)), ((), ())), preferred_element_type=jnp.float32
    )


def block_scores(queries, keys_block, query_seg, key_seg, query_places, key_start):
    row_count, key_len, width = keys_block.shape
    keys_heads = keys_block.reshape(row_count, key_len, H, HD)
    scores = jnp.einsum(
        "rqhd,rkhd->rhqk", queries, keys_heads, preferred_element_type=jnp.float32
    ) * HD ** (-0.5)
    key_places = key_start + jnp.arange(key_len, dtype=jnp.int32)
    allowed = (query_seg[:, None, :, None] == key_seg[:, None, None, :]) & (
        key_places[None, None, None, :] <= query_places[None, None, :, None]
    )
    return (scores, allowed)


def attend_block(state, queries, block, query_seg, query_places, key_start):
    run_max, run_sum, running = state
    keys_block, values_block, key_seg = block
    row_count, key_len, width = values_block.shape
    query_len = queries.shape[1]
    scores, allowed = block_scores(queries, keys_block, query_seg, key_seg, query_places, key_start)
    block_max = jnp.max(jnp.where(allowed, scores, NEGATIVE), -1)
    new_max = jnp.maximum(run_max, block_max)
    exponent = jnp.where(allowed, jnp.exp(scores - new_max[..., None]), 0.0)
    factor = jnp.exp(run_max - new_max)
    new_sum = run_sum * factor + jnp.sum(exponent, -1)
    values_heads = values_block.reshape(row_count, key_len, H, HD)
    addition = jnp.einsum(
        "rhqk,rkhd->rqhd",
        exponent.astype(jnp.bfloat16),
        values_heads,
        preferred_element_type=jnp.float32,
    )
    scaled = (
        running.reshape(row_count, query_len, H, HD) * jnp.transpose(factor, (0, 2, 1))[..., None]
    )
    return (new_max, new_sum, (scaled + addition).reshape(row_count, query_len, width))


def grad_block(queries, out_grad, log_sum, delta, block, query_seg, query_places, key_start):
    keys_block, values_block, key_seg = block
    row_count, key_len, width = keys_block.shape
    scores, allowed = block_scores(queries, keys_block, query_seg, key_seg, query_places, key_start)
    weights_block = jnp.where(allowed, jnp.exp(scores - log_sum[..., None]), 0.0)
    keys_heads = keys_block.reshape(row_count, key_len, H, HD)
    values_heads = values_block.reshape(row_count, key_len, H, HD)
    value_dots = jnp.einsum(
        "rqhd,rkhd->rhqk", out_grad, values_heads, preferred_element_type=jnp.float32
    )
    score_grad = (weights_block * (value_dots - delta[..., None]) * HD ** (-0.5)).astype(
        jnp.bfloat16
    )
    query_part = jnp.einsum(
        "rhqk,rkhd->rqhd", score_grad, keys_heads, preferred_element_type=jnp.float32
    ).reshape(row_count, -1, width)
    key_part = jnp.einsum(
        "rhqk,rqhd->rkhd", score_grad, queries, preferred_element_type=jnp.float32
    ).reshape(row_count, key_len, width)
    value_part = jnp.einsum(
        "rhqk,rqhd->rkhd",
        weights_block.astype(jnp.bfloat16),
        out_grad,
        preferred_element_type=jnp.float32,
    ).reshape(row_count, key_len, width)
    return (query_part, key_part, value_part)


def local(
    activations,
    segments,
    first_gain,
    first_shift,
    input_weight,
    query_bias,
    value_bias,
    output_weight,
    output_bias,
    second_gain,
    second_shift,
    expand_weight,
    expand_bias,
    reduce_weight,
    reduce_bias,
    cotangent,
):
    row_total, span_len, width = activations.shape
    cycle_size = lax.axis_size("seq")
    position = lax.axis_index("seq")
    micro_rows = row_total // MICRO
    branch = DEPTH ** (-0.5)
    bias_all = jnp.concatenate([query_bias, jnp.zeros_like(query_bias), value_bias])
    query_places = position * span_len + jnp.arange(span_len, dtype=jnp.int32)
    totals = [
        jnp.zeros(argument.shape, jnp.float32)
        for argument in (
            first_gain,
            first_shift,
            input_weight,
            query_bias,
            value_bias,
            output_weight,
            output_bias,
            second_gain,
            second_shift,
            expand_weight,
            expand_bias,
            reduce_weight,
            reduce_bias,
        )
    ]
    outputs_list = []
    grads_list = []
    for micro in range(MICRO):
        lower = micro * micro_rows
        values_in = activations[lower : lower + micro_rows].astype(jnp.float32)
        query_seg = segments[lower : lower + micro_rows]
        out_cot = cotangent[lower : lower + micro_rows].astype(jnp.float32)
        normed, first_pull = jax.vjp(layer_norm, values_in, first_gain, first_shift)
        normed_low = normed.astype(jnp.bfloat16).reshape(-1, width)
        projected = (plain_dot(normed_low, input_weight) + bias_all).astype(jnp.bfloat16)
        queries = projected[:, :width].reshape(micro_rows, span_len, H, HD)
        keys_own = projected[:, width : 2 * width].reshape(micro_rows, span_len, width)
        values_own = projected[:, 2 * width :].reshape(micro_rows, span_len, width)
        own_block = (keys_own, values_own, query_seg)
        start_state = (
            jnp.full((micro_rows, H, span_len), NEGATIVE, jnp.float32),
            jnp.zeros((micro_rows, H, span_len), jnp.float32),
            jnp.zeros((micro_rows, span_len, width), jnp.float32),
        )
        state = attend_block(
            start_state, queries, own_block, query_seg, query_places, position * span_len
        )

        def cycle_forward(step_index, carry):
            block, inner_state = carry
            block = passed_along((block[0], block[1], block[2]), "seq", 1)
            source = (position - step_index) % cycle_size
            inner_state = lax.cond(
                source < position,
                lambda current: attend_block(
                    current, queries, block, query_seg, query_places, source * span_len
                ),
                lambda current: current,
                inner_state,
            )
            return (block, inner_state)

        unused_block, state = lax.fori_loop(1, cycle_size, cycle_forward, (own_block, state))
        run_max, run_sum, running = state
        attended = (
            running.reshape(micro_rows, span_len, H, HD)
            / jnp.transpose(run_sum, (0, 2, 1))[..., None]
        ).reshape(micro_rows, span_len, width)
        log_sum = run_max + jnp.log(run_sum)
        attended_low = attended.astype(jnp.bfloat16).reshape(-1, width)
        mixed_out = plain_dot(attended_low, output_weight) + output_bias
        middle = values_in + branch * mixed_out.reshape(values_in.shape)
        second_norm, second_pull = jax.vjp(layer_norm, middle, second_gain, second_shift)
        second_low = second_norm.astype(jnp.bfloat16).reshape(-1, width)
        expanded = plain_dot(second_low, expand_weight) + expand_bias
        hidden, gelu_pull = jax.vjp(gelu_tanh, expanded)
        hidden_low = hidden.astype(jnp.bfloat16)
        reduced = plain_dot(hidden_low, reduce_weight) + reduce_bias
        outputs_list.append(
            (middle + branch * reduced.reshape(values_in.shape)).astype(jnp.bfloat16)
        )
        reduced_grad = (branch * out_cot).reshape(-1, width).astype(jnp.bfloat16)
        totals[12] = totals[12] + jnp.sum(reduced_grad.astype(jnp.float32), 0)
        totals[11] = totals[11] + left_dot(hidden_low, reduced_grad)
        (expanded_grad,) = gelu_pull(right_dot(reduced_grad, reduce_weight))
        expanded_low = expanded_grad.astype(jnp.bfloat16)
        totals[10] = totals[10] + jnp.sum(expanded_low.astype(jnp.float32), 0)
        totals[9] = totals[9] + left_dot(second_low, expanded_low)
        norm_in_grad = right_dot(expanded_low, expand_weight).reshape(values_in.shape)
        middle_part, gain_part, shift_part = second_pull(norm_in_grad)
        totals[7] = totals[7] + gain_part
        totals[8] = totals[8] + shift_part
        middle_grad = out_cot + middle_part
        mixed_grad = (branch * middle_grad).reshape(-1, width).astype(jnp.bfloat16)
        totals[6] = totals[6] + jnp.sum(mixed_grad.astype(jnp.float32), 0)
        totals[5] = totals[5] + left_dot(attended_low, mixed_grad)
        attended_grad = (
            right_dot(mixed_grad, output_weight)
            .astype(jnp.bfloat16)
            .reshape(micro_rows, span_len, H, HD)
        )
        delta = jnp.transpose(
            jnp.sum(
                attended_grad.astype(jnp.float32) * attended.reshape(micro_rows, span_len, H, HD),
                -1,
            ),
            (0, 2, 1),
        )
        query_grad, key_grad, value_grad = grad_block(
            queries,
            attended_grad,
            log_sum,
            delta,
            own_block,
            query_seg,
            query_places,
            position * span_len,
        )

        def cycle_backward(step_index, carry):
            block, partial_value, query_acc = carry
            block = passed_along((block[0], block[1], block[2]), "seq", 1)
            partial_value = (
                from_behind(partial_value[0].astype(jnp.bfloat16), "seq", 1).astype(jnp.float32),
                from_behind(partial_value[1].astype(jnp.bfloat16), "seq", 1).astype(jnp.float32),
            )
            source = (position - step_index) % cycle_size

            def work(current):
                partial_in, query_in = current
                query_part, key_part, value_part = grad_block(
                    queries,
                    attended_grad,
                    log_sum,
                    delta,
                    block,
                    query_seg,
                    query_places,
                    source * span_len,
                )
                return (
                    (partial_in[0] + key_part, partial_in[1] + value_part),
                    query_in + query_part,
                )

            partial_value, query_acc = lax.cond(
                source < position, work, lambda current: current, (partial_value, query_acc)
            )
            return (block, partial_value, query_acc)

        unused_block, partial_value, query_grad = lax.fori_loop(
            1, cycle_size, cycle_backward, (own_block, (key_grad, value_grad), query_grad)
        )
        key_grad, value_grad = (
            from_behind(partial_value[0].astype(jnp.bfloat16), "seq", 1).astype(jnp.float32),
            from_behind(partial_value[1].astype(jnp.bfloat16), "seq", 1).astype(jnp.float32),
        )
        qkv_grad = (
            jnp.concatenate([query_grad, key_grad, value_grad], -1)
            .reshape(-1, 3 * width)
            .astype(jnp.bfloat16)
        )
        totals[3] = totals[3] + jnp.sum(qkv_grad[:, :width].astype(jnp.float32), 0)
        totals[4] = totals[4] + jnp.sum(qkv_grad[:, 2 * width :].astype(jnp.float32), 0)
        totals[2] = totals[2] + left_dot(normed_low, qkv_grad)
        norm_grad = right_dot(qkv_grad, input_weight).reshape(values_in.shape)
        input_part, gain_one, shift_one = first_pull(norm_grad)
        totals[0] = totals[0] + gain_one
        totals[1] = totals[1] + shift_one
        grads_list.append(middle_grad + input_part)
    summed = lax.psum(
        (
            totals[0],
            totals[1],
            totals[2],
            totals[3],
            totals[4],
            totals[5],
            totals[6],
            totals[7],
            totals[8],
            totals[9],
            totals[10],
            totals[11],
            totals[12],
        ),
        ("dp", "seq"),
    )
    return (
        jnp.concatenate(outputs_list, 0),
        jnp.concatenate(grads_list, 0),
        summed[0],
        summed[1],
        summed[2],
        summed[3],
        summed[4],
        summed[5],
        summed[6],
        summed[7],
        summed[8],
        summed[9],
        summed[10],
        summed[11],
        summed[12],
    )


def local_rows(
    activations,
    segments,
    first_gain,
    first_shift,
    input_weight,
    query_bias,
    value_bias,
    output_weight,
    output_bias,
    second_gain,
    second_shift,
    expand_weight,
    expand_bias,
    reduce_weight,
    reduce_bias,
    cotangent,
):
    rows, span, width = activations.shape
    mine = lax.axis_index("seq")
    half = mine.astype(jnp.int32)[None]
    core = lax.axis_index("dp").astype(jnp.int32)[None] % 2
    place = jnp.concatenate([half, core])
    take = lambda array, index: lax.dynamic_index_in_dim(array, index, 0, keepdims=False)
    row = lambda vector: vector.reshape(1, -1)
    seg_got = swapped(take(segments, 1 - mine))
    x_got = swapped(after(take(activations, 1 - mine), seg_got))
    bias = jnp.concatenate([query_bias, jnp.zeros_like(query_bias), value_bias])
    gain, shift = row(first_gain), row(first_shift)
    weights = (gain, shift, input_weight, row(bias))
    start, table = documents(half, row(take(segments, mine)), row(seg_got), BLOCK)
    *before, norms = project(True, half, activations, *weights, (), TILE)
    cot_got = swapped(after(take(cotangent, 1 - mine), (x_got, norms)))
    q, k, v, more = project(False, half, x_got, *weights, before, TILE)
    norms = jnp.maximum(norms, more)
    limit = jnp.max(norms[0] * norms[1]) * (SCALE2 * SCALE2)
    small = (limit < SMALL * SMALL).astype(jnp.int32)[None]
    att_t, lse = attend(table, small, q, k, v, start, BLOCK)
    tokens = (x_got, activations, cot_got, cotangent)
    out_bias, gain_two = row(output_bias), row(second_gain)
    hid, exg, keep, send, vec_expand = feed_part(
        place, att_t, *tokens, output_weight, out_bias, gain_two, row(second_shift), expand_weight,
        row(expand_bias), reduce_weight, TILE, CHUNK,
    )

    core_hop, plane, line, pair = hops()
    one, two = ([hop] for hop in plane)
    sums = AllSum(keep, send, core_hop)
    result, result_send, mid_grad, att_grad, delta, d_output, vec = sums.beside(
        lambda place: middle_part(
            place, att_t, *tokens, hid, exg, output_weight, out_bias, gain_two, expand_weight,
            reduce_weight, row(reduce_bias), TILE,
        ),
        place, sums.split,
    )
    result_got = swapped(result_send)
    moves = [
        (sums.cross, one, two),
        (sums.cross, two, one),
        (sums.narrow, line + pair),
        (sums.widen, line + pair),
    ]
    grads = []
    for n, move in enumerate(moves):
        call = lambda table: attend_back(
            n * BACKWARD_HEADS, BACKWARD_HEADS, table, q, k, v, att_grad, start, lse, delta, BLOCK
        )
        grads.append(sums.beside(call, table, *move))
    grads = [[g[n] for g in grads] for n in range(3)]
    keep, send = sums.beside(
        lambda place: weight_part(place, grads, x_got, activations, gain, shift, d_output, TILE),
        place, sums.uncross, two, one,
    )
    tail = AllSum(keep, send, core_hop)
    tail.split()
    sums.state = after(sums.state, tail.state)
    grad, grad_send, vec_last = tail.beside(
        lambda place: last_part(
            place, grads, x_got, activations, mid_grad, gain, input_weight, TILE
        ),
        place, tail.narrow, plane,
    )
    vectors = jnp.concatenate([vec[:4], vec_expand[:4], vec_last], 0).astype(BF)
    tail.narrow(line)
    tail.meet(pair)
    tail.ride(vectors, pair)
    grad_got = swapped(after(grad_send, (tail.state, tail.whole)))
    tail.widen(line)
    sums.state = after(sums.state, tail.state)
    sums.uncross(one, two)
    sums.join()
    tail.widen(plane)
    tail.widen(core_hop)
    part, dw = sums.state[0], tail.state[0]
    put = lambda whole, got: lax.dynamic_update_index_in_dim(
        whole, got.astype(whole.dtype), 1 - mine, 0
    )
    total = expand_weight.shape[1]

    def beside(stack):
        blocks = stack.shape[0] // width
        return jnp.concatenate([stack[n * width : (n + 1) * width] for n in range(blocks)], 1).astype(F32)

    vectors = tail.whole.astype(F32)
    return (
        put(result, result_got),
        put(grad, grad_got),
        vectors[8],
        vectors[9],
        beside(dw[: 3 * width]),
        vectors[10],
        vectors[11],
        dw[3 * width :].astype(F32),
        vectors[2],
        vectors[0],
        vectors[1],
        beside(part[total:]),
        vectors[4:8].reshape(-1),
        part[:total].astype(F32),
        vectors[3],
    )


TILE = 512
CHUNK = 512
BLOCK = 512
SMALL = 60.0
FORWARD_HEADS = 4
BACKWARD_HEADS = 2


def solution(mesh):
    sizes = dict(zip(mesh.axis_names, mesh.devices.shape))
    tokens, places, whole = P("dp", "seq", None), P("dp", "seq"), P()
    in_specs = (tokens, places) + (whole,) * 13 + (tokens,)
    out_specs = (tokens, tokens) + (whole,) * 13

    def program(activations, *rest):
        rows = activations.shape[0] // sizes["dp"]
        span = activations.shape[1] // sizes["seq"]
        by_rows = sizes["seq"] == 2 and rows == 2 and span % BLOCK == 0 and sizes["dp"] == 16
        return jax.shard_map(
            local_rows if by_rows else local,
            mesh=mesh,
            in_specs=in_specs,
            out_specs=out_specs,
            check_vma=False,
        )(activations, *rest)

    return program
```

```python
import functools

import jax
import jax.numpy as jnp
from jax import lax
from jax.experimental import pallas as pl
from jax.experimental.pallas import tpu as pltpu
from jax.sharding import PartitionSpec as P

H = 8
HD = 64
DEPTH = 48
MICRO = 2
EPSILON = 1e-05
NEGATIVE = -1e30
BRANCH = DEPTH ** (-0.5)
SCALE = HD ** (-0.5)
SCALE2 = SCALE * 1.4426950408889634
GELU_A = 0.7978845608028654
GELU_B = GELU_A * 0.044715

BF = jnp.bfloat16
F32 = jnp.float32
NN = (((1,), (0,)), ((), ()))
NT = (((1,), (1,)), ((), ()))
VMEM_LIMIT = 58 << 20
SHORT = pl.CostEstimate(flops=1000, bytes_accessed=1000, transcendentals=0)


def mm(left, right, dims=NN):
    return lax.dot_general(left, right, dims, preferred_element_type=F32)


def shape_of(dims, dtype):
    return jax.ShapeDtypeStruct(dims, dtype)


def params(limit=VMEM_LIMIT):
    return pltpu.CompilerParams(vmem_limit_bytes=limit)


def norm_parts(values):
    center = jnp.mean(values, -1, keepdims=True)
    centered = values - center
    variance = jnp.mean(centered * centered, -1, keepdims=True)
    scale = lax.rsqrt(variance + EPSILON)
    return centered * scale, scale


def norm_back(grad, unit, scale, gain):
    inner = grad * gain
    first = jnp.mean(inner, -1, keepdims=True)
    second = jnp.mean(inner * unit, -1, keepdims=True)
    return scale * (inner - first - unit * second)


def own_and_got(tiles):
    part = tiles // 2
    return (
        lambda t, h: (t + (1 - h[0]) * part) % tiles,
        lambda t, h: jnp.minimum(t, part - 1),
        lambda t, h: jnp.maximum(t - part, 0),
    )


def row_specs(tile, width, tiles):
    where, got, own = own_and_got(tiles)
    return (
        pl.BlockSpec((tile, width), lambda t, h: (got(t, h), 0)),
        pl.BlockSpec((1, tile, width), lambda t, h: (h[0], own(t, h), 0)),
    )


def either(got_ref, own_ref):
    early = pl.program_id(0) < pl.num_programs(0) // 2
    return jnp.where(early, got_ref[...], own_ref[0])


def once(array):
    return pl.BlockSpec(array.shape, lambda t, *_: (0,) * array.ndim, pipeline_mode=pl.Buffered(1))


def kept(dims):
    return pl.BlockSpec(dims, lambda t, *_: (0,) * len(dims))


def largest_norms(block):
    lane = lax.broadcasted_iota(jnp.int32, (block.shape[1], 128), 1)
    column = lax.broadcasted_iota(jnp.int32, (block.shape[1], 128), 0)
    member = jnp.where(column // HD == lane, 1.0, 0.0).astype(BF)
    wide = block.astype(F32)
    return jnp.max(mm((wide * wide).astype(BF), member), 0, keepdims=True)


def project_kernel(place, x_ref, gain_ref, shift_ref, weight_ref, bias_ref, *refs):
    q_ref, k_ref, v_ref, norm_ref = refs[-4:]
    width = weight_ref.shape[0]
    unit, _ = norm_parts(x_ref[...].reshape(-1, width).astype(F32))
    normed = (unit * gain_ref[...] + shift_ref[...]).astype(BF)

    @pl.when(pl.program_id(0) == 0)
    def _():
        norm_ref[...] = jnp.zeros(norm_ref.shape, F32)

    for n, ref in enumerate((q_ref, k_ref, v_ref)):
        cols = slice(n * width, (n + 1) * width)
        out = (mm(normed, weight_ref[:, cols]) + bias_ref[:, cols]).astype(BF)
        ref[...] = out
        if n < 2:
            norm_ref[n : n + 1, :] = jnp.maximum(norm_ref[n : n + 1, :], largest_norms(out))


def project(own, half, x, gain, shift, weight, bias, before, tile):
    span, width = x.shape[-2:]
    count = span // tile
    length = 2 * span
    if own:
        x_spec = pl.BlockSpec((1, tile, width), lambda t, h: (h[0], t, 0))
        here = lambda h: h[0]
    else:
        x_spec = pl.BlockSpec((tile, width), lambda t, h: (t, 0))
        here = lambda h: 1 - h[0]
    rows = pl.BlockSpec((tile, width), lambda t, h: (here(h) * count + t, 0))
    nat = shape_of((length, width), BF)
    return pl.pallas_call(
        project_kernel,
        grid_spec=pltpu.PrefetchScalarGridSpec(
            num_scalar_prefetch=1,
            grid=(count,),
            in_specs=[x_spec, once(gain), once(shift), once(weight), once(bias)]
            + [pl.BlockSpec(memory_space=pl.ANY)] * len(before),
            out_specs=[rows, rows, rows, kept((8, 128))],
        ),
        out_shape=[nat, nat, nat, shape_of((8, 128), F32)],
        input_output_aliases={6 + i: i for i in range(len(before))},
        compiler_params=params(),
        name="project",
    )(half, x, gain, shift, weight, bias, *before)


def document_kernel(size, half_ref, own_ref, got_ref, start_ref, table_ref):
    span = own_ref.shape[1]
    place = lambda half: pl.ds(pl.multiple_of(half * span, span), span)
    start_ref[0:1, place(half_ref[0])] = own_ref[...]
    start_ref[0:1, place(1 - half_ref[0])] = got_ref[...]
    numbers = start_ref[...]
    start = jnp.zeros_like(numbers)
    for number in range(1, 8):
        before = jnp.sum((numbers < number).astype(jnp.int32), 1, keepdims=True)
        start = jnp.where(numbers == number, before, start)
    start_ref[...] = start
    count = start.shape[1] // size
    slots = table_ref.shape[0] - 1
    for slot in range(slots):
        table_ref[slot] = 0
    filled = jnp.int32(0)
    for i in range(count):
        block = start[:, i * size : (i + 1) * size]
        low, high = jnp.min(block), jnp.max(block)
        for j in range(i + 1):
            kind = jnp.where(high > j * size, 2, 1 if i == j else 0)
            active = low < (j + 1) * size

            table_ref[filled] = jnp.where(active, i + 256 * j + 65536 * kind, 0)
            filled = filled + active.astype(jnp.int32)
    table_ref[slots] = filled


def documents(half, own, got, size):
    length = 2 * own.shape[1]
    count = length // size
    row = lambda wide: pl.BlockSpec((1, wide), lambda t, h: (0, 0))
    return pl.pallas_call(
        functools.partial(document_kernel, size),
        grid_spec=pltpu.PrefetchScalarGridSpec(
            num_scalar_prefetch=1,
            grid=(1,),
            in_specs=[row(length // 2), row(length // 2)],
            out_specs=[row(length), pl.BlockSpec(memory_space=pltpu.SMEM)],
        ),
        out_shape=[
            shape_of((1, length), jnp.int32),
            shape_of((count * (count + 1) // 2 + 2,), jnp.int32),
        ],
        compiler_params=params(),
        name="documents",
    )(half, own, got)


def head_half(block, head):
    lane = lax.broadcasted_iota(jnp.int32, block.shape, 1)
    keep = (lane < HD) if head % 2 == 0 else (lane >= HD)
    return jnp.where(keep, block, jnp.zeros_like(block))


def lanes_of(heads, group, head):
    low = HD * heads * group + 2 * HD * (head // 2)
    return pl.ds(pl.multiple_of(low, 2 * HD), 2 * HD)


def rows_of(heads, group, head):
    return pl.ds(pl.multiple_of(HD * heads * group + HD * head, HD), HD)


class Blocks:
    def __init__(self, size, list_ref, start_ref, mask_ref, values):
        self.size, self.list = size, list_ref
        self.start, self.mask, self.values = start_ref, mask_ref, values

    def at(self, index):
        return pl.ds(pl.multiple_of(index * self.size, self.size), self.size)

    def places(self):
        dims = (self.size, self.size)
        return lax.broadcasted_iota(jnp.int32, dims, 0), lax.broadcasted_iota(jnp.int32, dims, 1)

    def fill(self, slot, i, j):
        key, query = self.places()
        key, query = key + j * self.size, query + i * self.size
        allowed = (key >= self.start[0:1, self.at(i)]) & (key <= query)
        self.mask[slot] = jnp.where(allowed, *self.values).astype(self.mask.dtype)

    def entry(self, step):
        packed = self.list[step]
        kind = packed // 65536
        return packed % 256, (packed // 256) % 256, jnp.where(kind == 2, 2 + lax.rem(step, 2), kind)

    def prepare(self, slot, i, j):
        pl.when(slot >= 2)(lambda: self.fill(slot, i, j))

    def walk(self, variants, heads, loops, early, late, row_begin, step_end, row_end):
        steps = self.list[self.list.shape[0] - 1]
        self.mask[0] = jnp.full(self.mask.shape[1:], self.values[0], self.mask.dtype)
        key, query = self.places()
        self.mask[1] = jnp.where(key <= query, *self.values).astype(self.mask.dtype)
        i, j, slot = self.entry(0)
        self.prepare(slot, i, j)
        row_begin(i)
        zero = jnp.int32(0)
        early(zero, 0, i, j, slot, False)

        def body(turn, carry):
            i, j, slot = carry
            group = lax.rem(turn, loops)
            last = group == loops - 1
            after = self.entry(turn // loops + 1)
            ni, nj, nslot = (jnp.where(last, new, old) for new, old in zip(after, carry))
            ngroup = jnp.where(last, 0, group + 1)
            pl.when(last)(lambda: self.prepare(nslot, ni, nj))
            pl.when(ni > i)(lambda: row_begin(ni))

            def work(corner, slot):
                for head in range(heads):
                    if head + 1 < heads:
                        early(group, head + 1, i, j, slot, corner)
                    else:
                        early(ngroup, 0, ni, nj, nslot, False)
                    late(group, head, i, j, corner)

            if variants == 1:
                work(False, slot)
            elif variants == 2:
                pl.when(i != j)(lambda: work(False, slot))
                pl.when(i == j)(lambda: work(True, slot))
            else:
                pl.when(slot == 0)(lambda: work(False, None))
                pl.when((slot > 0) & (i == j))(lambda: work(True, slot))
                pl.when((slot > 0) & (i != j))(lambda: work(False, slot))

            @pl.when(last)
            def _():
                step_end(i, j)
                pl.when(j == i)(lambda: row_end(i))

            return ni, nj, nslot

        lax.fori_loop(0, steps * loops, body, (i, j, slot))


def pieces(corner, size):
    if not corner:
        return [(slice(0, size), slice(0, size))]
    mid = size // 2
    return [(slice(0, mid), slice(0, size)), (slice(mid, size), slice(mid, size))]


def part_at(size, index, part):
    low = index * size + part.start
    return pl.ds(pl.multiple_of(low, size // 2), part.stop - part.start)


class Blockwise:
    def __init__(self, size, first, source, target, sems):
        self.size, self.first = size, first
        self.source, self.target, self.sems = source, target, sems

    def copy(self, block):
        rows = pl.ds(pl.multiple_of(block * self.size, self.size), self.size)
        lanes = pl.ds(self.first, self.target.shape[1])
        return pltpu.make_async_copy(
            self.source.at[rows, lanes], self.target.at[rows, :], self.sems.at[block]
        )


def forward_kernel(
    size, list_ref, small_ref, q_hbm, k_hbm, v_hbm, start_ref, out_hbm, lse_ref, q_ref, k_ref, v_ref,
    vt_ref, stage_ref, in_sems, out_sems, max_ref, new_ref, acc_ref, bias_ref, mask_ref, *slots,
):
    heads = FORWARD_HEADS
    loops = H // heads
    scores, probs_of = slots[:heads], slots[heads:]
    plain = Blocks(size, list_ref, start_ref, mask_ref, (1.0, 0.0))
    general = Blocks(size, list_ref, start_ref, bias_ref, (0.0, NEGATIVE))
    at = plain.at
    count = q_ref.shape[0] // size
    loads = [
        Blockwise(size, 0, source, target, in_sems.at[n])
        for n, (source, target) in enumerate(((k_hbm, k_ref), (q_hbm, q_ref), (v_hbm, v_ref)))
    ]
    for block in range(count):
        for load in loads:
            load.copy(block).start()

    def store(i):
        cols = pl.ds(pl.multiple_of(i * size, size), size)
        return pltpu.make_async_copy(stage_ref.at[:, cols], out_hbm.at[:, cols], out_sems.at[i])

    def row_begin(i):
        for load in loads:
            load.copy(i).wait()
        vt_ref[:, at(i)] = v_ref[at(i), :].T

    def products(group, head, i, j, keys, queries):
        lanes = lanes_of(heads, group, head)
        block = head_half(k_ref[part_at(size, j, keys), lanes], head)
        return mm(block, q_ref[part_at(size, i, queries), lanes], NT)

    def values(group, head, j, keys):
        block = vt_ref[rows_of(heads, group, head), part_at(size, j, keys)]
        return jnp.concatenate([block, jnp.ones((16, keys.stop - keys.start), BF)], 0)

    def early_plain(group, head, i, j, slot, corner):
        for keys, queries in pieces(corner, size):
            probs = jnp.exp2(products(group, head, i, j, keys, queries) * SCALE2).astype(BF)
            if slot is not None:
                probs = probs * mask_ref[slot, keys, queries]
            probs_of[head][keys, queries] = probs

    def late_plain(group, head, i, j, corner):
        for keys, queries in pieces(corner, size):
            acc_ref[heads * group + head, :, queries] += mm(values(group, head, j, keys), probs_of[head][keys, queries])

    whole = slice(0, size)

    def early(group, head, i, j, slot, corner):
        s = products(group, head, i, j, whole, whole)
        if slot is not None:
            s = s + bias_ref[slot]
        scores[head][...] = s
        new_ref[heads * group + head] = jnp.max(s, 0, keepdims=True)

    def late(group, head, i, j, corner):
        place = heads * group + head
        old = max_ref[place]
        new = jnp.maximum(old, new_ref[place])
        max_ref[place] = new
        probs = jnp.exp2(scores[head][...] * SCALE2 - new * SCALE2)
        factor = jnp.exp2((old - new) * SCALE2)
        acc_ref[place] = acc_ref[place] * factor + mm(
            values(group, head, j, whole), probs.astype(BF)
        )

    def reset(largest):
        max_ref[...] = jnp.full(max_ref.shape, largest, F32)
        acc_ref[...] = jnp.zeros(acc_ref.shape, F32)

    def row_end(largest, i):
        def one(head, carry):
            total = acc_ref[head, HD : HD + 1, :]
            rows = pl.ds(pl.multiple_of(HD * head, HD), HD)
            stage_ref[rows, at(i)] = (acc_ref[head, :HD, :] * (1.0 / total)).astype(BF)
            lse_ref[head, :, at(i)] = max_ref[head] * SCALE2 + jnp.log2(total)
            return carry

        lax.fori_loop(0, H, one, 0)
        store(i).start()
        reset(largest)

    def run(variants, blocks, largest, early, late):
        reset(largest)
        blocks.walk(
            variants, heads, loops, early, late, row_begin, lambda i, j: None, functools.partial(row_end, largest)
        )

    pl.when(small_ref[0] == 1)(lambda: run(2, plain, 0.0, early_plain, late_plain))
    pl.when(small_ref[0] != 1)(lambda: run(1, general, NEGATIVE, early, late))
    for i in range(count):
        store(i).wait()


def attend(table, small, q, k, v, start, size):
    length, width = q.shape
    count = length // size
    far = pl.BlockSpec(memory_space=pl.ANY)
    near = pltpu.VMEM((length, width), BF)
    return pl.pallas_call(
        functools.partial(forward_kernel, size),
        grid_spec=pltpu.PrefetchScalarGridSpec(
            num_scalar_prefetch=2,
            grid=(1,),
            in_specs=[far, far, far, once(start)],
            out_specs=[far, kept((H, 1, length))],
            scratch_shapes=[
                near,
                near,
                near,
                pltpu.VMEM((width, length), BF),
                pltpu.VMEM((width, length), BF),
                pltpu.SemaphoreType.DMA((3, count)),
                pltpu.SemaphoreType.DMA((count,)),
                pltpu.VMEM((H, 1, size), F32),
                pltpu.VMEM((H, 1, size), F32),
                pltpu.VMEM((H, HD + 16, size), F32),
                pltpu.VMEM((4, size, size), F32),
                pltpu.VMEM((4, size, size), BF),
            ]
            + [pltpu.VMEM((size, size), F32)] * FORWARD_HEADS
            + [pltpu.VMEM((size, size), BF)] * FORWARD_HEADS,
        ),
        out_shape=[shape_of((width, length), BF), shape_of((H, 1, length), F32)],
        compiler_params=params(),
        name="attend",
    )(table, small, q, k, v, start)


def backward_kernel(
    size, heads, loops, first, list_ref, q_hbm, k_hbm, v_hbm, do_hbm, start_ref, lse_ref, delta_ref,
    dq_hbm, dk_hbm, dv_hbm, q_ref, k_ref, v_ref, do_ref, kt_ref, dq_ref, dk_ref, dv_ref, in_sems,
    out_sems, dqt_acc, dk_acc, dv_acc, bias_ref, *slots,
):
    probs_of, grads_of = slots[:heads], slots[heads:]
    walk = Blocks(size, list_ref, start_ref, bias_ref, (0.0, NEGATIVE))
    at = walk.at
    count = q_ref.shape[0] // size
    pairs = ((k_hbm, k_ref), (q_hbm, q_ref), (v_hbm, v_ref), (do_hbm, do_ref))
    loads = [
        Blockwise(size, first * HD, source, target, in_sems.at[n])
        for n, (source, target) in enumerate(pairs)
    ]
    for block in range(count):
        for load in loads:
            load.copy(block).start()

    def store(n, block):
        source, target = ((dq_ref, dq_hbm), (dk_ref, dk_hbm), (dv_ref, dv_hbm))[n]
        rows = at(block)
        return pltpu.make_async_copy(
            source.at[rows, :], target.at[rows, :], out_sems.at[n, block]
        )

    def row_begin(i):
        for load in loads:
            load.copy(i).wait()
        kt_ref[:, at(i)] = k_ref[at(i), :].T
        dk_acc[at(i), :] = jnp.zeros((size, dk_acc.shape[1]), F32)
        dv_acc[at(i), :] = jnp.zeros((size, dv_acc.shape[1]), F32)

    def early(group, head, i, j, slot, corner):
        lanes = lanes_of(heads, group, head)
        for keys, queries in pieces(corner, size):
            at_j, at_i = part_at(size, j, keys), part_at(size, i, queries)
            stat = (first + heads * group + head, slice(None), at_i)
            s = mm(head_half(k_ref[at_j, lanes], head), q_ref[at_i, lanes], NT)
            dots = mm(head_half(v_ref[at_j, lanes], head), do_ref[at_i, lanes], NT)
            if slot is not None:
                s = s + bias_ref[slot, keys, queries]
            probs = jnp.exp2(s * SCALE2 - lse_ref[stat])
            probs_of[head][keys, queries] = probs.astype(BF)
            grads_of[head][keys, queries] = (probs * (dots - delta_ref[stat])).astype(BF)

    def late(group, head, i, j, corner):
        lanes = lanes_of(heads, group, head)
        rows = rows_of(heads, group, head)
        for keys, queries in pieces(corner, size):
            at_j, at_i = part_at(size, j, keys), part_at(size, i, queries)
            grads = grads_of[head][keys, queries]
            dv_acc[at_j, lanes] += mm(
                probs_of[head][keys, queries], head_half(do_ref[at_i, lanes], head)
            )
            dk_acc[at_j, lanes] += mm(grads, head_half(q_ref[at_i, lanes], head))
            dqt_acc[rows, queries] += mm(kt_ref[rows, at_j], grads)

    def finish(j):
        dk_ref[at(j), :] = (dk_acc[at(j), :] * SCALE).astype(BF)
        dv_ref[at(j), :] = dv_acc[at(j), :].astype(BF)
        store(1, j).start()
        store(2, j).start()

    def step_end(i, j):
        pl.when(i == count - 1)(lambda: finish(j))

    def row_end(i):
        dq_ref[at(i), :] = (dqt_acc[...] * SCALE).T.astype(BF)
        store(0, i).start()
        dqt_acc[...] = jnp.zeros(dqt_acc.shape, F32)

    dqt_acc[...] = jnp.zeros(dqt_acc.shape, F32)
    walk.walk(3, heads, loops, early, late, row_begin, step_end, row_end)
    lowest = jnp.int32(count)
    for slot in range(list_ref.shape[0] - 1):
        lowest = lowest - jnp.where(list_ref[slot] % 256 == count - 1, 1, 0)
    for j in range(count):
        pl.when(j < lowest)(functools.partial(finish, j))
    for j in range(count):
        for n in range(3):
            store(n, j).wait()


def attend_back(first, groups, table, q, k, v, do, start, lse, delta, size):
    length = q.shape[0]
    part = HD * groups
    count = length // size
    far = pl.BlockSpec(memory_space=pl.ANY)
    near = pltpu.VMEM((length, part), BF)
    pairs = count * (count + 1) // 2 * size * size * groups
    return pl.pallas_call(
        functools.partial(backward_kernel, size, BACKWARD_HEADS, groups // BACKWARD_HEADS, first),
        cost_estimate=SHORT,
        grid_spec=pltpu.PrefetchScalarGridSpec(
            num_scalar_prefetch=1,
            grid=(1,),
            in_specs=[far] * 4 + [once(start), once(lse), once(delta)],
            out_specs=[far] * 3,
            scratch_shapes=[near] * 4
            + [pltpu.VMEM((part, length), BF)]
            + [near] * 3
            + [
                pltpu.SemaphoreType.DMA((4, count)),
                pltpu.SemaphoreType.DMA((3, count)),
                pltpu.VMEM((part, size), F32),
                pltpu.VMEM((length, part), F32),
                pltpu.VMEM((length, part), F32),
                pltpu.VMEM((4, size, size), F32),
            ]
            + [pltpu.VMEM((size, size), BF)] * (2 * BACKWARD_HEADS),
        ),
        out_shape=[shape_of((length, part), BF)] * 3,
        compiler_params=params(),
        name="attend_back",
    )(table, q, k, v, do, start, lse, delta)


def feed_kernel(
    chunk, place_ref, att_ref, x_got, x_own, cot_got, cot_own, wo_ref, ob_ref, g2_ref, s2_ref, we_ref,
    eb_ref, wr_ref, hid_ref, exg_ref, keep_ref, send_ref, deb_ref, acc_ref, deb_acc, wet_ref, ebt_ref,
):
    step = pl.program_id(0)
    tile, width = x_got.shape
    total = wr_ref.shape[0]

    @pl.when(step == 0)
    def _():
        for ref in (acc_ref, deb_acc):
            ref[...] = jnp.zeros(ref.shape, F32)
        wet_ref[...] = we_ref[...].T
        ebt_ref[...] = jnp.broadcast_to(eb_ref[...], (128, total)).T

    mixed = mm(att_ref[...].T, wo_ref[...]) + ob_ref[...]
    middle = either(x_got, x_own).astype(F32) + BRANCH * mixed
    unit, _ = norm_parts(middle)
    second = (unit * g2_ref[...] + s2_ref[...]).astype(BF)
    second_t = second.T
    reduced_grad = (BRANCH * either(cot_got, cot_own).astype(F32)).astype(BF)

    def stage_one(c):
        rows = slice(c * chunk, (c + 1) * chunk)
        bias = jnp.concatenate([ebt_ref[rows, :]] * (tile // 128), 1)
        v = mm(wet_ref[rows, :], second, NT) + bias
        v2 = v * v
        t = jnp.tanh(v * (GELU_A + GELU_B * v2))
        h1 = 0.5 * t + 0.5
        gelu = v * h1
        slope = h1 + gelu * (1.0 - h1) * (2.0 * GELU_A + 6.0 * GELU_B * v2)
        hid_ref[rows, :] = gelu.astype(BF)
        grads = (mm(wr_ref[rows, :], reduced_grad, NT) * slope).astype(BF)
        exg_ref[rows, :] = grads
        wide = grads.astype(F32)
        part = wide[:, 0:128]
        for n in range(1, tile // 128):
            part = part + wide[:, n * 128 : (n + 1) * 128]
        deb_acc[rows, :] += part

    stage_one(0)
    for c in range(total // chunk):
        if (c + 1) * chunk < total:
            stage_one(c + 1)
        rows = slice(c * chunk, (c + 1) * chunk)
        acc_ref[rows, :] += mm(hid_ref[rows, :], reduced_grad)
        block, low = divmod(c * chunk, width)
        there = slice(total + block * width, total + (block + 1) * width)
        acc_ref[there, low : low + chunk] += mm(second_t, exg_ref[rows, :], NT)

    last = step == pl.num_programs(0) - 1
    halves = slice(0, total), slice(total, 2 * total)
    for core in range(2):

        @pl.when(last & (place_ref[1] == core))
        def _():
            keep_ref[...] = acc_ref[halves[core], :].astype(BF)
            send_ref[...] = acc_ref[halves[1 - core], :].astype(BF)

    @pl.when(last)
    def _():
        flat = jnp.sum(deb_acc[...].T, 0, keepdims=True)
        deb_ref[...] = jnp.zeros(deb_ref.shape, F32)
        for n in range(total // width):
            deb_ref[n : n + 1, :] = flat[:, n * width : (n + 1) * width]


def feed_part(place, att_t, x_got, x_own, cot_got, cot_own, wo, ob, g2, s2, we, eb, wr, tile, chunk):
    width, length = att_t.shape
    total = wr.shape[0]
    tiles = length // tile
    where, _, _ = own_and_got(tiles)
    pair = list(row_specs(tile, width, tiles))
    cols = lambda high: pl.BlockSpec((high, tile), lambda t, h: (0, where(t, h)))
    return pl.pallas_call(
        functools.partial(feed_kernel, chunk),
        grid_spec=pltpu.PrefetchScalarGridSpec(
            num_scalar_prefetch=1,
            grid=(tiles,),
            in_specs=[cols(width)] + pair * 2 + [once(a) for a in (wo, ob, g2, s2, we, eb, wr)],
            out_specs=[cols(total), cols(total), kept((total, width)), kept((total, width)), kept((8, width))],
            scratch_shapes=[
                pltpu.VMEM((2 * total, width), F32),
                pltpu.VMEM((total, 128), F32),
                pltpu.VMEM((total, width), BF),
                pltpu.VMEM((total, 128), F32),
            ],
        ),
        out_shape=[
            shape_of((total, length), BF),
            shape_of((total, length), BF),
            shape_of((total, width), BF),
            shape_of((total, width), BF),
            shape_of((8, width), F32),
        ],
        compiler_params=params(),
        name="feed",
    )(place, att_t, x_got, x_own, cot_got, cot_own, wo, ob, g2, s2, we, eb, wr)


def middle_kernel(
    place_ref, att_ref, x_got, x_own, cot_got, cot_own, hid_ref, exg_ref, wo_ref, ob_ref, g2_ref,
    we_ref, wr_ref, rb_ref, res_own, res_send, grad_ref, ag_ref, delta_ref, dwo_ref, vec_ref, acc_ref,
    wrt_ref,
):
    step = pl.program_id(0)
    tiles = pl.num_programs(0)

    @pl.when(step == 0)
    def _():
        for ref in (acc_ref, vec_ref):
            ref[...] = jnp.zeros(ref.shape, F32)
        wrt_ref[...] = wr_ref[...].T

    att_t = att_ref[...]
    mixed = mm(att_t.T, wo_ref[...]) + ob_ref[...]
    middle = either(x_got, x_own).astype(F32) + BRANCH * mixed
    cot = either(cot_got, cot_own).astype(F32)
    unit, scale = norm_parts(middle)
    norm_grad = mm(we_ref[...], exg_ref[...]).T
    result = (middle + BRANCH * (mm(wrt_ref[...], hid_ref[...]).T + rb_ref[...])).astype(BF)

    @pl.when(step < tiles // 2)
    def _():
        res_send[...] = result

    @pl.when(step >= tiles // 2)
    def _():
        res_own[0] = result

    middle_grad = cot + norm_back(norm_grad, unit, scale, g2_ref[...])
    grad_ref[...] = middle_grad
    mixed_grad = (BRANCH * middle_grad).astype(BF)
    acc_ref[...] += mm(att_t, mixed_grad)
    att_grad = mm(mixed_grad, wo_ref[...], NT).astype(BF)
    ag_ref[...] = att_grad
    dots = att_grad.T.astype(F32) * att_t.astype(F32)
    for head in range(H):
        delta_ref[head] = jnp.sum(dots[HD * head : HD * head + HD, :], 0, keepdims=True)
    reduced_grad = (BRANCH * cot).astype(BF)
    sums = (norm_grad * unit, norm_grad, mixed_grad.astype(F32), reduced_grad.astype(F32))
    for n, value in enumerate(sums):
        vec_ref[n : n + 1, :] += jnp.sum(value, 0, keepdims=True)

    @pl.when(step == tiles - 1)
    def _():
        dwo_ref[...] = acc_ref[...].astype(BF)


def middle_part(place, att_t, x_got, x_own, cot_got, cot_own, hid, exg, wo, ob, g2, we, wr, rb, tile):
    width, length = att_t.shape
    total = wr.shape[0]
    tiles = length // tile
    where, got, own = own_and_got(tiles)
    pair = list(row_specs(tile, width, tiles))
    rows = pl.BlockSpec((tile, width), lambda t, h: (where(t, h), 0))
    cols = lambda high: pl.BlockSpec((high, tile), lambda t, h: (0, where(t, h)))
    return pl.pallas_call(
        middle_kernel,
        cost_estimate=SHORT,
        grid_spec=pltpu.PrefetchScalarGridSpec(
            num_scalar_prefetch=1,
            grid=(tiles,),
            in_specs=[cols(width)]
            + pair * 2
            + [cols(total), cols(total)]
            + [once(a) for a in (wo, ob, g2, we, wr, rb)],
            out_specs=[
                pair[1],
                pair[0],
                rows,
                rows,
                pl.BlockSpec((H, 1, tile), lambda t, h: (0, 0, where(t, h))),
                kept((width, width)),
                kept((8, width)),
            ],
            scratch_shapes=[pltpu.VMEM((width, width), F32), pltpu.VMEM((width, total), BF)],
        ),
        out_shape=[
            shape_of((2, length // 2, width), BF),
            shape_of((length // 2, width), BF),
            shape_of((length, width), F32),
            shape_of((length, width), BF),
            shape_of((H, 1, length), F32),
            shape_of((width, width), BF),
            shape_of((8, width), F32),
        ],
        compiler_params=params(),
        name="middle",
    )(place, att_t, x_got, x_own, cot_got, cot_own, hid, exg, wo, ob, g2, we, wr, rb)


def weight_kernel(parts, place_ref, *refs):
    ins = refs[: 3 * parts]
    x_got, x_own, gain_ref, shift_ref, extra_ref, keep_ref, send_ref, acc_ref = refs[3 * parts :]
    step = pl.program_id(0)

    @pl.when(step == 0)
    def _():
        acc_ref[...] = jnp.zeros(acc_ref.shape, F32)

    width = x_got.shape[1]
    unit, _ = norm_parts(either(x_got, x_own).astype(F32))
    normed_t = (unit * gain_ref[...] + shift_ref[...]).astype(BF).T
    for n in range(3):
        grad = jnp.concatenate([ref[...] for ref in ins[n * parts : (n + 1) * parts]], 1)
        acc_ref[n * width : (n + 1) * width, :] += mm(normed_t, grad)

    last = step == pl.num_programs(0) - 1
    for core in range(2):

        @pl.when(last & (place_ref[1] == core))
        def _():
            lower, upper = (keep_ref, send_ref) if core == 0 else (send_ref, keep_ref)
            lower[...] = acc_ref[: 2 * width, :].astype(BF)
            upper[:width, :] = acc_ref[2 * width :, :].astype(BF)
            upper[width:, :] = extra_ref[...]


def weight_part(place, grads, x_got, x_own, gain, shift, extra, tile):
    span, width = x_got.shape
    tiles = 2 * span // tile
    where, _, _ = own_and_got(tiles)
    flat = [part for group in grads for part in group]
    out = shape_of((2 * width, width), BF)
    return pl.pallas_call(
        functools.partial(weight_kernel, len(grads[0])),
        cost_estimate=SHORT,
        grid_spec=pltpu.PrefetchScalarGridSpec(
            num_scalar_prefetch=1,
            grid=(tiles,),
            in_specs=[
                pl.BlockSpec((tile, a.shape[1]), lambda t, h: (where(t, h), 0)) for a in flat
            ]
            + list(row_specs(tile, width, tiles))
            + [once(a) for a in (gain, shift, extra)],
            out_specs=[kept(out.shape)] * 2,
            scratch_shapes=[pltpu.VMEM((3 * width, width), F32)],
        ),
        out_shape=[out, out],
        compiler_params=params(),
        name="weight",
    )(place, *flat, x_got, x_own, gain, shift, extra)


def last_kernel(parts, place_ref, *refs):
    ins, rest = refs[: 3 * parts], refs[3 * parts :]
    x_got, x_own, mid_ref, gain_ref, weight_ref, own_ref, send_ref, vec_ref = rest
    step = pl.program_id(0)
    tiles = pl.num_programs(0)

    @pl.when(step == 0)
    def _():
        vec_ref[...] = jnp.zeros(vec_ref.shape, F32)

    width = x_got.shape[1]
    unit, scale = norm_parts(either(x_got, x_own).astype(F32))
    back = None
    grads = []
    for n in range(3):
        grad = jnp.concatenate([ref[...] for ref in ins[n * parts : (n + 1) * parts]], 1)
        one = mm(grad, weight_ref[:, n * width : (n + 1) * width], NT)
        back = one if back is None else back + one
        grads.append(grad)
    total = mid_ref[...] + norm_back(back, unit, scale, gain_ref[...])

    @pl.when(step < tiles // 2)
    def _():
        send_ref[...] = total.astype(BF)

    @pl.when(step >= tiles // 2)
    def _():
        own_ref[0] = total

    sums = (back * unit, back, grads[0].astype(F32), grads[2].astype(F32))
    for n, value in enumerate(sums):
        vec_ref[n : n + 1, :] += jnp.sum(value, 0, keepdims=True)


def last_part(place, grads, x_got, x_own, mid, gain, weight, tile):
    length, width = mid.shape
    tiles = length // tile
    where, _, _ = own_and_got(tiles)
    rows = pl.BlockSpec((tile, width), lambda t, h: (where(t, h), 0))
    flat = [part for group in grads for part in group]
    pair = list(row_specs(tile, width, tiles))
    return pl.pallas_call(
        functools.partial(last_kernel, len(grads[0])),
        cost_estimate=SHORT,
        grid_spec=pltpu.PrefetchScalarGridSpec(
            num_scalar_prefetch=1,
            grid=(tiles,),
            in_specs=[
                pl.BlockSpec((tile, a.shape[1]), lambda t, h: (where(t, h), 0)) for a in flat
            ]
            + pair
            + [rows, once(gain), once(weight)],
            out_specs=[pair[1], pair[0], kept((8, width))],
        ),
        out_shape=[
            shape_of((2, length // 2, width), F32),
            shape_of((length // 2, width), BF),
            shape_of((8, width), F32),
        ],
        compiler_params=params(),
        name="last",
    )(place, *flat, x_got, x_own, mid, gain, weight)


def swapped(value):
    return lax.ppermute(value, "seq", [(0, 1), (1, 0)])


def side(hop):
    axis, bit = hop
    return (lax.axis_index(axis) // bit) % 2


def place_of(hops):
    place = 0
    for hop in hops:
        place = 2 * place + side(hop)
    return place


def exchanged(value, hops):
    axes = tuple(dict.fromkeys(axis for axis, _ in hops))
    flips = [sum(bit for axis, bit in hops if axis == name) for name in axes]
    sizes = [lax.axis_size(name) for name in axes]
    if len(axes) == 1:
        return lax.ppermute(value, axes[0], [(i, i ^ flips[0]) for i in range(sizes[0])])
    pairs = [
        (i * sizes[1] + j, (i ^ flips[0]) * sizes[1] + (j ^ flips[1]))
        for i in range(sizes[0])
        for j in range(sizes[1])
    ]
    return lax.ppermute(value, axes, pairs)


def partners(hops):
    count = len(hops)
    return [
        ([hop for n, hop in enumerate(hops) if (flip >> (count - 1 - n)) & 1], flip)
        for flip in range(1, 1 << count)
    ]


def added(*values):
    total = values[0].astype(F32)
    for value in values[1:]:
        total = total + value.astype(F32)
    return total.astype(BF)


def scatter(part, hops):
    rows = part.shape[1] >> len(hops)
    mine = place_of(hops)
    piece = lambda place: lax.dynamic_slice_in_dim(part, place * rows, rows, 1)
    got = [exchanged(piece(mine ^ flip), chosen) for chosen, flip in partners(hops)]
    return added(piece(mine), *got)


def gather(part, hops, whole=None):
    mine = place_of(hops)
    blocks, rows, width = part.shape
    got, others = [(part, mine)], []
    for chosen, flip in partners(hops):
        if whole is None:
            got.append((exchanged(part, chosen), mine ^ flip))
            continue
        both = exchanged(jnp.concatenate([part.reshape(-1, width), whole], 0), chosen)
        got.append((both[: blocks * rows].reshape(part.shape), mine ^ flip))
        others.append(both[blocks * rows :])
    if len(hops) == 1:
        one, two = got[0][0], got[1][0]
        out = jnp.where(mine == 0, jnp.concatenate([one, two], 1), jnp.concatenate([two, one], 1))
    else:
        out = jnp.zeros((blocks, rows << len(hops), width), part.dtype)
        for piece, place in got:
            out = lax.dynamic_update_slice_in_dim(out, piece, place * rows, 1)
    return out if whole is None else (out, added(whole, *others))


def hops():
    found = []
    for axis in ("dp", "seq"):
        size = lax.axis_size(axis)
        found.append([(axis, 1 << n) for n in range(size.bit_length() - 1)])
    core, one, two, far = found[0]
    return [core], [one, two], [far], found[1]


class AllSum:
    def __init__(self, keep, send, core):
        self.core, self.whole = core, None
        self.state = (keep[None], send[None])

    def split(self):
        keep, send = self.state
        self.state = added(keep, exchanged(send, self.core))

    def cross(self, one, two):
        if not isinstance(self.state, tuple):
            mid = self.state.shape[1] // 2
            self.state = (self.state[:, :mid], self.state[:, mid:])
        self.state = tuple(scatter(part, hops) for part, hops in zip(self.state, (one, two)))

    def uncross(self, one, two):
        if not isinstance(self.state, tuple):
            self.state = (self.state[:1], self.state[1:])
        self.state = tuple(gather(part, hops) for part, hops in zip(self.state, (one, two)))

    def join(self):
        self.state = gather(jnp.concatenate(self.state, 1), self.core)

    def ride(self, whole, hops):
        self.whole = added(whole, exchanged(whole, hops))

    def narrow(self, hops):
        if isinstance(self.state, tuple):
            self.state = jnp.concatenate(self.state, 0)
        self.state = scatter(self.state, hops)

    def meet(self, hops):
        self.state = added(self.state, exchanged(self.state, hops))

    def widen(self, hops):
        if self.whole is None:
            self.state = gather(self.state, hops)
        else:
            self.state, self.whole = gather(self.state, hops, self.whole)

    def beside(self, call, argument, step, *hops):
        argument = after(argument, self.state)
        step(*hops)
        out = call(argument)
        self.state = after(self.state, out)
        return out


def after(value, earlier):
    return lax.optimization_barrier((value, earlier))[0]


def passed_along(block, axis, distance):
    devices = range(lax.axis_size(axis))
    route = [(i - distance, i) for i in devices if i - distance in devices]
    return lax.ppermute(block, axis, route)


def from_behind(value, axis, steps):
    count = lax.axis_size(axis)
    pairs = [(source, (source + steps) % count) for source in range(count)]
    return lax.ppermute(value, axis, pairs)


def layer_norm(values, gain_vec, shift_vec):
    center = jnp.mean(values, -1, keepdims=True)
    centered = values - center
    variance = jnp.mean(centered * centered, -1, keepdims=True)
    return centered * lax.rsqrt(variance + EPSILON) * gain_vec + shift_vec


def gelu_tanh(values):
    return jax.nn.gelu(values, approximate=True)


def plain_dot(left, right):
    return jnp.dot(left, right, preferred_element_type=jnp.float32)


def left_dot(left, right):
    return lax.dot_general(
        left, right, (((0,), (0,)), ((), ())), preferred_element_type=jnp.float32
    )


def right_dot(left, right):
    return lax.dot_general(
        left, right, (((1,), (1,)), ((), ())), preferred_element_type=jnp.float32
    )


def block_scores(queries, keys_block, query_seg, key_seg, query_places, key_start):
    row_count, key_len, width = keys_block.shape
    keys_heads = keys_block.reshape(row_count, key_len, H, HD)
    scores = jnp.einsum(
        "rqhd,rkhd->rhqk", queries, keys_heads, preferred_element_type=jnp.float32
    ) * HD ** (-0.5)
    key_places = key_start + jnp.arange(key_len, dtype=jnp.int32)
    allowed = (query_seg[:, None, :, None] == key_seg[:, None, None, :]) & (
        key_places[None, None, None, :] <= query_places[None, None, :, None]
    )
    return (scores, allowed)


def attend_block(state, queries, block, query_seg, query_places, key_start):
    run_max, run_sum, running = state
    keys_block, values_block, key_seg = block
    row_count, key_len, width = values_block.shape
    query_len = queries.shape[1]
    scores, allowed = block_scores(queries, keys_block, query_seg, key_seg, query_places, key_start)
    block_max = jnp.max(jnp.where(allowed, scores, NEGATIVE), -1)
    new_max = jnp.maximum(run_max, block_max)
    exponent = jnp.where(allowed, jnp.exp(scores - new_max[..., None]), 0.0)
    factor = jnp.exp(run_max - new_max)
    new_sum = run_sum * factor + jnp.sum(exponent, -1)
    values_heads = values_block.reshape(row_count, key_len, H, HD)
    addition = jnp.einsum(
        "rhqk,rkhd->rqhd",
        exponent.astype(jnp.bfloat16),
        values_heads,
        preferred_element_type=jnp.float32,
    )
    scaled = (
        running.reshape(row_count, query_len, H, HD) * jnp.transpose(factor, (0, 2, 1))[..., None]
    )
    return (new_max, new_sum, (scaled + addition).reshape(row_count, query_len, width))


def grad_block(queries, out_grad, log_sum, delta, block, query_seg, query_places, key_start):
    keys_block, values_block, key_seg = block
    row_count, key_len, width = keys_block.shape
    scores, allowed = block_scores(queries, keys_block, query_seg, key_seg, query_places, key_start)
    weights_block = jnp.where(allowed, jnp.exp(scores - log_sum[..., None]), 0.0)
    keys_heads = keys_block.reshape(row_count, key_len, H, HD)
    values_heads = values_block.reshape(row_count, key_len, H, HD)
    value_dots = jnp.einsum(
        "rqhd,rkhd->rhqk", out_grad, values_heads, preferred_element_type=jnp.float32
    )
    score_grad = (weights_block * (value_dots - delta[..., None]) * HD ** (-0.5)).astype(
        jnp.bfloat16
    )
    query_part = jnp.einsum(
        "rhqk,rkhd->rqhd", score_grad, keys_heads, preferred_element_type=jnp.float32
    ).reshape(row_count, -1, width)
    key_part = jnp.einsum(
        "rhqk,rqhd->rkhd", score_grad, queries, preferred_element_type=jnp.float32
    ).reshape(row_count, key_len, width)
    value_part = jnp.einsum(
        "rhqk,rqhd->rkhd",
        weights_block.astype(jnp.bfloat16),
        out_grad,
        preferred_element_type=jnp.float32,
    ).reshape(row_count, key_len, width)
    return (query_part, key_part, value_part)


def local(
    activations,
    segments,
    first_gain,
    first_shift,
    input_weight,
    query_bias,
    value_bias,
    output_weight,
    output_bias,
    second_gain,
    second_shift,
    expand_weight,
    expand_bias,
    reduce_weight,
    reduce_bias,
    cotangent,
):
    row_total, span_len, width = activations.shape
    cycle_size = lax.axis_size("seq")
    position = lax.axis_index("seq")
    micro_rows = row_total // MICRO
    branch = DEPTH ** (-0.5)
    bias_all = jnp.concatenate([query_bias, jnp.zeros_like(query_bias), value_bias])
    query_places = position * span_len + jnp.arange(span_len, dtype=jnp.int32)
    totals = [
        jnp.zeros(argument.shape, jnp.float32)
        for argument in (
            first_gain,
            first_shift,
            input_weight,
            query_bias,
            value_bias,
            output_weight,
            output_bias,
            second_gain,
            second_shift,
            expand_weight,
            expand_bias,
            reduce_weight,
            reduce_bias,
        )
    ]
    outputs_list = []
    grads_list = []
    for micro in range(MICRO):
        lower = micro * micro_rows
        values_in = activations[lower : lower + micro_rows].astype(jnp.float32)
        query_seg = segments[lower : lower + micro_rows]
        out_cot = cotangent[lower : lower + micro_rows].astype(jnp.float32)
        normed, first_pull = jax.vjp(layer_norm, values_in, first_gain, first_shift)
        normed_low = normed.astype(jnp.bfloat16).reshape(-1, width)
        projected = (plain_dot(normed_low, input_weight) + bias_all).astype(jnp.bfloat16)
        queries = projected[:, :width].reshape(micro_rows, span_len, H, HD)
        keys_own = projected[:, width : 2 * width].reshape(micro_rows, span_len, width)
        values_own = projected[:, 2 * width :].reshape(micro_rows, span_len, width)
        own_block = (keys_own, values_own, query_seg)
        start_state = (
            jnp.full((micro_rows, H, span_len), NEGATIVE, jnp.float32),
            jnp.zeros((micro_rows, H, span_len), jnp.float32),
            jnp.zeros((micro_rows, span_len, width), jnp.float32),
        )
        state = attend_block(
            start_state, queries, own_block, query_seg, query_places, position * span_len
        )

        def cycle_forward(step_index, carry):
            block, inner_state = carry
            block = passed_along((block[0], block[1], block[2]), "seq", 1)
            source = (position - step_index) % cycle_size
            inner_state = lax.cond(
                source < position,
                lambda current: attend_block(
                    current, queries, block, query_seg, query_places, source * span_len
                ),
                lambda current: current,
                inner_state,
            )
            return (block, inner_state)

        unused_block, state = lax.fori_loop(1, cycle_size, cycle_forward, (own_block, state))
        run_max, run_sum, running = state
        attended = (
            running.reshape(micro_rows, span_len, H, HD)
            / jnp.transpose(run_sum, (0, 2, 1))[..., None]
        ).reshape(micro_rows, span_len, width)
        log_sum = run_max + jnp.log(run_sum)
        attended_low = attended.astype(jnp.bfloat16).reshape(-1, width)
        mixed_out = plain_dot(attended_low, output_weight) + output_bias
        middle = values_in + branch * mixed_out.reshape(values_in.shape)
        second_norm, second_pull = jax.vjp(layer_norm, middle, second_gain, second_shift)
        second_low = second_norm.astype(jnp.bfloat16).reshape(-1, width)
        expanded = plain_dot(second_low, expand_weight) + expand_bias
        hidden, gelu_pull = jax.vjp(gelu_tanh, expanded)
        hidden_low = hidden.astype(jnp.bfloat16)
        reduced = plain_dot(hidden_low, reduce_weight) + reduce_bias
        outputs_list.append(
            (middle + branch * reduced.reshape(values_in.shape)).astype(jnp.bfloat16)
        )
        reduced_grad = (branch * out_cot).reshape(-1, width).astype(jnp.bfloat16)
        totals[12] = totals[12] + jnp.sum(reduced_grad.astype(jnp.float32), 0)
        totals[11] = totals[11] + left_dot(hidden_low, reduced_grad)
        (expanded_grad,) = gelu_pull(right_dot(reduced_grad, reduce_weight))
        expanded_low = expanded_grad.astype(jnp.bfloat16)
        totals[10] = totals[10] + jnp.sum(expanded_low.astype(jnp.float32), 0)
        totals[9] = totals[9] + left_dot(second_low, expanded_low)
        norm_in_grad = right_dot(expanded_low, expand_weight).reshape(values_in.shape)
        middle_part, gain_part, shift_part = second_pull(norm_in_grad)
        totals[7] = totals[7] + gain_part
        totals[8] = totals[8] + shift_part
        middle_grad = out_cot + middle_part
        mixed_grad = (branch * middle_grad).reshape(-1, width).astype(jnp.bfloat16)
        totals[6] = totals[6] + jnp.sum(mixed_grad.astype(jnp.float32), 0)
        totals[5] = totals[5] + left_dot(attended_low, mixed_grad)
        attended_grad = (
            right_dot(mixed_grad, output_weight)
            .astype(jnp.bfloat16)
            .reshape(micro_rows, span_len, H, HD)
        )
        delta = jnp.transpose(
            jnp.sum(
                attended_grad.astype(jnp.float32) * attended.reshape(micro_rows, span_len, H, HD),
                -1,
            ),
            (0, 2, 1),
        )
        query_grad, key_grad, value_grad = grad_block(
            queries,
            attended_grad,
            log_sum,
            delta,
            own_block,
            query_seg,
            query_places,
            position * span_len,
        )

        def cycle_backward(step_index, carry):
            block, partial_value, query_acc = carry
            block = passed_along((block[0], block[1], block[2]), "seq", 1)
            partial_value = (
                from_behind(partial_value[0].astype(jnp.bfloat16), "seq", 1).astype(jnp.float32),
                from_behind(partial_value[1].astype(jnp.bfloat16), "seq", 1).astype(jnp.float32),
            )
            source = (position - step_index) % cycle_size

            def work(current):
                partial_in, query_in = current
                query_part, key_part, value_part = grad_block(
                    queries,
                    attended_grad,
                    log_sum,
                    delta,
                    block,
                    query_seg,
                    query_places,
                    source * span_len,
                )
                return (
                    (partial_in[0] + key_part, partial_in[1] + value_part),
                    query_in + query_part,
                )

            partial_value, query_acc = lax.cond(
                source < position, work, lambda current: current, (partial_value, query_acc)
            )
            return (block, partial_value, query_acc)

        unused_block, partial_value, query_grad = lax.fori_loop(
            1, cycle_size, cycle_backward, (own_block, (key_grad, value_grad), query_grad)
        )
        key_grad, value_grad = (
            from_behind(partial_value[0].astype(jnp.bfloat16), "seq", 1).astype(jnp.float32),
            from_behind(partial_value[1].astype(jnp.bfloat16), "seq", 1).astype(jnp.float32),
        )
        qkv_grad = (
            jnp.concatenate([query_grad, key_grad, value_grad], -1)
            .reshape(-1, 3 * width)
            .astype(jnp.bfloat16)
        )
        totals[3] = totals[3] + jnp.sum(qkv_grad[:, :width].astype(jnp.float32), 0)
        totals[4] = totals[4] + jnp.sum(qkv_grad[:, 2 * width :].astype(jnp.float32), 0)
        totals[2] = totals[2] + left_dot(normed_low, qkv_grad)
        norm_grad = right_dot(qkv_grad, input_weight).reshape(values_in.shape)
        input_part, gain_one, shift_one = first_pull(norm_grad)
        totals[0] = totals[0] + gain_one
        totals[1] = totals[1] + shift_one
        grads_list.append(middle_grad + input_part)
    summed = lax.psum(
        (
            totals[0],
            totals[1],
            totals[2],
            totals[3],
            totals[4],
            totals[5],
            totals[6],
            totals[7],
            totals[8],
            totals[9],
            totals[10],
            totals[11],
            totals[12],
        ),
        ("dp", "seq"),
    )
    return (
        jnp.concatenate(outputs_list, 0),
        jnp.concatenate(grads_list, 0),
        summed[0],
        summed[1],
        summed[2],
        summed[3],
        summed[4],
        summed[5],
        summed[6],
        summed[7],
        summed[8],
        summed[9],
        summed[10],
        summed[11],
        summed[12],
    )


def local_rows(
    activations,
    segments,
    first_gain,
    first_shift,
    input_weight,
    query_bias,
    value_bias,
    output_weight,
    output_bias,
    second_gain,
    second_shift,
    expand_weight,
    expand_bias,
    reduce_weight,
    reduce_bias,
    cotangent,
):
    rows, span, width = activations.shape
    mine = lax.axis_index("seq")
    half = mine.astype(jnp.int32)[None]
    core = lax.axis_index("dp").astype(jnp.int32)[None] % 2
    place = jnp.concatenate([half, core])
    take = lambda array, index: lax.dynamic_index_in_dim(array, index, 0, keepdims=False)
    row = lambda vector: vector.reshape(1, -1)
    seg_got = swapped(take(segments, 1 - mine))
    x_got = swapped(after(take(activations, 1 - mine), seg_got))
    bias = jnp.concatenate([query_bias, jnp.zeros_like(query_bias), value_bias])
    gain, shift = row(first_gain), row(first_shift)
    weights = (gain, shift, input_weight, row(bias))
    start, table = documents(half, row(take(segments, mine)), row(seg_got), BLOCK)
    *before, norms = project(True, half, activations, *weights, (), TILE)
    cot_got = swapped(after(take(cotangent, 1 - mine), (x_got, norms)))
    q, k, v, more = project(False, half, x_got, *weights, before, TILE)
    norms = jnp.maximum(norms, more)
    limit = jnp.max(norms[0] * norms[1]) * (SCALE2 * SCALE2)
    small = (limit < SMALL * SMALL).astype(jnp.int32)[None]
    att_t, lse = attend(table, small, q, k, v, start, BLOCK)
    tokens = (x_got, activations, cot_got, cotangent)
    out_bias, gain_two = row(output_bias), row(second_gain)
    hid, exg, keep, send, vec_expand = feed_part(
        place, att_t, *tokens, output_weight, out_bias, gain_two, row(second_shift), expand_weight,
        row(expand_bias), reduce_weight, TILE, CHUNK,
    )

    core_hop, plane, line, pair = hops()
    one, two = ([hop] for hop in plane)
    sums = AllSum(keep, send, core_hop)
    result, result_send, mid_grad, att_grad, delta, d_output, vec = sums.beside(
        lambda place: middle_part(
            place, att_t, *tokens, hid, exg, output_weight, out_bias, gain_two, expand_weight,
            reduce_weight, row(reduce_bias), TILE,
        ),
        place, sums.split,
    )
    result_got = swapped(result_send)
    grads = []
    for first, ways in ((0, (one, two)), (H // 2, (two, one))):
        call = lambda table: attend_back(
            first, H // 2, table, q, k, v, att_grad, start, lse, delta, BLOCK
        )
        grads.append(sums.beside(call, table, sums.cross, *ways))
    grads = [[g[n] for g in grads] for n in range(3)]
    keep, send = sums.beside(
        lambda place: weight_part(place, grads, x_got, activations, gain, shift, d_output, TILE),
        after(place, result_got), sums.narrow, line + pair,
    )
    keep, send = after((keep, send), sums.state)
    tail = AllSum(keep, send, core_hop)
    sums.widen(line + pair)
    tail.split()
    ready = after(place, tail.state)
    tail.narrow(plane)
    grad, grad_send, vec_last = last_part(
        ready, grads, x_got, activations, mid_grad, gain, input_weight, TILE
    )
    tail.state = after(tail.state, grad)
    sums.state = after(sums.state, grad)
    vectors = jnp.concatenate([vec[:4], vec_expand[:4], vec_last], 0).astype(BF)
    sums.uncross(two, one)
    tail.meet(pair)
    tail.ride(vectors, pair)
    grad_got = swapped(after(grad_send, (tail.state, tail.whole)))
    tail.narrow(line)
    sums.state = after(sums.state, tail.state)
    sums.uncross(one, two)
    sums.join()
    tail.widen(line)
    tail.widen(plane)
    tail.widen(core_hop)
    part, dw = sums.state[0], tail.state[0]
    put = lambda whole, got: lax.dynamic_update_index_in_dim(
        whole, got.astype(whole.dtype), 1 - mine, 0
    )
    total = expand_weight.shape[1]

    def beside(stack):
        blocks = stack.shape[0] // width
        return jnp.concatenate([stack[n * width : (n + 1) * width] for n in range(blocks)], 1).astype(F32)

    vectors = tail.whole.astype(F32)
    return (
        put(result, result_got),
        put(grad, grad_got),
        vectors[8],
        vectors[9],
        beside(dw[: 3 * width]),
        vectors[10],
        vectors[11],
        dw[3 * width :].astype(F32),
        vectors[2],
        vectors[0],
        vectors[1],
        beside(part[total:]),
        vectors[4:8].reshape(-1),
        part[:total].astype(F32),
        vectors[3],
    )


TILE = 512
CHUNK = 256
BLOCK = 512
SMALL = 60.0
FORWARD_HEADS = 4
BACKWARD_HEADS = 2


def solution(mesh):
    sizes = dict(zip(mesh.axis_names, mesh.devices.shape))
    tokens, places, whole = P("dp", "seq", None), P("dp", "seq"), P()
    in_specs = (tokens, places) + (whole,) * 13 + (tokens,)
    out_specs = (tokens, tokens) + (whole,) * 13

    def program(activations, *rest):
        rows = activations.shape[0] // sizes["dp"]
        span = activations.shape[1] // sizes["seq"]
        by_rows = sizes["seq"] == 2 and rows == 2 and span % BLOCK == 0 and sizes["dp"] == 16
        return jax.shard_map(
            local_rows if by_rows else local,
            mesh=mesh,
            in_specs=in_specs,
            out_specs=out_specs,
            check_vma=False,
        )(activations, *rest)

    return program
```

```python
import functools

import jax
import jax.numpy as jnp
from jax import lax
from jax.experimental import pallas as pl
from jax.experimental.pallas import tpu as pltpu
from jax.sharding import PartitionSpec as P

H = 8
HD = 64
DEPTH = 48
MICRO = 2
EPSILON = 1e-05
NEGATIVE = -1e30
BRANCH = DEPTH ** (-0.5)
SCALE = HD ** (-0.5)
SCALE2 = SCALE * 1.4426950408889634
GELU_A = 0.7978845608028654
GELU_B = GELU_A * 0.044715

BF = jnp.bfloat16
F32 = jnp.float32
NN = (((1,), (0,)), ((), ()))
NT = (((1,), (1,)), ((), ()))
VMEM_LIMIT = 58 << 20
SHORT = pl.CostEstimate(flops=1000, bytes_accessed=1000, transcendentals=0)


def mm(left, right, dims=NN):
    return lax.dot_general(left, right, dims, preferred_element_type=F32)


def shape_of(dims, dtype):
    return jax.ShapeDtypeStruct(dims, dtype)


def params(limit=VMEM_LIMIT):
    return pltpu.CompilerParams(vmem_limit_bytes=limit)


def norm_parts(values):
    center = jnp.mean(values, -1, keepdims=True)
    centered = values - center
    variance = jnp.mean(centered * centered, -1, keepdims=True)
    scale = lax.rsqrt(variance + EPSILON)
    return centered * scale, scale


def norm_back(grad, unit, scale, gain):
    inner = grad * gain
    first = jnp.mean(inner, -1, keepdims=True)
    second = jnp.mean(inner * unit, -1, keepdims=True)
    return scale * (inner - first - unit * second)


def own_and_got(tiles):
    part = tiles // 2
    return (
        lambda t, h: (t + (1 - h[0]) * part) % tiles,
        lambda t, h: jnp.minimum(t, part - 1),
        lambda t, h: jnp.maximum(t - part, 0),
    )


def row_specs(tile, width, tiles):
    where, got, own = own_and_got(tiles)
    return (
        pl.BlockSpec((tile, width), lambda t, h: (got(t, h), 0)),
        pl.BlockSpec((1, tile, width), lambda t, h: (h[0], own(t, h), 0)),
    )


def either(got_ref, own_ref):
    early = pl.program_id(0) < pl.num_programs(0) // 2
    return jnp.where(early, got_ref[...], own_ref[0])


def once(array):
    return pl.BlockSpec(array.shape, lambda t, *_: (0,) * array.ndim, pipeline_mode=pl.Buffered(1))


def kept(dims):
    return pl.BlockSpec(dims, lambda t, *_: (0,) * len(dims))


def largest_norms(block):
    lane = lax.broadcasted_iota(jnp.int32, (block.shape[1], 128), 1)
    column = lax.broadcasted_iota(jnp.int32, (block.shape[1], 128), 0)
    member = jnp.where(column // HD == lane, 1.0, 0.0).astype(BF)
    wide = block.astype(F32)
    return jnp.max(mm((wide * wide).astype(BF), member), 0, keepdims=True)


def project_kernel(place, x_ref, gain_ref, shift_ref, weight_ref, bias_ref, *refs):
    q_ref, k_ref, v_ref, norm_ref = refs[-4:]
    width = weight_ref.shape[0]
    unit, _ = norm_parts(x_ref[...].reshape(-1, width).astype(F32))
    normed = (unit * gain_ref[...] + shift_ref[...]).astype(BF)

    @pl.when(pl.program_id(0) == 0)
    def _():
        norm_ref[...] = jnp.zeros(norm_ref.shape, F32)

    for n, ref in enumerate((q_ref, k_ref, v_ref)):
        cols = slice(n * width, (n + 1) * width)
        out = (mm(normed, weight_ref[:, cols]) + bias_ref[:, cols]).astype(BF)
        ref[...] = out
        if n < 2:
            norm_ref[n : n + 1, :] = jnp.maximum(norm_ref[n : n + 1, :], largest_norms(out))


def project(own, half, x, gain, shift, weight, bias, before, tile):
    span, width = x.shape[-2:]
    count = span // tile
    length = 2 * span
    if own:
        x_spec = pl.BlockSpec((1, tile, width), lambda t, h: (h[0], t, 0))
        here = lambda h: h[0]
    else:
        x_spec = pl.BlockSpec((tile, width), lambda t, h: (t, 0))
        here = lambda h: 1 - h[0]
    rows = pl.BlockSpec((tile, width), lambda t, h: (here(h) * count + t, 0))
    nat = shape_of((length, width), BF)
    return pl.pallas_call(
        project_kernel,
        grid_spec=pltpu.PrefetchScalarGridSpec(
            num_scalar_prefetch=1,
            grid=(count,),
            in_specs=[x_spec, once(gain), once(shift), once(weight), once(bias)]
            + [pl.BlockSpec(memory_space=pl.ANY)] * len(before),
            out_specs=[rows, rows, rows, kept((8, 128))],
        ),
        out_shape=[nat, nat, nat, shape_of((8, 128), F32)],
        input_output_aliases={6 + i: i for i in range(len(before))},
        compiler_params=params(),
        name="project",
    )(half, x, gain, shift, weight, bias, *before)


def document_kernel(size, half_ref, own_ref, got_ref, start_ref, table_ref):
    span = own_ref.shape[1]
    place = lambda half: pl.ds(pl.multiple_of(half * span, span), span)
    start_ref[0:1, place(half_ref[0])] = own_ref[...]
    start_ref[0:1, place(1 - half_ref[0])] = got_ref[...]
    numbers = start_ref[...]
    start = jnp.zeros_like(numbers)
    for number in range(1, 8):
        before = jnp.sum((numbers < number).astype(jnp.int32), 1, keepdims=True)
        start = jnp.where(numbers == number, before, start)
    start_ref[...] = start
    count = start.shape[1] // size
    slots = table_ref.shape[0] - 1
    for slot in range(slots):
        table_ref[slot] = 0
    filled = jnp.int32(0)
    for i in range(count):
        block = start[:, i * size : (i + 1) * size]
        low, high = jnp.min(block), jnp.max(block)
        for j in range(i + 1):
            kind = jnp.where(high > j * size, 2, 1 if i == j else 0)
            active = low < (j + 1) * size

            table_ref[filled] = jnp.where(active, i + 256 * j + 65536 * kind, 0)
            filled = filled + active.astype(jnp.int32)
    table_ref[slots] = filled


def documents(half, own, got, size):
    length = 2 * own.shape[1]
    count = length // size
    row = lambda wide: pl.BlockSpec((1, wide), lambda t, h: (0, 0))
    return pl.pallas_call(
        functools.partial(document_kernel, size),
        grid_spec=pltpu.PrefetchScalarGridSpec(
            num_scalar_prefetch=1,
            grid=(1,),
            in_specs=[row(length // 2), row(length // 2)],
            out_specs=[row(length), pl.BlockSpec(memory_space=pltpu.SMEM)],
        ),
        out_shape=[
            shape_of((1, length), jnp.int32),
            shape_of((count * (count + 1) // 2 + 2,), jnp.int32),
        ],
        compiler_params=params(),
        name="documents",
    )(half, own, got)


def head_half(block, head):
    lane = lax.broadcasted_iota(jnp.int32, block.shape, 1)
    keep = (lane < HD) if head % 2 == 0 else (lane >= HD)
    return jnp.where(keep, block, jnp.zeros_like(block))


def lanes_of(heads, group, head):
    low = HD * heads * group + 2 * HD * (head // 2)
    return pl.ds(pl.multiple_of(low, 2 * HD), 2 * HD)


def rows_of(heads, group, head):
    return pl.ds(pl.multiple_of(HD * heads * group + HD * head, HD), HD)


class Blocks:
    def __init__(self, size, list_ref, start_ref, mask_ref, values):
        self.size, self.list = size, list_ref
        self.start, self.mask, self.values = start_ref, mask_ref, values

    def at(self, index):
        return pl.ds(pl.multiple_of(index * self.size, self.size), self.size)

    def places(self):
        dims = (self.size, self.size)
        return lax.broadcasted_iota(jnp.int32, dims, 0), lax.broadcasted_iota(jnp.int32, dims, 1)

    def fill(self, slot, i, j):
        key, query = self.places()
        key, query = key + j * self.size, query + i * self.size
        allowed = (key >= self.start[0:1, self.at(i)]) & (key <= query)
        self.mask[slot] = jnp.where(allowed, *self.values).astype(self.mask.dtype)

    def entry(self, step):
        packed = self.list[step]
        kind = packed // 65536
        return packed % 256, (packed // 256) % 256, jnp.where(kind == 2, 2 + lax.rem(step, 2), kind)

    def prepare(self, slot, i, j):
        pl.when(slot >= 2)(lambda: self.fill(slot, i, j))

    def walk(self, variants, heads, loops, early, late, row_begin, step_end, row_end):
        steps = self.list[self.list.shape[0] - 1]
        self.mask[0] = jnp.full(self.mask.shape[1:], self.values[0], self.mask.dtype)
        key, query = self.places()
        self.mask[1] = jnp.where(key <= query, *self.values).astype(self.mask.dtype)
        i, j, slot = self.entry(0)
        self.prepare(slot, i, j)
        row_begin(i)
        zero = jnp.int32(0)
        early(zero, 0, i, j, slot, False)

        def body(turn, carry):
            i, j, slot = carry
            group = lax.rem(turn, loops)
            last = group == loops - 1
            after = self.entry(turn // loops + 1)
            ni, nj, nslot = (jnp.where(last, new, old) for new, old in zip(after, carry))
            ngroup = jnp.where(last, 0, group + 1)
            pl.when(last)(lambda: self.prepare(nslot, ni, nj))
            pl.when(ni > i)(lambda: row_begin(ni))

            def work(corner, slot):
                for head in range(heads):
                    if head + 1 < heads:
                        early(group, head + 1, i, j, slot, corner)
                    else:
                        early(ngroup, 0, ni, nj, nslot, False)
                    late(group, head, i, j, corner)

            if variants == 1:
                work(False, slot)
            elif variants == 2:
                pl.when(i != j)(lambda: work(False, slot))
                pl.when(i == j)(lambda: work(True, slot))
            else:
                pl.when(slot == 0)(lambda: work(False, None))
                pl.when((slot > 0) & (i == j))(lambda: work(True, slot))
                pl.when((slot > 0) & (i != j))(lambda: work(False, slot))

            @pl.when(last)
            def _():
                step_end(i, j)
                pl.when(j == i)(lambda: row_end(i))

            return ni, nj, nslot

        lax.fori_loop(0, steps * loops, body, (i, j, slot))


def pieces(corner, size):
    if not corner:
        return [(slice(0, size), slice(0, size))]
    mid = size // 2
    return [(slice(0, mid), slice(0, size)), (slice(mid, size), slice(mid, size))]


def part_at(size, index, part):
    low = index * size + part.start
    return pl.ds(pl.multiple_of(low, size // 2), part.stop - part.start)


class Blockwise:
    def __init__(self, size, first, source, target, sems):
        self.size, self.first = size, first
        self.source, self.target, self.sems = source, target, sems

    def copy(self, block):
        rows = pl.ds(pl.multiple_of(block * self.size, self.size), self.size)
        lanes = pl.ds(self.first, self.target.shape[1])
        return pltpu.make_async_copy(
            self.source.at[rows, lanes], self.target.at[rows, :], self.sems.at[block]
        )


def forward_kernel(
    size, list_ref, small_ref, q_hbm, k_hbm, v_hbm, start_ref, out_hbm, lse_ref, q_ref, k_ref, v_ref,
    vt_ref, stage_ref, in_sems, out_sems, max_ref, new_ref, acc_ref, bias_ref, mask_ref, *slots,
):
    heads = FORWARD_HEADS
    loops = H // heads
    scores, probs_of = slots[:heads], slots[heads:]
    plain = Blocks(size, list_ref, start_ref, mask_ref, (1.0, 0.0))
    general = Blocks(size, list_ref, start_ref, bias_ref, (0.0, NEGATIVE))
    at = plain.at
    count = q_ref.shape[0] // size
    loads = [
        Blockwise(size, 0, source, target, in_sems.at[n])
        for n, (source, target) in enumerate(((k_hbm, k_ref), (q_hbm, q_ref), (v_hbm, v_ref)))
    ]
    for block in range(count):
        for load in loads:
            load.copy(block).start()

    def store(i):
        cols = pl.ds(pl.multiple_of(i * size, size), size)
        return pltpu.make_async_copy(stage_ref.at[:, cols], out_hbm.at[:, cols], out_sems.at[i])

    def row_begin(i):
        for load in loads:
            load.copy(i).wait()
        vt_ref[:, at(i)] = v_ref[at(i), :].T

    def products(group, head, i, j, keys, queries):
        lanes = lanes_of(heads, group, head)
        block = head_half(k_ref[part_at(size, j, keys), lanes], head)
        return mm(block, q_ref[part_at(size, i, queries), lanes], NT)

    def values(group, head, j, keys):
        block = vt_ref[rows_of(heads, group, head), part_at(size, j, keys)]
        return jnp.concatenate([block, jnp.ones((16, keys.stop - keys.start), BF)], 0)

    def early_plain(group, head, i, j, slot, corner):
        for keys, queries in pieces(corner, size):
            probs = jnp.exp2(products(group, head, i, j, keys, queries) * SCALE2).astype(BF)
            if slot is not None:
                probs = probs * mask_ref[slot, keys, queries]
            probs_of[head][keys, queries] = probs

    def late_plain(group, head, i, j, corner):
        for keys, queries in pieces(corner, size):
            acc_ref[heads * group + head, :, queries] += mm(values(group, head, j, keys), probs_of[head][keys, queries])

    whole = slice(0, size)

    def early(group, head, i, j, slot, corner):
        s = products(group, head, i, j, whole, whole)
        if slot is not None:
            s = s + bias_ref[slot]
        scores[head][...] = s
        new_ref[heads * group + head] = jnp.max(s, 0, keepdims=True)

    def late(group, head, i, j, corner):
        place = heads * group + head
        old = max_ref[place]
        new = jnp.maximum(old, new_ref[place])
        max_ref[place] = new
        probs = jnp.exp2(scores[head][...] * SCALE2 - new * SCALE2)
        factor = jnp.exp2((old - new) * SCALE2)
        acc_ref[place] = acc_ref[place] * factor + mm(
            values(group, head, j, whole), probs.astype(BF)
        )

    def reset(largest):
        max_ref[...] = jnp.full(max_ref.shape, largest, F32)
        acc_ref[...] = jnp.zeros(acc_ref.shape, F32)

    def row_end(largest, i):
        def one(head, carry):
            total = acc_ref[head, HD : HD + 1, :]
            rows = pl.ds(pl.multiple_of(HD * head, HD), HD)
            stage_ref[rows, at(i)] = (acc_ref[head, :HD, :] * (1.0 / total)).astype(BF)
            lse_ref[head, :, at(i)] = max_ref[head] * SCALE2 + jnp.log2(total)
            return carry

        lax.fori_loop(0, H, one, 0)
        store(i).start()
        reset(largest)

    def run(variants, blocks, largest, early, late):
        reset(largest)
        blocks.walk(
            variants, heads, loops, early, late, row_begin, lambda i, j: None, functools.partial(row_end, largest)
        )

    pl.when(small_ref[0] == 1)(lambda: run(2, plain, 0.0, early_plain, late_plain))
    pl.when(small_ref[0] != 1)(lambda: run(1, general, NEGATIVE, early, late))
    for i in range(count):
        store(i).wait()


def attend(table, small, q, k, v, start, size):
    length, width = q.shape
    count = length // size
    far = pl.BlockSpec(memory_space=pl.ANY)
    near = pltpu.VMEM((length, width), BF)
    return pl.pallas_call(
        functools.partial(forward_kernel, size),
        grid_spec=pltpu.PrefetchScalarGridSpec(
            num_scalar_prefetch=2,
            grid=(1,),
            in_specs=[far, far, far, once(start)],
            out_specs=[far, kept((H, 1, length))],
            scratch_shapes=[
                near,
                near,
                near,
                pltpu.VMEM((width, length), BF),
                pltpu.VMEM((width, length), BF),
                pltpu.SemaphoreType.DMA((3, count)),
                pltpu.SemaphoreType.DMA((count,)),
                pltpu.VMEM((H, 1, size), F32),
                pltpu.VMEM((H, 1, size), F32),
                pltpu.VMEM((H, HD + 16, size), F32),
                pltpu.VMEM((4, size, size), F32),
                pltpu.VMEM((4, size, size), BF),
            ]
            + [pltpu.VMEM((size, size), F32)] * FORWARD_HEADS
            + [pltpu.VMEM((size, size), BF)] * FORWARD_HEADS,
        ),
        out_shape=[shape_of((width, length), BF), shape_of((H, 1, length), F32)],
        compiler_params=params(),
        name="attend",
    )(table, small, q, k, v, start)


def backward_kernel(
    size, heads, loops, first, list_ref, q_hbm, k_hbm, v_hbm, do_hbm, start_ref, lse_ref, delta_ref,
    dq_hbm, dk_hbm, dv_hbm, q_ref, k_ref, v_ref, do_ref, kt_ref, dq_ref, dk_ref, dv_ref, in_sems,
    out_sems, dqt_acc, dk_acc, dv_acc, bias_ref, *slots,
):
    probs_of, grads_of = slots[:heads], slots[heads:]
    walk = Blocks(size, list_ref, start_ref, bias_ref, (0.0, NEGATIVE))
    at = walk.at
    count = q_ref.shape[0] // size
    pairs = ((k_hbm, k_ref), (q_hbm, q_ref), (v_hbm, v_ref), (do_hbm, do_ref))
    loads = [
        Blockwise(size, first * HD, source, target, in_sems.at[n])
        for n, (source, target) in enumerate(pairs)
    ]
    for block in range(count):
        for load in loads:
            load.copy(block).start()

    def store(n, block):
        source, target = ((dq_ref, dq_hbm), (dk_ref, dk_hbm), (dv_ref, dv_hbm))[n]
        rows = at(block)
        return pltpu.make_async_copy(
            source.at[rows, :], target.at[rows, :], out_sems.at[n, block]
        )

    def row_begin(i):
        for load in loads:
            load.copy(i).wait()
        kt_ref[:, at(i)] = k_ref[at(i), :].T
        dk_acc[at(i), :] = jnp.zeros((size, dk_acc.shape[1]), F32)
        dv_acc[at(i), :] = jnp.zeros((size, dv_acc.shape[1]), F32)

    def early(group, head, i, j, slot, corner):
        lanes = lanes_of(heads, group, head)
        for keys, queries in pieces(corner, size):
            at_j, at_i = part_at(size, j, keys), part_at(size, i, queries)
            stat = (first + heads * group + head, slice(None), at_i)
            s = mm(head_half(k_ref[at_j, lanes], head), q_ref[at_i, lanes], NT)
            dots = mm(head_half(v_ref[at_j, lanes], head), do_ref[at_i, lanes], NT)
            if slot is not None:
                s = s + bias_ref[slot, keys, queries]
            probs = jnp.exp2(s * SCALE2 - lse_ref[stat])
            probs_of[head][keys, queries] = probs.astype(BF)
            grads_of[head][keys, queries] = (probs * (dots - delta_ref[stat])).astype(BF)

    def late(group, head, i, j, corner):
        lanes = lanes_of(heads, group, head)
        rows = rows_of(heads, group, head)
        for keys, queries in pieces(corner, size):
            at_j, at_i = part_at(size, j, keys), part_at(size, i, queries)
            grads = grads_of[head][keys, queries]
            dv_acc[at_j, lanes] += mm(
                probs_of[head][keys, queries], head_half(do_ref[at_i, lanes], head)
            )
            dk_acc[at_j, lanes] += mm(grads, head_half(q_ref[at_i, lanes], head))
            dqt_acc[rows, queries] += mm(kt_ref[rows, at_j], grads)

    def finish(j):
        dk_ref[at(j), :] = (dk_acc[at(j), :] * SCALE).astype(BF)
        dv_ref[at(j), :] = dv_acc[at(j), :].astype(BF)
        store(1, j).start()
        store(2, j).start()

    def step_end(i, j):
        pl.when(i == count - 1)(lambda: finish(j))

    def row_end(i):
        dq_ref[at(i), :] = (dqt_acc[...] * SCALE).T.astype(BF)
        store(0, i).start()
        dqt_acc[...] = jnp.zeros(dqt_acc.shape, F32)

    dqt_acc[...] = jnp.zeros(dqt_acc.shape, F32)
    walk.walk(3, heads, loops, early, late, row_begin, step_end, row_end)
    lowest = jnp.int32(count)
    for slot in range(list_ref.shape[0] - 1):
        lowest = lowest - jnp.where(list_ref[slot] % 256 == count - 1, 1, 0)
    for j in range(count):
        pl.when(j < lowest)(functools.partial(finish, j))
    for j in range(count):
        for n in range(3):
            store(n, j).wait()


def attend_back(first, groups, table, q, k, v, do, start, lse, delta, size):
    length = q.shape[0]
    part = HD * groups
    count = length // size
    far = pl.BlockSpec(memory_space=pl.ANY)
    near = pltpu.VMEM((length, part), BF)
    pairs = count * (count + 1) // 2 * size * size * groups
    return pl.pallas_call(
        functools.partial(backward_kernel, size, BACKWARD_HEADS, groups // BACKWARD_HEADS, first),
        cost_estimate=SHORT,
        grid_spec=pltpu.PrefetchScalarGridSpec(
            num_scalar_prefetch=1,
            grid=(1,),
            in_specs=[far] * 4 + [once(start), once(lse), once(delta)],
            out_specs=[far] * 3,
            scratch_shapes=[near] * 4
            + [pltpu.VMEM((part, length), BF)]
            + [near] * 3
            + [
                pltpu.SemaphoreType.DMA((4, count)),
                pltpu.SemaphoreType.DMA((3, count)),
                pltpu.VMEM((part, size), F32),
                pltpu.VMEM((length, part), F32),
                pltpu.VMEM((length, part), F32),
                pltpu.VMEM((4, size, size), F32),
            ]
            + [pltpu.VMEM((size, size), BF)] * (2 * BACKWARD_HEADS),
        ),
        out_shape=[shape_of((length, part), BF)] * 3,
        compiler_params=params(),
        name="attend_back",
    )(table, q, k, v, do, start, lse, delta)


def feed_kernel(
    chunk, place_ref, att_ref, x_got, x_own, cot_got, cot_own, wo_ref, ob_ref, g2_ref, s2_ref, we_ref,
    eb_ref, wr_ref, hid_ref, exg_ref, keep_ref, send_ref, deb_ref, acc_ref, deb_acc, wet_ref, ebt_ref,
):
    step = pl.program_id(0)
    tile, width = x_got.shape
    total = wr_ref.shape[0]

    @pl.when(step == 0)
    def _():
        for ref in (acc_ref, deb_acc):
            ref[...] = jnp.zeros(ref.shape, F32)
        wet_ref[...] = we_ref[...].T
        ebt_ref[...] = jnp.broadcast_to(eb_ref[...], (128, total)).T

    mixed = mm(att_ref[...].T, wo_ref[...]) + ob_ref[...]
    middle = either(x_got, x_own).astype(F32) + BRANCH * mixed
    unit, _ = norm_parts(middle)
    second = (unit * g2_ref[...] + s2_ref[...]).astype(BF)
    second_t = second.T
    reduced_grad = (BRANCH * either(cot_got, cot_own).astype(F32)).astype(BF)

    def stage_one(c):
        rows = slice(c * chunk, (c + 1) * chunk)
        bias = jnp.concatenate([ebt_ref[rows, :]] * (tile // 128), 1)
        v = mm(wet_ref[rows, :], second, NT) + bias
        v2 = v * v
        t = jnp.tanh(v * (GELU_A + GELU_B * v2))
        h1 = 0.5 * t + 0.5
        gelu = v * h1
        slope = h1 + gelu * (1.0 - h1) * (2.0 * GELU_A + 6.0 * GELU_B * v2)
        hid_ref[rows, :] = gelu.astype(BF)
        grads = (mm(wr_ref[rows, :], reduced_grad, NT) * slope).astype(BF)
        exg_ref[rows, :] = grads
        wide = grads.astype(F32)
        part = wide[:, 0:128]
        for n in range(1, tile // 128):
            part = part + wide[:, n * 128 : (n + 1) * 128]
        deb_acc[rows, :] += part

    stage_one(0)
    for c in range(total // chunk):
        if (c + 1) * chunk < total:
            stage_one(c + 1)
        rows = slice(c * chunk, (c + 1) * chunk)
        acc_ref[rows, :] += mm(hid_ref[rows, :], reduced_grad)
        block, low = divmod(c * chunk, width)
        there = slice(total + block * width, total + (block + 1) * width)
        acc_ref[there, low : low + chunk] += mm(second_t, exg_ref[rows, :], NT)

    last = step == pl.num_programs(0) - 1
    halves = slice(0, total), slice(total, 2 * total)
    for core in range(2):

        @pl.when(last & (place_ref[1] == core))
        def _():
            keep_ref[...] = acc_ref[halves[core], :].astype(BF)
            send_ref[...] = acc_ref[halves[1 - core], :].astype(BF)

    @pl.when(last)
    def _():
        flat = jnp.sum(deb_acc[...].T, 0, keepdims=True)
        deb_ref[...] = jnp.zeros(deb_ref.shape, F32)
        for n in range(total // width):
            deb_ref[n : n + 1, :] = flat[:, n * width : (n + 1) * width]


def feed_part(place, att_t, x_got, x_own, cot_got, cot_own, wo, ob, g2, s2, we, eb, wr, tile, chunk):
    width, length = att_t.shape
    total = wr.shape[0]
    tiles = length // tile
    where, _, _ = own_and_got(tiles)
    pair = list(row_specs(tile, width, tiles))
    cols = lambda high: pl.BlockSpec((high, tile), lambda t, h: (0, where(t, h)))
    return pl.pallas_call(
        functools.partial(feed_kernel, chunk),
        grid_spec=pltpu.PrefetchScalarGridSpec(
            num_scalar_prefetch=1,
            grid=(tiles,),
            in_specs=[cols(width)] + pair * 2 + [once(a) for a in (wo, ob, g2, s2, we, eb, wr)],
            out_specs=[cols(total), cols(total), kept((total, width)), kept((total, width)), kept((8, width))],
            scratch_shapes=[
                pltpu.VMEM((2 * total, width), F32),
                pltpu.VMEM((total, 128), F32),
                pltpu.VMEM((total, width), BF),
                pltpu.VMEM((total, 128), F32),
            ],
        ),
        out_shape=[
            shape_of((total, length), BF),
            shape_of((total, length), BF),
            shape_of((total, width), BF),
            shape_of((total, width), BF),
            shape_of((8, width), F32),
        ],
        compiler_params=params(),
        name="feed",
    )(place, att_t, x_got, x_own, cot_got, cot_own, wo, ob, g2, s2, we, eb, wr)


def middle_kernel(
    place_ref, att_ref, x_got, x_own, cot_got, cot_own, hid_ref, exg_ref, wo_ref, ob_ref, g2_ref,
    we_ref, wr_ref, rb_ref, res_own, res_send, grad_ref, ag_ref, delta_ref, dwo_ref, vec_ref, acc_ref,
    wrt_ref,
):
    step = pl.program_id(0)
    tiles = pl.num_programs(0)

    @pl.when(step == 0)
    def _():
        for ref in (acc_ref, vec_ref):
            ref[...] = jnp.zeros(ref.shape, F32)
        wrt_ref[...] = wr_ref[...].T

    att_t = att_ref[...]
    mixed = mm(att_t.T, wo_ref[...]) + ob_ref[...]
    middle = either(x_got, x_own).astype(F32) + BRANCH * mixed
    cot = either(cot_got, cot_own).astype(F32)
    unit, scale = norm_parts(middle)
    norm_grad = mm(we_ref[...], exg_ref[...]).T
    result = (middle + BRANCH * (mm(wrt_ref[...], hid_ref[...]).T + rb_ref[...])).astype(BF)

    @pl.when(step < tiles // 2)
    def _():
        res_send[...] = result

    @pl.when(step >= tiles // 2)
    def _():
        res_own[0] = result

    middle_grad = cot + norm_back(norm_grad, unit, scale, g2_ref[...])
    grad_ref[...] = middle_grad
    mixed_grad = (BRANCH * middle_grad).astype(BF)
    acc_ref[...] += mm(att_t, mixed_grad)
    att_grad = mm(mixed_grad, wo_ref[...], NT).astype(BF)
    ag_ref[...] = att_grad
    dots = att_grad.T.astype(F32) * att_t.astype(F32)
    for head in range(H):
        delta_ref[head] = jnp.sum(dots[HD * head : HD * head + HD, :], 0, keepdims=True)
    reduced_grad = (BRANCH * cot).astype(BF)
    sums = (norm_grad * unit, norm_grad, mixed_grad.astype(F32), reduced_grad.astype(F32))
    for n, value in enumerate(sums):
        vec_ref[n : n + 1, :] += jnp.sum(value, 0, keepdims=True)

    @pl.when(step == tiles - 1)
    def _():
        dwo_ref[...] = acc_ref[...].astype(BF)


def middle_part(place, att_t, x_got, x_own, cot_got, cot_own, hid, exg, wo, ob, g2, we, wr, rb, tile):
    width, length = att_t.shape
    total = wr.shape[0]
    tiles = length // tile
    where, got, own = own_and_got(tiles)
    pair = list(row_specs(tile, width, tiles))
    rows = pl.BlockSpec((tile, width), lambda t, h: (where(t, h), 0))
    cols = lambda high: pl.BlockSpec((high, tile), lambda t, h: (0, where(t, h)))
    return pl.pallas_call(
        middle_kernel,
        cost_estimate=SHORT,
        grid_spec=pltpu.PrefetchScalarGridSpec(
            num_scalar_prefetch=1,
            grid=(tiles,),
            in_specs=[cols(width)]
            + pair * 2
            + [cols(total), cols(total)]
            + [once(a) for a in (wo, ob, g2, we, wr, rb)],
            out_specs=[
                pair[1],
                pair[0],
                rows,
                rows,
                pl.BlockSpec((H, 1, tile), lambda t, h: (0, 0, where(t, h))),
                kept((width, width)),
                kept((8, width)),
            ],
            scratch_shapes=[pltpu.VMEM((width, width), F32), pltpu.VMEM((width, total), BF)],
        ),
        out_shape=[
            shape_of((2, length // 2, width), BF),
            shape_of((length // 2, width), BF),
            shape_of((length, width), F32),
            shape_of((length, width), BF),
            shape_of((H, 1, length), F32),
            shape_of((width, width), BF),
            shape_of((8, width), F32),
        ],
        compiler_params=params(),
        name="middle",
    )(place, att_t, x_got, x_own, cot_got, cot_own, hid, exg, wo, ob, g2, we, wr, rb)


def weight_kernel(parts, place_ref, *refs):
    ins = refs[: 3 * parts]
    x_got, x_own, gain_ref, shift_ref, extra_ref, keep_ref, send_ref, acc_ref = refs[3 * parts :]
    step = pl.program_id(0)

    @pl.when(step == 0)
    def _():
        acc_ref[...] = jnp.zeros(acc_ref.shape, F32)

    width = x_got.shape[1]
    unit, _ = norm_parts(either(x_got, x_own).astype(F32))
    normed_t = (unit * gain_ref[...] + shift_ref[...]).astype(BF).T
    for n in range(3):
        grad = jnp.concatenate([ref[...] for ref in ins[n * parts : (n + 1) * parts]], 1)
        acc_ref[n * width : (n + 1) * width, :] += mm(normed_t, grad)

    last = step == pl.num_programs(0) - 1
    for core in range(2):

        @pl.when(last & (place_ref[1] == core))
        def _():
            lower, upper = (keep_ref, send_ref) if core == 0 else (send_ref, keep_ref)
            lower[...] = acc_ref[: 2 * width, :].astype(BF)
            upper[:width, :] = acc_ref[2 * width :, :].astype(BF)
            upper[width:, :] = extra_ref[...]


def weight_part(place, grads, x_got, x_own, gain, shift, extra, tile):
    span, width = x_got.shape
    tiles = 2 * span // tile
    where, _, _ = own_and_got(tiles)
    flat = [part for group in grads for part in group]
    out = shape_of((2 * width, width), BF)
    return pl.pallas_call(
        functools.partial(weight_kernel, len(grads[0])),
        cost_estimate=SHORT,
        grid_spec=pltpu.PrefetchScalarGridSpec(
            num_scalar_prefetch=1,
            grid=(tiles,),
            in_specs=[
                pl.BlockSpec((tile, a.shape[1]), lambda t, h: (where(t, h), 0)) for a in flat
            ]
            + list(row_specs(tile, width, tiles))
            + [once(a) for a in (gain, shift, extra)],
            out_specs=[kept(out.shape)] * 2,
            scratch_shapes=[pltpu.VMEM((3 * width, width), F32)],
        ),
        out_shape=[out, out],
        compiler_params=params(),
        name="weight",
    )(place, *flat, x_got, x_own, gain, shift, extra)


def last_kernel(parts, place_ref, *refs):
    ins, rest = refs[: 3 * parts], refs[3 * parts :]
    x_got, x_own, mid_ref, gain_ref, weight_ref, own_ref, send_ref, vec_ref = rest
    step = pl.program_id(0)
    tiles = pl.num_programs(0)

    @pl.when(step == 0)
    def _():
        vec_ref[...] = jnp.zeros(vec_ref.shape, F32)

    width = x_got.shape[1]
    unit, scale = norm_parts(either(x_got, x_own).astype(F32))
    back = None
    grads = []
    for n in range(3):
        grad = jnp.concatenate([ref[...] for ref in ins[n * parts : (n + 1) * parts]], 1)
        one = mm(grad, weight_ref[:, n * width : (n + 1) * width], NT)
        back = one if back is None else back + one
        grads.append(grad)
    total = mid_ref[...] + norm_back(back, unit, scale, gain_ref[...])

    @pl.when(step < tiles // 2)
    def _():
        send_ref[...] = total.astype(BF)

    @pl.when(step >= tiles // 2)
    def _():
        own_ref[0] = total

    sums = (back * unit, back, grads[0].astype(F32), grads[2].astype(F32))
    for n, value in enumerate(sums):
        vec_ref[n : n + 1, :] += jnp.sum(value, 0, keepdims=True)


def last_part(place, grads, x_got, x_own, mid, gain, weight, tile):
    length, width = mid.shape
    tiles = length // tile
    where, _, _ = own_and_got(tiles)
    rows = pl.BlockSpec((tile, width), lambda t, h: (where(t, h), 0))
    flat = [part for group in grads for part in group]
    pair = list(row_specs(tile, width, tiles))
    return pl.pallas_call(
        functools.partial(last_kernel, len(grads[0])),
        cost_estimate=SHORT,
        grid_spec=pltpu.PrefetchScalarGridSpec(
            num_scalar_prefetch=1,
            grid=(tiles,),
            in_specs=[
                pl.BlockSpec((tile, a.shape[1]), lambda t, h: (where(t, h), 0)) for a in flat
            ]
            + pair
            + [rows, once(gain), once(weight)],
            out_specs=[pair[1], pair[0], kept((8, width))],
        ),
        out_shape=[
            shape_of((2, length // 2, width), F32),
            shape_of((length // 2, width), BF),
            shape_of((8, width), F32),
        ],
        compiler_params=params(),
        name="last",
    )(place, *flat, x_got, x_own, mid, gain, weight)


def swapped(value):
    return lax.ppermute(value, "seq", [(0, 1), (1, 0)])


def side(hop):
    axis, bit = hop
    return (lax.axis_index(axis) // bit) % 2


def place_of(hops):
    place = 0
    for hop in hops:
        place = 2 * place + side(hop)
    return place


def exchanged(value, hops):
    axes = tuple(dict.fromkeys(axis for axis, _ in hops))
    flips = [sum(bit for axis, bit in hops if axis == name) for name in axes]
    sizes = [lax.axis_size(name) for name in axes]
    if len(axes) == 1:
        return lax.ppermute(value, axes[0], [(i, i ^ flips[0]) for i in range(sizes[0])])
    pairs = [
        (i * sizes[1] + j, (i ^ flips[0]) * sizes[1] + (j ^ flips[1]))
        for i in range(sizes[0])
        for j in range(sizes[1])
    ]
    return lax.ppermute(value, axes, pairs)


def partners(hops):
    count = len(hops)
    return [
        ([hop for n, hop in enumerate(hops) if (flip >> (count - 1 - n)) & 1], flip)
        for flip in range(1, 1 << count)
    ]


def added(*values):
    total = values[0].astype(F32)
    for value in values[1:]:
        total = total + value.astype(F32)
    return total.astype(BF)


def scatter(part, hops):
    rows = part.shape[1] >> len(hops)
    mine = place_of(hops)
    piece = lambda place: lax.dynamic_slice_in_dim(part, place * rows, rows, 1)
    got = [exchanged(piece(mine ^ flip), chosen) for chosen, flip in partners(hops)]
    return added(piece(mine), *got)


def gather(part, hops, whole=None):
    mine = place_of(hops)
    blocks, rows, width = part.shape
    got, others = [(part, mine)], []
    for chosen, flip in partners(hops):
        if whole is None:
            got.append((exchanged(part, chosen), mine ^ flip))
            continue
        both = exchanged(jnp.concatenate([part.reshape(-1, width), whole], 0), chosen)
        got.append((both[: blocks * rows].reshape(part.shape), mine ^ flip))
        others.append(both[blocks * rows :])
    if len(hops) == 1:
        one, two = got[0][0], got[1][0]
        out = jnp.where(mine == 0, jnp.concatenate([one, two], 1), jnp.concatenate([two, one], 1))
    else:
        out = jnp.zeros((blocks, rows << len(hops), width), part.dtype)
        for piece, place in got:
            out = lax.dynamic_update_slice_in_dim(out, piece, place * rows, 1)
    return out if whole is None else (out, added(whole, *others))


def hops():
    found = []
    for axis in ("dp", "seq"):
        size = lax.axis_size(axis)
        found.append([(axis, 1 << n) for n in range(size.bit_length() - 1)])
    core, one, two, far = found[0]
    return [core], [one, two], [far], found[1]


class AllSum:
    def __init__(self, keep, send, core):
        self.core, self.whole = core, None
        self.state = (keep[None], send[None])

    def split(self):
        keep, send = self.state
        self.state = added(keep, exchanged(send, self.core))

    def cross(self, one, two):
        if not isinstance(self.state, tuple):
            mid = self.state.shape[1] // 2
            self.state = (self.state[:, :mid], self.state[:, mid:])
        self.state = tuple(scatter(part, hops) for part, hops in zip(self.state, (one, two)))

    def uncross(self, one, two):
        if not isinstance(self.state, tuple):
            self.state = (self.state[:1], self.state[1:])
        self.state = tuple(gather(part, hops) for part, hops in zip(self.state, (one, two)))

    def join(self):
        self.state = gather(jnp.concatenate(self.state, 1), self.core)

    def ride(self, whole, hops):
        self.whole = added(whole, exchanged(whole, hops))

    def narrow(self, hops):
        if isinstance(self.state, tuple):
            self.state = jnp.concatenate(self.state, 0)
        self.state = scatter(self.state, hops)

    def meet(self, hops):
        self.state = added(self.state, exchanged(self.state, hops))

    def widen(self, hops):
        if self.whole is None:
            self.state = gather(self.state, hops)
        else:
            self.state, self.whole = gather(self.state, hops, self.whole)

    def beside(self, call, argument, step, *hops):
        argument = after(argument, self.state)
        step(*hops)
        out = call(argument)
        self.state = after(self.state, out)
        return out


def after(value, earlier):
    return lax.optimization_barrier((value, earlier))[0]


def passed_along(block, axis, distance):
    devices = range(lax.axis_size(axis))
    route = [(i - distance, i) for i in devices if i - distance in devices]
    return lax.ppermute(block, axis, route)


def from_behind(value, axis, steps):
    count = lax.axis_size(axis)
    pairs = [(source, (source + steps) % count) for source in range(count)]
    return lax.ppermute(value, axis, pairs)


def layer_norm(values, gain_vec, shift_vec):
    center = jnp.mean(values, -1, keepdims=True)
    centered = values - center
    variance = jnp.mean(centered * centered, -1, keepdims=True)
    return centered * lax.rsqrt(variance + EPSILON) * gain_vec + shift_vec


def gelu_tanh(values):
    return jax.nn.gelu(values, approximate=True)


def plain_dot(left, right):
    return jnp.dot(left, right, preferred_element_type=jnp.float32)


def left_dot(left, right):
    return lax.dot_general(
        left, right, (((0,), (0,)), ((), ())), preferred_element_type=jnp.float32
    )


def right_dot(left, right):
    return lax.dot_general(
        left, right, (((1,), (1,)), ((), ())), preferred_element_type=jnp.float32
    )


def block_scores(queries, keys_block, query_seg, key_seg, query_places, key_start):
    row_count, key_len, width = keys_block.shape
    keys_heads = keys_block.reshape(row_count, key_len, H, HD)
    scores = jnp.einsum(
        "rqhd,rkhd->rhqk", queries, keys_heads, preferred_element_type=jnp.float32
    ) * HD ** (-0.5)
    key_places = key_start + jnp.arange(key_len, dtype=jnp.int32)
    allowed = (query_seg[:, None, :, None] == key_seg[:, None, None, :]) & (
        key_places[None, None, None, :] <= query_places[None, None, :, None]
    )
    return (scores, allowed)


def attend_block(state, queries, block, query_seg, query_places, key_start):
    run_max, run_sum, running = state
    keys_block, values_block, key_seg = block
    row_count, key_len, width = values_block.shape
    query_len = queries.shape[1]
    scores, allowed = block_scores(queries, keys_block, query_seg, key_seg, query_places, key_start)
    block_max = jnp.max(jnp.where(allowed, scores, NEGATIVE), -1)
    new_max = jnp.maximum(run_max, block_max)
    exponent = jnp.where(allowed, jnp.exp(scores - new_max[..., None]), 0.0)
    factor = jnp.exp(run_max - new_max)
    new_sum = run_sum * factor + jnp.sum(exponent, -1)
    values_heads = values_block.reshape(row_count, key_len, H, HD)
    addition = jnp.einsum(
        "rhqk,rkhd->rqhd",
        exponent.astype(jnp.bfloat16),
        values_heads,
        preferred_element_type=jnp.float32,
    )
    scaled = (
        running.reshape(row_count, query_len, H, HD) * jnp.transpose(factor, (0, 2, 1))[..., None]
    )
    return (new_max, new_sum, (scaled + addition).reshape(row_count, query_len, width))


def grad_block(queries, out_grad, log_sum, delta, block, query_seg, query_places, key_start):
    keys_block, values_block, key_seg = block
    row_count, key_len, width = keys_block.shape
    scores, allowed = block_scores(queries, keys_block, query_seg, key_seg, query_places, key_start)
    weights_block = jnp.where(allowed, jnp.exp(scores - log_sum[..., None]), 0.0)
    keys_heads = keys_block.reshape(row_count, key_len, H, HD)
    values_heads = values_block.reshape(row_count, key_len, H, HD)
    value_dots = jnp.einsum(
        "rqhd,rkhd->rhqk", out_grad, values_heads, preferred_element_type=jnp.float32
    )
    score_grad = (weights_block * (value_dots - delta[..., None]) * HD ** (-0.5)).astype(
        jnp.bfloat16
    )
    query_part = jnp.einsum(
        "rhqk,rkhd->rqhd", score_grad, keys_heads, preferred_element_type=jnp.float32
    ).reshape(row_count, -1, width)
    key_part = jnp.einsum(
        "rhqk,rqhd->rkhd", score_grad, queries, preferred_element_type=jnp.float32
    ).reshape(row_count, key_len, width)
    value_part = jnp.einsum(
        "rhqk,rqhd->rkhd",
        weights_block.astype(jnp.bfloat16),
        out_grad,
        preferred_element_type=jnp.float32,
    ).reshape(row_count, key_len, width)
    return (query_part, key_part, value_part)


def local(
    activations,
    segments,
    first_gain,
    first_shift,
    input_weight,
    query_bias,
    value_bias,
    output_weight,
    output_bias,
    second_gain,
    second_shift,
    expand_weight,
    expand_bias,
    reduce_weight,
    reduce_bias,
    cotangent,
):
    row_total, span_len, width = activations.shape
    cycle_size = lax.axis_size("seq")
    position = lax.axis_index("seq")
    micro_rows = row_total // MICRO
    branch = DEPTH ** (-0.5)
    bias_all = jnp.concatenate([query_bias, jnp.zeros_like(query_bias), value_bias])
    query_places = position * span_len + jnp.arange(span_len, dtype=jnp.int32)
    totals = [
        jnp.zeros(argument.shape, jnp.float32)
        for argument in (
            first_gain,
            first_shift,
            input_weight,
            query_bias,
            value_bias,
            output_weight,
            output_bias,
            second_gain,
            second_shift,
            expand_weight,
            expand_bias,
            reduce_weight,
            reduce_bias,
        )
    ]
    outputs_list = []
    grads_list = []
    for micro in range(MICRO):
        lower = micro * micro_rows
        values_in = activations[lower : lower + micro_rows].astype(jnp.float32)
        query_seg = segments[lower : lower + micro_rows]
        out_cot = cotangent[lower : lower + micro_rows].astype(jnp.float32)
        normed, first_pull = jax.vjp(layer_norm, values_in, first_gain, first_shift)
        normed_low = normed.astype(jnp.bfloat16).reshape(-1, width)
        projected = (plain_dot(normed_low, input_weight) + bias_all).astype(jnp.bfloat16)
        queries = projected[:, :width].reshape(micro_rows, span_len, H, HD)
        keys_own = projected[:, width : 2 * width].reshape(micro_rows, span_len, width)
        values_own = projected[:, 2 * width :].reshape(micro_rows, span_len, width)
        own_block = (keys_own, values_own, query_seg)
        start_state = (
            jnp.full((micro_rows, H, span_len), NEGATIVE, jnp.float32),
            jnp.zeros((micro_rows, H, span_len), jnp.float32),
            jnp.zeros((micro_rows, span_len, width), jnp.float32),
        )
        state = attend_block(
            start_state, queries, own_block, query_seg, query_places, position * span_len
        )

        def cycle_forward(step_index, carry):
            block, inner_state = carry
            block = passed_along((block[0], block[1], block[2]), "seq", 1)
            source = (position - step_index) % cycle_size
            inner_state = lax.cond(
                source < position,
                lambda current: attend_block(
                    current, queries, block, query_seg, query_places, source * span_len
                ),
                lambda current: current,
                inner_state,
            )
            return (block, inner_state)

        unused_block, state = lax.fori_loop(1, cycle_size, cycle_forward, (own_block, state))
        run_max, run_sum, running = state
        attended = (
            running.reshape(micro_rows, span_len, H, HD)
            / jnp.transpose(run_sum, (0, 2, 1))[..., None]
        ).reshape(micro_rows, span_len, width)
        log_sum = run_max + jnp.log(run_sum)
        attended_low = attended.astype(jnp.bfloat16).reshape(-1, width)
        mixed_out = plain_dot(attended_low, output_weight) + output_bias
        middle = values_in + branch * mixed_out.reshape(values_in.shape)
        second_norm, second_pull = jax.vjp(layer_norm, middle, second_gain, second_shift)
        second_low = second_norm.astype(jnp.bfloat16).reshape(-1, width)
        expanded = plain_dot(second_low, expand_weight) + expand_bias
        hidden, gelu_pull = jax.vjp(gelu_tanh, expanded)
        hidden_low = hidden.astype(jnp.bfloat16)
        reduced = plain_dot(hidden_low, reduce_weight) + reduce_bias
        outputs_list.append(
            (middle + branch * reduced.reshape(values_in.shape)).astype(jnp.bfloat16)
        )
        reduced_grad = (branch * out_cot).reshape(-1, width).astype(jnp.bfloat16)
        totals[12] = totals[12] + jnp.sum(reduced_grad.astype(jnp.float32), 0)
        totals[11] = totals[11] + left_dot(hidden_low, reduced_grad)
        (expanded_grad,) = gelu_pull(right_dot(reduced_grad, reduce_weight))
        expanded_low = expanded_grad.astype(jnp.bfloat16)
        totals[10] = totals[10] + jnp.sum(expanded_low.astype(jnp.float32), 0)
        totals[9] = totals[9] + left_dot(second_low, expanded_low)
        norm_in_grad = right_dot(expanded_low, expand_weight).reshape(values_in.shape)
        middle_part, gain_part, shift_part = second_pull(norm_in_grad)
        totals[7] = totals[7] + gain_part
        totals[8] = totals[8] + shift_part
        middle_grad = out_cot + middle_part
        mixed_grad = (branch * middle_grad).reshape(-1, width).astype(jnp.bfloat16)
        totals[6] = totals[6] + jnp.sum(mixed_grad.astype(jnp.float32), 0)
        totals[5] = totals[5] + left_dot(attended_low, mixed_grad)
        attended_grad = (
            right_dot(mixed_grad, output_weight)
            .astype(jnp.bfloat16)
            .reshape(micro_rows, span_len, H, HD)
        )
        delta = jnp.transpose(
            jnp.sum(
                attended_grad.astype(jnp.float32) * attended.reshape(micro_rows, span_len, H, HD),
                -1,
            ),
            (0, 2, 1),
        )
        query_grad, key_grad, value_grad = grad_block(
            queries,
            attended_grad,
            log_sum,
            delta,
            own_block,
            query_seg,
            query_places,
            position * span_len,
        )

        def cycle_backward(step_index, carry):
            block, partial_value, query_acc = carry
            block = passed_along((block[0], block[1], block[2]), "seq", 1)
            partial_value = (
                from_behind(partial_value[0].astype(jnp.bfloat16), "seq", 1).astype(jnp.float32),
                from_behind(partial_value[1].astype(jnp.bfloat16), "seq", 1).astype(jnp.float32),
            )
            source = (position - step_index) % cycle_size

            def work(current):
                partial_in, query_in = current
                query_part, key_part, value_part = grad_block(
                    queries,
                    attended_grad,
                    log_sum,
                    delta,
                    block,
                    query_seg,
                    query_places,
                    source * span_len,
                )
                return (
                    (partial_in[0] + key_part, partial_in[1] + value_part),
                    query_in + query_part,
                )

            partial_value, query_acc = lax.cond(
                source < position, work, lambda current: current, (partial_value, query_acc)
            )
            return (block, partial_value, query_acc)

        unused_block, partial_value, query_grad = lax.fori_loop(
            1, cycle_size, cycle_backward, (own_block, (key_grad, value_grad), query_grad)
        )
        key_grad, value_grad = (
            from_behind(partial_value[0].astype(jnp.bfloat16), "seq", 1).astype(jnp.float32),
            from_behind(partial_value[1].astype(jnp.bfloat16), "seq", 1).astype(jnp.float32),
        )
        qkv_grad = (
            jnp.concatenate([query_grad, key_grad, value_grad], -1)
            .reshape(-1, 3 * width)
            .astype(jnp.bfloat16)
        )
        totals[3] = totals[3] + jnp.sum(qkv_grad[:, :width].astype(jnp.float32), 0)
        totals[4] = totals[4] + jnp.sum(qkv_grad[:, 2 * width :].astype(jnp.float32), 0)
        totals[2] = totals[2] + left_dot(normed_low, qkv_grad)
        norm_grad = right_dot(qkv_grad, input_weight).reshape(values_in.shape)
        input_part, gain_one, shift_one = first_pull(norm_grad)
        totals[0] = totals[0] + gain_one
        totals[1] = totals[1] + shift_one
        grads_list.append(middle_grad + input_part)
    summed = lax.psum(
        (
            totals[0],
            totals[1],
            totals[2],
            totals[3],
            totals[4],
            totals[5],
            totals[6],
            totals[7],
            totals[8],
            totals[9],
            totals[10],
            totals[11],
            totals[12],
        ),
        ("dp", "seq"),
    )
    return (
        jnp.concatenate(outputs_list, 0),
        jnp.concatenate(grads_list, 0),
        summed[0],
        summed[1],
        summed[2],
        summed[3],
        summed[4],
        summed[5],
        summed[6],
        summed[7],
        summed[8],
        summed[9],
        summed[10],
        summed[11],
        summed[12],
    )


def local_rows(
    activations,
    segments,
    first_gain,
    first_shift,
    input_weight,
    query_bias,
    value_bias,
    output_weight,
    output_bias,
    second_gain,
    second_shift,
    expand_weight,
    expand_bias,
    reduce_weight,
    reduce_bias,
    cotangent,
):
    rows, span, width = activations.shape
    mine = lax.axis_index("seq")
    half = mine.astype(jnp.int32)[None]
    core = lax.axis_index("dp").astype(jnp.int32)[None] % 2
    place = jnp.concatenate([half, core])
    take = lambda array, index: lax.dynamic_index_in_dim(array, index, 0, keepdims=False)
    row = lambda vector: vector.reshape(1, -1)
    seg_got = swapped(take(segments, 1 - mine))
    x_got = swapped(after(take(activations, 1 - mine), seg_got))
    bias = jnp.concatenate([query_bias, jnp.zeros_like(query_bias), value_bias])
    gain, shift = row(first_gain), row(first_shift)
    weights = (gain, shift, input_weight, row(bias))
    start, table = documents(half, row(take(segments, mine)), row(seg_got), BLOCK)
    *before, norms = project(True, half, activations, *weights, (), TILE)
    cot_got = swapped(after(take(cotangent, 1 - mine), (x_got, norms)))
    q, k, v, more = project(False, half, x_got, *weights, before, TILE)
    norms = jnp.maximum(norms, more)
    limit = jnp.max(norms[0] * norms[1]) * (SCALE2 * SCALE2)
    small = (limit < SMALL * SMALL).astype(jnp.int32)[None]
    att_t, lse = attend(table, small, q, k, v, start, BLOCK)
    tokens = (x_got, activations, cot_got, cotangent)
    out_bias, gain_two = row(output_bias), row(second_gain)
    hid, exg, keep, send, vec_expand = feed_part(
        place, att_t, *tokens, output_weight, out_bias, gain_two, row(second_shift), expand_weight,
        row(expand_bias), reduce_weight, TILE, CHUNK,
    )

    core_hop, plane, line, pair = hops()
    one, two = ([hop] for hop in plane)
    sums = AllSum(keep, send, core_hop)
    result, result_send, mid_grad, att_grad, delta, d_output, vec = sums.beside(
        lambda place: middle_part(
            place, att_t, *tokens, hid, exg, output_weight, out_bias, gain_two, expand_weight,
            reduce_weight, row(reduce_bias), TILE,
        ),
        place, sums.split,
    )
    result_got = swapped(result_send)
    grads = []
    for first, ways in ((0, (one, two)), (H // 2, (two, one))):
        call = lambda table: attend_back(
            first, H // 2, table, q, k, v, att_grad, start, lse, delta, BLOCK
        )
        grads.append(sums.beside(call, table, sums.cross, *ways))
    grads = [[g[n] for g in grads] for n in range(3)]
    keep, send = sums.beside(
        lambda place: weight_part(place, grads, x_got, activations, gain, shift, d_output, span),
        after(place, result_got), sums.narrow, line + pair,
    )
    keep, send = after((keep, send), sums.state)
    tail = AllSum(keep, send, core_hop)
    sums.widen(line + pair)
    tail.split()
    ready = after(place, tail.state)
    tail.narrow(plane)
    grad, grad_send, vec_last = last_part(
        ready, grads, x_got, activations, mid_grad, gain, input_weight, TILE
    )
    tail.state = after(tail.state, grad)
    sums.state = after(sums.state, grad)
    vectors = jnp.concatenate([vec[:4], vec_expand[:4], vec_last], 0).astype(BF)
    sums.uncross(two, one)
    tail.meet(pair)
    tail.ride(vectors, pair)
    grad_got = swapped(after(grad_send, (tail.state, tail.whole)))
    tail.narrow(line)
    sums.state = after(sums.state, tail.state)
    sums.uncross(one, two)
    sums.join()
    tail.widen(line)
    tail.widen(plane)
    tail.widen(core_hop)
    part, dw = sums.state[0], tail.state[0]
    put = lambda whole, got: lax.dynamic_update_index_in_dim(
        whole, got.astype(whole.dtype), 1 - mine, 0
    )
    total = expand_weight.shape[1]

    def beside(stack):
        blocks = stack.shape[0] // width
        return jnp.concatenate([stack[n * width : (n + 1) * width] for n in range(blocks)], 1).astype(F32)

    vectors = tail.whole.astype(F32)
    return (
        put(result, result_got),
        put(grad, grad_got),
        vectors[8],
        vectors[9],
        beside(dw[: 3 * width]),
        vectors[10],
        vectors[11],
        dw[3 * width :].astype(F32),
        vectors[2],
        vectors[0],
        vectors[1],
        beside(part[total:]),
        vectors[4:8].reshape(-1),
        part[:total].astype(F32),
        vectors[3],
    )


TILE = 512
CHUNK = 256
BLOCK = 512
SMALL = 60.0
FORWARD_HEADS = 4
BACKWARD_HEADS = 4


def solution(mesh):
    sizes = dict(zip(mesh.axis_names, mesh.devices.shape))
    tokens, places, whole = P("dp", "seq", None), P("dp", "seq"), P()
    in_specs = (tokens, places) + (whole,) * 13 + (tokens,)
    out_specs = (tokens, tokens) + (whole,) * 13

    def program(activations, *rest):
        rows = activations.shape[0] // sizes["dp"]
        span = activations.shape[1] // sizes["seq"]
        by_rows = sizes["seq"] == 2 and rows == 2 and span % BLOCK == 0 and sizes["dp"] == 16
        return jax.shard_map(
            local_rows if by_rows else local,
            mesh=mesh,
            in_specs=in_specs,
            out_specs=out_specs,
            check_vma=False,
        )(activations, *rest)

    return program
```

```python
import functools

import jax
import jax.numpy as jnp
from jax import lax
from jax.experimental import pallas as pl
from jax.experimental.pallas import tpu as pltpu
from jax.sharding import PartitionSpec as P

H = 8
HD = 64
DEPTH = 48
MICRO = 2
EPSILON = 1e-05
NEGATIVE = -1e30
BRANCH = DEPTH ** (-0.5)
SCALE = HD ** (-0.5)
SCALE2 = SCALE * 1.4426950408889634
GELU_A = 0.7978845608028654
GELU_B = GELU_A * 0.044715

BF = jnp.bfloat16
F32 = jnp.float32
NN = (((1,), (0,)), ((), ()))
NT = (((1,), (1,)), ((), ()))
VMEM_LIMIT = 58 << 20
SHORT = pl.CostEstimate(flops=1000, bytes_accessed=1000, transcendentals=0)


def mm(left, right, dims=NN):
    return lax.dot_general(left, right, dims, preferred_element_type=F32)


def shape_of(dims, dtype):
    return jax.ShapeDtypeStruct(dims, dtype)


def params(limit=VMEM_LIMIT):
    return pltpu.CompilerParams(vmem_limit_bytes=limit)


def norm_parts(values):
    center = jnp.mean(values, -1, keepdims=True)
    centered = values - center
    variance = jnp.mean(centered * centered, -1, keepdims=True)
    scale = lax.rsqrt(variance + EPSILON)
    return centered * scale, scale


def norm_back(grad, unit, scale, gain):
    inner = grad * gain
    first = jnp.mean(inner, -1, keepdims=True)
    second = jnp.mean(inner * unit, -1, keepdims=True)
    return scale * (inner - first - unit * second)


def own_and_got(tiles):
    part = tiles // 2
    return (
        lambda t, h: (t + (1 - h[0]) * part) % tiles,
        lambda t, h: jnp.minimum(t, part - 1),
        lambda t, h: jnp.maximum(t - part, 0),
    )


def row_specs(tile, width, tiles):
    where, got, own = own_and_got(tiles)
    return (
        pl.BlockSpec((tile, width), lambda t, h: (got(t, h), 0)),
        pl.BlockSpec((1, tile, width), lambda t, h: (h[0], own(t, h), 0)),
    )


def either(got_ref, own_ref):
    early = pl.program_id(0) < pl.num_programs(0) // 2
    return jnp.where(early, got_ref[...], own_ref[0])


def once(array):
    return pl.BlockSpec(array.shape, lambda t, *_: (0,) * array.ndim, pipeline_mode=pl.Buffered(1))


def kept(dims):
    return pl.BlockSpec(dims, lambda t, *_: (0,) * len(dims))


def largest_norms(block):
    lane = lax.broadcasted_iota(jnp.int32, (block.shape[1], 128), 1)
    column = lax.broadcasted_iota(jnp.int32, (block.shape[1], 128), 0)
    member = jnp.where(column // HD == lane, 1.0, 0.0).astype(BF)
    wide = block.astype(F32)
    return jnp.max(mm((wide * wide).astype(BF), member), 0, keepdims=True)


def project_kernel(place, x_ref, gain_ref, shift_ref, weight_ref, bias_ref, *refs):
    q_ref, k_ref, v_ref, norm_ref = refs[-4:]
    width = weight_ref.shape[0]
    unit, _ = norm_parts(x_ref[...].reshape(-1, width).astype(F32))
    normed = (unit * gain_ref[...] + shift_ref[...]).astype(BF)

    @pl.when(pl.program_id(0) == 0)
    def _():
        norm_ref[...] = jnp.zeros(norm_ref.shape, F32)

    for n, ref in enumerate((q_ref, k_ref, v_ref)):
        cols = slice(n * width, (n + 1) * width)
        out = (mm(normed, weight_ref[:, cols]) + bias_ref[:, cols]).astype(BF)
        ref[...] = out
        if n < 2:
            norm_ref[n : n + 1, :] = jnp.maximum(norm_ref[n : n + 1, :], largest_norms(out))


def project(own, half, x, gain, shift, weight, bias, before, tile):
    span, width = x.shape[-2:]
    count = span // tile
    length = 2 * span
    if own:
        x_spec = pl.BlockSpec((1, tile, width), lambda t, h: (h[0], t, 0))
        here = lambda h: h[0]
    else:
        x_spec = pl.BlockSpec((tile, width), lambda t, h: (t, 0))
        here = lambda h: 1 - h[0]
    rows = pl.BlockSpec((tile, width), lambda t, h: (here(h) * count + t, 0))
    nat = shape_of((length, width), BF)
    return pl.pallas_call(
        project_kernel,
        grid_spec=pltpu.PrefetchScalarGridSpec(
            num_scalar_prefetch=1,
            grid=(count,),
            in_specs=[x_spec, once(gain), once(shift), once(weight), once(bias)]
            + [pl.BlockSpec(memory_space=pl.ANY)] * len(before),
            out_specs=[rows, rows, rows, kept((8, 128))],
        ),
        out_shape=[nat, nat, nat, shape_of((8, 128), F32)],
        input_output_aliases={6 + i: i for i in range(len(before))},
        compiler_params=params(),
        name="project",
    )(half, x, gain, shift, weight, bias, *before)


def document_kernel(size, half_ref, own_ref, got_ref, start_ref, table_ref):
    span = own_ref.shape[1]
    place = lambda half: pl.ds(pl.multiple_of(half * span, span), span)
    start_ref[0:1, place(half_ref[0])] = own_ref[...]
    start_ref[0:1, place(1 - half_ref[0])] = got_ref[...]
    numbers = start_ref[...]
    start = jnp.zeros_like(numbers)
    for number in range(1, 8):
        before = jnp.sum((numbers < number).astype(jnp.int32), 1, keepdims=True)
        start = jnp.where(numbers == number, before, start)
    start_ref[...] = start
    count = start.shape[1] // size
    slots = table_ref.shape[0] - 1
    for slot in range(slots):
        table_ref[slot] = 0
    filled = jnp.int32(0)
    for i in range(count):
        block = start[:, i * size : (i + 1) * size]
        low, high = jnp.min(block), jnp.max(block)
        for j in range(i + 1):
            kind = jnp.where(high > j * size, 2, 1 if i == j else 0)
            active = low < (j + 1) * size

            table_ref[filled] = jnp.where(active, i + 256 * j + 65536 * kind, 0)
            filled = filled + active.astype(jnp.int32)
    table_ref[slots] = filled


def documents(half, own, got, size):
    length = 2 * own.shape[1]
    count = length // size
    row = lambda wide: pl.BlockSpec((1, wide), lambda t, h: (0, 0))
    return pl.pallas_call(
        functools.partial(document_kernel, size),
        grid_spec=pltpu.PrefetchScalarGridSpec(
            num_scalar_prefetch=1,
            grid=(1,),
            in_specs=[row(length // 2), row(length // 2)],
            out_specs=[row(length), pl.BlockSpec(memory_space=pltpu.SMEM)],
        ),
        out_shape=[
            shape_of((1, length), jnp.int32),
            shape_of((count * (count + 1) // 2 + 2,), jnp.int32),
        ],
        compiler_params=params(),
        name="documents",
    )(half, own, got)


def head_half(block, head):
    lane = lax.broadcasted_iota(jnp.int32, block.shape, 1)
    keep = (lane < HD) if head % 2 == 0 else (lane >= HD)
    return jnp.where(keep, block, jnp.zeros_like(block))


def lanes_of(heads, group, head):
    low = HD * heads * group + 2 * HD * (head // 2)
    return pl.ds(pl.multiple_of(low, 2 * HD), 2 * HD)


def rows_of(heads, group, head):
    return pl.ds(pl.multiple_of(HD * heads * group + HD * head, HD), HD)


class Blocks:
    def __init__(self, size, list_ref, start_ref, mask_ref, values):
        self.size, self.list = size, list_ref
        self.start, self.mask, self.values = start_ref, mask_ref, values

    def at(self, index):
        return pl.ds(pl.multiple_of(index * self.size, self.size), self.size)

    def places(self):
        dims = (self.size, self.size)
        return lax.broadcasted_iota(jnp.int32, dims, 0), lax.broadcasted_iota(jnp.int32, dims, 1)

    def fill(self, slot, i, j):
        key, query = self.places()
        key, query = key + j * self.size, query + i * self.size
        allowed = (key >= self.start[0:1, self.at(i)]) & (key <= query)
        self.mask[slot] = jnp.where(allowed, *self.values).astype(self.mask.dtype)

    def entry(self, step):
        packed = self.list[step]
        kind = packed // 65536
        return packed % 256, (packed // 256) % 256, jnp.where(kind == 2, 2 + lax.rem(step, 2), kind)

    def prepare(self, slot, i, j):
        pl.when(slot >= 2)(lambda: self.fill(slot, i, j))

    def walk(self, variants, heads, loops, early, late, row_begin, step_end, row_end):
        steps = self.list[self.list.shape[0] - 1]
        self.mask[0] = jnp.full(self.mask.shape[1:], self.values[0], self.mask.dtype)
        key, query = self.places()
        self.mask[1] = jnp.where(key <= query, *self.values).astype(self.mask.dtype)
        i, j, slot = self.entry(0)
        self.prepare(slot, i, j)
        row_begin(i)
        zero = jnp.int32(0)
        early(zero, 0, i, j, slot, False)

        def body(turn, carry):
            i, j, slot = carry
            group = lax.rem(turn, loops)
            last = group == loops - 1
            after = self.entry(turn // loops + 1)
            ni, nj, nslot = (jnp.where(last, new, old) for new, old in zip(after, carry))
            ngroup = jnp.where(last, 0, group + 1)
            pl.when(last)(lambda: self.prepare(nslot, ni, nj))
            pl.when(ni > i)(lambda: row_begin(ni))

            def work(corner, slot):
                for head in range(heads):
                    if head + 1 < heads:
                        early(group, head + 1, i, j, slot, corner)
                    else:
                        early(ngroup, 0, ni, nj, nslot, False)
                    late(group, head, i, j, corner)

            if variants == 1:
                work(False, slot)
            elif variants == 2:
                pl.when(i != j)(lambda: work(False, slot))
                pl.when(i == j)(lambda: work(True, slot))
            else:
                pl.when(slot == 0)(lambda: work(False, None))
                pl.when((slot > 0) & (i == j))(lambda: work(True, slot))
                pl.when((slot > 0) & (i != j))(lambda: work(False, slot))

            @pl.when(last)
            def _():
                step_end(i, j)
                pl.when(j == i)(lambda: row_end(i))

            return ni, nj, nslot

        lax.fori_loop(0, steps * loops, body, (i, j, slot))


def pieces(corner, size):
    if not corner:
        return [(slice(0, size), slice(0, size))]
    mid = size // 2
    return [(slice(0, mid), slice(0, size)), (slice(mid, size), slice(mid, size))]


def part_at(size, index, part):
    low = index * size + part.start
    return pl.ds(pl.multiple_of(low, size // 2), part.stop - part.start)


class Blockwise:
    def __init__(self, size, first, source, target, sems):
        self.size, self.first = size, first
        self.source, self.target, self.sems = source, target, sems

    def copy(self, block):
        rows = pl.ds(pl.multiple_of(block * self.size, self.size), self.size)
        lanes = pl.ds(self.first, self.target.shape[1])
        return pltpu.make_async_copy(
            self.source.at[rows, lanes], self.target.at[rows, :], self.sems.at[block]
        )


def forward_kernel(
    size, list_ref, small_ref, q_hbm, k_hbm, v_hbm, start_ref, out_hbm, lse_ref, q_ref, k_ref, v_ref,
    vt_ref, stage_ref, in_sems, out_sems, max_ref, new_ref, acc_ref, bias_ref, mask_ref, *slots,
):
    heads = FORWARD_HEADS
    loops = H // heads
    scores, probs_of = slots[:heads], slots[heads:]
    plain = Blocks(size, list_ref, start_ref, mask_ref, (1.0, 0.0))
    general = Blocks(size, list_ref, start_ref, bias_ref, (0.0, NEGATIVE))
    at = plain.at
    count = q_ref.shape[0] // size
    loads = [
        Blockwise(size, 0, source, target, in_sems.at[n])
        for n, (source, target) in enumerate(((k_hbm, k_ref), (q_hbm, q_ref), (v_hbm, v_ref)))
    ]
    for block in range(count):
        for load in loads:
            load.copy(block).start()

    def store(i):
        cols = pl.ds(pl.multiple_of(i * size, size), size)
        return pltpu.make_async_copy(stage_ref.at[:, cols], out_hbm.at[:, cols], out_sems.at[i])

    def row_begin(i):
        for load in loads:
            load.copy(i).wait()
        vt_ref[:, at(i)] = v_ref[at(i), :].T

    def products(group, head, i, j, keys, queries):
        lanes = lanes_of(heads, group, head)
        block = head_half(k_ref[part_at(size, j, keys), lanes], head)
        return mm(block, q_ref[part_at(size, i, queries), lanes], NT)

    def values(group, head, j, keys):
        block = vt_ref[rows_of(heads, group, head), part_at(size, j, keys)]
        return jnp.concatenate([block, jnp.ones((16, keys.stop - keys.start), BF)], 0)

    def early_plain(group, head, i, j, slot, corner):
        for keys, queries in pieces(corner, size):
            probs = jnp.exp2(products(group, head, i, j, keys, queries) * SCALE2).astype(BF)
            if slot is not None:
                probs = probs * mask_ref[slot, keys, queries]
            probs_of[head][keys, queries] = probs

    def late_plain(group, head, i, j, corner):
        for keys, queries in pieces(corner, size):
            acc_ref[heads * group + head, :, queries] += mm(values(group, head, j, keys), probs_of[head][keys, queries])

    whole = slice(0, size)

    def early(group, head, i, j, slot, corner):
        s = products(group, head, i, j, whole, whole)
        if slot is not None:
            s = s + bias_ref[slot]
        scores[head][...] = s
        new_ref[heads * group + head] = jnp.max(s, 0, keepdims=True)

    def late(group, head, i, j, corner):
        place = heads * group + head
        old = max_ref[place]
        new = jnp.maximum(old, new_ref[place])
        max_ref[place] = new
        probs = jnp.exp2(scores[head][...] * SCALE2 - new * SCALE2)
        factor = jnp.exp2((old - new) * SCALE2)
        acc_ref[place] = acc_ref[place] * factor + mm(
            values(group, head, j, whole), probs.astype(BF)
        )

    def reset(largest):
        max_ref[...] = jnp.full(max_ref.shape, largest, F32)
        acc_ref[...] = jnp.zeros(acc_ref.shape, F32)

    def row_end(largest, i):
        def one(head, carry):
            total = acc_ref[head, HD : HD + 1, :]
            rows = pl.ds(pl.multiple_of(HD * head, HD), HD)
            stage_ref[rows, at(i)] = (acc_ref[head, :HD, :] * (1.0 / total)).astype(BF)
            lse_ref[head, :, at(i)] = max_ref[head] * SCALE2 + jnp.log2(total)
            return carry

        lax.fori_loop(0, H, one, 0)
        store(i).start()
        reset(largest)

    def run(variants, blocks, largest, early, late):
        reset(largest)
        blocks.walk(
            variants, heads, loops, early, late, row_begin, lambda i, j: None, functools.partial(row_end, largest)
        )

    pl.when(small_ref[0] == 1)(lambda: run(2, plain, 0.0, early_plain, late_plain))
    pl.when(small_ref[0] != 1)(lambda: run(1, general, NEGATIVE, early, late))
    for i in range(count):
        store(i).wait()


def attend(table, small, q, k, v, start, size):
    length, width = q.shape
    count = length // size
    far = pl.BlockSpec(memory_space=pl.ANY)
    near = pltpu.VMEM((length, width), BF)
    return pl.pallas_call(
        functools.partial(forward_kernel, size),
        grid_spec=pltpu.PrefetchScalarGridSpec(
            num_scalar_prefetch=2,
            grid=(1,),
            in_specs=[far, far, far, once(start)],
            out_specs=[far, kept((H, 1, length))],
            scratch_shapes=[
                near,
                near,
                near,
                pltpu.VMEM((width, length), BF),
                pltpu.VMEM((width, length), BF),
                pltpu.SemaphoreType.DMA((3, count)),
                pltpu.SemaphoreType.DMA((count,)),
                pltpu.VMEM((H, 1, size), F32),
                pltpu.VMEM((H, 1, size), F32),
                pltpu.VMEM((H, HD + 16, size), F32),
                pltpu.VMEM((4, size, size), F32),
                pltpu.VMEM((4, size, size), BF),
            ]
            + [pltpu.VMEM((size, size), F32)] * FORWARD_HEADS
            + [pltpu.VMEM((size, size), BF)] * FORWARD_HEADS,
        ),
        out_shape=[shape_of((width, length), BF), shape_of((H, 1, length), F32)],
        compiler_params=params(),
        name="attend",
    )(table, small, q, k, v, start)


def backward_kernel(
    size, heads, loops, first, list_ref, q_hbm, k_hbm, v_hbm, do_hbm, start_ref, lse_ref, delta_ref,
    dq_hbm, dk_hbm, dv_hbm, q_ref, k_ref, v_ref, do_ref, kt_ref, dq_ref, dk_ref, dv_ref, in_sems,
    out_sems, dqt_acc, dk_acc, dv_acc, bias_ref, *slots,
):
    probs_of, grads_of = slots[:heads], slots[heads:]
    walk = Blocks(size, list_ref, start_ref, bias_ref, (0.0, NEGATIVE))
    at = walk.at
    count = q_ref.shape[0] // size
    pairs = ((k_hbm, k_ref), (q_hbm, q_ref), (v_hbm, v_ref), (do_hbm, do_ref))
    loads = [
        Blockwise(size, first * HD, source, target, in_sems.at[n])
        for n, (source, target) in enumerate(pairs)
    ]
    for block in range(count):
        for load in loads:
            load.copy(block).start()

    def store(n, block):
        source, target = ((dq_ref, dq_hbm), (dk_ref, dk_hbm), (dv_ref, dv_hbm))[n]
        rows = at(block)
        return pltpu.make_async_copy(
            source.at[rows, :], target.at[rows, :], out_sems.at[n, block]
        )

    def row_begin(i):
        for load in loads:
            load.copy(i).wait()
        kt_ref[:, at(i)] = k_ref[at(i), :].T
        dk_acc[at(i), :] = jnp.zeros((size, dk_acc.shape[1]), F32)
        dv_acc[at(i), :] = jnp.zeros((size, dv_acc.shape[1]), F32)

    def early(group, head, i, j, slot, corner):
        lanes = lanes_of(heads, group, head)
        for keys, queries in pieces(corner, size):
            at_j, at_i = part_at(size, j, keys), part_at(size, i, queries)
            stat = (first + heads * group + head, slice(None), at_i)
            s = mm(head_half(k_ref[at_j, lanes], head), q_ref[at_i, lanes], NT)
            dots = mm(head_half(v_ref[at_j, lanes], head), do_ref[at_i, lanes], NT)
            if slot is not None:
                s = s + bias_ref[slot, keys, queries]
            probs = jnp.exp2(s * SCALE2 - lse_ref[stat])
            probs_of[head][keys, queries] = probs.astype(BF)
            grads_of[head][keys, queries] = (probs * (dots - delta_ref[stat])).astype(BF)

    def late(group, head, i, j, corner):
        lanes = lanes_of(heads, group, head)
        rows = rows_of(heads, group, head)
        for keys, queries in pieces(corner, size):
            at_j, at_i = part_at(size, j, keys), part_at(size, i, queries)
            grads = grads_of[head][keys, queries]
            dv_acc[at_j, lanes] += mm(
                probs_of[head][keys, queries], head_half(do_ref[at_i, lanes], head)
            )
            dk_acc[at_j, lanes] += mm(grads, head_half(q_ref[at_i, lanes], head))
            dqt_acc[rows, queries] += mm(kt_ref[rows, at_j], grads)

    def finish(j):
        dk_ref[at(j), :] = (dk_acc[at(j), :] * SCALE).astype(BF)
        dv_ref[at(j), :] = dv_acc[at(j), :].astype(BF)
        store(1, j).start()
        store(2, j).start()

    def step_end(i, j):
        pl.when(i == count - 1)(lambda: finish(j))

    def row_end(i):
        dq_ref[at(i), :] = (dqt_acc[...] * SCALE).T.astype(BF)
        store(0, i).start()
        dqt_acc[...] = jnp.zeros(dqt_acc.shape, F32)

    dqt_acc[...] = jnp.zeros(dqt_acc.shape, F32)
    walk.walk(3, heads, loops, early, late, row_begin, step_end, row_end)
    lowest = jnp.int32(count)
    for slot in range(list_ref.shape[0] - 1):
        lowest = lowest - jnp.where(list_ref[slot] % 256 == count - 1, 1, 0)
    for j in range(count):
        pl.when(j < lowest)(functools.partial(finish, j))
    for j in range(count):
        for n in range(3):
            store(n, j).wait()


def attend_back(first, groups, table, q, k, v, do, start, lse, delta, size):
    length = q.shape[0]
    part = HD * groups
    count = length // size
    far = pl.BlockSpec(memory_space=pl.ANY)
    near = pltpu.VMEM((length, part), BF)
    pairs = count * (count + 1) // 2 * size * size * groups
    return pl.pallas_call(
        functools.partial(backward_kernel, size, BACKWARD_HEADS, groups // BACKWARD_HEADS, first),
        cost_estimate=SHORT,
        grid_spec=pltpu.PrefetchScalarGridSpec(
            num_scalar_prefetch=1,
            grid=(1,),
            in_specs=[far] * 4 + [once(start), once(lse), once(delta)],
            out_specs=[far] * 3,
            scratch_shapes=[near] * 4
            + [pltpu.VMEM((part, length), BF)]
            + [near] * 3
            + [
                pltpu.SemaphoreType.DMA((4, count)),
                pltpu.SemaphoreType.DMA((3, count)),
                pltpu.VMEM((part, size), F32),
                pltpu.VMEM((length, part), F32),
                pltpu.VMEM((length, part), F32),
                pltpu.VMEM((4, size, size), F32),
            ]
            + [pltpu.VMEM((size, size), BF)] * (2 * BACKWARD_HEADS),
        ),
        out_shape=[shape_of((length, part), BF)] * 3,
        compiler_params=params(),
        name="attend_back",
    )(table, q, k, v, do, start, lse, delta)


def feed_kernel(
    chunk, place_ref, att_ref, x_got, x_own, cot_got, cot_own, wo_ref, ob_ref, g2_ref, s2_ref, we_ref,
    eb_ref, wr_ref, hid_ref, exg_ref, keep_ref, send_ref, deb_ref, acc_ref, deb_acc, wet_ref, ebt_ref,
):
    step = pl.program_id(0)
    tile, width = x_got.shape
    total = wr_ref.shape[0]

    @pl.when(step == 0)
    def _():
        for ref in (acc_ref, deb_acc):
            ref[...] = jnp.zeros(ref.shape, F32)
        wet_ref[...] = we_ref[...].T
        ebt_ref[...] = jnp.broadcast_to(eb_ref[...], (128, total)).T

    mixed = mm(att_ref[...].T, wo_ref[...]) + ob_ref[...]
    middle = either(x_got, x_own).astype(F32) + BRANCH * mixed
    unit, _ = norm_parts(middle)
    second = (unit * g2_ref[...] + s2_ref[...]).astype(BF)
    second_t = second.T
    reduced_grad = (BRANCH * either(cot_got, cot_own).astype(F32)).astype(BF)

    def stage_one(c):
        rows = slice(c * chunk, (c + 1) * chunk)
        bias = jnp.concatenate([ebt_ref[rows, :]] * (tile // 128), 1)
        v = mm(wet_ref[rows, :], second, NT) + bias
        v2 = v * v
        t = jnp.tanh(v * (GELU_A + GELU_B * v2))
        h1 = 0.5 * t + 0.5
        gelu = v * h1
        slope = h1 + gelu * (1.0 - h1) * (2.0 * GELU_A + 6.0 * GELU_B * v2)
        hid_ref[rows, :] = gelu.astype(BF)
        grads = (mm(wr_ref[rows, :], reduced_grad, NT) * slope).astype(BF)
        exg_ref[rows, :] = grads
        wide = grads.astype(F32)
        part = wide[:, 0:128]
        for n in range(1, tile // 128):
            part = part + wide[:, n * 128 : (n + 1) * 128]
        deb_acc[rows, :] += part

    stage_one(0)
    for c in range(total // chunk):
        if (c + 1) * chunk < total:
            stage_one(c + 1)
        rows = slice(c * chunk, (c + 1) * chunk)
        acc_ref[rows, :] += mm(hid_ref[rows, :], reduced_grad)
        block, low = divmod(c * chunk, width)
        there = slice(total + block * width, total + (block + 1) * width)
        acc_ref[there, low : low + chunk] += mm(second_t, exg_ref[rows, :], NT)

    last = step == pl.num_programs(0) - 1
    halves = slice(0, total), slice(total, 2 * total)
    for core in range(2):

        @pl.when(last & (place_ref[1] == core))
        def _():
            keep_ref[...] = acc_ref[halves[core], :].astype(BF)
            send_ref[...] = acc_ref[halves[1 - core], :].astype(BF)

    @pl.when(last)
    def _():
        flat = jnp.sum(deb_acc[...].T, 0, keepdims=True)
        deb_ref[...] = jnp.zeros(deb_ref.shape, F32)
        for n in range(total // width):
            deb_ref[n : n + 1, :] = flat[:, n * width : (n + 1) * width]


def feed_part(place, att_t, x_got, x_own, cot_got, cot_own, wo, ob, g2, s2, we, eb, wr, tile, chunk):
    width, length = att_t.shape
    total = wr.shape[0]
    tiles = length // tile
    where, _, _ = own_and_got(tiles)
    pair = list(row_specs(tile, width, tiles))
    cols = lambda high: pl.BlockSpec((high, tile), lambda t, h: (0, where(t, h)))
    return pl.pallas_call(
        functools.partial(feed_kernel, chunk),
        grid_spec=pltpu.PrefetchScalarGridSpec(
            num_scalar_prefetch=1,
            grid=(tiles,),
            in_specs=[cols(width)] + pair * 2 + [once(a) for a in (wo, ob, g2, s2, we, eb, wr)],
            out_specs=[cols(total), cols(total), kept((total, width)), kept((total, width)), kept((8, width))],
            scratch_shapes=[
                pltpu.VMEM((2 * total, width), F32),
                pltpu.VMEM((total, 128), F32),
                pltpu.VMEM((total, width), BF),
                pltpu.VMEM((total, 128), F32),
            ],
        ),
        out_shape=[
            shape_of((total, length), BF),
            shape_of((total, length), BF),
            shape_of((total, width), BF),
            shape_of((total, width), BF),
            shape_of((8, width), F32),
        ],
        compiler_params=params(),
        name="feed",
    )(place, att_t, x_got, x_own, cot_got, cot_own, wo, ob, g2, s2, we, eb, wr)


def middle_kernel(
    place_ref, att_ref, x_got, x_own, cot_got, cot_own, hid_ref, exg_ref, wo_ref, ob_ref, g2_ref,
    we_ref, wr_ref, rb_ref, res_own, res_send, grad_ref, ag_ref, delta_ref, dwo_ref, vec_ref, acc_ref,
    wrt_ref,
):
    step = pl.program_id(0)
    tiles = pl.num_programs(0)

    @pl.when(step == 0)
    def _():
        for ref in (acc_ref, vec_ref):
            ref[...] = jnp.zeros(ref.shape, F32)
        wrt_ref[...] = wr_ref[...].T

    att_t = att_ref[...]
    mixed = mm(att_t.T, wo_ref[...]) + ob_ref[...]
    middle = either(x_got, x_own).astype(F32) + BRANCH * mixed
    cot = either(cot_got, cot_own).astype(F32)
    unit, scale = norm_parts(middle)
    norm_grad = mm(we_ref[...], exg_ref[...]).T
    result = (middle + BRANCH * (mm(wrt_ref[...], hid_ref[...]).T + rb_ref[...])).astype(BF)

    @pl.when(step < tiles // 2)
    def _():
        res_send[...] = result

    @pl.when(step >= tiles // 2)
    def _():
        res_own[0] = result

    middle_grad = cot + norm_back(norm_grad, unit, scale, g2_ref[...])
    grad_ref[...] = middle_grad
    mixed_grad = (BRANCH * middle_grad).astype(BF)
    acc_ref[...] += mm(att_t, mixed_grad)
    att_grad = mm(mixed_grad, wo_ref[...], NT).astype(BF)
    ag_ref[...] = att_grad
    dots = att_grad.T.astype(F32) * att_t.astype(F32)
    for head in range(H):
        delta_ref[head] = jnp.sum(dots[HD * head : HD * head + HD, :], 0, keepdims=True)
    reduced_grad = (BRANCH * cot).astype(BF)
    sums = (norm_grad * unit, norm_grad, mixed_grad.astype(F32), reduced_grad.astype(F32))
    for n, value in enumerate(sums):
        vec_ref[n : n + 1, :] += jnp.sum(value, 0, keepdims=True)

    @pl.when(step == tiles - 1)
    def _():
        dwo_ref[...] = acc_ref[...].astype(BF)


def middle_part(place, att_t, x_got, x_own, cot_got, cot_own, hid, exg, wo, ob, g2, we, wr, rb, tile):
    width, length = att_t.shape
    total = wr.shape[0]
    tiles = length // tile
    where, got, own = own_and_got(tiles)
    pair = list(row_specs(tile, width, tiles))
    rows = pl.BlockSpec((tile, width), lambda t, h: (where(t, h), 0))
    cols = lambda high: pl.BlockSpec((high, tile), lambda t, h: (0, where(t, h)))
    return pl.pallas_call(
        middle_kernel,
        cost_estimate=SHORT,
        grid_spec=pltpu.PrefetchScalarGridSpec(
            num_scalar_prefetch=1,
            grid=(tiles,),
            in_specs=[cols(width)]
            + pair * 2
            + [cols(total), cols(total)]
            + [once(a) for a in (wo, ob, g2, we, wr, rb)],
            out_specs=[
                pair[1],
                pair[0],
                rows,
                rows,
                pl.BlockSpec((H, 1, tile), lambda t, h: (0, 0, where(t, h))),
                kept((width, width)),
                kept((8, width)),
            ],
            scratch_shapes=[pltpu.VMEM((width, width), F32), pltpu.VMEM((width, total), BF)],
        ),
        out_shape=[
            shape_of((2, length // 2, width), BF),
            shape_of((length // 2, width), BF),
            shape_of((length, width), F32),
            shape_of((length, width), BF),
            shape_of((H, 1, length), F32),
            shape_of((width, width), BF),
            shape_of((8, width), F32),
        ],
        compiler_params=params(),
        name="middle",
    )(place, att_t, x_got, x_own, cot_got, cot_own, hid, exg, wo, ob, g2, we, wr, rb)


def weight_kernel(parts, place_ref, *refs):
    ins = refs[: 3 * parts]
    x_got, x_own, gain_ref, shift_ref, extra_ref, keep_ref, send_ref, acc_ref = refs[3 * parts :]
    step = pl.program_id(0)

    @pl.when(step == 0)
    def _():
        acc_ref[...] = jnp.zeros(acc_ref.shape, F32)

    width = x_got.shape[1]
    unit, _ = norm_parts(either(x_got, x_own).astype(F32))
    normed_t = (unit * gain_ref[...] + shift_ref[...]).astype(BF).T
    for n in range(3):
        grad = jnp.concatenate([ref[...] for ref in ins[n * parts : (n + 1) * parts]], 1)
        acc_ref[n * width : (n + 1) * width, :] += mm(normed_t, grad)

    last = step == pl.num_programs(0) - 1
    for core in range(2):

        @pl.when(last & (place_ref[1] == core))
        def _():
            lower, upper = (keep_ref, send_ref) if core == 0 else (send_ref, keep_ref)
            lower[...] = acc_ref[: 2 * width, :].astype(BF)
            upper[:width, :] = acc_ref[2 * width :, :].astype(BF)
            upper[width:, :] = extra_ref[...]


def weight_part(place, grads, x_got, x_own, gain, shift, extra, tile):
    span, width = x_got.shape
    tiles = 2 * span // tile
    where, _, _ = own_and_got(tiles)
    flat = [part for group in grads for part in group]
    out = shape_of((2 * width, width), BF)
    return pl.pallas_call(
        functools.partial(weight_kernel, len(grads[0])),
        cost_estimate=SHORT,
        grid_spec=pltpu.PrefetchScalarGridSpec(
            num_scalar_prefetch=1,
            grid=(tiles,),
            in_specs=[
                pl.BlockSpec((tile, a.shape[1]), lambda t, h: (where(t, h), 0)) for a in flat
            ]
            + list(row_specs(tile, width, tiles))
            + [once(a) for a in (gain, shift, extra)],
            out_specs=[kept(out.shape)] * 2,
            scratch_shapes=[pltpu.VMEM((3 * width, width), F32)],
        ),
        out_shape=[out, out],
        compiler_params=params(),
        name="weight",
    )(place, *flat, x_got, x_own, gain, shift, extra)


def last_kernel(parts, place_ref, *refs):
    ins, rest = refs[: 3 * parts], refs[3 * parts :]
    x_got, x_own, mid_ref, gain_ref, weight_ref, own_ref, send_ref, vec_ref = rest
    step = pl.program_id(0)
    tiles = pl.num_programs(0)

    @pl.when(step == 0)
    def _():
        vec_ref[...] = jnp.zeros(vec_ref.shape, F32)

    width = x_got.shape[1]
    unit, scale = norm_parts(either(x_got, x_own).astype(F32))
    back = None
    grads = []
    for n in range(3):
        grad = jnp.concatenate([ref[...] for ref in ins[n * parts : (n + 1) * parts]], 1)
        one = mm(grad, weight_ref[:, n * width : (n + 1) * width], NT)
        back = one if back is None else back + one
        grads.append(grad)
    total = mid_ref[...] + norm_back(back, unit, scale, gain_ref[...])

    @pl.when(step < tiles // 2)
    def _():
        send_ref[...] = total.astype(BF)

    @pl.when(step >= tiles // 2)
    def _():
        own_ref[0] = total

    sums = (back * unit, back, grads[0].astype(F32), grads[2].astype(F32))
    for n, value in enumerate(sums):
        vec_ref[n : n + 1, :] += jnp.sum(value, 0, keepdims=True)


def last_part(place, grads, x_got, x_own, mid, gain, weight, tile):
    length, width = mid.shape
    tiles = length // tile
    where, _, _ = own_and_got(tiles)
    rows = pl.BlockSpec((tile, width), lambda t, h: (where(t, h), 0))
    flat = [part for group in grads for part in group]
    pair = list(row_specs(tile, width, tiles))
    return pl.pallas_call(
        functools.partial(last_kernel, len(grads[0])),
        cost_estimate=SHORT,
        grid_spec=pltpu.PrefetchScalarGridSpec(
            num_scalar_prefetch=1,
            grid=(tiles,),
            in_specs=[
                pl.BlockSpec((tile, a.shape[1]), lambda t, h: (where(t, h), 0)) for a in flat
            ]
            + pair
            + [rows, once(gain), once(weight)],
            out_specs=[pair[1], pair[0], kept((8, width))],
        ),
        out_shape=[
            shape_of((2, length // 2, width), F32),
            shape_of((length // 2, width), BF),
            shape_of((8, width), F32),
        ],
        compiler_params=params(),
        name="last",
    )(place, *flat, x_got, x_own, mid, gain, weight)


def swapped(value):
    return lax.ppermute(value, "seq", [(0, 1), (1, 0)])


def side(hop):
    axis, bit = hop
    return (lax.axis_index(axis) // bit) % 2


def place_of(hops):
    place = 0
    for hop in hops:
        place = 2 * place + side(hop)
    return place


def exchanged(value, hops):
    axes = tuple(dict.fromkeys(axis for axis, _ in hops))
    flips = [sum(bit for axis, bit in hops if axis == name) for name in axes]
    sizes = [lax.axis_size(name) for name in axes]
    if len(axes) == 1:
        return lax.ppermute(value, axes[0], [(i, i ^ flips[0]) for i in range(sizes[0])])
    pairs = [
        (i * sizes[1] + j, (i ^ flips[0]) * sizes[1] + (j ^ flips[1]))
        for i in range(sizes[0])
        for j in range(sizes[1])
    ]
    return lax.ppermute(value, axes, pairs)


def partners(hops):
    count = len(hops)
    return [
        ([hop for n, hop in enumerate(hops) if (flip >> (count - 1 - n)) & 1], flip)
        for flip in range(1, 1 << count)
    ]


def added(*values):
    total = values[0].astype(F32)
    for value in values[1:]:
        total = total + value.astype(F32)
    return total.astype(BF)


def scatter(part, hops):
    rows = part.shape[1] >> len(hops)
    mine = place_of(hops)
    piece = lambda place: lax.dynamic_slice_in_dim(part, place * rows, rows, 1)
    got = [exchanged(piece(mine ^ flip), chosen) for chosen, flip in partners(hops)]
    return added(piece(mine), *got)


def gather(part, hops, whole=None, first=()):
    mine = place_of(hops)
    blocks, rows, width = part.shape
    got, others = [(part, mine)], []
    for chosen, flip in partners(hops):
        if whole is None:
            got.append((after(exchanged(part, chosen), first), mine ^ flip))
            continue
        both = exchanged(jnp.concatenate([part.reshape(-1, width), whole], 0), chosen)
        both = after(both, first)
        got.append((both[: blocks * rows].reshape(part.shape), mine ^ flip))
        others.append(both[blocks * rows :])
    if len(hops) == 1:
        one, two = got[0][0], got[1][0]
        out = jnp.where(mine == 0, jnp.concatenate([one, two], 1), jnp.concatenate([two, one], 1))
    else:
        out = jnp.zeros((blocks, rows << len(hops), width), part.dtype)
        for piece, place in got:
            out = lax.dynamic_update_slice_in_dim(out, piece, place * rows, 1)
    return out if whole is None else (out, added(whole, *others))


def hops():
    found = []
    for axis in ("dp", "seq"):
        size = lax.axis_size(axis)
        found.append([(axis, 1 << n) for n in range(size.bit_length() - 1)])
    core, one, two, far = found[0]
    return [core], [one, two], [far], found[1]


class AllSum:
    def __init__(self, keep, send, core):
        self.core, self.whole = core, None
        self.state = (keep[None], send[None])

    def split(self):
        keep, send = self.state
        self.state = added(keep, exchanged(send, self.core))

    def cross(self, one, two):
        if not isinstance(self.state, tuple):
            mid = self.state.shape[1] // 2
            self.state = (self.state[:, :mid], self.state[:, mid:])
        self.state = tuple(scatter(part, hops) for part, hops in zip(self.state, (one, two)))

    def uncross(self, one, two):
        if not isinstance(self.state, tuple):
            self.state = (self.state[:1], self.state[1:])
        self.state = tuple(gather(part, hops) for part, hops in zip(self.state, (one, two)))

    def join(self):
        self.state = gather(jnp.concatenate(self.state, 1), self.core)

    def ride(self, whole, hops):
        self.whole = added(whole, exchanged(whole, hops))

    def narrow(self, hops):
        if isinstance(self.state, tuple):
            self.state = jnp.concatenate(self.state, 0)
        self.state = scatter(self.state, hops)

    def meet(self, hops):
        self.state = added(self.state, exchanged(self.state, hops))

    def widen(self, hops, first=()):
        if self.whole is None:
            self.state = gather(self.state, hops, None, first)
        else:
            self.state, self.whole = gather(self.state, hops, self.whole, first)

    def beside(self, call, argument, step, *hops):
        argument = after(argument, self.state)
        step(*hops)
        out = call(argument)
        self.state = after(self.state, out)
        return out


def after(value, earlier):
    return lax.optimization_barrier((value, earlier))[0] if jax.tree.leaves(earlier) else value


def passed_along(block, axis, distance):
    devices = range(lax.axis_size(axis))
    route = [(i - distance, i) for i in devices if i - distance in devices]
    return lax.ppermute(block, axis, route)


def from_behind(value, axis, steps):
    count = lax.axis_size(axis)
    pairs = [(source, (source + steps) % count) for source in range(count)]
    return lax.ppermute(value, axis, pairs)


def layer_norm(values, gain_vec, shift_vec):
    center = jnp.mean(values, -1, keepdims=True)
    centered = values - center
    variance = jnp.mean(centered * centered, -1, keepdims=True)
    return centered * lax.rsqrt(variance + EPSILON) * gain_vec + shift_vec


def gelu_tanh(values):
    return jax.nn.gelu(values, approximate=True)


def plain_dot(left, right):
    return jnp.dot(left, right, preferred_element_type=jnp.float32)


def left_dot(left, right):
    return lax.dot_general(
        left, right, (((0,), (0,)), ((), ())), preferred_element_type=jnp.float32
    )


def right_dot(left, right):
    return lax.dot_general(
        left, right, (((1,), (1,)), ((), ())), preferred_element_type=jnp.float32
    )


def block_scores(queries, keys_block, query_seg, key_seg, query_places, key_start):
    row_count, key_len, width = keys_block.shape
    keys_heads = keys_block.reshape(row_count, key_len, H, HD)
    scores = jnp.einsum(
        "rqhd,rkhd->rhqk", queries, keys_heads, preferred_element_type=jnp.float32
    ) * HD ** (-0.5)
    key_places = key_start + jnp.arange(key_len, dtype=jnp.int32)
    allowed = (query_seg[:, None, :, None] == key_seg[:, None, None, :]) & (
        key_places[None, None, None, :] <= query_places[None, None, :, None]
    )
    return (scores, allowed)


def attend_block(state, queries, block, query_seg, query_places, key_start):
    run_max, run_sum, running = state
    keys_block, values_block, key_seg = block
    row_count, key_len, width = values_block.shape
    query_len = queries.shape[1]
    scores, allowed = block_scores(queries, keys_block, query_seg, key_seg, query_places, key_start)
    block_max = jnp.max(jnp.where(allowed, scores, NEGATIVE), -1)
    new_max = jnp.maximum(run_max, block_max)
    exponent = jnp.where(allowed, jnp.exp(scores - new_max[..., None]), 0.0)
    factor = jnp.exp(run_max - new_max)
    new_sum = run_sum * factor + jnp.sum(exponent, -1)
    values_heads = values_block.reshape(row_count, key_len, H, HD)
    addition = jnp.einsum(
        "rhqk,rkhd->rqhd",
        exponent.astype(jnp.bfloat16),
        values_heads,
        preferred_element_type=jnp.float32,
    )
    scaled = (
        running.reshape(row_count, query_len, H, HD) * jnp.transpose(factor, (0, 2, 1))[..., None]
    )
    return (new_max, new_sum, (scaled + addition).reshape(row_count, query_len, width))


def grad_block(queries, out_grad, log_sum, delta, block, query_seg, query_places, key_start):
    keys_block, values_block, key_seg = block
    row_count, key_len, width = keys_block.shape
    scores, allowed = block_scores(queries, keys_block, query_seg, key_seg, query_places, key_start)
    weights_block = jnp.where(allowed, jnp.exp(scores - log_sum[..., None]), 0.0)
    keys_heads = keys_block.reshape(row_count, key_len, H, HD)
    values_heads = values_block.reshape(row_count, key_len, H, HD)
    value_dots = jnp.einsum(
        "rqhd,rkhd->rhqk", out_grad, values_heads, preferred_element_type=jnp.float32
    )
    score_grad = (weights_block * (value_dots - delta[..., None]) * HD ** (-0.5)).astype(
        jnp.bfloat16
    )
    query_part = jnp.einsum(
        "rhqk,rkhd->rqhd", score_grad, keys_heads, preferred_element_type=jnp.float32
    ).reshape(row_count, -1, width)
    key_part = jnp.einsum(
        "rhqk,rqhd->rkhd", score_grad, queries, preferred_element_type=jnp.float32
    ).reshape(row_count, key_len, width)
    value_part = jnp.einsum(
        "rhqk,rqhd->rkhd",
        weights_block.astype(jnp.bfloat16),
        out_grad,
        preferred_element_type=jnp.float32,
    ).reshape(row_count, key_len, width)
    return (query_part, key_part, value_part)


def local(
    activations,
    segments,
    first_gain,
    first_shift,
    input_weight,
    query_bias,
    value_bias,
    output_weight,
    output_bias,
    second_gain,
    second_shift,
    expand_weight,
    expand_bias,
    reduce_weight,
    reduce_bias,
    cotangent,
):
    row_total, span_len, width = activations.shape
    cycle_size = lax.axis_size("seq")
    position = lax.axis_index("seq")
    micro_rows = row_total // MICRO
    branch = DEPTH ** (-0.5)
    bias_all = jnp.concatenate([query_bias, jnp.zeros_like(query_bias), value_bias])
    query_places = position * span_len + jnp.arange(span_len, dtype=jnp.int32)
    totals = [
        jnp.zeros(argument.shape, jnp.float32)
        for argument in (
            first_gain,
            first_shift,
            input_weight,
            query_bias,
            value_bias,
            output_weight,
            output_bias,
            second_gain,
            second_shift,
            expand_weight,
            expand_bias,
            reduce_weight,
            reduce_bias,
        )
    ]
    outputs_list = []
    grads_list = []
    for micro in range(MICRO):
        lower = micro * micro_rows
        values_in = activations[lower : lower + micro_rows].astype(jnp.float32)
        query_seg = segments[lower : lower + micro_rows]
        out_cot = cotangent[lower : lower + micro_rows].astype(jnp.float32)
        normed, first_pull = jax.vjp(layer_norm, values_in, first_gain, first_shift)
        normed_low = normed.astype(jnp.bfloat16).reshape(-1, width)
        projected = (plain_dot(normed_low, input_weight) + bias_all).astype(jnp.bfloat16)
        queries = projected[:, :width].reshape(micro_rows, span_len, H, HD)
        keys_own = projected[:, width : 2 * width].reshape(micro_rows, span_len, width)
        values_own = projected[:, 2 * width :].reshape(micro_rows, span_len, width)
        own_block = (keys_own, values_own, query_seg)
        start_state = (
            jnp.full((micro_rows, H, span_len), NEGATIVE, jnp.float32),
            jnp.zeros((micro_rows, H, span_len), jnp.float32),
            jnp.zeros((micro_rows, span_len, width), jnp.float32),
        )
        state = attend_block(
            start_state, queries, own_block, query_seg, query_places, position * span_len
        )

        def cycle_forward(step_index, carry):
            block, inner_state = carry
            block = passed_along((block[0], block[1], block[2]), "seq", 1)
            source = (position - step_index) % cycle_size
            inner_state = lax.cond(
                source < position,
                lambda current: attend_block(
                    current, queries, block, query_seg, query_places, source * span_len
                ),
                lambda current: current,
                inner_state,
            )
            return (block, inner_state)

        unused_block, state = lax.fori_loop(1, cycle_size, cycle_forward, (own_block, state))
        run_max, run_sum, running = state
        attended = (
            running.reshape(micro_rows, span_len, H, HD)
            / jnp.transpose(run_sum, (0, 2, 1))[..., None]
        ).reshape(micro_rows, span_len, width)
        log_sum = run_max + jnp.log(run_sum)
        attended_low = attended.astype(jnp.bfloat16).reshape(-1, width)
        mixed_out = plain_dot(attended_low, output_weight) + output_bias
        middle = values_in + branch * mixed_out.reshape(values_in.shape)
        second_norm, second_pull = jax.vjp(layer_norm, middle, second_gain, second_shift)
        second_low = second_norm.astype(jnp.bfloat16).reshape(-1, width)
        expanded = plain_dot(second_low, expand_weight) + expand_bias
        hidden, gelu_pull = jax.vjp(gelu_tanh, expanded)
        hidden_low = hidden.astype(jnp.bfloat16)
        reduced = plain_dot(hidden_low, reduce_weight) + reduce_bias
        outputs_list.append(
            (middle + branch * reduced.reshape(values_in.shape)).astype(jnp.bfloat16)
        )
        reduced_grad = (branch * out_cot).reshape(-1, width).astype(jnp.bfloat16)
        totals[12] = totals[12] + jnp.sum(reduced_grad.astype(jnp.float32), 0)
        totals[11] = totals[11] + left_dot(hidden_low, reduced_grad)
        (expanded_grad,) = gelu_pull(right_dot(reduced_grad, reduce_weight))
        expanded_low = expanded_grad.astype(jnp.bfloat16)
        totals[10] = totals[10] + jnp.sum(expanded_low.astype(jnp.float32), 0)
        totals[9] = totals[9] + left_dot(second_low, expanded_low)
        norm_in_grad = right_dot(expanded_low, expand_weight).reshape(values_in.shape)
        middle_part, gain_part, shift_part = second_pull(norm_in_grad)
        totals[7] = totals[7] + gain_part
        totals[8] = totals[8] + shift_part
        middle_grad = out_cot + middle_part
        mixed_grad = (branch * middle_grad).reshape(-1, width).astype(jnp.bfloat16)
        totals[6] = totals[6] + jnp.sum(mixed_grad.astype(jnp.float32), 0)
        totals[5] = totals[5] + left_dot(attended_low, mixed_grad)
        attended_grad = (
            right_dot(mixed_grad, output_weight)
            .astype(jnp.bfloat16)
            .reshape(micro_rows, span_len, H, HD)
        )
        delta = jnp.transpose(
            jnp.sum(
                attended_grad.astype(jnp.float32) * attended.reshape(micro_rows, span_len, H, HD),
                -1,
            ),
            (0, 2, 1),
        )
        query_grad, key_grad, value_grad = grad_block(
            queries,
            attended_grad,
            log_sum,
            delta,
            own_block,
            query_seg,
            query_places,
            position * span_len,
        )

        def cycle_backward(step_index, carry):
            block, partial_value, query_acc = carry
            block = passed_along((block[0], block[1], block[2]), "seq", 1)
            partial_value = (
                from_behind(partial_value[0].astype(jnp.bfloat16), "seq", 1).astype(jnp.float32),
                from_behind(partial_value[1].astype(jnp.bfloat16), "seq", 1).astype(jnp.float32),
            )
            source = (position - step_index) % cycle_size

            def work(current):
                partial_in, query_in = current
                query_part, key_part, value_part = grad_block(
                    queries,
                    attended_grad,
                    log_sum,
                    delta,
                    block,
                    query_seg,
                    query_places,
                    source * span_len,
                )
                return (
                    (partial_in[0] + key_part, partial_in[1] + value_part),
                    query_in + query_part,
                )

            partial_value, query_acc = lax.cond(
                source < position, work, lambda current: current, (partial_value, query_acc)
            )
            return (block, partial_value, query_acc)

        unused_block, partial_value, query_grad = lax.fori_loop(
            1, cycle_size, cycle_backward, (own_block, (key_grad, value_grad), query_grad)
        )
        key_grad, value_grad = (
            from_behind(partial_value[0].astype(jnp.bfloat16), "seq", 1).astype(jnp.float32),
            from_behind(partial_value[1].astype(jnp.bfloat16), "seq", 1).astype(jnp.float32),
        )
        qkv_grad = (
            jnp.concatenate([query_grad, key_grad, value_grad], -1)
            .reshape(-1, 3 * width)
            .astype(jnp.bfloat16)
        )
        totals[3] = totals[3] + jnp.sum(qkv_grad[:, :width].astype(jnp.float32), 0)
        totals[4] = totals[4] + jnp.sum(qkv_grad[:, 2 * width :].astype(jnp.float32), 0)
        totals[2] = totals[2] + left_dot(normed_low, qkv_grad)
        norm_grad = right_dot(qkv_grad, input_weight).reshape(values_in.shape)
        input_part, gain_one, shift_one = first_pull(norm_grad)
        totals[0] = totals[0] + gain_one
        totals[1] = totals[1] + shift_one
        grads_list.append(middle_grad + input_part)
    summed = lax.psum(
        (
            totals[0],
            totals[1],
            totals[2],
            totals[3],
            totals[4],
            totals[5],
            totals[6],
            totals[7],
            totals[8],
            totals[9],
            totals[10],
            totals[11],
            totals[12],
        ),
        ("dp", "seq"),
    )
    return (
        jnp.concatenate(outputs_list, 0),
        jnp.concatenate(grads_list, 0),
        summed[0],
        summed[1],
        summed[2],
        summed[3],
        summed[4],
        summed[5],
        summed[6],
        summed[7],
        summed[8],
        summed[9],
        summed[10],
        summed[11],
        summed[12],
    )


def local_rows(
    activations,
    segments,
    first_gain,
    first_shift,
    input_weight,
    query_bias,
    value_bias,
    output_weight,
    output_bias,
    second_gain,
    second_shift,
    expand_weight,
    expand_bias,
    reduce_weight,
    reduce_bias,
    cotangent,
):
    rows, span, width = activations.shape
    mine = lax.axis_index("seq")
    half = mine.astype(jnp.int32)[None]
    core = lax.axis_index("dp").astype(jnp.int32)[None] % 2
    place = jnp.concatenate([half, core])
    take = lambda array, index: lax.dynamic_index_in_dim(array, index, 0, keepdims=False)
    row = lambda vector: vector.reshape(1, -1)

    def beside(stack):
        blocks = stack.shape[0] // width
        return jnp.concatenate([stack[n * width : (n + 1) * width] for n in range(blocks)], 1).astype(F32)

    seg_got = swapped(take(segments, 1 - mine))
    x_got = swapped(after(take(activations, 1 - mine), seg_got))
    bias = jnp.concatenate([query_bias, jnp.zeros_like(query_bias), value_bias])
    gain, shift = row(first_gain), row(first_shift)
    weights = (gain, shift, input_weight, row(bias))
    start, table = documents(half, row(take(segments, mine)), row(seg_got), BLOCK)
    *before, norms = project(True, half, activations, *weights, (), TILE)
    cot_got = swapped(after(take(cotangent, 1 - mine), (x_got, norms)))
    q, k, v, more = project(False, half, x_got, *weights, before, TILE)
    norms = jnp.maximum(norms, more)
    limit = jnp.max(norms[0] * norms[1]) * (SCALE2 * SCALE2)
    small = (limit < SMALL * SMALL).astype(jnp.int32)[None]
    att_t, lse = attend(table, small, q, k, v, start, BLOCK)
    tokens = (x_got, activations, cot_got, cotangent)
    out_bias, gain_two = row(output_bias), row(second_gain)
    hid, exg, keep, send, vec_expand = feed_part(
        place, att_t, *tokens, output_weight, out_bias, gain_two, row(second_shift), expand_weight,
        row(expand_bias), reduce_weight, TILE, CHUNK,
    )

    core_hop, plane, line, pair = hops()
    one, two = ([hop] for hop in plane)
    sums = AllSum(keep, send, core_hop)
    result, result_send, mid_grad, att_grad, delta, d_output, vec = sums.beside(
        lambda place: middle_part(
            place, att_t, *tokens, hid, exg, output_weight, out_bias, gain_two, expand_weight,
            reduce_weight, row(reduce_bias), TILE,
        ),
        place, sums.split,
    )
    result_got = swapped(result_send)
    grads = []
    for first, ways in ((0, (one, two)), (H // 2, (two, one))):
        call = lambda table: attend_back(
            first, H // 2, table, q, k, v, att_grad, start, lse, delta, BLOCK
        )
        grads.append(sums.beside(call, table, sums.cross, *ways))
    grads = [[g[n] for g in grads] for n in range(3)]
    keep, send = sums.beside(
        lambda place: weight_part(place, grads, x_got, activations, gain, shift, d_output, span),
        after(place, result_got), sums.narrow, line + pair,
    )
    keep, send = after((keep, send), sums.state)
    tail = AllSum(keep, send, core_hop)
    tail.split()
    ready = after(place, tail.state)
    tail.narrow(plane)
    grad, grad_send, vec_last = last_part(
        ready, grads, x_got, activations, mid_grad, gain, input_weight, TILE
    )
    tail.state = after(tail.state, grad)
    sums.widen(line + pair, vec_last)
    vectors = jnp.concatenate([vec[:4], vec_expand[:4], vec_last], 0).astype(BF)
    sums.uncross(two, one)
    tail.meet(pair)
    tail.ride(vectors, pair)
    grad_got = swapped(after(grad_send, (tail.state, tail.whole)))
    tail.state = after(tail.state, sums.state)
    tail.narrow(line)
    sums.uncross(one, two)
    sums.join()
    tail.widen(line)
    tail.widen(plane)
    part = sums.state[0]
    total = expand_weight.shape[1]
    d_reduce, d_expand = part[:total].astype(F32), beside(part[total:])
    tail.widen(core_hop, (d_reduce, d_expand))
    dw = tail.state[0]
    put = lambda whole, got: lax.dynamic_update_index_in_dim(
        whole, got.astype(whole.dtype), 1 - mine, 0
    )
    vectors = tail.whole.astype(F32)
    return (
        put(result, result_got),
        put(grad, grad_got),
        vectors[8],
        vectors[9],
        beside(dw[: 3 * width]),
        vectors[10],
        vectors[11],
        dw[3 * width :].astype(F32),
        vectors[2],
        vectors[0],
        vectors[1],
        d_expand,
        vectors[4:8].reshape(-1),
        d_reduce,
        vectors[3],
    )


TILE = 512
CHUNK = 256
BLOCK = 512
SMALL = 60.0
FORWARD_HEADS = 4
BACKWARD_HEADS = 4


def solution(mesh):
    sizes = dict(zip(mesh.axis_names, mesh.devices.shape))
    tokens, places, whole = P("dp", "seq", None), P("dp", "seq"), P()
    in_specs = (tokens, places) + (whole,) * 13 + (tokens,)
    out_specs = (tokens, tokens) + (whole,) * 13

    def program(activations, *rest):
        rows = activations.shape[0] // sizes["dp"]
        span = activations.shape[1] // sizes["seq"]
        by_rows = sizes["seq"] == 2 and rows == 2 and span % BLOCK == 0 and sizes["dp"] == 16
        return jax.shard_map(
            local_rows if by_rows else local,
            mesh=mesh,
            in_specs=in_specs,
            out_specs=out_specs,
            check_vma=False,
        )(activations, *rest)

    return program
```

```python
import functools

import jax
import jax.numpy as jnp
from jax import lax
from jax.experimental import pallas as pl
from jax.experimental.pallas import tpu as pltpu
from jax.sharding import PartitionSpec as P

H = 8
HD = 64
DEPTH = 48
MICRO = 2
EPSILON = 1e-05
NEGATIVE = -1e30
BRANCH = DEPTH ** (-0.5)
SCALE = HD ** (-0.5)
SCALE2 = SCALE * 1.4426950408889634
GELU_A = 0.7978845608028654
GELU_B = GELU_A * 0.044715

BF = jnp.bfloat16
F32 = jnp.float32
NN = (((1,), (0,)), ((), ()))
NT = (((1,), (1,)), ((), ()))
VMEM_LIMIT = 58 << 20
SHORT = pl.CostEstimate(flops=1000, bytes_accessed=1000, transcendentals=0)


def mm(left, right, dims=NN):
    return lax.dot_general(left, right, dims, preferred_element_type=F32)


def shape_of(dims, dtype):
    return jax.ShapeDtypeStruct(dims, dtype)


def params(limit=VMEM_LIMIT):
    return pltpu.CompilerParams(vmem_limit_bytes=limit)


def norm_parts(values):
    center = jnp.mean(values, -1, keepdims=True)
    centered = values - center
    variance = jnp.mean(centered * centered, -1, keepdims=True)
    scale = lax.rsqrt(variance + EPSILON)
    return centered * scale, scale


def norm_back(grad, unit, scale, gain):
    inner = grad * gain
    first = jnp.mean(inner, -1, keepdims=True)
    second = jnp.mean(inner * unit, -1, keepdims=True)
    return scale * (inner - first - unit * second)


def own_and_got(tiles):
    part = tiles // 2
    return (
        lambda t, h: (t + (1 - h[0]) * part) % tiles,
        lambda t, h: jnp.minimum(t, part - 1),
        lambda t, h: jnp.maximum(t - part, 0),
    )


def row_specs(tile, width, tiles):
    where, got, own = own_and_got(tiles)
    return (
        pl.BlockSpec((tile, width), lambda t, h: (got(t, h), 0)),
        pl.BlockSpec((1, tile, width), lambda t, h: (h[0], own(t, h), 0)),
    )


def either(got_ref, own_ref):
    early = pl.program_id(0) < pl.num_programs(0) // 2
    return jnp.where(early, got_ref[...], own_ref[0])


def once(array):
    return pl.BlockSpec(array.shape, lambda t, *_: (0,) * array.ndim, pipeline_mode=pl.Buffered(1))


def kept(dims):
    return pl.BlockSpec(dims, lambda t, *_: (0,) * len(dims))


def largest_norms(block):
    lane = lax.broadcasted_iota(jnp.int32, (block.shape[1], 128), 1)
    column = lax.broadcasted_iota(jnp.int32, (block.shape[1], 128), 0)
    member = jnp.where(column // HD == lane, 1.0, 0.0).astype(BF)
    wide = block.astype(F32)
    return jnp.max(mm((wide * wide).astype(BF), member), 0, keepdims=True)


def project_kernel(place, x_ref, gain_ref, shift_ref, weight_ref, bias_ref, *refs):
    q_ref, k_ref, v_ref, norm_ref = refs[-4:]
    width = weight_ref.shape[0]
    unit, _ = norm_parts(x_ref[...].reshape(-1, width).astype(F32))
    normed = (unit * gain_ref[...] + shift_ref[...]).astype(BF)

    @pl.when(pl.program_id(0) == 0)
    def _():
        norm_ref[...] = jnp.zeros(norm_ref.shape, F32)

    for n, ref in enumerate((q_ref, k_ref, v_ref)):
        cols = slice(n * width, (n + 1) * width)
        out = (mm(normed, weight_ref[:, cols]) + bias_ref[:, cols]).astype(BF)
        ref[...] = out
        if n < 2:
            norm_ref[n : n + 1, :] = jnp.maximum(norm_ref[n : n + 1, :], largest_norms(out))


def project(own, half, x, gain, shift, weight, bias, before, tile):
    span, width = x.shape[-2:]
    count = span // tile
    length = 2 * span
    if own:
        x_spec = pl.BlockSpec((1, tile, width), lambda t, h: (h[0], t, 0))
        here = lambda h: h[0]
    else:
        x_spec = pl.BlockSpec((tile, width), lambda t, h: (t, 0))
        here = lambda h: 1 - h[0]
    rows = pl.BlockSpec((tile, width), lambda t, h: (here(h) * count + t, 0))
    nat = shape_of((length, width), BF)
    return pl.pallas_call(
        project_kernel,
        grid_spec=pltpu.PrefetchScalarGridSpec(
            num_scalar_prefetch=1,
            grid=(count,),
            in_specs=[x_spec, once(gain), once(shift), once(weight), once(bias)]
            + [pl.BlockSpec(memory_space=pl.ANY)] * len(before),
            out_specs=[rows, rows, rows, kept((8, 128))],
        ),
        out_shape=[nat, nat, nat, shape_of((8, 128), F32)],
        input_output_aliases={6 + i: i for i in range(len(before))},
        compiler_params=params(),
        name="project",
    )(half, x, gain, shift, weight, bias, *before)


def document_kernel(size, half_ref, own_ref, got_ref, start_ref, table_ref):
    span = own_ref.shape[1]
    place = lambda half: pl.ds(pl.multiple_of(half * span, span), span)
    start_ref[0:1, place(half_ref[0])] = own_ref[...]
    start_ref[0:1, place(1 - half_ref[0])] = got_ref[...]
    numbers = start_ref[...]
    start = jnp.zeros_like(numbers)
    for number in range(1, 8):
        before = jnp.sum((numbers < number).astype(jnp.int32), 1, keepdims=True)
        start = jnp.where(numbers == number, before, start)
    start_ref[...] = start
    count = start.shape[1] // size
    slots = table_ref.shape[0] - 1
    for slot in range(slots):
        table_ref[slot] = 0
    filled = jnp.int32(0)
    for i in range(count):
        block = start[:, i * size : (i + 1) * size]
        low, high = jnp.min(block), jnp.max(block)
        for j in range(i + 1):
            kind = jnp.where(high > j * size, 2, 1 if i == j else 0)
            active = low < (j + 1) * size

            table_ref[filled] = jnp.where(active, i + 256 * j + 65536 * kind, 0)
            filled = filled + active.astype(jnp.int32)
    table_ref[slots] = filled


def documents(half, own, got, size):
    length = 2 * own.shape[1]
    count = length // size
    row = lambda wide: pl.BlockSpec((1, wide), lambda t, h: (0, 0))
    return pl.pallas_call(
        functools.partial(document_kernel, size),
        grid_spec=pltpu.PrefetchScalarGridSpec(
            num_scalar_prefetch=1,
            grid=(1,),
            in_specs=[row(length // 2), row(length // 2)],
            out_specs=[row(length), pl.BlockSpec(memory_space=pltpu.SMEM)],
        ),
        out_shape=[
            shape_of((1, length), jnp.int32),
            shape_of((count * (count + 1) // 2 + 2,), jnp.int32),
        ],
        compiler_params=params(),
        name="documents",
    )(half, own, got)


def head_half(block, head):
    lane = lax.broadcasted_iota(jnp.int32, block.shape, 1)
    keep = (lane < HD) if head % 2 == 0 else (lane >= HD)
    return jnp.where(keep, block, jnp.zeros_like(block))


def lanes_of(heads, group, head):
    low = HD * heads * group + 2 * HD * (head // 2)
    return pl.ds(pl.multiple_of(low, 2 * HD), 2 * HD)


def rows_of(heads, group, head):
    return pl.ds(pl.multiple_of(HD * heads * group + HD * head, HD), HD)


class Blocks:
    def __init__(self, size, list_ref, start_ref, mask_ref, values):
        self.size, self.list = size, list_ref
        self.start, self.mask, self.values = start_ref, mask_ref, values

    def at(self, index):
        return pl.ds(pl.multiple_of(index * self.size, self.size), self.size)

    def places(self):
        dims = (self.size, self.size)
        return lax.broadcasted_iota(jnp.int32, dims, 0), lax.broadcasted_iota(jnp.int32, dims, 1)

    def fill(self, slot, i, j):
        key, query = self.places()
        key, query = key + j * self.size, query + i * self.size
        allowed = (key >= self.start[0:1, self.at(i)]) & (key <= query)
        self.mask[slot] = jnp.where(allowed, *self.values).astype(self.mask.dtype)

    def entry(self, step):
        packed = self.list[step]
        kind = packed // 65536
        return packed % 256, (packed // 256) % 256, jnp.where(kind == 2, 2 + lax.rem(step, 2), kind)

    def prepare(self, slot, i, j):
        pl.when(slot >= 2)(lambda: self.fill(slot, i, j))

    def walk(self, variants, heads, loops, early, late, row_begin, step_end, row_end):
        steps = self.list[self.list.shape[0] - 1]
        self.mask[0] = jnp.full(self.mask.shape[1:], self.values[0], self.mask.dtype)
        key, query = self.places()
        self.mask[1] = jnp.where(key <= query, *self.values).astype(self.mask.dtype)
        i, j, slot = self.entry(0)
        self.prepare(slot, i, j)
        row_begin(i)
        zero = jnp.int32(0)
        early(zero, 0, i, j, slot, False)

        def body(turn, carry):
            i, j, slot = carry
            group = lax.rem(turn, loops)
            last = group == loops - 1
            after = self.entry(turn // loops + 1)
            ni, nj, nslot = (jnp.where(last, new, old) for new, old in zip(after, carry))
            ngroup = jnp.where(last, 0, group + 1)
            pl.when(last)(lambda: self.prepare(nslot, ni, nj))
            pl.when(ni > i)(lambda: row_begin(ni))

            def work(corner, slot):
                for head in range(heads):
                    if head + 1 < heads:
                        early(group, head + 1, i, j, slot, corner)
                    else:
                        early(ngroup, 0, ni, nj, nslot, False)
                    late(group, head, i, j, corner)

            if variants == 1:
                work(False, slot)
            elif variants == 2:
                pl.when(i != j)(lambda: work(False, slot))
                pl.when(i == j)(lambda: work(True, slot))
            else:
                pl.when(slot == 0)(lambda: work(False, None))
                pl.when((slot > 0) & (i == j))(lambda: work(True, slot))
                pl.when((slot > 0) & (i != j))(lambda: work(False, slot))

            @pl.when(last)
            def _():
                step_end(i, j)
                pl.when(j == i)(lambda: row_end(i))

            return ni, nj, nslot

        lax.fori_loop(0, steps * loops, body, (i, j, slot))


def pieces(corner, size):
    if not corner:
        return [(slice(0, size), slice(0, size))]
    mid = size // 2
    return [(slice(0, mid), slice(0, size)), (slice(mid, size), slice(mid, size))]


def part_at(size, index, part):
    low = index * size + part.start
    return pl.ds(pl.multiple_of(low, size // 2), part.stop - part.start)


class Blockwise:
    def __init__(self, size, first, source, target, sems):
        self.size, self.first = size, first
        self.source, self.target, self.sems = source, target, sems

    def copy(self, block):
        rows = pl.ds(pl.multiple_of(block * self.size, self.size), self.size)
        lanes = pl.ds(self.first, self.target.shape[1])
        return pltpu.make_async_copy(
            self.source.at[rows, lanes], self.target.at[rows, :], self.sems.at[block]
        )


def forward_kernel(
    size, list_ref, q_hbm, k_hbm, v_hbm, start_ref, one_ref, two_ref, out_hbm, lse_ref, q_ref, k_ref, v_ref,
    vt_ref, stage_ref, in_sems, out_sems, max_ref, new_ref, acc_ref, bias_ref, mask_ref, *slots,
):
    heads = FORWARD_HEADS
    loops = H // heads
    scores, probs_of = slots[:heads], slots[heads:]
    plain = Blocks(size, list_ref, start_ref, mask_ref, (1.0, 0.0))
    general = Blocks(size, list_ref, start_ref, bias_ref, (0.0, NEGATIVE))
    at = plain.at
    count = q_ref.shape[0] // size
    loads = [
        Blockwise(size, 0, source, target, in_sems.at[n])
        for n, (source, target) in enumerate(((k_hbm, k_ref), (q_hbm, q_ref), (v_hbm, v_ref)))
    ]
    for block in range(count):
        for load in loads:
            load.copy(block).start()

    def store(i):
        cols = pl.ds(pl.multiple_of(i * size, size), size)
        return pltpu.make_async_copy(stage_ref.at[:, cols], out_hbm.at[:, cols], out_sems.at[i])

    def row_begin(i):
        for load in loads:
            load.copy(i).wait()
        vt_ref[:, at(i)] = v_ref[at(i), :].T

    def products(group, head, i, j, keys, queries):
        lanes = lanes_of(heads, group, head)
        block = head_half(k_ref[part_at(size, j, keys), lanes], head)
        return mm(block, q_ref[part_at(size, i, queries), lanes], NT)

    def values(group, head, j, keys):
        block = vt_ref[rows_of(heads, group, head), part_at(size, j, keys)]
        return jnp.concatenate([block, jnp.ones((16, keys.stop - keys.start), BF)], 0)

    def early_plain(group, head, i, j, slot, corner):
        for keys, queries in pieces(corner, size):
            probs = jnp.exp2(products(group, head, i, j, keys, queries) * SCALE2).astype(BF)
            if slot is not None:
                probs = probs * mask_ref[slot, keys, queries]
            probs_of[head][keys, queries] = probs

    def late_plain(group, head, i, j, corner):
        for keys, queries in pieces(corner, size):
            acc_ref[heads * group + head, :, queries] += mm(values(group, head, j, keys), probs_of[head][keys, queries])

    whole = slice(0, size)

    def early(group, head, i, j, slot, corner):
        s = products(group, head, i, j, whole, whole)
        if slot is not None:
            s = s + bias_ref[slot]
        scores[head][...] = s
        new_ref[heads * group + head] = jnp.max(s, 0, keepdims=True)

    def late(group, head, i, j, corner):
        place = heads * group + head
        old = max_ref[place]
        new = jnp.maximum(old, new_ref[place])
        max_ref[place] = new
        probs = jnp.exp2(scores[head][...] * SCALE2 - new * SCALE2)
        factor = jnp.exp2((old - new) * SCALE2)
        acc_ref[place] = acc_ref[place] * factor + mm(
            values(group, head, j, whole), probs.astype(BF)
        )

    def reset(largest):
        max_ref[...] = jnp.full(max_ref.shape, largest, F32)
        acc_ref[...] = jnp.zeros(acc_ref.shape, F32)

    def row_end(largest, i):
        def one(head, carry):
            total = acc_ref[head, HD : HD + 1, :]
            rows = pl.ds(pl.multiple_of(HD * head, HD), HD)
            stage_ref[rows, at(i)] = (acc_ref[head, :HD, :] * (1.0 / total)).astype(BF)
            lse_ref[head, :, at(i)] = max_ref[head] * SCALE2 + jnp.log2(total)
            return carry

        lax.fori_loop(0, H, one, 0)
        store(i).start()
        reset(largest)

    def run(variants, blocks, largest, early, late):
        reset(largest)
        blocks.walk(
            variants, heads, loops, early, late, row_begin, lambda i, j: None, functools.partial(row_end, largest)
        )

    norms = jnp.maximum(one_ref[...], two_ref[...])
    limit = jnp.max(norms[0:1] * norms[1:2]) * (SCALE2 * SCALE2)
    small = limit < SMALL * SMALL
    pl.when(small)(lambda: run(2, plain, 0.0, early_plain, late_plain))
    pl.when(jnp.logical_not(small))(lambda: run(1, general, NEGATIVE, early, late))
    for i in range(count):
        store(i).wait()


def attend(table, q, k, v, start, norms, more, size):
    length, width = q.shape
    count = length // size
    far = pl.BlockSpec(memory_space=pl.ANY)
    near = pltpu.VMEM((length, width), BF)
    return pl.pallas_call(
        functools.partial(forward_kernel, size),
        grid_spec=pltpu.PrefetchScalarGridSpec(
            num_scalar_prefetch=1,
            grid=(1,),
            in_specs=[far, far, far, once(start), once(norms), once(more)],
            out_specs=[far, kept((H, 1, length))],
            scratch_shapes=[
                near,
                near,
                near,
                pltpu.VMEM((width, length), BF),
                pltpu.VMEM((width, length), BF),
                pltpu.SemaphoreType.DMA((3, count)),
                pltpu.SemaphoreType.DMA((count,)),
                pltpu.VMEM((H, 1, size), F32),
                pltpu.VMEM((H, 1, size), F32),
                pltpu.VMEM((H, HD + 16, size), F32),
                pltpu.VMEM((4, size, size), F32),
                pltpu.VMEM((4, size, size), BF),
            ]
            + [pltpu.VMEM((size, size), F32)] * FORWARD_HEADS
            + [pltpu.VMEM((size, size), BF)] * FORWARD_HEADS,
        ),
        out_shape=[shape_of((width, length), BF), shape_of((H, 1, length), F32)],
        compiler_params=params(),
        name="attend",
    )(table, q, k, v, start, norms, more)


def backward_kernel(
    size, heads, loops, first, list_ref, q_hbm, k_hbm, v_hbm, do_hbm, start_ref, lse_ref, delta_ref,
    dq_hbm, dk_hbm, dv_hbm, q_ref, k_ref, v_ref, do_ref, kt_ref, dq_ref, dk_ref, dv_ref, in_sems,
    out_sems, dqt_acc, dk_acc, dv_acc, bias_ref, *slots,
):
    probs_of, grads_of = slots[:heads], slots[heads:]
    walk = Blocks(size, list_ref, start_ref, bias_ref, (0.0, NEGATIVE))
    at = walk.at
    count = q_ref.shape[0] // size
    pairs = ((k_hbm, k_ref), (q_hbm, q_ref), (v_hbm, v_ref), (do_hbm, do_ref))
    loads = [
        Blockwise(size, first * HD, source, target, in_sems.at[n])
        for n, (source, target) in enumerate(pairs)
    ]
    for block in range(count):
        for load in loads:
            load.copy(block).start()

    def store(n, block):
        source, target = ((dq_ref, dq_hbm), (dk_ref, dk_hbm), (dv_ref, dv_hbm))[n]
        rows = at(block)
        return pltpu.make_async_copy(
            source.at[rows, :], target.at[rows, :], out_sems.at[n, block]
        )

    def row_begin(i):
        for load in loads:
            load.copy(i).wait()
        kt_ref[:, at(i)] = k_ref[at(i), :].T
        dk_acc[at(i), :] = jnp.zeros((size, dk_acc.shape[1]), F32)
        dv_acc[at(i), :] = jnp.zeros((size, dv_acc.shape[1]), F32)

    def early(group, head, i, j, slot, corner):
        lanes = lanes_of(heads, group, head)
        for keys, queries in pieces(corner, size):
            at_j, at_i = part_at(size, j, keys), part_at(size, i, queries)
            stat = (first + heads * group + head, slice(None), at_i)
            s = mm(head_half(k_ref[at_j, lanes], head), q_ref[at_i, lanes], NT)
            dots = mm(head_half(v_ref[at_j, lanes], head), do_ref[at_i, lanes], NT)
            if slot is not None:
                s = s + bias_ref[slot, keys, queries]
            probs = jnp.exp2(s * SCALE2 - lse_ref[stat])
            probs_of[head][keys, queries] = probs.astype(BF)
            grads_of[head][keys, queries] = (probs * (dots - delta_ref[stat])).astype(BF)

    def late(group, head, i, j, corner):
        lanes = lanes_of(heads, group, head)
        rows = rows_of(heads, group, head)
        for keys, queries in pieces(corner, size):
            at_j, at_i = part_at(size, j, keys), part_at(size, i, queries)
            grads = grads_of[head][keys, queries]
            dv_acc[at_j, lanes] += mm(
                probs_of[head][keys, queries], head_half(do_ref[at_i, lanes], head)
            )
            dk_acc[at_j, lanes] += mm(grads, head_half(q_ref[at_i, lanes], head))
            dqt_acc[rows, queries] += mm(kt_ref[rows, at_j], grads)

    def finish(j):
        dk_ref[at(j), :] = (dk_acc[at(j), :] * SCALE).astype(BF)
        dv_ref[at(j), :] = dv_acc[at(j), :].astype(BF)
        store(1, j).start()
        store(2, j).start()

    def step_end(i, j):
        pl.when(i == count - 1)(lambda: finish(j))

    def row_end(i):
        dq_ref[at(i), :] = (dqt_acc[...] * SCALE).T.astype(BF)
        store(0, i).start()
        dqt_acc[...] = jnp.zeros(dqt_acc.shape, F32)

    dqt_acc[...] = jnp.zeros(dqt_acc.shape, F32)
    walk.walk(3, heads, loops, early, late, row_begin, step_end, row_end)
    lowest = jnp.int32(count)
    for slot in range(list_ref.shape[0] - 1):
        lowest = lowest - jnp.where(list_ref[slot] % 256 == count - 1, 1, 0)
    for j in range(count):
        pl.when(j < lowest)(functools.partial(finish, j))
    for j in range(count):
        for n in range(3):
            store(n, j).wait()


def attend_back(first, groups, table, q, k, v, do, start, lse, delta, size):
    length = q.shape[0]
    part = HD * groups
    count = length // size
    far = pl.BlockSpec(memory_space=pl.ANY)
    near = pltpu.VMEM((length, part), BF)
    pairs = count * (count + 1) // 2 * size * size * groups
    return pl.pallas_call(
        functools.partial(backward_kernel, size, BACKWARD_HEADS, groups // BACKWARD_HEADS, first),
        cost_estimate=SHORT,
        grid_spec=pltpu.PrefetchScalarGridSpec(
            num_scalar_prefetch=1,
            grid=(1,),
            in_specs=[far] * 4 + [once(start), once(lse), once(delta)],
            out_specs=[far] * 3,
            scratch_shapes=[near] * 4
            + [pltpu.VMEM((part, length), BF)]
            + [near] * 3
            + [
                pltpu.SemaphoreType.DMA((4, count)),
                pltpu.SemaphoreType.DMA((3, count)),
                pltpu.VMEM((part, size), F32),
                pltpu.VMEM((length, part), F32),
                pltpu.VMEM((length, part), F32),
                pltpu.VMEM((4, size, size), F32),
            ]
            + [pltpu.VMEM((size, size), BF)] * (2 * BACKWARD_HEADS),
        ),
        out_shape=[shape_of((length, part), BF)] * 3,
        compiler_params=params(),
        name="attend_back",
    )(table, q, k, v, do, start, lse, delta)


def feed_kernel(
    chunk, place_ref, att_ref, x_got, x_own, cot_got, cot_own, wo_ref, ob_ref, g2_ref, s2_ref, we_ref,
    eb_ref, wr_ref, hid_ref, exg_ref, keep_ref, send_ref, deb_ref, acc_ref, deb_acc, wet_ref, ebt_ref,
):
    step = pl.program_id(0)
    tile, width = x_got.shape
    total = wr_ref.shape[0]

    @pl.when(step == 0)
    def _():
        for ref in (acc_ref, deb_acc):
            ref[...] = jnp.zeros(ref.shape, F32)
        wet_ref[...] = we_ref[...].T
        ebt_ref[...] = jnp.broadcast_to(eb_ref[...], (128, total)).T

    mixed = mm(att_ref[...].T, wo_ref[...]) + ob_ref[...]
    middle = either(x_got, x_own).astype(F32) + BRANCH * mixed
    unit, _ = norm_parts(middle)
    second = (unit * g2_ref[...] + s2_ref[...]).astype(BF)
    second_t = second.T
    reduced_grad = (BRANCH * either(cot_got, cot_own).astype(F32)).astype(BF)

    def stage_one(c):
        rows = slice(c * chunk, (c + 1) * chunk)
        bias = jnp.concatenate([ebt_ref[rows, :]] * (tile // 128), 1)
        v = mm(wet_ref[rows, :], second, NT) + bias
        v2 = v * v
        t = jnp.tanh(v * (GELU_A + GELU_B * v2))
        h1 = 0.5 * t + 0.5
        gelu = v * h1
        slope = h1 + gelu * (1.0 - h1) * (2.0 * GELU_A + 6.0 * GELU_B * v2)
        hid_ref[rows, :] = gelu.astype(BF)
        grads = (mm(wr_ref[rows, :], reduced_grad, NT) * slope).astype(BF)
        exg_ref[rows, :] = grads
        wide = grads.astype(F32)
        part = wide[:, 0:128]
        for n in range(1, tile // 128):
            part = part + wide[:, n * 128 : (n + 1) * 128]
        deb_acc[rows, :] += part

    stage_one(0)
    for c in range(total // chunk):
        if (c + 1) * chunk < total:
            stage_one(c + 1)
        rows = slice(c * chunk, (c + 1) * chunk)
        acc_ref[rows, :] += mm(hid_ref[rows, :], reduced_grad)
        block, low = divmod(c * chunk, width)
        there = slice(total + block * width, total + (block + 1) * width)
        acc_ref[there, low : low + chunk] += mm(second_t, exg_ref[rows, :], NT)

    last = step == pl.num_programs(0) - 1
    halves = slice(0, total), slice(total, 2 * total)
    for core in range(2):

        @pl.when(last & (place_ref[1] == core))
        def _():
            keep_ref[...] = acc_ref[halves[core], :].astype(BF)
            send_ref[...] = acc_ref[halves[1 - core], :].astype(BF)

    @pl.when(last)
    def _():
        flat = jnp.sum(deb_acc[...].T, 0, keepdims=True)
        deb_ref[...] = jnp.zeros(deb_ref.shape, F32)
        for n in range(total // width):
            deb_ref[n : n + 1, :] = flat[:, n * width : (n + 1) * width]


def feed_part(place, att_t, x_got, x_own, cot_got, cot_own, wo, ob, g2, s2, we, eb, wr, tile, chunk):
    width, length = att_t.shape
    total = wr.shape[0]
    tiles = length // tile
    where, _, _ = own_and_got(tiles)
    pair = list(row_specs(tile, width, tiles))
    cols = lambda high: pl.BlockSpec((high, tile), lambda t, h: (0, where(t, h)))
    return pl.pallas_call(
        functools.partial(feed_kernel, chunk),
        grid_spec=pltpu.PrefetchScalarGridSpec(
            num_scalar_prefetch=1,
            grid=(tiles,),
            in_specs=[cols(width)] + pair * 2 + [once(a) for a in (wo, ob, g2, s2, we, eb, wr)],
            out_specs=[cols(total), cols(total), kept((total, width)), kept((total, width)), kept((8, width))],
            scratch_shapes=[
                pltpu.VMEM((2 * total, width), F32),
                pltpu.VMEM((total, 128), F32),
                pltpu.VMEM((total, width), BF),
                pltpu.VMEM((total, 128), F32),
            ],
        ),
        out_shape=[
            shape_of((total, length), BF),
            shape_of((total, length), BF),
            shape_of((total, width), BF),
            shape_of((total, width), BF),
            shape_of((8, width), F32),
        ],
        compiler_params=params(),
        name="feed",
    )(place, att_t, x_got, x_own, cot_got, cot_own, wo, ob, g2, s2, we, eb, wr)


def middle_kernel(
    place_ref, att_ref, x_got, x_own, cot_got, cot_own, hid_ref, exg_ref, wo_ref, ob_ref, g2_ref,
    we_ref, wr_ref, rb_ref, res_own, res_send, grad_ref, ag_ref, delta_ref, dwo_ref, vec_ref, acc_ref,
    wrt_ref,
):
    step = pl.program_id(0)
    tiles = pl.num_programs(0)

    @pl.when(step == 0)
    def _():
        for ref in (acc_ref, vec_ref):
            ref[...] = jnp.zeros(ref.shape, F32)
        wrt_ref[...] = wr_ref[...].T

    att_t = att_ref[...]
    mixed = mm(att_t.T, wo_ref[...]) + ob_ref[...]
    middle = either(x_got, x_own).astype(F32) + BRANCH * mixed
    cot = either(cot_got, cot_own).astype(F32)
    unit, scale = norm_parts(middle)
    norm_grad = mm(we_ref[...], exg_ref[...]).T
    result = (middle + BRANCH * (mm(wrt_ref[...], hid_ref[...]).T + rb_ref[...])).astype(BF)

    @pl.when(step < tiles // 2)
    def _():
        res_send[...] = result

    @pl.when(step >= tiles // 2)
    def _():
        res_own[0] = result

    middle_grad = cot + norm_back(norm_grad, unit, scale, g2_ref[...])
    grad_ref[...] = middle_grad
    mixed_grad = (BRANCH * middle_grad).astype(BF)
    acc_ref[...] += mm(att_t, mixed_grad)
    att_grad = mm(mixed_grad, wo_ref[...], NT).astype(BF)
    ag_ref[...] = att_grad
    dots = att_grad.T.astype(F32) * att_t.astype(F32)
    for head in range(H):
        delta_ref[head] = jnp.sum(dots[HD * head : HD * head + HD, :], 0, keepdims=True)
    reduced_grad = (BRANCH * cot).astype(BF)
    sums = (norm_grad * unit, norm_grad, mixed_grad.astype(F32), reduced_grad.astype(F32))
    for n, value in enumerate(sums):
        vec_ref[n : n + 1, :] += jnp.sum(value, 0, keepdims=True)

    @pl.when(step == tiles - 1)
    def _():
        dwo_ref[...] = acc_ref[...].astype(BF)


def middle_part(place, att_t, x_got, x_own, cot_got, cot_own, hid, exg, wo, ob, g2, we, wr, rb, tile):
    width, length = att_t.shape
    total = wr.shape[0]
    tiles = length // tile
    where, got, own = own_and_got(tiles)
    pair = list(row_specs(tile, width, tiles))
    rows = pl.BlockSpec((tile, width), lambda t, h: (where(t, h), 0))
    cols = lambda high: pl.BlockSpec((high, tile), lambda t, h: (0, where(t, h)))
    return pl.pallas_call(
        middle_kernel,
        cost_estimate=SHORT,
        grid_spec=pltpu.PrefetchScalarGridSpec(
            num_scalar_prefetch=1,
            grid=(tiles,),
            in_specs=[cols(width)]
            + pair * 2
            + [cols(total), cols(total)]
            + [once(a) for a in (wo, ob, g2, we, wr, rb)],
            out_specs=[
                pair[1],
                pair[0],
                rows,
                rows,
                pl.BlockSpec((H, 1, tile), lambda t, h: (0, 0, where(t, h))),
                kept((width, width)),
                kept((8, width)),
            ],
            scratch_shapes=[pltpu.VMEM((width, width), F32), pltpu.VMEM((width, total), BF)],
        ),
        out_shape=[
            shape_of((2, length // 2, width), BF),
            shape_of((length // 2, width), BF),
            shape_of((length, width), F32),
            shape_of((length, width), BF),
            shape_of((H, 1, length), F32),
            shape_of((width, width), BF),
            shape_of((8, width), F32),
        ],
        compiler_params=params(),
        name="middle",
    )(place, att_t, x_got, x_own, cot_got, cot_own, hid, exg, wo, ob, g2, we, wr, rb)


def weight_kernel(parts, place_ref, *refs):
    ins = refs[: 3 * parts]
    x_got, x_own, gain_ref, shift_ref, extra_ref, keep_ref, send_ref, acc_ref = refs[3 * parts :]
    step = pl.program_id(0)

    @pl.when(step == 0)
    def _():
        acc_ref[...] = jnp.zeros(acc_ref.shape, F32)

    width = x_got.shape[1]
    unit, _ = norm_parts(either(x_got, x_own).astype(F32))
    normed_t = (unit * gain_ref[...] + shift_ref[...]).astype(BF).T
    for n in range(3):
        grad = jnp.concatenate([ref[...] for ref in ins[n * parts : (n + 1) * parts]], 1)
        acc_ref[n * width : (n + 1) * width, :] += mm(normed_t, grad)

    last = step == pl.num_programs(0) - 1
    for core in range(2):

        @pl.when(last & (place_ref[1] == core))
        def _():
            lower, upper = (keep_ref, send_ref) if core == 0 else (send_ref, keep_ref)
            lower[...] = acc_ref[: 2 * width, :].astype(BF)
            upper[:width, :] = acc_ref[2 * width :, :].astype(BF)
            upper[width:, :] = extra_ref[...]


def weight_part(place, grads, x_got, x_own, gain, shift, extra, tile):
    span, width = x_got.shape
    tiles = 2 * span // tile
    where, _, _ = own_and_got(tiles)
    flat = [part for group in grads for part in group]
    out = shape_of((2 * width, width), BF)
    return pl.pallas_call(
        functools.partial(weight_kernel, len(grads[0])),
        cost_estimate=SHORT,
        grid_spec=pltpu.PrefetchScalarGridSpec(
            num_scalar_prefetch=1,
            grid=(tiles,),
            in_specs=[
                pl.BlockSpec((tile, a.shape[1]), lambda t, h: (where(t, h), 0)) for a in flat
            ]
            + list(row_specs(tile, width, tiles))
            + [once(a) for a in (gain, shift, extra)],
            out_specs=[kept(out.shape)] * 2,
            scratch_shapes=[pltpu.VMEM((3 * width, width), F32)],
        ),
        out_shape=[out, out],
        compiler_params=params(),
        name="weight",
    )(place, *flat, x_got, x_own, gain, shift, extra)


def last_kernel(parts, place_ref, *refs):
    ins, rest = refs[: 3 * parts], refs[3 * parts :]
    x_got, x_own, mid_ref, gain_ref, weight_ref, own_ref, send_ref, vec_ref = rest
    step = pl.program_id(0)
    tiles = pl.num_programs(0)

    @pl.when(step == 0)
    def _():
        vec_ref[...] = jnp.zeros(vec_ref.shape, F32)

    width = x_got.shape[1]
    unit, scale = norm_parts(either(x_got, x_own).astype(F32))
    back = None
    grads = []
    for n in range(3):
        grad = jnp.concatenate([ref[...] for ref in ins[n * parts : (n + 1) * parts]], 1)
        one = mm(grad, weight_ref[:, n * width : (n + 1) * width], NT)
        back = one if back is None else back + one
        grads.append(grad)
    total = mid_ref[...] + norm_back(back, unit, scale, gain_ref[...])

    @pl.when(step < tiles // 2)
    def _():
        send_ref[...] = total.astype(BF)

    @pl.when(step >= tiles // 2)
    def _():
        own_ref[0] = total

    sums = (back * unit, back, grads[0].astype(F32), grads[2].astype(F32))
    for n, value in enumerate(sums):
        vec_ref[n : n + 1, :] += jnp.sum(value, 0, keepdims=True)


def last_part(place, grads, x_got, x_own, mid, gain, weight, tile):
    length, width = mid.shape
    tiles = length // tile
    where, _, _ = own_and_got(tiles)
    rows = pl.BlockSpec((tile, width), lambda t, h: (where(t, h), 0))
    flat = [part for group in grads for part in group]
    pair = list(row_specs(tile, width, tiles))
    return pl.pallas_call(
        functools.partial(last_kernel, len(grads[0])),
        cost_estimate=SHORT,
        grid_spec=pltpu.PrefetchScalarGridSpec(
            num_scalar_prefetch=1,
            grid=(tiles,),
            in_specs=[
                pl.BlockSpec((tile, a.shape[1]), lambda t, h: (where(t, h), 0)) for a in flat
            ]
            + pair
            + [rows, once(gain), once(weight)],
            out_specs=[pair[1], pair[0], kept((8, width))],
        ),
        out_shape=[
            shape_of((2, length // 2, width), F32),
            shape_of((length // 2, width), BF),
            shape_of((8, width), F32),
        ],
        compiler_params=params(),
        name="last",
    )(place, *flat, x_got, x_own, mid, gain, weight)


def swapped(value):
    return lax.ppermute(value, "seq", [(0, 1), (1, 0)])


def side(hop):
    axis, bit = hop
    return (lax.axis_index(axis) // bit) % 2


def place_of(hops):
    place = 0
    for hop in hops:
        place = 2 * place + side(hop)
    return place


def exchanged(value, hops):
    axes = tuple(dict.fromkeys(axis for axis, _ in hops))
    flips = [sum(bit for axis, bit in hops if axis == name) for name in axes]
    sizes = [lax.axis_size(name) for name in axes]
    if len(axes) == 1:
        return lax.ppermute(value, axes[0], [(i, i ^ flips[0]) for i in range(sizes[0])])
    pairs = [
        (i * sizes[1] + j, (i ^ flips[0]) * sizes[1] + (j ^ flips[1]))
        for i in range(sizes[0])
        for j in range(sizes[1])
    ]
    return lax.ppermute(value, axes, pairs)


def partners(hops):
    count = len(hops)
    return [
        ([hop for n, hop in enumerate(hops) if (flip >> (count - 1 - n)) & 1], flip)
        for flip in range(1, 1 << count)
    ]


def added(*values):
    total = values[0].astype(F32)
    for value in values[1:]:
        total = total + value.astype(F32)
    return total.astype(BF)


def scatter(part, hops):
    rows = part.shape[1] >> len(hops)
    mine = place_of(hops)
    piece = lambda place: lax.dynamic_slice_in_dim(part, place * rows, rows, 1)
    got = [exchanged(piece(mine ^ flip), chosen) for chosen, flip in partners(hops)]
    return added(piece(mine), *got)


def gather(part, hops, whole=None, first=()):
    mine = place_of(hops)
    blocks, rows, width = part.shape
    got, others = [(part, mine)], []
    for chosen, flip in partners(hops):
        if whole is None:
            got.append((after(exchanged(part, chosen), first), mine ^ flip))
            continue
        both = exchanged(jnp.concatenate([part.reshape(-1, width), whole], 0), chosen)
        both = after(both, first)
        got.append((both[: blocks * rows].reshape(part.shape), mine ^ flip))
        others.append(both[blocks * rows :])
    if len(hops) == 1:
        one, two = got[0][0], got[1][0]
        out = jnp.where(mine == 0, jnp.concatenate([one, two], 1), jnp.concatenate([two, one], 1))
    else:
        out = jnp.zeros((blocks, rows << len(hops), width), part.dtype)
        for piece, place in got:
            out = lax.dynamic_update_slice_in_dim(out, piece, place * rows, 1)
    return out if whole is None else (out, added(whole, *others))


def hops():
    found = []
    for axis in ("dp", "seq"):
        size = lax.axis_size(axis)
        found.append([(axis, 1 << n) for n in range(size.bit_length() - 1)])
    core, one, two, far = found[0]
    return [core], [one, two], [far], found[1]


class AllSum:
    def __init__(self, keep, send, core):
        self.core, self.whole = core, None
        self.state = (keep[None], send[None])

    def split(self):
        keep, send = self.state
        self.state = added(keep, exchanged(send, self.core))

    def cross(self, one, two):
        if not isinstance(self.state, tuple):
            mid = self.state.shape[1] // 2
            self.state = (self.state[:, :mid], self.state[:, mid:])
        self.state = tuple(scatter(part, hops) for part, hops in zip(self.state, (one, two)))

    def uncross(self, one, two):
        if not isinstance(self.state, tuple):
            self.state = (self.state[:1], self.state[1:])
        self.state = tuple(gather(part, hops) for part, hops in zip(self.state, (one, two)))

    def join(self):
        part = jnp.concatenate(self.state, 1)
        got = exchanged(part, self.core)
        lower = place_of(self.core) == 0
        return jnp.where(lower, part, got)[0], jnp.where(lower, got, part)[0]

    def ride(self, whole, hops):
        self.whole = added(whole, exchanged(whole, hops))

    def narrow(self, hops):
        if isinstance(self.state, tuple):
            self.state = jnp.concatenate(self.state, 0)
        self.state = scatter(self.state, hops)

    def meet(self, hops):
        self.state = added(self.state, exchanged(self.state, hops))

    def widen(self, hops, first=()):
        if self.whole is None:
            self.state = gather(self.state, hops, None, first)
        else:
            self.state, self.whole = gather(self.state, hops, self.whole, first)

    def beside(self, call, argument, step, *hops):
        argument = after(argument, self.state)
        step(*hops)
        out = call(argument)
        self.state = after(self.state, out)
        return out


def after(value, earlier):
    return lax.optimization_barrier((value, earlier))[0] if jax.tree.leaves(earlier) else value


def passed_along(block, axis, distance):
    devices = range(lax.axis_size(axis))
    route = [(i - distance, i) for i in devices if i - distance in devices]
    return lax.ppermute(block, axis, route)


def from_behind(value, axis, steps):
    count = lax.axis_size(axis)
    pairs = [(source, (source + steps) % count) for source in range(count)]
    return lax.ppermute(value, axis, pairs)


def layer_norm(values, gain_vec, shift_vec):
    center = jnp.mean(values, -1, keepdims=True)
    centered = values - center
    variance = jnp.mean(centered * centered, -1, keepdims=True)
    return centered * lax.rsqrt(variance + EPSILON) * gain_vec + shift_vec


def gelu_tanh(values):
    return jax.nn.gelu(values, approximate=True)


def plain_dot(left, right):
    return jnp.dot(left, right, preferred_element_type=jnp.float32)


def left_dot(left, right):
    return lax.dot_general(
        left, right, (((0,), (0,)), ((), ())), preferred_element_type=jnp.float32
    )


def right_dot(left, right):
    return lax.dot_general(
        left, right, (((1,), (1,)), ((), ())), preferred_element_type=jnp.float32
    )


def block_scores(queries, keys_block, query_seg, key_seg, query_places, key_start):
    row_count, key_len, width = keys_block.shape
    keys_heads = keys_block.reshape(row_count, key_len, H, HD)
    scores = jnp.einsum(
        "rqhd,rkhd->rhqk", queries, keys_heads, preferred_element_type=jnp.float32
    ) * HD ** (-0.5)
    key_places = key_start + jnp.arange(key_len, dtype=jnp.int32)
    allowed = (query_seg[:, None, :, None] == key_seg[:, None, None, :]) & (
        key_places[None, None, None, :] <= query_places[None, None, :, None]
    )
    return (scores, allowed)


def attend_block(state, queries, block, query_seg, query_places, key_start):
    run_max, run_sum, running = state
    keys_block, values_block, key_seg = block
    row_count, key_len, width = values_block.shape
    query_len = queries.shape[1]
    scores, allowed = block_scores(queries, keys_block, query_seg, key_seg, query_places, key_start)
    block_max = jnp.max(jnp.where(allowed, scores, NEGATIVE), -1)
    new_max = jnp.maximum(run_max, block_max)
    exponent = jnp.where(allowed, jnp.exp(scores - new_max[..., None]), 0.0)
    factor = jnp.exp(run_max - new_max)
    new_sum = run_sum * factor + jnp.sum(exponent, -1)
    values_heads = values_block.reshape(row_count, key_len, H, HD)
    addition = jnp.einsum(
        "rhqk,rkhd->rqhd",
        exponent.astype(jnp.bfloat16),
        values_heads,
        preferred_element_type=jnp.float32,
    )
    scaled = (
        running.reshape(row_count, query_len, H, HD) * jnp.transpose(factor, (0, 2, 1))[..., None]
    )
    return (new_max, new_sum, (scaled + addition).reshape(row_count, query_len, width))


def grad_block(queries, out_grad, log_sum, delta, block, query_seg, query_places, key_start):
    keys_block, values_block, key_seg = block
    row_count, key_len, width = keys_block.shape
    scores, allowed = block_scores(queries, keys_block, query_seg, key_seg, query_places, key_start)
    weights_block = jnp.where(allowed, jnp.exp(scores - log_sum[..., None]), 0.0)
    keys_heads = keys_block.reshape(row_count, key_len, H, HD)
    values_heads = values_block.reshape(row_count, key_len, H, HD)
    value_dots = jnp.einsum(
        "rqhd,rkhd->rhqk", out_grad, values_heads, preferred_element_type=jnp.float32
    )
    score_grad = (weights_block * (value_dots - delta[..., None]) * HD ** (-0.5)).astype(
        jnp.bfloat16
    )
    query_part = jnp.einsum(
        "rhqk,rkhd->rqhd", score_grad, keys_heads, preferred_element_type=jnp.float32
    ).reshape(row_count, -1, width)
    key_part = jnp.einsum(
        "rhqk,rqhd->rkhd", score_grad, queries, preferred_element_type=jnp.float32
    ).reshape(row_count, key_len, width)
    value_part = jnp.einsum(
        "rhqk,rqhd->rkhd",
        weights_block.astype(jnp.bfloat16),
        out_grad,
        preferred_element_type=jnp.float32,
    ).reshape(row_count, key_len, width)
    return (query_part, key_part, value_part)


def local(
    activations,
    segments,
    first_gain,
    first_shift,
    input_weight,
    query_bias,
    value_bias,
    output_weight,
    output_bias,
    second_gain,
    second_shift,
    expand_weight,
    expand_bias,
    reduce_weight,
    reduce_bias,
    cotangent,
):
    row_total, span_len, width = activations.shape
    cycle_size = lax.axis_size("seq")
    position = lax.axis_index("seq")
    micro_rows = row_total // MICRO
    branch = DEPTH ** (-0.5)
    bias_all = jnp.concatenate([query_bias, jnp.zeros_like(query_bias), value_bias])
    query_places = position * span_len + jnp.arange(span_len, dtype=jnp.int32)
    totals = [
        jnp.zeros(argument.shape, jnp.float32)
        for argument in (
            first_gain,
            first_shift,
            input_weight,
            query_bias,
            value_bias,
            output_weight,
            output_bias,
            second_gain,
            second_shift,
            expand_weight,
            expand_bias,
            reduce_weight,
            reduce_bias,
        )
    ]
    outputs_list = []
    grads_list = []
    for micro in range(MICRO):
        lower = micro * micro_rows
        values_in = activations[lower : lower + micro_rows].astype(jnp.float32)
        query_seg = segments[lower : lower + micro_rows]
        out_cot = cotangent[lower : lower + micro_rows].astype(jnp.float32)
        normed, first_pull = jax.vjp(layer_norm, values_in, first_gain, first_shift)
        normed_low = normed.astype(jnp.bfloat16).reshape(-1, width)
        projected = (plain_dot(normed_low, input_weight) + bias_all).astype(jnp.bfloat16)
        queries = projected[:, :width].reshape(micro_rows, span_len, H, HD)
        keys_own = projected[:, width : 2 * width].reshape(micro_rows, span_len, width)
        values_own = projected[:, 2 * width :].reshape(micro_rows, span_len, width)
        own_block = (keys_own, values_own, query_seg)
        start_state = (
            jnp.full((micro_rows, H, span_len), NEGATIVE, jnp.float32),
            jnp.zeros((micro_rows, H, span_len), jnp.float32),
            jnp.zeros((micro_rows, span_len, width), jnp.float32),
        )
        state = attend_block(
            start_state, queries, own_block, query_seg, query_places, position * span_len
        )

        def cycle_forward(step_index, carry):
            block, inner_state = carry
            block = passed_along((block[0], block[1], block[2]), "seq", 1)
            source = (position - step_index) % cycle_size
            inner_state = lax.cond(
                source < position,
                lambda current: attend_block(
                    current, queries, block, query_seg, query_places, source * span_len
                ),
                lambda current: current,
                inner_state,
            )
            return (block, inner_state)

        unused_block, state = lax.fori_loop(1, cycle_size, cycle_forward, (own_block, state))
        run_max, run_sum, running = state
        attended = (
            running.reshape(micro_rows, span_len, H, HD)
            / jnp.transpose(run_sum, (0, 2, 1))[..., None]
        ).reshape(micro_rows, span_len, width)
        log_sum = run_max + jnp.log(run_sum)
        attended_low = attended.astype(jnp.bfloat16).reshape(-1, width)
        mixed_out = plain_dot(attended_low, output_weight) + output_bias
        middle = values_in + branch * mixed_out.reshape(values_in.shape)
        second_norm, second_pull = jax.vjp(layer_norm, middle, second_gain, second_shift)
        second_low = second_norm.astype(jnp.bfloat16).reshape(-1, width)
        expanded = plain_dot(second_low, expand_weight) + expand_bias
        hidden, gelu_pull = jax.vjp(gelu_tanh, expanded)
        hidden_low = hidden.astype(jnp.bfloat16)
        reduced = plain_dot(hidden_low, reduce_weight) + reduce_bias
        outputs_list.append(
            (middle + branch * reduced.reshape(values_in.shape)).astype(jnp.bfloat16)
        )
        reduced_grad = (branch * out_cot).reshape(-1, width).astype(jnp.bfloat16)
        totals[12] = totals[12] + jnp.sum(reduced_grad.astype(jnp.float32), 0)
        totals[11] = totals[11] + left_dot(hidden_low, reduced_grad)
        (expanded_grad,) = gelu_pull(right_dot(reduced_grad, reduce_weight))
        expanded_low = expanded_grad.astype(jnp.bfloat16)
        totals[10] = totals[10] + jnp.sum(expanded_low.astype(jnp.float32), 0)
        totals[9] = totals[9] + left_dot(second_low, expanded_low)
        norm_in_grad = right_dot(expanded_low, expand_weight).reshape(values_in.shape)
        middle_part, gain_part, shift_part = second_pull(norm_in_grad)
        totals[7] = totals[7] + gain_part
        totals[8] = totals[8] + shift_part
        middle_grad = out_cot + middle_part
        mixed_grad = (branch * middle_grad).reshape(-1, width).astype(jnp.bfloat16)
        totals[6] = totals[6] + jnp.sum(mixed_grad.astype(jnp.float32), 0)
        totals[5] = totals[5] + left_dot(attended_low, mixed_grad)
        attended_grad = (
            right_dot(mixed_grad, output_weight)
            .astype(jnp.bfloat16)
            .reshape(micro_rows, span_len, H, HD)
        )
        delta = jnp.transpose(
            jnp.sum(
                attended_grad.astype(jnp.float32) * attended.reshape(micro_rows, span_len, H, HD),
                -1,
            ),
            (0, 2, 1),
        )
        query_grad, key_grad, value_grad = grad_block(
            queries,
            attended_grad,
            log_sum,
            delta,
            own_block,
            query_seg,
            query_places,
            position * span_len,
        )

        def cycle_backward(step_index, carry):
            block, partial_value, query_acc = carry
            block = passed_along((block[0], block[1], block[2]), "seq", 1)
            partial_value = (
                from_behind(partial_value[0].astype(jnp.bfloat16), "seq", 1).astype(jnp.float32),
                from_behind(partial_value[1].astype(jnp.bfloat16), "seq", 1).astype(jnp.float32),
            )
            source = (position - step_index) % cycle_size

            def work(current):
                partial_in, query_in = current
                query_part, key_part, value_part = grad_block(
                    queries,
                    attended_grad,
                    log_sum,
                    delta,
                    block,
                    query_seg,
                    query_places,
                    source * span_len,
                )
                return (
                    (partial_in[0] + key_part, partial_in[1] + value_part),
                    query_in + query_part,
                )

            partial_value, query_acc = lax.cond(
                source < position, work, lambda current: current, (partial_value, query_acc)
            )
            return (block, partial_value, query_acc)

        unused_block, partial_value, query_grad = lax.fori_loop(
            1, cycle_size, cycle_backward, (own_block, (key_grad, value_grad), query_grad)
        )
        key_grad, value_grad = (
            from_behind(partial_value[0].astype(jnp.bfloat16), "seq", 1).astype(jnp.float32),
            from_behind(partial_value[1].astype(jnp.bfloat16), "seq", 1).astype(jnp.float32),
        )
        qkv_grad = (
            jnp.concatenate([query_grad, key_grad, value_grad], -1)
            .reshape(-1, 3 * width)
            .astype(jnp.bfloat16)
        )
        totals[3] = totals[3] + jnp.sum(qkv_grad[:, :width].astype(jnp.float32), 0)
        totals[4] = totals[4] + jnp.sum(qkv_grad[:, 2 * width :].astype(jnp.float32), 0)
        totals[2] = totals[2] + left_dot(normed_low, qkv_grad)
        norm_grad = right_dot(qkv_grad, input_weight).reshape(values_in.shape)
        input_part, gain_one, shift_one = first_pull(norm_grad)
        totals[0] = totals[0] + gain_one
        totals[1] = totals[1] + shift_one
        grads_list.append(middle_grad + input_part)
    summed = lax.psum(
        (
            totals[0],
            totals[1],
            totals[2],
            totals[3],
            totals[4],
            totals[5],
            totals[6],
            totals[7],
            totals[8],
            totals[9],
            totals[10],
            totals[11],
            totals[12],
        ),
        ("dp", "seq"),
    )
    return (
        jnp.concatenate(outputs_list, 0),
        jnp.concatenate(grads_list, 0),
        summed[0],
        summed[1],
        summed[2],
        summed[3],
        summed[4],
        summed[5],
        summed[6],
        summed[7],
        summed[8],
        summed[9],
        summed[10],
        summed[11],
        summed[12],
    )


def local_rows(
    activations,
    segments,
    first_gain,
    first_shift,
    input_weight,
    query_bias,
    value_bias,
    output_weight,
    output_bias,
    second_gain,
    second_shift,
    expand_weight,
    expand_bias,
    reduce_weight,
    reduce_bias,
    cotangent,
):
    rows, span, width = activations.shape
    mine = lax.axis_index("seq")
    half = mine.astype(jnp.int32)[None]
    core = lax.axis_index("dp").astype(jnp.int32)[None] % 2
    place = jnp.concatenate([half, core])
    take = lambda array, index: lax.dynamic_index_in_dim(array, index, 0, keepdims=False)
    row = lambda vector: vector.reshape(1, -1)

    def beside(stack):
        blocks = stack.shape[0] // width
        return jnp.concatenate([stack[n * width : (n + 1) * width] for n in range(blocks)], 1).astype(F32)

    seg_got = swapped(take(segments, 1 - mine))
    x_got = swapped(after(take(activations, 1 - mine), seg_got))
    bias = jnp.concatenate([query_bias, jnp.zeros_like(query_bias), value_bias])
    gain, shift = row(first_gain), row(first_shift)
    weights = (gain, shift, input_weight, row(bias))
    start, table = documents(place, row(take(segments, mine)), row(seg_got), BLOCK)
    *before, norms = project(True, after(place, table), activations, *weights, (), span)
    cot_got = swapped(after(take(cotangent, 1 - mine), (x_got, norms)))
    q, k, v, more = project(False, place, x_got, *weights, before, span)
    att_t, lse = attend(table, q, k, v, start, norms, more, BLOCK)
    tokens = (x_got, activations, cot_got, cotangent)
    out_bias, gain_two = row(output_bias), row(second_gain)
    hid, exg, keep, send, vec_expand = feed_part(
        place, att_t, *tokens, output_weight, out_bias, gain_two, row(second_shift), expand_weight,
        row(expand_bias), reduce_weight, TILE, CHUNK,
    )

    core_hop, plane, line, pair = hops()
    one, two = ([hop] for hop in plane)
    sums = AllSum(keep, send, core_hop)
    result, result_send, mid_grad, att_grad, delta, d_output, vec = sums.beside(
        lambda place: middle_part(
            place, att_t, *tokens, hid, exg, output_weight, out_bias, gain_two, expand_weight,
            reduce_weight, row(reduce_bias), TILE,
        ),
        place, sums.split,
    )
    result_got = swapped(result_send)
    grads = []
    for first, ways in ((0, (one, two)), (H // 2, (two, one))):
        call = lambda table: attend_back(
            first, H // 2, table, q, k, v, att_grad, start, lse, delta, BLOCK
        )
        grads.append(sums.beside(call, table, sums.cross, *ways))
    grads = [[g[n] for g in grads] for n in range(3)]
    keep, send = sums.beside(
        lambda place: weight_part(place, grads, x_got, activations, gain, shift, d_output, span),
        after(place, result_got), sums.narrow, line + pair,
    )
    keep, send = after((keep, send), sums.state)
    tail = AllSum(keep, send, core_hop)
    tail.split()
    ready = after(place, tail.state)
    tail.narrow(plane)
    grad, grad_send, vec_last = last_part(
        ready, grads, x_got, activations, mid_grad, gain, input_weight, TILE
    )
    tail.state = after(tail.state, grad)
    sums.widen(line + pair, vec_last)
    vectors = jnp.concatenate([vec[:4], vec_expand[:4], vec_last], 0).astype(BF)
    sums.uncross(two, one)
    tail.meet(pair)
    tail.ride(vectors, pair)
    grad_got = swapped(after(grad_send, (tail.state, tail.whole)))
    tail.state = after(tail.state, sums.state)
    tail.narrow(line)
    sums.uncross(one, two)
    d_reduce, d_expand = sums.join()
    tail.widen(line)
    tail.widen(plane, grad_got)
    d_reduce, d_expand = d_reduce.astype(F32), beside(d_expand)
    tail.widen(core_hop, (d_reduce, d_expand))
    dw = tail.state[0]
    put = lambda whole, got: lax.dynamic_update_index_in_dim(
        whole, got.astype(whole.dtype), 1 - mine, 0
    )
    vectors = tail.whole.astype(F32)
    return (
        put(result, result_got),
        put(grad, grad_got),
        vectors[8],
        vectors[9],
        beside(dw[: 3 * width]),
        vectors[10],
        vectors[11],
        dw[3 * width :].astype(F32),
        vectors[2],
        vectors[0],
        vectors[1],
        d_expand,
        vectors[4:8].reshape(-1),
        d_reduce,
        vectors[3],
    )


TILE = 512
CHUNK = 256
BLOCK = 512
SMALL = 60.0
FORWARD_HEADS = 4
BACKWARD_HEADS = 4


def solution(mesh):
    sizes = dict(zip(mesh.axis_names, mesh.devices.shape))
    tokens, places, whole = P("dp", "seq", None), P("dp", "seq"), P()
    in_specs = (tokens, places) + (whole,) * 13 + (tokens,)
    out_specs = (tokens, tokens) + (whole,) * 13

    def program(activations, *rest):
        rows = activations.shape[0] // sizes["dp"]
        span = activations.shape[1] // sizes["seq"]
        by_rows = sizes["seq"] == 2 and rows == 2 and span % BLOCK == 0 and sizes["dp"] == 16
        return jax.shard_map(
            local_rows if by_rows else local,
            mesh=mesh,
            in_specs=in_specs,
            out_specs=out_specs,
            check_vma=False,
        )(activations, *rest)

    return program
```

```python
import functools

import jax
import jax.numpy as jnp
from jax import lax
from jax.experimental import pallas as pl
from jax.experimental.pallas import tpu as pltpu
from jax.sharding import PartitionSpec as P

H = 8
HD = 64
DEPTH = 48
MICRO = 2
EPSILON = 1e-05
NEGATIVE = -1e30
BRANCH = DEPTH ** (-0.5)
SCALE = HD ** (-0.5)
SCALE2 = SCALE * 1.4426950408889634
GELU_A = 0.7978845608028654
GELU_B = GELU_A * 0.044715

BF = jnp.bfloat16
F32 = jnp.float32
NN = (((1,), (0,)), ((), ()))
NT = (((1,), (1,)), ((), ()))
VMEM_LIMIT = 58 << 20
SHORT = pl.CostEstimate(flops=1000, bytes_accessed=1000, transcendentals=0)


def mm(left, right, dims=NN):
    return lax.dot_general(left, right, dims, preferred_element_type=F32)


def shape_of(dims, dtype):
    return jax.ShapeDtypeStruct(dims, dtype)


def params(limit=VMEM_LIMIT):
    return pltpu.CompilerParams(vmem_limit_bytes=limit)


def norm_parts(values):
    center = jnp.mean(values, -1, keepdims=True)
    centered = values - center
    variance = jnp.mean(centered * centered, -1, keepdims=True)
    scale = lax.rsqrt(variance + EPSILON)
    return centered * scale, scale


def norm_back(grad, unit, scale, gain):
    inner = grad * gain
    first = jnp.mean(inner, -1, keepdims=True)
    second = jnp.mean(inner * unit, -1, keepdims=True)
    return scale * (inner - first - unit * second)


def own_and_got(tiles):
    part = tiles // 2
    return (
        lambda t, h: (t + (1 - h[0]) * part) % tiles,
        lambda t, h: jnp.minimum(t, part - 1),
        lambda t, h: jnp.maximum(t - part, 0),
    )


def row_specs(tile, width, tiles):
    where, got, own = own_and_got(tiles)
    return (
        pl.BlockSpec((tile, width), lambda t, h: (got(t, h), 0)),
        pl.BlockSpec((1, tile, width), lambda t, h: (h[0], own(t, h), 0)),
    )


def either(got_ref, own_ref):
    early = pl.program_id(0) < pl.num_programs(0) // 2
    return jnp.where(early, got_ref[...], own_ref[0])


def once(array):
    return pl.BlockSpec(array.shape, lambda t, *_: (0,) * array.ndim, pipeline_mode=pl.Buffered(1))


def kept(dims):
    return pl.BlockSpec(dims, lambda t, *_: (0,) * len(dims))


def largest_norms(block):
    lane = lax.broadcasted_iota(jnp.int32, (block.shape[1], 128), 1)
    column = lax.broadcasted_iota(jnp.int32, (block.shape[1], 128), 0)
    member = jnp.where(column // HD == lane, 1.0, 0.0).astype(BF)
    wide = block.astype(F32)
    return jnp.max(mm((wide * wide).astype(BF), member), 0, keepdims=True)


def project_kernel(place, x_ref, gain_ref, shift_ref, weight_ref, bias_ref, *refs):
    q_ref, k_ref, v_ref, norm_ref = refs[-4:]
    width = weight_ref.shape[0]
    unit, _ = norm_parts(x_ref[...].reshape(-1, width).astype(F32))
    normed = (unit * gain_ref[...] + shift_ref[...]).astype(BF)

    @pl.when(pl.program_id(0) == 0)
    def _():
        norm_ref[...] = jnp.zeros(norm_ref.shape, F32)

    for n, ref in enumerate((q_ref, k_ref, v_ref)):
        cols = slice(n * width, (n + 1) * width)
        out = (mm(normed, weight_ref[:, cols]) + bias_ref[:, cols]).astype(BF)
        ref[...] = out
        if n < 2:
            norm_ref[n : n + 1, :] = jnp.maximum(norm_ref[n : n + 1, :], largest_norms(out))


def project(own, half, x, gain, shift, weight, bias, before, tile):
    span, width = x.shape[-2:]
    count = span // tile
    length = 2 * span
    if own:
        x_spec = pl.BlockSpec((1, tile, width), lambda t, h: (h[0], t, 0))
        here = lambda h: h[0]
    else:
        x_spec = pl.BlockSpec((tile, width), lambda t, h: (t, 0))
        here = lambda h: 1 - h[0]
    rows = pl.BlockSpec((tile, width), lambda t, h: (here(h) * count + t, 0))
    nat = shape_of((length, width), BF)
    return pl.pallas_call(
        project_kernel,
        grid_spec=pltpu.PrefetchScalarGridSpec(
            num_scalar_prefetch=1,
            grid=(count,),
            in_specs=[x_spec, once(gain), once(shift), once(weight), once(bias)]
            + [pl.BlockSpec(memory_space=pl.ANY)] * len(before),
            out_specs=[rows, rows, rows, kept((8, 128))],
        ),
        out_shape=[nat, nat, nat, shape_of((8, 128), F32)],
        input_output_aliases={6 + i: i for i in range(len(before))},
        compiler_params=params(),
        name="project",
    )(half, x, gain, shift, weight, bias, *before)


def document_kernel(size, half_ref, own_ref, got_ref, start_ref, table_ref):
    span = own_ref.shape[1]
    place = lambda half: pl.ds(pl.multiple_of(half * span, span), span)
    start_ref[0:1, place(half_ref[0])] = own_ref[...]
    start_ref[0:1, place(1 - half_ref[0])] = got_ref[...]
    numbers = start_ref[...]
    start = jnp.zeros_like(numbers)
    for number in range(1, 8):
        before = jnp.sum((numbers < number).astype(jnp.int32), 1, keepdims=True)
        start = jnp.where(numbers == number, before, start)
    start_ref[...] = start
    count = start.shape[1] // size
    slots = table_ref.shape[0] - 1
    for slot in range(slots):
        table_ref[slot] = 0
    filled = jnp.int32(0)
    for i in range(count):
        block = start[:, i * size : (i + 1) * size]
        low, high = jnp.min(block), jnp.max(block)
        for j in range(i + 1):
            kind = jnp.where(high > j * size, 2, 1 if i == j else 0)
            active = low < (j + 1) * size

            table_ref[filled] = jnp.where(active, i + 256 * j + 65536 * kind, 0)
            filled = filled + active.astype(jnp.int32)
    table_ref[slots] = filled


def documents(half, own, got, size):
    length = 2 * own.shape[1]
    count = length // size
    row = lambda wide: pl.BlockSpec((1, wide), lambda t, h: (0, 0))
    return pl.pallas_call(
        functools.partial(document_kernel, size),
        grid_spec=pltpu.PrefetchScalarGridSpec(
            num_scalar_prefetch=1,
            grid=(1,),
            in_specs=[row(length // 2), row(length // 2)],
            out_specs=[row(length), pl.BlockSpec(memory_space=pltpu.SMEM)],
        ),
        out_shape=[
            shape_of((1, length), jnp.int32),
            shape_of((count * (count + 1) // 2 + 2,), jnp.int32),
        ],
        compiler_params=params(),
        name="documents",
    )(half, own, got)


def head_half(block, head):
    lane = lax.broadcasted_iota(jnp.int32, block.shape, 1)
    keep = (lane < HD) if head % 2 == 0 else (lane >= HD)
    return jnp.where(keep, block, jnp.zeros_like(block))


def lanes_of(heads, group, head):
    low = HD * heads * group + 2 * HD * (head // 2)
    return pl.ds(pl.multiple_of(low, 2 * HD), 2 * HD)


def rows_of(heads, group, head):
    return pl.ds(pl.multiple_of(HD * heads * group + HD * head, HD), HD)


class Blocks:
    def __init__(self, size, list_ref, start_ref, mask_ref, values):
        self.size, self.list = size, list_ref
        self.start, self.mask, self.values = start_ref, mask_ref, values

    def at(self, index):
        return pl.ds(pl.multiple_of(index * self.size, self.size), self.size)

    def places(self):
        dims = (self.size, self.size)
        return lax.broadcasted_iota(jnp.int32, dims, 0), lax.broadcasted_iota(jnp.int32, dims, 1)

    def fill(self, slot, i, j):
        key, query = self.places()
        key, query = key + j * self.size, query + i * self.size
        allowed = (key >= self.start[0:1, self.at(i)]) & (key <= query)
        self.mask[slot] = jnp.where(allowed, *self.values).astype(self.mask.dtype)

    def entry(self, step):
        packed = self.list[step]
        kind = packed // 65536
        return packed % 256, (packed // 256) % 256, jnp.where(kind == 2, 2 + lax.rem(step, 2), kind)

    def prepare(self, slot, i, j):
        pl.when(slot >= 2)(lambda: self.fill(slot, i, j))

    def walk(self, variants, heads, loops, early, late, row_begin, step_end, row_end):
        steps = self.list[self.list.shape[0] - 1]
        self.mask[0] = jnp.full(self.mask.shape[1:], self.values[0], self.mask.dtype)
        key, query = self.places()
        self.mask[1] = jnp.where(key <= query, *self.values).astype(self.mask.dtype)
        i, j, slot = self.entry(0)
        self.prepare(slot, i, j)
        row_begin(i)
        zero = jnp.int32(0)
        early(zero, 0, i, j, slot, False)

        def body(turn, carry):
            i, j, slot = carry
            group = lax.rem(turn, loops)
            last = group == loops - 1
            after = self.entry(turn // loops + 1)
            ni, nj, nslot = (jnp.where(last, new, old) for new, old in zip(after, carry))
            ngroup = jnp.where(last, 0, group + 1)
            pl.when(last)(lambda: self.prepare(nslot, ni, nj))
            pl.when(ni > i)(lambda: row_begin(ni))

            def work(corner, slot):
                for head in range(heads):
                    if head + 1 < heads:
                        early(group, head + 1, i, j, slot, corner)
                    else:
                        early(ngroup, 0, ni, nj, nslot, False)
                    late(group, head, i, j, corner)

            if variants == 1:
                work(False, slot)
            elif variants == 2:
                pl.when(i != j)(lambda: work(False, slot))
                pl.when(i == j)(lambda: work(True, slot))
            else:
                pl.when(slot == 0)(lambda: work(False, None))
                pl.when((slot > 0) & (i == j))(lambda: work(True, slot))
                pl.when((slot > 0) & (i != j))(lambda: work(False, slot))

            @pl.when(last)
            def _():
                step_end(i, j)
                pl.when(j == i)(lambda: row_end(i))

            return ni, nj, nslot

        lax.fori_loop(0, steps * loops, body, (i, j, slot))


def pieces(corner, size):
    if not corner:
        return [(slice(0, size), slice(0, size))]
    mid = size // 2
    return [(slice(0, mid), slice(0, size)), (slice(mid, size), slice(mid, size))]


def part_at(size, index, part):
    low = index * size + part.start
    return pl.ds(pl.multiple_of(low, size // 2), part.stop - part.start)


class Blockwise:
    def __init__(self, size, first, source, target, sems):
        self.size, self.first = size, first
        self.source, self.target, self.sems = source, target, sems

    def copy(self, block):
        rows = pl.ds(pl.multiple_of(block * self.size, self.size), self.size)
        lanes = pl.ds(self.first, self.target.shape[1])
        return pltpu.make_async_copy(
            self.source.at[rows, lanes], self.target.at[rows, :], self.sems.at[block]
        )


def forward_kernel(
    size, list_ref, q_hbm, k_hbm, v_hbm, start_ref, one_ref, two_ref, out_hbm, lse_ref, q_ref, k_ref, v_ref,
    vt_ref, stage_ref, in_sems, out_sems, max_ref, new_ref, acc_ref, bias_ref, mask_ref, *slots,
):
    heads = FORWARD_HEADS
    loops = H // heads
    scores, probs_of = slots[:heads], slots[heads:]
    plain = Blocks(size, list_ref, start_ref, mask_ref, (1.0, 0.0))
    general = Blocks(size, list_ref, start_ref, bias_ref, (0.0, NEGATIVE))
    at = plain.at
    count = q_ref.shape[0] // size
    loads = [
        Blockwise(size, 0, source, target, in_sems.at[n])
        for n, (source, target) in enumerate(((k_hbm, k_ref), (q_hbm, q_ref), (v_hbm, v_ref)))
    ]
    for block in range(count):
        for load in loads:
            load.copy(block).start()

    def store(i):
        cols = pl.ds(pl.multiple_of(i * size, size), size)
        return pltpu.make_async_copy(stage_ref.at[:, cols], out_hbm.at[:, cols], out_sems.at[i])

    def row_begin(i):
        for load in loads:
            load.copy(i).wait()
        vt_ref[:, at(i)] = v_ref[at(i), :].T

    def products(group, head, i, j, keys, queries):
        lanes = lanes_of(heads, group, head)
        block = head_half(k_ref[part_at(size, j, keys), lanes], head)
        return mm(block, q_ref[part_at(size, i, queries), lanes], NT)

    def values(group, head, j, keys):
        block = vt_ref[rows_of(heads, group, head), part_at(size, j, keys)]
        return jnp.concatenate([block, jnp.ones((16, keys.stop - keys.start), BF)], 0)

    def early_plain(group, head, i, j, slot, corner):
        for keys, queries in pieces(corner, size):
            probs = jnp.exp2(products(group, head, i, j, keys, queries) * SCALE2).astype(BF)
            if slot is not None:
                probs = probs * mask_ref[slot, keys, queries]
            probs_of[head][keys, queries] = probs

    def late_plain(group, head, i, j, corner):
        for keys, queries in pieces(corner, size):
            acc_ref[heads * group + head, :, queries] += mm(values(group, head, j, keys), probs_of[head][keys, queries])

    whole = slice(0, size)

    def early(group, head, i, j, slot, corner):
        s = products(group, head, i, j, whole, whole)
        if slot is not None:
            s = s + bias_ref[slot]
        scores[head][...] = s
        new_ref[heads * group + head] = jnp.max(s, 0, keepdims=True)

    def late(group, head, i, j, corner):
        place = heads * group + head
        old = max_ref[place]
        new = jnp.maximum(old, new_ref[place])
        max_ref[place] = new
        probs = jnp.exp2(scores[head][...] * SCALE2 - new * SCALE2)
        factor = jnp.exp2((old - new) * SCALE2)
        acc_ref[place] = acc_ref[place] * factor + mm(
            values(group, head, j, whole), probs.astype(BF)
        )

    def reset(largest):
        max_ref[...] = jnp.full(max_ref.shape, largest, F32)
        acc_ref[...] = jnp.zeros(acc_ref.shape, F32)

    def row_end(largest, i):
        def one(head, carry):
            total = acc_ref[head, HD : HD + 1, :]
            rows = pl.ds(pl.multiple_of(HD * head, HD), HD)
            stage_ref[rows, at(i)] = (acc_ref[head, :HD, :] * (1.0 / total)).astype(BF)
            lse_ref[head, :, at(i)] = max_ref[head] * SCALE2 + jnp.log2(total)
            return carry

        lax.fori_loop(0, H, one, 0)
        store(i).start()
        reset(largest)

    def run(variants, blocks, largest, early, late):
        reset(largest)
        blocks.walk(
            variants, heads, loops, early, late, row_begin, lambda i, j: None, functools.partial(row_end, largest)
        )

    norms = jnp.maximum(one_ref[...], two_ref[...])
    limit = jnp.max(norms[0:1] * norms[1:2]) * (SCALE2 * SCALE2)
    small = limit < SMALL * SMALL
    pl.when(small)(lambda: run(2, plain, 0.0, early_plain, late_plain))
    pl.when(jnp.logical_not(small))(lambda: run(1, general, NEGATIVE, early, late))
    for i in range(count):
        store(i).wait()


def attend(table, q, k, v, start, norms, more, size):
    length, width = q.shape
    count = length // size
    far = pl.BlockSpec(memory_space=pl.ANY)
    near = pltpu.VMEM((length, width), BF)
    return pl.pallas_call(
        functools.partial(forward_kernel, size),
        grid_spec=pltpu.PrefetchScalarGridSpec(
            num_scalar_prefetch=1,
            grid=(1,),
            in_specs=[far, far, far, once(start), once(norms), once(more)],
            out_specs=[far, kept((H, 1, length))],
            scratch_shapes=[
                near,
                near,
                near,
                pltpu.VMEM((width, length), BF),
                pltpu.VMEM((width, length), BF),
                pltpu.SemaphoreType.DMA((3, count)),
                pltpu.SemaphoreType.DMA((count,)),
                pltpu.VMEM((H, 1, size), F32),
                pltpu.VMEM((H, 1, size), F32),
                pltpu.VMEM((H, HD + 16, size), F32),
                pltpu.VMEM((4, size, size), F32),
                pltpu.VMEM((4, size, size), BF),
            ]
            + [pltpu.VMEM((size, size), F32)] * FORWARD_HEADS
            + [pltpu.VMEM((size, size), BF)] * FORWARD_HEADS,
        ),
        out_shape=[shape_of((width, length), BF), shape_of((H, 1, length), F32)],
        compiler_params=params(),
        name="attend",
    )(table, q, k, v, start, norms, more)


def backward_kernel(
    size, heads, loops, first, list_ref, q_hbm, k_hbm, v_hbm, do_hbm, start_ref, lse_ref, delta_ref,
    dq_hbm, dk_hbm, dv_hbm, q_ref, k_ref, v_ref, do_ref, kt_ref, dq_ref, dk_ref, dv_ref, in_sems,
    out_sems, dqt_acc, dk_acc, dv_acc, bias_ref, *slots,
):
    probs_of, grads_of = slots[:heads], slots[heads:]
    walk = Blocks(size, list_ref, start_ref, bias_ref, (0.0, NEGATIVE))
    at = walk.at
    count = q_ref.shape[0] // size
    pairs = ((k_hbm, k_ref), (q_hbm, q_ref), (v_hbm, v_ref), (do_hbm, do_ref))
    loads = [
        Blockwise(size, first * HD, source, target, in_sems.at[n])
        for n, (source, target) in enumerate(pairs)
    ]
    for block in range(count):
        for load in loads:
            load.copy(block).start()

    def store(n, block):
        source, target = ((dq_ref, dq_hbm), (dk_ref, dk_hbm), (dv_ref, dv_hbm))[n]
        rows = at(block)
        return pltpu.make_async_copy(
            source.at[rows, :], target.at[rows, :], out_sems.at[n, block]
        )

    def row_begin(i):
        for load in loads:
            load.copy(i).wait()
        kt_ref[:, at(i)] = k_ref[at(i), :].T
        dk_acc[at(i), :] = jnp.zeros((size, dk_acc.shape[1]), F32)
        dv_acc[at(i), :] = jnp.zeros((size, dv_acc.shape[1]), F32)

    def early(group, head, i, j, slot, corner):
        lanes = lanes_of(heads, group, head)
        for keys, queries in pieces(corner, size):
            at_j, at_i = part_at(size, j, keys), part_at(size, i, queries)
            stat = (first + heads * group + head, slice(None), at_i)
            s = mm(head_half(k_ref[at_j, lanes], head), q_ref[at_i, lanes], NT)
            dots = mm(head_half(v_ref[at_j, lanes], head), do_ref[at_i, lanes], NT)
            if slot is not None:
                s = s + bias_ref[slot, keys, queries]
            probs = jnp.exp2(s * SCALE2 - lse_ref[stat])
            probs_of[head][keys, queries] = probs.astype(BF)
            grads_of[head][keys, queries] = (probs * (dots - delta_ref[stat])).astype(BF)

    def late(group, head, i, j, corner):
        lanes = lanes_of(heads, group, head)
        rows = rows_of(heads, group, head)
        for keys, queries in pieces(corner, size):
            at_j, at_i = part_at(size, j, keys), part_at(size, i, queries)
            grads = grads_of[head][keys, queries]
            dv_acc[at_j, lanes] += mm(
                probs_of[head][keys, queries], head_half(do_ref[at_i, lanes], head)
            )
            dk_acc[at_j, lanes] += mm(grads, head_half(q_ref[at_i, lanes], head))
            dqt_acc[rows, queries] += mm(kt_ref[rows, at_j], grads)

    def finish(j):
        dk_ref[at(j), :] = (dk_acc[at(j), :] * SCALE).astype(BF)
        dv_ref[at(j), :] = dv_acc[at(j), :].astype(BF)
        store(1, j).start()
        store(2, j).start()

    def step_end(i, j):
        pl.when(i == count - 1)(lambda: finish(j))

    def row_end(i):
        dq_ref[at(i), :] = (dqt_acc[...] * SCALE).T.astype(BF)
        store(0, i).start()
        dqt_acc[...] = jnp.zeros(dqt_acc.shape, F32)

    dqt_acc[...] = jnp.zeros(dqt_acc.shape, F32)
    walk.walk(3, heads, loops, early, late, row_begin, step_end, row_end)
    lowest = jnp.int32(count)
    for slot in range(list_ref.shape[0] - 1):
        lowest = lowest - jnp.where(list_ref[slot] % 256 == count - 1, 1, 0)
    for j in range(count):
        pl.when(j < lowest)(functools.partial(finish, j))
    for j in range(count):
        for n in range(3):
            store(n, j).wait()


def attend_back(first, groups, table, q, k, v, do, start, lse, delta, size):
    length = q.shape[0]
    part = HD * groups
    count = length // size
    far = pl.BlockSpec(memory_space=pl.ANY)
    near = pltpu.VMEM((length, part), BF)
    pairs = count * (count + 1) // 2 * size * size * groups
    return pl.pallas_call(
        functools.partial(backward_kernel, size, BACKWARD_HEADS, groups // BACKWARD_HEADS, first),
        cost_estimate=SHORT,
        grid_spec=pltpu.PrefetchScalarGridSpec(
            num_scalar_prefetch=1,
            grid=(1,),
            in_specs=[far] * 4 + [once(start), once(lse), once(delta)],
            out_specs=[far] * 3,
            scratch_shapes=[near] * 4
            + [pltpu.VMEM((part, length), BF)]
            + [near] * 3
            + [
                pltpu.SemaphoreType.DMA((4, count)),
                pltpu.SemaphoreType.DMA((3, count)),
                pltpu.VMEM((part, size), F32),
                pltpu.VMEM((length, part), F32),
                pltpu.VMEM((length, part), F32),
                pltpu.VMEM((4, size, size), F32),
            ]
            + [pltpu.VMEM((size, size), BF)] * (2 * BACKWARD_HEADS),
        ),
        out_shape=[shape_of((length, part), BF)] * 3,
        compiler_params=params(),
        name="attend_back",
    )(table, q, k, v, do, start, lse, delta)


def feed_kernel(
    chunk, place_ref, att_ref, x_got, x_own, cot_got, cot_own, wo_ref, ob_ref, g2_ref, s2_ref, we_ref,
    eb_ref, wr_ref, hid_ref, exg_ref, keep_ref, send_ref, deb_ref, acc_ref, deb_acc, wet_ref, ebt_ref,
):
    step = pl.program_id(0)
    tile, width = x_got.shape
    total = wr_ref.shape[0]

    @pl.when(step == 0)
    def _():
        for ref in (acc_ref, deb_acc):
            ref[...] = jnp.zeros(ref.shape, F32)
        wet_ref[...] = we_ref[...].T
        ebt_ref[...] = jnp.broadcast_to(eb_ref[...], (128, total)).T

    mixed = mm(att_ref[...].T, wo_ref[...]) + ob_ref[...]
    middle = either(x_got, x_own).astype(F32) + BRANCH * mixed
    unit, _ = norm_parts(middle)
    second = (unit * g2_ref[...] + s2_ref[...]).astype(BF)
    second_t = second.T
    reduced_grad = (BRANCH * either(cot_got, cot_own).astype(F32)).astype(BF)

    def stage_one(c):
        rows = slice(c * chunk, (c + 1) * chunk)
        bias = jnp.concatenate([ebt_ref[rows, :]] * (tile // 128), 1)
        v = mm(wet_ref[rows, :], second, NT) + bias
        v2 = v * v
        t = jnp.tanh(v * (GELU_A + GELU_B * v2))
        h1 = 0.5 * t + 0.5
        gelu = v * h1
        slope = h1 + gelu * (1.0 - h1) * (2.0 * GELU_A + 6.0 * GELU_B * v2)
        hid_ref[rows, :] = gelu.astype(BF)
        grads = (mm(wr_ref[rows, :], reduced_grad, NT) * slope).astype(BF)
        exg_ref[rows, :] = grads
        wide = grads.astype(F32)
        part = wide[:, 0:128]
        for n in range(1, tile // 128):
            part = part + wide[:, n * 128 : (n + 1) * 128]
        deb_acc[rows, :] += part

    stage_one(0)
    for c in range(total // chunk):
        if (c + 1) * chunk < total:
            stage_one(c + 1)
        rows = slice(c * chunk, (c + 1) * chunk)
        acc_ref[rows, :] += mm(hid_ref[rows, :], reduced_grad)
        block, low = divmod(c * chunk, width)
        there = slice(total + block * width, total + (block + 1) * width)
        acc_ref[there, low : low + chunk] += mm(second_t, exg_ref[rows, :], NT)

    last = step == pl.num_programs(0) - 1
    halves = slice(0, total), slice(total, 2 * total)
    for core in range(2):

        @pl.when(last & (place_ref[1] == core))
        def _():
            keep_ref[...] = acc_ref[halves[core], :].astype(BF)
            send_ref[...] = acc_ref[halves[1 - core], :].astype(BF)

    @pl.when(last)
    def _():
        flat = jnp.sum(deb_acc[...].T, 0, keepdims=True)
        deb_ref[...] = jnp.zeros(deb_ref.shape, F32)
        for n in range(total // width):
            deb_ref[n : n + 1, :] = flat[:, n * width : (n + 1) * width]


def feed_part(place, att_t, x_got, x_own, cot_got, cot_own, wo, ob, g2, s2, we, eb, wr, tile, chunk):
    width, length = att_t.shape
    total = wr.shape[0]
    tiles = length // tile
    where, _, _ = own_and_got(tiles)
    pair = list(row_specs(tile, width, tiles))
    cols = lambda high: pl.BlockSpec((high, tile), lambda t, h: (0, where(t, h)))
    return pl.pallas_call(
        functools.partial(feed_kernel, chunk),
        grid_spec=pltpu.PrefetchScalarGridSpec(
            num_scalar_prefetch=1,
            grid=(tiles,),
            in_specs=[cols(width)] + pair * 2 + [once(a) for a in (wo, ob, g2, s2, we, eb, wr)],
            out_specs=[cols(total), cols(total), kept((total, width)), kept((total, width)), kept((8, width))],
            scratch_shapes=[
                pltpu.VMEM((2 * total, width), F32),
                pltpu.VMEM((total, 128), F32),
                pltpu.VMEM((total, width), BF),
                pltpu.VMEM((total, 128), F32),
            ],
        ),
        out_shape=[
            shape_of((total, length), BF),
            shape_of((total, length), BF),
            shape_of((total, width), BF),
            shape_of((total, width), BF),
            shape_of((8, width), F32),
        ],
        compiler_params=params(),
        name="feed",
    )(place, att_t, x_got, x_own, cot_got, cot_own, wo, ob, g2, s2, we, eb, wr)


def middle_kernel(
    place_ref, att_ref, x_got, x_own, cot_got, cot_own, hid_ref, exg_ref, wo_ref, ob_ref, g2_ref,
    we_ref, wr_ref, rb_ref, res_own, res_send, grad_ref, ag_ref, delta_ref, dwo_ref, vec_ref, acc_ref,
    wrt_ref,
):
    step = pl.program_id(0)
    tiles = pl.num_programs(0)

    @pl.when(step == 0)
    def _():
        for ref in (acc_ref, vec_ref):
            ref[...] = jnp.zeros(ref.shape, F32)
        wrt_ref[...] = wr_ref[...].T

    att_t = att_ref[...]
    mixed = mm(att_t.T, wo_ref[...]) + ob_ref[...]
    middle = either(x_got, x_own).astype(F32) + BRANCH * mixed
    cot = either(cot_got, cot_own).astype(F32)
    unit, scale = norm_parts(middle)
    norm_grad = mm(we_ref[...], exg_ref[...]).T
    result = (middle + BRANCH * (mm(wrt_ref[...], hid_ref[...]).T + rb_ref[...])).astype(BF)

    @pl.when(step < tiles // 2)
    def _():
        res_send[...] = result

    @pl.when(step >= tiles // 2)
    def _():
        res_own[0] = result

    middle_grad = cot + norm_back(norm_grad, unit, scale, g2_ref[...])
    grad_ref[...] = middle_grad
    mixed_grad = (BRANCH * middle_grad).astype(BF)
    acc_ref[...] += mm(att_t, mixed_grad)
    att_grad = mm(mixed_grad, wo_ref[...], NT).astype(BF)
    ag_ref[...] = att_grad
    dots = att_grad.T.astype(F32) * att_t.astype(F32)
    for head in range(H):
        delta_ref[head] = jnp.sum(dots[HD * head : HD * head + HD, :], 0, keepdims=True)
    reduced_grad = (BRANCH * cot).astype(BF)
    sums = (norm_grad * unit, norm_grad, mixed_grad.astype(F32), reduced_grad.astype(F32))
    for n, value in enumerate(sums):
        vec_ref[n : n + 1, :] += jnp.sum(value, 0, keepdims=True)

    @pl.when(step == tiles - 1)
    def _():
        dwo_ref[...] = acc_ref[...].astype(BF)


def middle_part(place, att_t, x_got, x_own, cot_got, cot_own, hid, exg, wo, ob, g2, we, wr, rb, tile):
    width, length = att_t.shape
    total = wr.shape[0]
    tiles = length // tile
    where, got, own = own_and_got(tiles)
    pair = list(row_specs(tile, width, tiles))
    rows = pl.BlockSpec((tile, width), lambda t, h: (where(t, h), 0))
    cols = lambda high: pl.BlockSpec((high, tile), lambda t, h: (0, where(t, h)))
    return pl.pallas_call(
        middle_kernel,
        cost_estimate=SHORT,
        grid_spec=pltpu.PrefetchScalarGridSpec(
            num_scalar_prefetch=1,
            grid=(tiles,),
            in_specs=[cols(width)]
            + pair * 2
            + [cols(total), cols(total)]
            + [once(a) for a in (wo, ob, g2, we, wr, rb)],
            out_specs=[
                pair[1],
                pair[0],
                rows,
                rows,
                pl.BlockSpec((H, 1, tile), lambda t, h: (0, 0, where(t, h))),
                kept((width, width)),
                kept((8, width)),
            ],
            scratch_shapes=[pltpu.VMEM((width, width), F32), pltpu.VMEM((width, total), BF)],
        ),
        out_shape=[
            shape_of((2, length // 2, width), BF),
            shape_of((length // 2, width), BF),
            shape_of((length, width), F32),
            shape_of((length, width), BF),
            shape_of((H, 1, length), F32),
            shape_of((width, width), BF),
            shape_of((8, width), F32),
        ],
        compiler_params=params(),
        name="middle",
    )(place, att_t, x_got, x_own, cot_got, cot_own, hid, exg, wo, ob, g2, we, wr, rb)


def weight_kernel(parts, place_ref, *refs):
    ins = refs[: 3 * parts]
    x_got, x_own, gain_ref, shift_ref, extra_ref, keep_ref, send_ref, acc_ref = refs[3 * parts :]
    step = pl.program_id(0)

    @pl.when(step == 0)
    def _():
        acc_ref[...] = jnp.zeros(acc_ref.shape, F32)

    width = x_got.shape[1]
    unit, _ = norm_parts(either(x_got, x_own).astype(F32))
    normed_t = (unit * gain_ref[...] + shift_ref[...]).astype(BF).T
    for n in range(3):
        grad = jnp.concatenate([ref[...] for ref in ins[n * parts : (n + 1) * parts]], 1)
        acc_ref[n * width : (n + 1) * width, :] += mm(normed_t, grad)

    last = step == pl.num_programs(0) - 1
    for core in range(2):

        @pl.when(last & (place_ref[1] == core))
        def _():
            lower, upper = (keep_ref, send_ref) if core == 0 else (send_ref, keep_ref)
            lower[...] = acc_ref[: 2 * width, :].astype(BF)
            upper[:width, :] = acc_ref[2 * width :, :].astype(BF)
            upper[width:, :] = extra_ref[...]


def weight_part(place, grads, x_got, x_own, gain, shift, extra, tile):
    span, width = x_got.shape
    tiles = 2 * span // tile
    where, _, _ = own_and_got(tiles)
    flat = [part for group in grads for part in group]
    out = shape_of((2 * width, width), BF)
    return pl.pallas_call(
        functools.partial(weight_kernel, len(grads[0])),
        cost_estimate=SHORT,
        grid_spec=pltpu.PrefetchScalarGridSpec(
            num_scalar_prefetch=1,
            grid=(tiles,),
            in_specs=[
                pl.BlockSpec((tile, a.shape[1]), lambda t, h: (where(t, h), 0)) for a in flat
            ]
            + list(row_specs(tile, width, tiles))
            + [once(a) for a in (gain, shift, extra)],
            out_specs=[kept(out.shape)] * 2,
            scratch_shapes=[pltpu.VMEM((3 * width, width), F32)],
        ),
        out_shape=[out, out],
        compiler_params=params(),
        name="weight",
    )(place, *flat, x_got, x_own, gain, shift, extra)


def last_kernel(parts, place_ref, *refs):
    ins, rest = refs[: 3 * parts], refs[3 * parts :]
    x_got, x_own, mid_ref, gain_ref, weight_ref, own_ref, send_ref, vec_ref = rest
    step = pl.program_id(0)
    tiles = pl.num_programs(0)

    @pl.when(step == 0)
    def _():
        vec_ref[...] = jnp.zeros(vec_ref.shape, F32)

    width = x_got.shape[1]
    unit, scale = norm_parts(either(x_got, x_own).astype(F32))
    back = None
    grads = []
    for n in range(3):
        grad = jnp.concatenate([ref[...] for ref in ins[n * parts : (n + 1) * parts]], 1)
        one = mm(grad, weight_ref[:, n * width : (n + 1) * width], NT)
        back = one if back is None else back + one
        grads.append(grad)
    total = mid_ref[...] + norm_back(back, unit, scale, gain_ref[...])

    @pl.when(step < tiles // 2)
    def _():
        send_ref[...] = total.astype(BF)

    @pl.when(step >= tiles // 2)
    def _():
        own_ref[0] = total

    sums = (back * unit, back, grads[0].astype(F32), grads[2].astype(F32))
    for n, value in enumerate(sums):
        vec_ref[n : n + 1, :] += jnp.sum(value, 0, keepdims=True)


def last_part(place, grads, x_got, x_own, mid, gain, weight, tile):
    length, width = mid.shape
    tiles = length // tile
    where, _, _ = own_and_got(tiles)
    rows = pl.BlockSpec((tile, width), lambda t, h: (where(t, h), 0))
    flat = [part for group in grads for part in group]
    pair = list(row_specs(tile, width, tiles))
    return pl.pallas_call(
        functools.partial(last_kernel, len(grads[0])),
        cost_estimate=SHORT,
        grid_spec=pltpu.PrefetchScalarGridSpec(
            num_scalar_prefetch=1,
            grid=(tiles,),
            in_specs=[
                pl.BlockSpec((tile, a.shape[1]), lambda t, h: (where(t, h), 0)) for a in flat
            ]
            + pair
            + [rows, once(gain), once(weight)],
            out_specs=[pair[1], pair[0], kept((8, width))],
        ),
        out_shape=[
            shape_of((2, length // 2, width), F32),
            shape_of((length // 2, width), BF),
            shape_of((8, width), F32),
        ],
        compiler_params=params(),
        name="last",
    )(place, *flat, x_got, x_own, mid, gain, weight)


def swapped(value):
    return lax.ppermute(value, "seq", [(0, 1), (1, 0)])


def side(hop):
    axis, bit = hop
    return (lax.axis_index(axis) // bit) % 2


def place_of(hops):
    place = 0
    for hop in hops:
        place = 2 * place + side(hop)
    return place


def exchanged(value, hops):
    axes = tuple(dict.fromkeys(axis for axis, _ in hops))
    flips = [sum(bit for axis, bit in hops if axis == name) for name in axes]
    sizes = [lax.axis_size(name) for name in axes]
    if len(axes) == 1:
        return lax.ppermute(value, axes[0], [(i, i ^ flips[0]) for i in range(sizes[0])])
    pairs = [
        (i * sizes[1] + j, (i ^ flips[0]) * sizes[1] + (j ^ flips[1]))
        for i in range(sizes[0])
        for j in range(sizes[1])
    ]
    return lax.ppermute(value, axes, pairs)


def partners(hops):
    count = len(hops)
    return [
        ([hop for n, hop in enumerate(hops) if (flip >> (count - 1 - n)) & 1], flip)
        for flip in range(1, 1 << count)
    ]


def added(*values):
    total = values[0].astype(F32)
    for value in values[1:]:
        total = total + value.astype(F32)
    return total.astype(BF)


def scatter(part, hops):
    rows = part.shape[1] >> len(hops)
    mine = place_of(hops)
    piece = lambda place: lax.dynamic_slice_in_dim(part, place * rows, rows, 1)
    got = [exchanged(piece(mine ^ flip), chosen) for chosen, flip in partners(hops)]
    return added(piece(mine), *got)


def gather(part, hops, whole=None, first=()):
    mine = place_of(hops)
    blocks, rows, width = part.shape
    got, others = [(part, mine)], []
    for chosen, flip in partners(hops):
        if whole is None:
            got.append((after(exchanged(part, chosen), first), mine ^ flip))
            continue
        both = exchanged(jnp.concatenate([part.reshape(-1, width), whole], 0), chosen)
        both = after(both, first)
        got.append((both[: blocks * rows].reshape(part.shape), mine ^ flip))
        others.append(both[blocks * rows :])
    if len(hops) == 1:
        one, two = got[0][0], got[1][0]
        out = jnp.where(mine == 0, jnp.concatenate([one, two], 1), jnp.concatenate([two, one], 1))
    else:
        out = jnp.zeros((blocks, rows << len(hops), width), part.dtype)
        for piece, place in got:
            out = lax.dynamic_update_slice_in_dim(out, piece, place * rows, 1)
    return out if whole is None else (out, added(whole, *others))


def hops():
    found = []
    for axis in ("dp", "seq"):
        size = lax.axis_size(axis)
        found.append([(axis, 1 << n) for n in range(size.bit_length() - 1)])
    core, one, two, far = found[0]
    return [core], [one, two], [far], found[1]


class AllSum:
    def __init__(self, keep, send, core):
        self.core, self.whole = core, None
        self.state = (keep[None], send[None])

    def split(self):
        keep, send = self.state
        self.state = added(keep, exchanged(send, self.core))

    def cross(self, one, two):
        if not isinstance(self.state, tuple):
            mid = self.state.shape[1] // 2
            self.state = (self.state[:, :mid], self.state[:, mid:])
        self.state = tuple(scatter(part, hops) for part, hops in zip(self.state, (one, two)))

    def uncross(self, one, two):
        if not isinstance(self.state, tuple):
            self.state = (self.state[:1], self.state[1:])
        self.state = tuple(gather(part, hops) for part, hops in zip(self.state, (one, two)))

    def join(self, first=()):
        part = self.state
        if isinstance(part, tuple):
            part = jnp.concatenate(part, 1)
        got = after(exchanged(part, self.core), first)
        lower = place_of(self.core) == 0
        return jnp.where(lower, part, got)[0], jnp.where(lower, got, part)[0]

    def ride(self, whole, hops):
        self.whole = added(whole, exchanged(whole, hops))

    def narrow(self, hops):
        if isinstance(self.state, tuple):
            self.state = jnp.concatenate(self.state, 0)
        self.state = scatter(self.state, hops)

    def meet(self, hops):
        self.state = added(self.state, exchanged(self.state, hops))

    def widen(self, hops, first=()):
        if self.whole is None:
            self.state = gather(self.state, hops, None, first)
        else:
            self.state, self.whole = gather(self.state, hops, self.whole, first)

    def beside(self, call, argument, step, *hops):
        argument = after(argument, self.state)
        step(*hops)
        out = call(argument)
        self.state = after(self.state, out)
        return out


def after(value, earlier):
    return lax.optimization_barrier((value, earlier))[0] if jax.tree.leaves(earlier) else value


def passed_along(block, axis, distance):
    devices = range(lax.axis_size(axis))
    route = [(i - distance, i) for i in devices if i - distance in devices]
    return lax.ppermute(block, axis, route)


def from_behind(value, axis, steps):
    count = lax.axis_size(axis)
    pairs = [(source, (source + steps) % count) for source in range(count)]
    return lax.ppermute(value, axis, pairs)


def layer_norm(values, gain_vec, shift_vec):
    center = jnp.mean(values, -1, keepdims=True)
    centered = values - center
    variance = jnp.mean(centered * centered, -1, keepdims=True)
    return centered * lax.rsqrt(variance + EPSILON) * gain_vec + shift_vec


def gelu_tanh(values):
    return jax.nn.gelu(values, approximate=True)


def plain_dot(left, right):
    return jnp.dot(left, right, preferred_element_type=jnp.float32)


def left_dot(left, right):
    return lax.dot_general(
        left, right, (((0,), (0,)), ((), ())), preferred_element_type=jnp.float32
    )


def right_dot(left, right):
    return lax.dot_general(
        left, right, (((1,), (1,)), ((), ())), preferred_element_type=jnp.float32
    )


def block_scores(queries, keys_block, query_seg, key_seg, query_places, key_start):
    row_count, key_len, width = keys_block.shape
    keys_heads = keys_block.reshape(row_count, key_len, H, HD)
    scores = jnp.einsum(
        "rqhd,rkhd->rhqk", queries, keys_heads, preferred_element_type=jnp.float32
    ) * HD ** (-0.5)
    key_places = key_start + jnp.arange(key_len, dtype=jnp.int32)
    allowed = (query_seg[:, None, :, None] == key_seg[:, None, None, :]) & (
        key_places[None, None, None, :] <= query_places[None, None, :, None]
    )
    return (scores, allowed)


def attend_block(state, queries, block, query_seg, query_places, key_start):
    run_max, run_sum, running = state
    keys_block, values_block, key_seg = block
    row_count, key_len, width = values_block.shape
    query_len = queries.shape[1]
    scores, allowed = block_scores(queries, keys_block, query_seg, key_seg, query_places, key_start)
    block_max = jnp.max(jnp.where(allowed, scores, NEGATIVE), -1)
    new_max = jnp.maximum(run_max, block_max)
    exponent = jnp.where(allowed, jnp.exp(scores - new_max[..., None]), 0.0)
    factor = jnp.exp(run_max - new_max)
    new_sum = run_sum * factor + jnp.sum(exponent, -1)
    values_heads = values_block.reshape(row_count, key_len, H, HD)
    addition = jnp.einsum(
        "rhqk,rkhd->rqhd",
        exponent.astype(jnp.bfloat16),
        values_heads,
        preferred_element_type=jnp.float32,
    )
    scaled = (
        running.reshape(row_count, query_len, H, HD) * jnp.transpose(factor, (0, 2, 1))[..., None]
    )
    return (new_max, new_sum, (scaled + addition).reshape(row_count, query_len, width))


def grad_block(queries, out_grad, log_sum, delta, block, query_seg, query_places, key_start):
    keys_block, values_block, key_seg = block
    row_count, key_len, width = keys_block.shape
    scores, allowed = block_scores(queries, keys_block, query_seg, key_seg, query_places, key_start)
    weights_block = jnp.where(allowed, jnp.exp(scores - log_sum[..., None]), 0.0)
    keys_heads = keys_block.reshape(row_count, key_len, H, HD)
    values_heads = values_block.reshape(row_count, key_len, H, HD)
    value_dots = jnp.einsum(
        "rqhd,rkhd->rhqk", out_grad, values_heads, preferred_element_type=jnp.float32
    )
    score_grad = (weights_block * (value_dots - delta[..., None]) * HD ** (-0.5)).astype(
        jnp.bfloat16
    )
    query_part = jnp.einsum(
        "rhqk,rkhd->rqhd", score_grad, keys_heads, preferred_element_type=jnp.float32
    ).reshape(row_count, -1, width)
    key_part = jnp.einsum(
        "rhqk,rqhd->rkhd", score_grad, queries, preferred_element_type=jnp.float32
    ).reshape(row_count, key_len, width)
    value_part = jnp.einsum(
        "rhqk,rqhd->rkhd",
        weights_block.astype(jnp.bfloat16),
        out_grad,
        preferred_element_type=jnp.float32,
    ).reshape(row_count, key_len, width)
    return (query_part, key_part, value_part)


def local(
    activations,
    segments,
    first_gain,
    first_shift,
    input_weight,
    query_bias,
    value_bias,
    output_weight,
    output_bias,
    second_gain,
    second_shift,
    expand_weight,
    expand_bias,
    reduce_weight,
    reduce_bias,
    cotangent,
):
    row_total, span_len, width = activations.shape
    cycle_size = lax.axis_size("seq")
    position = lax.axis_index("seq")
    micro_rows = row_total // MICRO
    branch = DEPTH ** (-0.5)
    bias_all = jnp.concatenate([query_bias, jnp.zeros_like(query_bias), value_bias])
    query_places = position * span_len + jnp.arange(span_len, dtype=jnp.int32)
    totals = [
        jnp.zeros(argument.shape, jnp.float32)
        for argument in (
            first_gain,
            first_shift,
            input_weight,
            query_bias,
            value_bias,
            output_weight,
            output_bias,
            second_gain,
            second_shift,
            expand_weight,
            expand_bias,
            reduce_weight,
            reduce_bias,
        )
    ]
    outputs_list = []
    grads_list = []
    for micro in range(MICRO):
        lower = micro * micro_rows
        values_in = activations[lower : lower + micro_rows].astype(jnp.float32)
        query_seg = segments[lower : lower + micro_rows]
        out_cot = cotangent[lower : lower + micro_rows].astype(jnp.float32)
        normed, first_pull = jax.vjp(layer_norm, values_in, first_gain, first_shift)
        normed_low = normed.astype(jnp.bfloat16).reshape(-1, width)
        projected = (plain_dot(normed_low, input_weight) + bias_all).astype(jnp.bfloat16)
        queries = projected[:, :width].reshape(micro_rows, span_len, H, HD)
        keys_own = projected[:, width : 2 * width].reshape(micro_rows, span_len, width)
        values_own = projected[:, 2 * width :].reshape(micro_rows, span_len, width)
        own_block = (keys_own, values_own, query_seg)
        start_state = (
            jnp.full((micro_rows, H, span_len), NEGATIVE, jnp.float32),
            jnp.zeros((micro_rows, H, span_len), jnp.float32),
            jnp.zeros((micro_rows, span_len, width), jnp.float32),
        )
        state = attend_block(
            start_state, queries, own_block, query_seg, query_places, position * span_len
        )

        def cycle_forward(step_index, carry):
            block, inner_state = carry
            block = passed_along((block[0], block[1], block[2]), "seq", 1)
            source = (position - step_index) % cycle_size
            inner_state = lax.cond(
                source < position,
                lambda current: attend_block(
                    current, queries, block, query_seg, query_places, source * span_len
                ),
                lambda current: current,
                inner_state,
            )
            return (block, inner_state)

        unused_block, state = lax.fori_loop(1, cycle_size, cycle_forward, (own_block, state))
        run_max, run_sum, running = state
        attended = (
            running.reshape(micro_rows, span_len, H, HD)
            / jnp.transpose(run_sum, (0, 2, 1))[..., None]
        ).reshape(micro_rows, span_len, width)
        log_sum = run_max + jnp.log(run_sum)
        attended_low = attended.astype(jnp.bfloat16).reshape(-1, width)
        mixed_out = plain_dot(attended_low, output_weight) + output_bias
        middle = values_in + branch * mixed_out.reshape(values_in.shape)
        second_norm, second_pull = jax.vjp(layer_norm, middle, second_gain, second_shift)
        second_low = second_norm.astype(jnp.bfloat16).reshape(-1, width)
        expanded = plain_dot(second_low, expand_weight) + expand_bias
        hidden, gelu_pull = jax.vjp(gelu_tanh, expanded)
        hidden_low = hidden.astype(jnp.bfloat16)
        reduced = plain_dot(hidden_low, reduce_weight) + reduce_bias
        outputs_list.append(
            (middle + branch * reduced.reshape(values_in.shape)).astype(jnp.bfloat16)
        )
        reduced_grad = (branch * out_cot).reshape(-1, width).astype(jnp.bfloat16)
        totals[12] = totals[12] + jnp.sum(reduced_grad.astype(jnp.float32), 0)
        totals[11] = totals[11] + left_dot(hidden_low, reduced_grad)
        (expanded_grad,) = gelu_pull(right_dot(reduced_grad, reduce_weight))
        expanded_low = expanded_grad.astype(jnp.bfloat16)
        totals[10] = totals[10] + jnp.sum(expanded_low.astype(jnp.float32), 0)
        totals[9] = totals[9] + left_dot(second_low, expanded_low)
        norm_in_grad = right_dot(expanded_low, expand_weight).reshape(values_in.shape)
        middle_part, gain_part, shift_part = second_pull(norm_in_grad)
        totals[7] = totals[7] + gain_part
        totals[8] = totals[8] + shift_part
        middle_grad = out_cot + middle_part
        mixed_grad = (branch * middle_grad).reshape(-1, width).astype(jnp.bfloat16)
        totals[6] = totals[6] + jnp.sum(mixed_grad.astype(jnp.float32), 0)
        totals[5] = totals[5] + left_dot(attended_low, mixed_grad)
        attended_grad = (
            right_dot(mixed_grad, output_weight)
            .astype(jnp.bfloat16)
            .reshape(micro_rows, span_len, H, HD)
        )
        delta = jnp.transpose(
            jnp.sum(
                attended_grad.astype(jnp.float32) * attended.reshape(micro_rows, span_len, H, HD),
                -1,
            ),
            (0, 2, 1),
        )
        query_grad, key_grad, value_grad = grad_block(
            queries,
            attended_grad,
            log_sum,
            delta,
            own_block,
            query_seg,
            query_places,
            position * span_len,
        )

        def cycle_backward(step_index, carry):
            block, partial_value, query_acc = carry
            block = passed_along((block[0], block[1], block[2]), "seq", 1)
            partial_value = (
                from_behind(partial_value[0].astype(jnp.bfloat16), "seq", 1).astype(jnp.float32),
                from_behind(partial_value[1].astype(jnp.bfloat16), "seq", 1).astype(jnp.float32),
            )
            source = (position - step_index) % cycle_size

            def work(current):
                partial_in, query_in = current
                query_part, key_part, value_part = grad_block(
                    queries,
                    attended_grad,
                    log_sum,
                    delta,
                    block,
                    query_seg,
                    query_places,
                    source * span_len,
                )
                return (
                    (partial_in[0] + key_part, partial_in[1] + value_part),
                    query_in + query_part,
                )

            partial_value, query_acc = lax.cond(
                source < position, work, lambda current: current, (partial_value, query_acc)
            )
            return (block, partial_value, query_acc)

        unused_block, partial_value, query_grad = lax.fori_loop(
            1, cycle_size, cycle_backward, (own_block, (key_grad, value_grad), query_grad)
        )
        key_grad, value_grad = (
            from_behind(partial_value[0].astype(jnp.bfloat16), "seq", 1).astype(jnp.float32),
            from_behind(partial_value[1].astype(jnp.bfloat16), "seq", 1).astype(jnp.float32),
        )
        qkv_grad = (
            jnp.concatenate([query_grad, key_grad, value_grad], -1)
            .reshape(-1, 3 * width)
            .astype(jnp.bfloat16)
        )
        totals[3] = totals[3] + jnp.sum(qkv_grad[:, :width].astype(jnp.float32), 0)
        totals[4] = totals[4] + jnp.sum(qkv_grad[:, 2 * width :].astype(jnp.float32), 0)
        totals[2] = totals[2] + left_dot(normed_low, qkv_grad)
        norm_grad = right_dot(qkv_grad, input_weight).reshape(values_in.shape)
        input_part, gain_one, shift_one = first_pull(norm_grad)
        totals[0] = totals[0] + gain_one
        totals[1] = totals[1] + shift_one
        grads_list.append(middle_grad + input_part)
    summed = lax.psum(
        (
            totals[0],
            totals[1],
            totals[2],
            totals[3],
            totals[4],
            totals[5],
            totals[6],
            totals[7],
            totals[8],
            totals[9],
            totals[10],
            totals[11],
            totals[12],
        ),
        ("dp", "seq"),
    )
    return (
        jnp.concatenate(outputs_list, 0),
        jnp.concatenate(grads_list, 0),
        summed[0],
        summed[1],
        summed[2],
        summed[3],
        summed[4],
        summed[5],
        summed[6],
        summed[7],
        summed[8],
        summed[9],
        summed[10],
        summed[11],
        summed[12],
    )


def local_rows(
    activations,
    segments,
    first_gain,
    first_shift,
    input_weight,
    query_bias,
    value_bias,
    output_weight,
    output_bias,
    second_gain,
    second_shift,
    expand_weight,
    expand_bias,
    reduce_weight,
    reduce_bias,
    cotangent,
):
    rows, span, width = activations.shape
    mine = lax.axis_index("seq")
    half = mine.astype(jnp.int32)[None]
    core = lax.axis_index("dp").astype(jnp.int32)[None] % 2
    place = jnp.concatenate([half, core])
    take = lambda array, index: lax.dynamic_index_in_dim(array, index, 0, keepdims=False)
    row = lambda vector: vector.reshape(1, -1)

    def beside(stack):
        blocks = stack.shape[0] // width
        return jnp.concatenate([stack[n * width : (n + 1) * width] for n in range(blocks)], 1).astype(F32)

    seg_got = swapped(take(segments, 1 - mine))
    x_got = swapped(after(take(activations, 1 - mine), seg_got))
    bias = jnp.concatenate([query_bias, jnp.zeros_like(query_bias), value_bias])
    gain, shift = row(first_gain), row(first_shift)
    weights = (gain, shift, input_weight, row(bias))
    start, table = documents(place, row(take(segments, mine)), row(seg_got), BLOCK)
    *before, norms = project(True, after(place, table), activations, *weights, (), span)
    cot_got = swapped(after(take(cotangent, 1 - mine), (x_got, norms)))
    q, k, v, more = project(False, place, x_got, *weights, before, span)
    att_t, lse = attend(table, q, k, v, start, norms, more, BLOCK)
    tokens = (x_got, activations, cot_got, cotangent)
    out_bias, gain_two = row(output_bias), row(second_gain)
    hid, exg, keep, send, vec_expand = feed_part(
        place, att_t, *tokens, output_weight, out_bias, gain_two, row(second_shift), expand_weight,
        row(expand_bias), reduce_weight, TILE, CHUNK,
    )

    core_hop, plane, line, pair = hops()
    one, two = ([hop] for hop in plane)
    sums = AllSum(keep, send, core_hop)
    result, result_send, mid_grad, att_grad, delta, d_output, vec = sums.beside(
        lambda place: middle_part(
            place, att_t, *tokens, hid, exg, output_weight, out_bias, gain_two, expand_weight,
            reduce_weight, row(reduce_bias), TILE,
        ),
        place, sums.split,
    )
    result_got = swapped(result_send)
    grads = []
    for first, ways in ((0, (one, two)), (H // 2, (two, one))):
        call = lambda table: attend_back(
            first, H // 2, table, q, k, v, att_grad, start, lse, delta, BLOCK
        )
        grads.append(sums.beside(call, table, sums.cross, *ways))
    grads = [[g[n] for g in grads] for n in range(3)]
    keep, send = sums.beside(
        lambda place: weight_part(place, grads, x_got, activations, gain, shift, d_output, span),
        after(place, result_got), sums.narrow, line + pair,
    )
    keep, send = after((keep, send), sums.state)
    tail = AllSum(keep, send, core_hop)
    tail.split()
    ready = after(place, tail.state)
    tail.narrow(plane)
    grad, grad_send, vec_last = last_part(
        ready, grads, x_got, activations, mid_grad, gain, input_weight, TILE
    )
    tail.state = after(tail.state, grad)
    sums.widen(line + pair, vec_last)
    vectors = jnp.concatenate([vec[:4], vec_expand[:4], vec_last], 0).astype(BF)
    sums.uncross(two, one)
    tail.meet(pair)
    tail.ride(vectors, pair)
    tail.ride(tail.whole, core_hop)
    grad_got = swapped(after(grad_send, (tail.state, tail.whole)))
    tail.state = after(tail.state, sums.state)
    tail.narrow(line)
    sums.uncross(one, two)
    d_reduce, d_expand = sums.join()
    tail.widen(line)
    tail.widen(plane, grad_got)
    d_reduce, d_expand = d_reduce.astype(F32), beside(d_expand)
    d_keys, d_values = tail.join((d_reduce, d_expand))
    put = lambda whole, got: lax.dynamic_update_index_in_dim(
        whole, got.astype(whole.dtype), 1 - mine, 0
    )
    vectors = tail.whole.astype(F32)
    return (
        put(result, result_got),
        put(grad, grad_got),
        vectors[8],
        vectors[9],
        jnp.concatenate([beside(d_keys), d_values[:width].astype(F32)], 1),
        vectors[10],
        vectors[11],
        d_values[width:].astype(F32),
        vectors[2],
        vectors[0],
        vectors[1],
        d_expand,
        vectors[4:8].reshape(-1),
        d_reduce,
        vectors[3],
    )


TILE = 512
CHUNK = 256
BLOCK = 512
SMALL = 60.0
FORWARD_HEADS = 4
BACKWARD_HEADS = 4


def solution(mesh):
    sizes = dict(zip(mesh.axis_names, mesh.devices.shape))
    tokens, places, whole = P("dp", "seq", None), P("dp", "seq"), P()
    in_specs = (tokens, places) + (whole,) * 13 + (tokens,)
    out_specs = (tokens, tokens) + (whole,) * 13

    def program(activations, *rest):
        rows = activations.shape[0] // sizes["dp"]
        span = activations.shape[1] // sizes["seq"]
        by_rows = sizes["seq"] == 2 and rows == 2 and span % BLOCK == 0 and sizes["dp"] == 16
        return jax.shard_map(
            local_rows if by_rows else local,
            mesh=mesh,
            in_specs=in_specs,
            out_specs=out_specs,
            check_vma=False,
        )(activations, *rest)

    return program
```
